32 devices in a mesh: section: 4 (over y, x), dp: 8 (over z, core).
Axes of the slice: x: 2, y: 2, z: 4, core: 2. Of those that a mesh axis runs over, the one named last changes fastest.
Arguments:
- state_start: float32 [32, 15, 1024], P('dp'), may hold values from -6 to 6
- static_maps: float32 [75, 1024], replicated, may hold values from -6 to 6
- grouping: int32 [8, 4], P('dp'), may hold values from 0 to 3, each once within a row
- cotangent: float32 [4, 32, 15, 1024], P('section', 'dp'), may hold values from -6 to 6
- w_input: float32 [9, 100, 128], replicated, may hold values from -0.1875 to 0.1875
- b_input: float32 [128], replicated, may hold values from -3 to 3
- w_first: float32 [9, 128, 128], replicated, may hold values from -0.1875 to 0.1875
- gain_first: float32 [128], replicated, may hold values from 0.1 to 1.9
- shift_first: float32 [128], replicated, may hold values from -3 to 3
- w_second: float32 [9, 128, 128], replicated, may hold values from -0.1875 to 0.1875
- gain_second: float32 [128], replicated, may hold values from 0.1 to 1.9
- shift_second: float32 [128], replicated, may hold values from -3 to 3
- w_query: float32 [128, 128], replicated, may hold values from -0.5 to 0.5
- w_key: float32 [128, 128], replicated, may hold values from -0.5 to 0.5
- w_value: float32 [128, 128], replicated, may hold values from -0.5 to 0.5
- w_mixer: float32 [128, 128], replicated, may hold values from -1.5 to 1.5
- w_velocity: float32 [9, 128, 10], replicated, may hold values from -0.1875 to 0.1875
- b_velocity: float32 [10], replicated, may hold values from -3 to 3
Outputs:
- trajectory: float32 [4, 32, 15, 1024], P('section', 'dp')
- state_grads: float32 [4, 32, 15, 1024], P('section', 'dp')
- grad_w_input: float32 [9, 100, 128], replicated
- grad_b_input: float32 [128], replicated
- grad_w_first: float32 [9, 128, 128], replicated
- grad_gain_first: float32 [128], replicated
- grad_shift_first: float32 [128], replicated
- grad_w_second: float32 [9, 128, 128], replicated
- grad_gain_second: float32 [128], replicated
- grad_shift_second: float32 [128], replicated
- grad_w_query: float32 [128, 128], replicated
- grad_w_key: float32 [128, 128], replicated
- grad_w_value: float32 [128, 128], replicated
- grad_w_mixer: float32 [128, 128], replicated
- grad_w_velocity: float32 [9, 128, 10], replicated
- grad_b_velocity: float32 [10], replicated
The draws below stay inside these ranges and needn't reach their ends.
Inputs may be any that keep to these rules, and one draw needn't show every extreme that they name: `grouping`: each row is an ordering of the 4 samples of one dp index.
All inputs are finite; a program needn't handle non-finite values.
Results may differ from the reference program's by a relative error of at most 0.0003.
Values sent between devices are 32-bit elements; how exact they have to be, the bound alone decides.
No kernel may reach another device: no remote copies, remote signals or barrier semaphores. Data moves between devices by JAX's collectives and lax.ppermute only.
A program may use at most 192 MiB of HBM per device.

```python
import math
import jax
import jax.numpy as jnp
from jax import lax

QUANT = 5
STATIC_CH = 75
CH = 128
HEADS = 4
LAT = 16
LON = 64
ATT_ROWS = 8
MB_SAMP = 2
C_IN = 100
STEPS = 4
MICRO = 2
SAMP_DEV = 4
SAMPLES = 32
N_DP = 8


def steps_of(rng, dims, pieces, low, top_value):
    gain, own = 1.0, jax.random.fold_in(rng, 6)
    for dim, parts in pieces:
        heights = jnp.exp(jax.random.uniform(jax.random.fold_in(own, dim), (parts,), jnp.float32, low / len(pieces), top_value / len(pieces)))
        gain = gain * jnp.repeat(heights, dims[dim] // parts).reshape([-1 if axis == dim else 1 for axis in range(len(dims))])
    return gain


def gaussian(key, dims, width, reach, cuts=(), kind=jnp.bfloat16):
    entries = width * jax.random.normal(key, dims, jnp.float32)
    if cuts:
        entries = entries * steps_of(key, dims, cuts, -0.22, 0.18)
    return jnp.clip(entries, -reach, reach).astype(kind)


def setup_inputs(seed: int = 0) -> dict:
    streams_of = jax.random.split(jax.random.key(seed), 19)
    state_start = gaussian(streams_of[0], (SAMPLES, 3 * QUANT, LAT * LON), 1.0, 6.0, ((0, 8),), jnp.float32)
    static_maps = gaussian(streams_of[1], (STATIC_CH, LAT * LON), 1.0, 6.0, (), jnp.float32)
    grouping = jax.vmap(lambda own: jax.random.permutation(own, SAMP_DEV))(jax.random.split(streams_of[2], N_DP)).reshape((N_DP, SAMP_DEV)).astype(jnp.int32)
    cotangent = gaussian(streams_of[3], (STEPS, SAMPLES, 3 * QUANT, LAT * LON), 1.0, 6.0, ((0, 4), (1, 8)), jnp.float32)
    w_input = gaussian(streams_of[4], (9, C_IN, CH), (9 * C_IN) ** -0.5, 0.1875, (), jnp.float32)
    b_input = gaussian(streams_of[5], (CH,), 0.5, 3.0, (), jnp.float32)
    w_first = gaussian(streams_of[6], (9, CH, CH), (9 * CH) ** -0.5, 0.1875, (), jnp.float32)
    gain_first = jnp.clip(1.0 + 0.18 * jax.random.normal(streams_of[7], (CH,), jnp.float32), 0.1, 1.9)
    shift_first = gaussian(streams_of[8], (CH,), 0.5, 3.0, (), jnp.float32)
    w_second = gaussian(streams_of[9], (9, CH, CH), (9 * CH) ** -0.5, 0.1875, (), jnp.float32)
    gain_second = jnp.clip(1.0 + 0.18 * jax.random.normal(streams_of[10], (CH,), jnp.float32), 0.1, 1.9)
    shift_second = gaussian(streams_of[11], (CH,), 0.5, 3.0, (), jnp.float32)
    w_query = gaussian(streams_of[12], (CH, CH), CH ** -0.5, 0.5, (), jnp.float32)
    w_key = gaussian(streams_of[13], (CH, CH), CH ** -0.5, 0.5, (), jnp.float32)
    w_value = gaussian(streams_of[14], (CH, CH), CH ** -0.5, 0.5, (), jnp.float32)
    w_mixer = gaussian(streams_of[15], (CH, CH), (CH // 8) ** -0.5, 1.5, (), jnp.float32)
    w_velocity = gaussian(streams_of[16], (9, CH, 2 * QUANT), (9 * CH) ** -0.5, 0.1875, (), jnp.float32)
    b_velocity = gaussian(streams_of[17], (2 * QUANT,), 0.5, 3.0, (), jnp.float32)
    return {"state_start": state_start, "static_maps": static_maps, "grouping": grouping, "cotangent": cotangent, "w_input": w_input, "b_input": b_input, "w_first": w_first, "gain_first": gain_first, "shift_first": shift_first, "w_second": w_second, "gain_second": gain_second, "shift_second": shift_second, "w_query": w_query, "w_key": w_key, "w_value": w_value, "w_mixer": w_mixer, "w_velocity": w_velocity, "b_velocity": b_velocity}


HIGHEST = lax.Precision.HIGHEST
EPSILON = 1e-05

def convolve(inputs, weight, lat_rows):
    count_items, pixels, channels = inputs.shape
    lon_cols = pixels // lat_rows
    planes = inputs.reshape(count_items, lat_rows, lon_cols, channels)
    padded = jnp.pad(planes, ((0, 0), (1, 1), (0, 0), (0, 0)))
    padded = jnp.concatenate([padded[:, :, -1:], padded, padded[:, :, :1]], axis=2)
    patches = jnp.concatenate([padded[:, row_off:row_off + lat_rows, col_off:col_off + lon_cols] for row_off in range(3) for col_off in range(3)], axis=3)
    patches = patches.reshape(count_items, pixels, 9 * channels)
    return jnp.dot(patches, weight.reshape(9 * channels, weight.shape[2]), precision=HIGHEST)

def differences(values, lat_rows):
    count_items, quantities, pixels = values.shape
    planes = values.reshape(count_items, quantities, lat_rows, pixels // lat_rows)
    along_lon = 0.5 * (jnp.roll(planes, -1, axis=3) - jnp.roll(planes, 1, axis=3))
    padded = jnp.pad(planes, ((0, 0), (0, 0), (1, 1), (0, 0)))
    along_lat = 0.5 * (padded[:, :, 2:] - padded[:, :, :-2])
    return (along_lon.reshape(values.shape), along_lat.reshape(values.shape))

def inlet_part(state_in, static_maps, w_input, b_input, w_first, lat_rows):
    quantities = state_in.shape[1] // 3
    along_lon, along_lat = differences(state_in[:, :quantities], lat_rows)
    statics = jnp.broadcast_to(static_maps[None], (state_in.shape[0],) + static_maps.shape)
    stacked = jnp.concatenate([state_in, along_lon, along_lat, statics], axis=1)
    inputs = jnp.swapaxes(stacked, 1, 2)
    act_one = jax.nn.silu(convolve(inputs, w_input, lat_rows) + b_input)
    return (act_one, convolve(act_one, w_first, lat_rows))

def middle_part(pre_one, total_one, squares_one, gain_first, shift_first, w_second, count, lat_rows):
    average = total_one / count
    spread = squares_one / count - average * average
    normed = gain_first * (pre_one - average) * lax.rsqrt(spread + EPSILON) + shift_first
    return convolve(jax.nn.silu(normed), w_second, lat_rows)

def attend(act_two, w_query, w_key, w_value, w_mixer, block_size, head_count):
    count_items, pixels, channels = act_two.shape
    blocks = act_two.reshape(count_items * pixels // block_size, block_size, channels)
    head_width = channels // head_count

    def project(weight):
        return jnp.dot(blocks, weight, precision=HIGHEST).reshape(blocks.shape[0], block_size, head_count, head_width)
    query_rows, key_rows, value_rows = (project(w_query), project(w_key), project(w_value))
    scores = jnp.einsum('bqhd,bkhd->bhqk', query_rows, key_rows, precision=HIGHEST) / math.sqrt(head_width)
    scores = scores - lax.optimization_barrier(jnp.max(scores, axis=3, keepdims=True))
    probs = jnp.exp(scores)
    probs = probs / lax.optimization_barrier(jnp.sum(probs, axis=3, keepdims=True))
    mixed_rows = jnp.einsum('bhqk,bkhd->bqhd', probs, value_rows, precision=HIGHEST).reshape(blocks.shape[0], block_size, channels)
    return jnp.dot(mixed_rows, w_mixer, precision=HIGHEST).reshape(act_two.shape)

def outlet_part(state_in, act_one, pre_two, total_two, squares_two, gain_second, shift_second, w_query, w_key, w_value, w_mixer, w_velocity, b_velocity, count, lat_rows, block_size, head_count, step_size):
    average = total_two / count
    spread = squares_two / count - average * average
    act_two = act_one + gain_second * (pre_two - average) * lax.rsqrt(spread + EPSILON) + shift_second
    act_three = act_two + attend(act_two, w_query, w_key, w_value, w_mixer, block_size, head_count)
    forcing = jnp.swapaxes(convolve(act_three, w_velocity, lat_rows) + b_velocity, 1, 2)
    quantities = state_in.shape[1] // 3
    amount = state_in[:, :quantities]
    flows = state_in[:, quantities:]
    flux_lon, unused_lat = differences(amount * state_in[:, quantities:2 * quantities], lat_rows)
    unused_lon, flux_lat = differences(amount * state_in[:, 2 * quantities:], lat_rows)
    new_amount = amount - step_size * (flux_lon + flux_lat)
    new_flows = flows + step_size * (forcing - flows)
    return jnp.concatenate([new_amount, new_flows], axis=1)

def reference(state_start, static_maps, grouping, cotangent, w_input, b_input, w_first, gain_first, shift_first, w_second, gain_second, shift_second, w_query, w_key, w_value, w_mixer, w_velocity, b_velocity):
    count = float(N_DP * MB_SAMP * LAT * LON)
    step_size = 2.0 / STEPS
    block_size = ATT_ROWS * LON
    order = (jnp.arange(N_DP, dtype=jnp.int32)[:, None] * SAMP_DEV + grouping).astype(jnp.int32)
    order = order.reshape(N_DP, MICRO, MB_SAMP).transpose(1, 0, 2).reshape(MICRO, N_DP * MB_SAMP)
    flat_order = order.reshape(-1)
    params = (w_input, b_input, w_first, gain_first, shift_first, w_second, gain_second, shift_second, w_query, w_key, w_value, w_mixer, w_velocity, b_velocity)

    def one_step(state_in, params):
        act_one, pre_one = inlet_part(state_in, static_maps, params[0], params[1], params[2], LAT)
        total_one = lax.optimization_barrier(jnp.sum(pre_one, axis=(0, 1)))
        squares_one = lax.optimization_barrier(jnp.sum(pre_one * pre_one, axis=(0, 1)))
        pre_two = middle_part(pre_one, total_one, squares_one, params[3], params[4], params[5], count, LAT)
        total_two = lax.optimization_barrier(jnp.sum(pre_two, axis=(0, 1)))
        squares_two = lax.optimization_barrier(jnp.sum(pre_two * pre_two, axis=(0, 1)))
        return outlet_part(state_in, act_one, pre_two, total_two, squares_two, params[6], params[7], params[8], params[9], params[10], params[11], params[12], params[13], count, LAT, block_size, HEADS, step_size)
    stepper = jax.checkpoint(one_step)

    def forward(start, probes, params):
        state_now = start[order]
        path_list = []
        for step_index in range(STEPS):
            state_now = state_now + probes[step_index][order]
            state_now = jax.vmap(stepper, in_axes=(0, None))(state_now, params)
            path_list.append(state_now)
        return jnp.stack(path_list)
    probes = jnp.zeros(cotangent.shape, jnp.float32)
    grouped_path, pull_back = jax.vjp(forward, state_start, probes, params)
    path = jnp.zeros(cotangent.shape, jnp.float32).at[:, flat_order].set(grouped_path.reshape(cotangent.shape))
    unused_start, probe_grads, param_grads = pull_back(cotangent[:, order])
    return (path, probe_grads, param_grads[0], param_grads[1], param_grads[2], param_grads[3], param_grads[4], param_grads[5], param_grads[6], param_grads[7], param_grads[8], param_grads[9], param_grads[10], param_grads[11], param_grads[12], param_grads[13])
```

```python
import math

import jax
import jax.numpy as jnp
from jax import lax
from jax.sharding import PartitionSpec as P

HEADS = 4
LAT = 16
ATT_ROWS = 8


HIGHEST = lax.Precision.HIGHEST
EPSILON = 1e-05


def passed_along(value, axis, steps):
    count = lax.axis_size(axis)
    first, last = (max(0, -steps), min(count, count - steps))
    return lax.ppermute(value, axis, [(source, source + steps) for source in range(first, last)])


def convolve(inputs, weight, lat_rows):
    count_items, pixels, channels = inputs.shape
    lon_cols = pixels // lat_rows
    planes = inputs.reshape(count_items, lat_rows, lon_cols, channels)
    padded = jnp.pad(planes, ((0, 0), (1, 1), (0, 0), (0, 0)))
    padded = jnp.concatenate([padded[:, :, -1:], padded, padded[:, :, :1]], axis=2)
    patches = jnp.concatenate(
        [
            padded[:, row_off : row_off + lat_rows, col_off : col_off + lon_cols]
            for row_off in range(3)
            for col_off in range(3)
        ],
        axis=3,
    )
    patches = patches.reshape(count_items, pixels, 9 * channels)
    return jnp.dot(patches, weight.reshape(9 * channels, weight.shape[2]), precision=HIGHEST)


def differences(values, lat_rows):
    count_items, quantities, pixels = values.shape
    planes = values.reshape(count_items, quantities, lat_rows, pixels // lat_rows)
    along_lon = 0.5 * (jnp.roll(planes, -1, axis=3) - jnp.roll(planes, 1, axis=3))
    padded = jnp.pad(planes, ((0, 0), (0, 0), (1, 1), (0, 0)))
    along_lat = 0.5 * (padded[:, :, 2:] - padded[:, :, :-2])
    return (along_lon.reshape(values.shape), along_lat.reshape(values.shape))


def inlet_part(state_in, static_maps, w_input, b_input, w_first, lat_rows):
    quantities = state_in.shape[1] // 3
    along_lon, along_lat = differences(state_in[:, :quantities], lat_rows)
    statics = jnp.broadcast_to(static_maps[None], (state_in.shape[0],) + static_maps.shape)
    stacked = jnp.concatenate([state_in, along_lon, along_lat, statics], axis=1)
    inputs = jnp.swapaxes(stacked, 1, 2)
    act_one = jax.nn.silu(convolve(inputs, w_input, lat_rows) + b_input)
    return (act_one, convolve(act_one, w_first, lat_rows))


def middle_part(
    pre_one, total_one, squares_one, gain_first, shift_first, w_second, count, lat_rows
):
    average = total_one / count
    spread = squares_one / count - average * average
    normed = gain_first * (pre_one - average) * lax.rsqrt(spread + EPSILON) + shift_first
    return convolve(jax.nn.silu(normed), w_second, lat_rows)


def attend(act_two, w_query, w_key, w_value, w_mixer, block_size, head_count):
    count_items, pixels, channels = act_two.shape
    blocks = act_two.reshape(count_items * pixels // block_size, block_size, channels)
    head_width = channels // head_count

    def project(weight):
        return jnp.dot(blocks, weight, precision=HIGHEST).reshape(
            blocks.shape[0], block_size, head_count, head_width
        )

    query_rows, key_rows, value_rows = (project(w_query), project(w_key), project(w_value))
    scores = jnp.einsum("bqhd,bkhd->bhqk", query_rows, key_rows, precision=HIGHEST) / math.sqrt(
        head_width
    )
    scores = scores - jnp.max(scores, axis=3, keepdims=True)
    probs = jnp.exp(scores)
    probs = probs / jnp.sum(probs, axis=3, keepdims=True)
    mixed_rows = jnp.einsum("bhqk,bkhd->bqhd", probs, value_rows, precision=HIGHEST).reshape(
        blocks.shape[0], block_size, channels
    )
    return jnp.dot(mixed_rows, w_mixer, precision=HIGHEST).reshape(act_two.shape)


def outlet_part(
    state_in,
    act_one,
    pre_two,
    total_two,
    squares_two,
    gain_second,
    shift_second,
    w_query,
    w_key,
    w_value,
    w_mixer,
    w_velocity,
    b_velocity,
    count,
    lat_rows,
    block_size,
    head_count,
    step_size,
):
    average = total_two / count
    spread = squares_two / count - average * average
    act_two = (
        act_one + gain_second * (pre_two - average) * lax.rsqrt(spread + EPSILON) + shift_second
    )
    act_three = act_two + attend(act_two, w_query, w_key, w_value, w_mixer, block_size, head_count)
    forcing = jnp.swapaxes(convolve(act_three, w_velocity, lat_rows) + b_velocity, 1, 2)
    quantities = state_in.shape[1] // 3
    amount = state_in[:, :quantities]
    flows = state_in[:, quantities:]
    flux_lon, unused_lat = differences(amount * state_in[:, quantities : 2 * quantities], lat_rows)
    unused_lon, flux_lat = differences(amount * state_in[:, 2 * quantities :], lat_rows)
    new_amount = amount - step_size * (flux_lon + flux_lat)
    new_flows = flows + step_size * (forcing - flows)
    return jnp.concatenate([new_amount, new_flows], axis=1)


def patches_of(inputs, lat_rows):
    count_items, pixels, channels = inputs.shape
    lon_cols = pixels // lat_rows
    planes = inputs.reshape(count_items, lat_rows, lon_cols, channels)
    padded = jnp.pad(planes, ((0, 0), (1, 1), (0, 0), (0, 0)))
    padded = jnp.concatenate([padded[:, :, -1:], padded, padded[:, :, :1]], axis=2)
    patches = jnp.concatenate(
        [
            padded[:, row_off : row_off + lat_rows, col_off : col_off + lon_cols]
            for row_off in range(3)
            for col_off in range(3)
        ],
        axis=3,
    )
    return patches.reshape(count_items, pixels, 9 * channels)


def shift_along(value, axis, steps):
    count = lax.axis_size(axis)
    return lax.ppermute(value, axis, [(own, (own + steps) % count) for own in range(count)])


def butterfly(value):
    pairs = [(own, own ^ 1) for own in range(lax.axis_size("section"))]
    reach = 1
    while reach < lax.axis_size("dp"):
        value = value + lax.ppermute(
            value, "dp", [(own, own ^ reach) for own in range(lax.axis_size("dp"))]
        )
        reach *= 2
    return value + lax.ppermute(value, "section", pairs)


def slotted(value, micro_slot, micro_count):
    wide = jnp.zeros((micro_count,) + value.shape, value.dtype)
    wide = lax.dynamic_update_index_in_dim(wide, value, micro_slot, 0)
    summed = lax.psum(wide, ("section", "dp"))
    return lax.dynamic_index_in_dim(summed, micro_slot, 0, keepdims=False)


def on_device(
    state_start,
    static_maps,
    grouping,
    cotangent,
    *weights_all,
):
    segments = lax.axis_size("section")
    segment_rank = lax.axis_index("section")
    micro_count = segments // 2
    per_micro = state_start.shape[0] // micro_count
    pixels = state_start.shape[2]
    count = float(per_micro * pixels * lax.axis_size("dp"))
    step_size = 2.0 / segments
    block_size = ATT_ROWS * (pixels // LAT)
    local_order = grouping[0]
    micro_slot = segment_rank // per_micro
    cot_local = cotangent[0]
    w_input, b_input, w_first, gain_first, shift_first, w_second = weights_all[:6]
    rest = weights_all[6:]
    quantities = state_start.shape[1] // 3
    moving = 5 * quantities

    def place(offset):
        return lax.rem(segment_rank + offset + segments, segments)

    def pick(array, index):
        return lax.dynamic_index_in_dim(array, index, 0, keepdims=False)

    got = [pick(cot_local, local_order[segment_rank])]
    for offset in range(1, segments):
        mine = pick(cot_local, local_order[place(offset)])
        got.append(shift_along(mine, "section", offset))
    got = jnp.stack(got)

    state = pick(state_start, local_order[segment_rank])[None]
    w_moving = w_input[:, :moving]
    w_static = w_input[:, moving:]
    static_patches = patches_of(jnp.swapaxes(static_maps, 0, 1)[None], LAT)[0]
    static_part = jnp.dot(static_patches, w_static.reshape(-1, w_static.shape[2]), precision=HIGHEST)

    def inlet(state_in, static_in, w_moving, b_input, w_first):
        along_lon, along_lat = differences(state_in[:, :quantities], LAT)
        inputs = jnp.swapaxes(jnp.concatenate([state_in, along_lon, along_lat], axis=1), 1, 2)
        act_one = jax.nn.silu(convolve(inputs, w_moving, LAT) + static_in[None] + b_input)
        return (act_one, convolve(act_one, w_first, LAT))

    def middle(pre_one, sums, gain_first, shift_first, w_second):
        return middle_part(
            pre_one, sums[0], sums[1], gain_first, shift_first, w_second, count, LAT
        )

    def outlet(state_in, act_one, pre_two, sums, *rest):
        return outlet_part(
            state_in, act_one, pre_two, sums[0], sums[1], *rest, count, LAT, block_size, HEADS, step_size
        )

    def sums_of(pre):
        return jnp.stack([jnp.sum(pre, axis=(0, 1)), jnp.sum(pre * pre, axis=(0, 1))])

    def forward(state_in, unused):
        act_one, pre_one = inlet(state_in, static_part, w_moving, b_input, w_first)
        sums_one = slotted(sums_of(pre_one), micro_slot, micro_count)
        pre_two = middle(pre_one, sums_one, gain_first, shift_first, w_second)
        sums_two = slotted(sums_of(pre_two), micro_slot, micro_count)
        state_out = outlet(state_in, act_one, pre_two, sums_two, *rest)
        return state_out, (state_in, state_out[0], act_one, pre_one, pre_two, sums_one, sums_two)

    unused_last, (entered, path, acts_one, pres_one, pres_two, all_sums_one, all_sums_two) = lax.scan(
        forward, state, None, length=segments
    )

    def to_steps(values):
        stacked = values
        back = [pick(stacked, segment_rank)]
        for offset in range(1, segments):
            back.append(shift_along(pick(stacked, place(offset)), "section", offset))
        back = jnp.stack(back)
        senders = local_order[lax.rem(segment_rank - jnp.arange(segments) + segments, segments)]
        return jnp.take(back, jnp.argsort(senders), axis=0)[None]

    path_out = to_steps(path)

    def backward(carry, saved):
        d_state, totals = carry
        cot_now, state_in, act_one, pre_one, pre_two, sums_one, sums_two = saved
        seed = d_state + cot_now
        unused_out, pull_three = jax.vjp(outlet, state_in, act_one, pre_two, sums_two, *rest)
        back_three = pull_three(seed)
        d_sums_two = butterfly(back_three[3])
        d_pre_two = back_three[2] + d_sums_two[0] + 2.0 * pre_two * d_sums_two[1]
        unused_out, pull_two = jax.vjp(middle, pre_one, sums_one, gain_first, shift_first, w_second)
        back_two = pull_two(d_pre_two)
        d_sums_one = butterfly(back_two[1])
        d_pre_one = back_two[0] + d_sums_one[0] + 2.0 * pre_one * d_sums_one[1]
        unused_out, pull_one = jax.vjp(inlet, state_in, static_part, w_moving, b_input, w_first)
        back_one = pull_one((back_three[1], d_pre_one))
        d_state = back_one[0] + back_three[0]
        step_grads = back_one[1:] + back_two[2:] + back_three[4:]
        return (d_state, jax.tree.map(jnp.add, totals, step_grads)), d_state[0]

    zeros = jax.tree.map(
        jnp.zeros_like, (static_part, w_moving, b_input, w_first, gain_first, shift_first, w_second) + rest
    )
    cots = jnp.stack([pick(got, place(-step)) for step in range(segments)])
    (unused_start, totals), grads = lax.scan(
        backward,
        (jnp.zeros_like(state), zeros),
        (cots, entered, acts_one, pres_one, pres_two, all_sums_one, all_sums_two),
        reverse=True,
    )
    grads_out = to_steps(grads)
    d_static = lax.dot_general(
        static_patches, totals[0], (((0,), (0,)), ((), ())), precision=HIGHEST
    ).reshape(w_static.shape)
    d_w_input = jnp.concatenate([totals[1], d_static], axis=1)
    totals = (d_w_input,) + tuple(totals[2:])
    flat = jnp.concatenate([total.reshape(-1) for total in totals])
    summed = lax.psum(flat.reshape(-1, 128), ("section", "dp")).reshape(-1) if flat.size % 128 == 0 else lax.psum(flat, ("section", "dp"))
    outs = []
    start = 0
    for total in totals:
        outs.append(summed[start : start + total.size].reshape(total.shape))
        start += total.size
    return (path_out, grads_out) + tuple(outs)


def solution(mesh):
    return jax.shard_map(
        on_device,
        mesh=mesh,
        in_specs=(
            P("dp", None, None),
            P(),
            P("dp", None),
            P("section", "dp", None, None),
            P(),
            P(),
            P(),
            P(),
            P(),
            P(),
            P(),
            P(),
            P(),
            P(),
            P(),
            P(),
            P(),
            P(),
        ),
        out_specs=(
            P("section", "dp", None, None),
            P("section", "dp", None, None),
            P(),
            P(),
            P(),
            P(),
            P(),
            P(),
            P(),
            P(),
            P(),
            P(),
            P(),
            P(),
            P(),
            P(),
        ),
        check_vma=False,
    )
```

```python
import functools
import math

import jax
import jax.numpy as jnp
from jax import lax
from jax.experimental import pallas as pl
from jax.experimental.pallas import tpu as pltpu
from jax.sharding import PartitionSpec as P

HEADS = 4
LAT = 16
ATT_ROWS = 8
EPSILON = 1e-05
F32 = jnp.float32
BF16 = jnp.bfloat16
GROUP = 8


def dot(left, right, left_dim=1, right_dim=0):
    return lax.dot_general(
        left, right, (((left_dim,), (right_dim,)), ((), ())), preferred_element_type=F32
    )


def halves(value):
    high = value.astype(BF16)
    return high, (value - high.astype(F32)).astype(BF16)


def thirds(value):
    high = value.astype(BF16)
    rest = value - high.astype(F32)
    middle = rest.astype(BF16)
    return high, middle, (rest - middle.astype(F32)).astype(BF16)


def stacked(value):
    return jnp.concatenate(halves(value), axis=0)


def beside(value):
    return jnp.concatenate(halves(value), axis=1)


def folded(value, axis):
    size = value.shape[axis] // 2
    if axis == 0:
        return value[:size] + value[size:]
    return value[:, :size] + value[:, size:]


def cells_of(value):
    return lax.broadcasted_iota(jnp.int32, value.shape, value.ndim - 1)


def lon_moved(value, offset, lon):
    cells = value.shape[1]
    column = lax.rem(cells_of(value), lon)
    near = pltpu.roll(value, (-offset) % cells, 1)
    wrapped = pltpu.roll(value, (offset * (lon - 1)) % cells, 1)
    edge = lon - 1 if offset > 0 else 0
    return jnp.where(column == edge, wrapped, near)


def lat_moved(value, offset, lon):
    cells = value.shape[1]
    moved = pltpu.roll(value, (-offset * lon) % cells, 1)
    cell = cells_of(value)
    if offset > 0:
        return jnp.where(cell < cells - lon, moved, 0.0)
    return jnp.where(cell >= lon, moved, 0.0)


def along_lon(value, lon):
    return 0.5 * (lon_moved(value, 1, lon) - lon_moved(value, -1, lon))


def along_lat(value, lon):
    return 0.5 * (lat_moved(value, 1, lon) - lat_moved(value, -1, lon))


def fill_patches(patches_ref, value, lon):
    cells, channels = value.shape
    planes = value.reshape(cells // lon, lon, channels)
    blank = jnp.zeros((lon, patches_ref.shape[1]), BF16)
    patches_ref[:lon] = blank
    patches_ref[lon + cells :] = blank
    for place, offset in enumerate((-1, 0, 1)):
        moved = value
        if offset:
            moved = pltpu.roll(planes, (-offset) % lon, 1).reshape(cells, channels)
        high, low = halves(moved)
        start = place * 2 * channels
        patches_ref[lon : lon + cells, start : start + channels] = high
        patches_ref[lon : lon + cells, start + channels : start + 2 * channels] = low


def conv_patches(patches_ref, weight_ref, lon):
    cells = patches_ref.shape[0] - 2 * lon
    rows = [patches_ref[lon * place : lon * place + cells] for place in range(3)]
    return folded(dot(jnp.concatenate(rows, axis=1), weight_ref[...]), 1)


def sigmoid(value):
    return 1.0 / (1.0 + jnp.exp(-value))


def norm_of(sums, gain, count):
    mean = sums[0:1] / count
    spread = sums[1:2] / count - mean * mean
    scale = lax.rsqrt(spread + EPSILON)
    return mean, scale, gain * scale


def sums_of(value, other):
    total = jnp.sum(value, axis=0, keepdims=True)
    product = jnp.sum(value * other, axis=0, keepdims=True)
    row = lax.broadcasted_iota(jnp.int32, (GROUP, value.shape[1]), 0)
    return jnp.where(row == 0, total, jnp.where(row == 1, product, 0.0))


def inlet_channels(state, lon):
    amount = state[:GROUP]
    groups = jnp.concatenate([state, along_lon(amount, lon), along_lat(amount, lon)], axis=0)
    blank = jnp.zeros((GROUP, state.shape[1]), F32)
    return jnp.concatenate(
        [lon_moved(groups, -1, lon), groups, lon_moved(groups, 1, lon), blank], axis=0
    )


def advected(state, step_size, lon):
    amount, east, north = state[:GROUP], state[GROUP : 2 * GROUP], state[2 * GROUP :]
    return amount - step_size * (along_lon(amount * east, lon) + along_lat(amount * north, lon))


def attention_scores(key_rows, query_rows):
    key_high, key_mid, key_low = thirds(key_rows)
    query_high, query_mid, query_low = thirds(query_rows)
    left = jnp.concatenate([key_high, key_high, key_mid, key_mid, key_high, key_low], axis=0)
    right = jnp.concatenate(
        [query_high, query_mid, query_high, query_mid, query_low, query_high], axis=0
    )
    return dot(left, right, 0, 0)


def by_halves(left_halves, right):
    high, low = halves(right)
    return folded(dot(left_halves, high) + dot(left_halves, low), 0)


def static_kernel(lon, maps_ref, weight_ref, bias_ref, out_ref, patches_ref):
    maps = maps_ref[...]
    fill_patches(patches_ref, maps.T, lon)
    out_ref[...] = conv_patches(patches_ref, weight_ref, lon) + bias_ref[...]


def inlet_kernel(
    lon, state_ref, static_ref, w_input_ref, w_first_ref,
    inner_ref, pre_ref, sums_ref, patches_ref,
):
    cells = state_ref.shape[1]
    moving = inlet_channels(state_ref[...], lon).T
    width = patches_ref.shape[1]
    blank = jnp.zeros((lon, width), BF16)
    patches_ref[:lon] = blank
    patches_ref[lon + cells :] = blank
    patches_ref[lon : lon + cells, :256] = beside(moving)
    rows = [patches_ref[lon * place : lon * place + cells, :256] for place in range(3)]
    inner = folded(dot(jnp.concatenate(rows, axis=1), w_input_ref[...]), 1) + static_ref[...]
    inner_ref[...] = inner
    fill_patches(patches_ref, inner * sigmoid(inner), lon)
    pre = conv_patches(patches_ref, w_first_ref, lon)
    pre_ref[...] = pre
    sums_ref[...] = sums_of(pre, pre)


def middle_kernel(
    lon, count, pre_one_ref, sums_one_ref, gain_ref, shift_ref, w_second_ref,
    pre_ref, sums_ref, patches_ref,
):
    mean, unused_scale, factor = norm_of(sums_one_ref[...], gain_ref[...], count)
    normed = (pre_one_ref[...] - mean) * factor + shift_ref[...]
    fill_patches(patches_ref, normed * sigmoid(normed), lon)
    pre = conv_patches(patches_ref, w_second_ref, lon)
    pre_ref[...] = pre
    sums_ref[...] = sums_of(pre, pre)


def act_two_channels(inner, pre_two, sums, gain, shift, count):
    mean, unused_scale, factor = norm_of(sums, gain, count)
    return (inner * sigmoid(inner) + (pre_two - mean) * factor + shift).T


def project(w_qkv_ref, act_two, head_width, qkv_ref):
    channels = act_two.shape[0]
    rows = folded(dot(w_qkv_ref[...], stacked(act_two)), 0)
    qkv_ref[:channels] = rows[:channels] * (1.0 / math.sqrt(head_width))
    qkv_ref[channels:] = rows[channels:]


def outlet_kernel(
    lon, count, block_size, step_size,
    state_ref, inner_ref, pre_two_ref, sums_two_ref, gain_ref, shift_ref,
    w_qkv_ref, w_mixer_ref, w_velocity_ref, b_velocity_ref,
    out_ref, qkv_ref, mixed_ref,
):
    channels = inner_ref.shape[1]
    cells = inner_ref.shape[0]
    head_width = channels // HEADS
    act_two = act_two_channels(
        inner_ref[...], pre_two_ref[...], sums_two_ref[...], gain_ref[...], shift_ref[...], count
    )
    project(w_qkv_ref, act_two, head_width, qkv_ref)

    def one_head(turn, unused):
        head, block = turn % HEADS, turn // HEADS
        lanes = pl.ds(pl.multiple_of(block * block_size, block_size), block_size)
        start = pl.multiple_of(head * head_width, head_width)
        query = qkv_ref[pl.ds(start, head_width), lanes]
        key = qkv_ref[pl.ds(start + channels, head_width), lanes]
        value = qkv_ref[pl.ds(start + 2 * channels, head_width), lanes]
        scores = attention_scores(key, query)
        top = jnp.max(scores, axis=0, keepdims=True)
        powers = jnp.exp(scores - top)
        total = jnp.sum(powers, axis=0, keepdims=True)
        mixed_ref[pl.ds(start, head_width), lanes] = by_halves(stacked(value), powers) / total
        return unused

    lax.fori_loop(0, HEADS * (cells // block_size), one_head, 0)
    act_three = act_two + folded(dot(w_mixer_ref[...], stacked(mixed_ref[...])), 0)
    parts = folded(dot(w_velocity_ref[...], stacked(act_three)), 0)
    forcing = jnp.zeros((2 * GROUP, cells), F32) + b_velocity_ref[...]
    for column, lon_offset in enumerate((-1, 0, 1)):
        total = None
        for row, lat_offset in enumerate((-1, 0, 1)):
            start = (row * 3 + column) * 2 * GROUP
            part = parts[start : start + 2 * GROUP]
            if lat_offset:
                part = lat_moved(part, lat_offset, lon)
            total = part if total is None else total + part
        forcing = forcing + (lon_moved(total, lon_offset, lon) if lon_offset else total)
    state = state_ref[...]
    flows = state[GROUP:]
    out_ref[:GROUP] = advected(state, step_size, lon)
    out_ref[GROUP:] = flows + step_size * (forcing - flows)


def outlet_back_kernel(
    lon, count, block_size, step_size,
    state_ref, seed_ref, inner_ref, pre_two_ref, sums_two_ref, gain_ref, shift_ref,
    w_qkv_ref, w_mixer_ref, w_qkv_back_ref, w_mixer_back_ref, w_velocity_back_ref,
    acc_qkv_ref, acc_mixer_ref, acc_velocity_ref, acc_small_ref,
    d_state_ref, d_two_ref, sums_ref,
    out_qkv_ref, out_mixer_ref, out_velocity_ref, out_small_ref,
    qkv_ref, mixed_ref, d_mixed_ref, d_qkv_ref,
):
    channels = inner_ref.shape[1]
    cells = inner_ref.shape[0]
    head_width = channels // HEADS
    state, seed = state_ref[...], seed_ref[...]
    amount, east, north = state[:GROUP], state[GROUP : 2 * GROUP], state[2 * GROUP :]
    d_amount = seed[:GROUP]
    d_lon = step_size * along_lon(d_amount, lon)
    d_lat = step_size * along_lat(d_amount, lon)
    d_state_ref[:GROUP] = d_amount + d_lon * east + d_lat * north
    d_state_ref[GROUP : 2 * GROUP] = (1.0 - step_size) * seed[GROUP : 2 * GROUP] + d_lon * amount
    d_state_ref[2 * GROUP :] = (1.0 - step_size) * seed[2 * GROUP :] + d_lat * amount
    d_forcing = step_size * seed[GROUP:]
    pieces = []
    for lat_offset in (-1, 0, 1):
        rows = lat_moved(d_forcing, -lat_offset, lon) if lat_offset else d_forcing
        for lon_offset in (-1, 0, 1):
            pieces.append(lon_moved(rows, -lon_offset, lon) if lon_offset else rows)
    d_parts = stacked(jnp.concatenate(pieces, axis=0))
    d_three = folded(dot(w_velocity_back_ref[...], d_parts), 0)
    d_three_halves = stacked(d_three)
    d_mixed_ref[...] = folded(dot(w_mixer_back_ref[...], d_three_halves), 0)
    act_two = act_two_channels(
        inner_ref[...], pre_two_ref[...], sums_two_ref[...], gain_ref[...], shift_ref[...], count
    )
    act_two_halves = stacked(act_two)
    project(w_qkv_ref, act_two, head_width, qkv_ref)

    def one_head(turn, unused):
        head, block = turn % HEADS, turn // HEADS
        lanes = pl.ds(pl.multiple_of(block * block_size, block_size), block_size)
        start = pl.multiple_of(head * head_width, head_width)
        query = qkv_ref[pl.ds(start, head_width), lanes]
        key = qkv_ref[pl.ds(start + channels, head_width), lanes]
        value = qkv_ref[pl.ds(start + 2 * channels, head_width), lanes]
        scores = attention_scores(key, query)
        top = jnp.max(scores, axis=0, keepdims=True)
        powers = jnp.exp(scores - top)
        weight = 1.0 / jnp.sum(powers, axis=0, keepdims=True)
        power_high, power_low = halves(powers)
        value_halves = stacked(value)
        mixed = folded(dot(value_halves, power_high) + dot(value_halves, power_low), 0) * weight
        mixed_ref[pl.ds(start, head_width), lanes] = mixed
        d_mixed = d_mixed_ref[pl.ds(start, head_width), lanes] * weight
        inner_sum = jnp.sum(d_mixed * mixed, axis=0, keepdims=True)
        d_mixed_cells = beside(d_mixed.T)
        d_value = folded(dot(power_high, d_mixed_cells) + dot(power_low, d_mixed_cells), 1)
        d_powers = attention_scores(value, d_mixed)
        d_high, d_low = halves(powers * (d_powers - inner_sum))
        query_cells = beside(query.T)
        d_key = folded(dot(d_high, query_cells) + dot(d_low, query_cells), 1)
        key_halves = stacked(key)
        d_query = folded(dot(key_halves, d_high) + dot(key_halves, d_low), 0)
        d_qkv_ref[pl.ds(start, head_width), lanes] = d_query * (1.0 / math.sqrt(head_width))
        d_qkv_ref[pl.ds(start + channels, head_width), lanes] = d_key.T
        d_qkv_ref[pl.ds(start + 2 * channels, head_width), lanes] = d_value.T
        return unused

    lax.fori_loop(0, HEADS * (cells // block_size), one_head, 0)
    mixed_halves = stacked(mixed_ref[...])
    act_three = act_two + folded(dot(w_mixer_ref[...], mixed_halves), 0)
    d_qkv_halves = stacked(d_qkv_ref[...])
    d_two = (d_three + folded(dot(w_qkv_back_ref[...], d_qkv_halves), 0)).T
    d_two_ref[...] = d_two
    mean, scale, unused_factor = norm_of(sums_two_ref[...], gain_ref[...], count)
    sums = sums_of(d_two, pre_two_ref[...] - mean)
    sums_ref[...] = sums
    def pairs(left, right):
        return folded(folded(dot(left, right, 1, 1), 0), 1)

    out_velocity_ref[...] = acc_velocity_ref[...] + pairs(d_parts, stacked(act_three))
    out_mixer_ref[...] = acc_mixer_ref[...] + pairs(mixed_halves, d_three_halves)
    out_qkv_ref[...] = acc_qkv_ref[...] + pairs(act_two_halves, d_qkv_halves)
    bias = jnp.sum(d_forcing, axis=1, keepdims=True)
    row = lax.broadcasted_iota(jnp.int32, (GROUP, channels), 0)
    small = jnp.where(row == 0, sums[1:2] * scale, jnp.where(row == 1, sums[0:1], 0.0))
    out_small_ref[:GROUP] = acc_small_ref[:GROUP] + small
    out_small_ref[GROUP:] = acc_small_ref[GROUP:] + bias


def d_pre_of(d_normed, centred, sums, all_grad_sums, gain, count):
    unused_mean, scale, factor = norm_of(sums, gain, count)
    d_spread = -0.5 * gain * scale * scale * scale * all_grad_sums[1:2]
    return factor * (d_normed - all_grad_sums[0:1] / count) + (2.0 * d_spread / count) * centred


def weight_pairs(acc_ref, out_ref, left_halves, patches_ref, lon):
    cells = patches_ref.shape[0] - 2 * lon
    width = patches_ref.shape[1] // 3
    for tap in range(9):
        row, column = divmod(8 - tap, 3)
        right = patches_ref[lon * row : lon * row + cells, column * width : (column + 1) * width]
        out_ref[tap] = acc_ref[tap] + folded(folded(dot(left_halves, right), 0), 1)


def middle_back_kernel(
    lon, count,
    d_two_ref, pre_two_ref, sums_two_ref, all_two_ref, gain_two_ref,
    pre_one_ref, sums_one_ref, gain_ref, shift_ref, w_second_back_ref,
    acc_weight_ref, acc_small_ref,
    d_normed_ref, sums_ref, out_weight_ref, out_small_ref,
    patches_ref,
):
    sums_two = sums_two_ref[...]
    d_pre = d_pre_of(
        d_two_ref[...], pre_two_ref[...] - sums_two[0:1] / count, sums_two, all_two_ref[...],
        gain_two_ref[...], count,
    )
    fill_patches(patches_ref, d_pre, lon)
    d_act = conv_patches(patches_ref, w_second_back_ref, lon)
    mean, scale, factor = norm_of(sums_one_ref[...], gain_ref[...], count)
    centred = pre_one_ref[...] - mean
    normed = centred * factor + shift_ref[...]
    gate = sigmoid(normed)
    d_normed = d_act * gate * (1.0 + normed * (1.0 - gate))
    d_normed_ref[...] = d_normed
    sums = sums_of(d_normed, centred)
    sums_ref[...] = sums
    weight_pairs(acc_weight_ref, out_weight_ref, stacked((normed * gate).T), patches_ref, lon)
    row = lax.broadcasted_iota(jnp.int32, sums.shape, 0)
    small = jnp.where(row == 0, sums[1:2] * scale, jnp.where(row == 1, sums[0:1], 0.0))
    out_small_ref[...] = acc_small_ref[...] + small


def inlet_back_kernel(
    lon, count,
    state_ref, d_normed_ref, pre_one_ref, sums_one_ref, all_one_ref, gain_ref,
    inner_ref, d_two_ref, d_state_in_ref, w_first_back_ref, w_input_back_ref,
    acc_first_ref, acc_input_ref, acc_inner_ref,
    d_state_ref, out_first_ref, out_input_ref, out_inner_ref,
    patches_ref,
):
    cells = inner_ref.shape[0]
    sums_one = sums_one_ref[...]
    d_pre = d_pre_of(
        d_normed_ref[...], pre_one_ref[...] - sums_one[0:1] / count, sums_one, all_one_ref[...],
        gain_ref[...], count,
    )
    fill_patches(patches_ref, d_pre, lon)
    d_act = conv_patches(patches_ref, w_first_back_ref, lon) + d_two_ref[...]
    inner = inner_ref[...]
    gate = sigmoid(inner)
    d_inner = d_act * gate * (1.0 + inner * (1.0 - gate))
    weight_pairs(acc_first_ref, out_first_ref, stacked((inner * gate).T), patches_ref, lon)
    out_inner_ref[...] = acc_inner_ref[...] + d_inner
    patches_ref[lon : lon + cells, :256] = beside(d_inner)
    rows = [patches_ref[lon * place : lon * place + cells, :256] for place in range(3)]
    d_moving = folded(dot(jnp.concatenate(rows, axis=1), w_input_back_ref[...]), 1).T
    state = state_ref[...]
    moving_halves = stacked(inlet_channels(state, lon))
    for place in range(3):
        out_input_ref[place] = acc_input_ref[place] + folded(
            folded(dot(moving_halves, rows[2 - place]), 0), 1
        )
    size = 5 * GROUP
    d_groups = (
        lon_moved(d_moving[:size], 1, lon)
        + d_moving[size : 2 * size]
        + lon_moved(d_moving[2 * size : 3 * size], -1, lon)
    )
    d_state = d_state_in_ref[...] + d_groups[: 3 * GROUP]
    d_state_ref[:GROUP] = (
        d_state[:GROUP]
        - along_lon(d_groups[3 * GROUP : 4 * GROUP], lon)
        - along_lat(d_groups[4 * GROUP :], lon)
    )
    d_state_ref[GROUP:] = d_state[GROUP:]


def static_back_kernel(lon, maps_ref, d_inner_ref, out_ref, bias_ref, patches_ref):
    d_inner = d_inner_ref[...]
    fill_patches(patches_ref, d_inner, lon)
    cells = d_inner.shape[0]
    width = patches_ref.shape[1] // 3
    left = stacked(maps_ref[...])
    for tap in range(9):
        row, column = divmod(8 - tap, 3)
        right = patches_ref[lon * row : lon * row + cells, column * width : (column + 1) * width]
        out_ref[tap] = folded(folded(dot(left, right), 0), 1)
    bias_ref[...] = jnp.zeros(bias_ref.shape, F32) + jnp.sum(d_inner, axis=0, keepdims=True)


def call(kernel, outs, scratch=(), aliases=None, name=None):
    return pl.pallas_call(
        kernel,
        out_shape=tuple(jax.ShapeDtypeStruct(shape, F32) for shape in outs),
        scratch_shapes=scratch,
        input_output_aliases=aliases or {},
        compiler_params=pltpu.CompilerParams(vmem_limit_bytes=VMEM_LIMIT),
        name=name,
        interpret=INTERPRET,
    )


VMEM_LIMIT = 48 * 1024 * 1024
INTERPRET = False


def cut(weight):
    high = lax.reduce_precision(weight, 8, 7)
    return high.astype(BF16), (weight - high).astype(BF16)


def conv_weight(weight):
    wide = jnp.concatenate(cut(weight), axis=2)
    return jnp.stack([wide, wide], axis=1).reshape(-1, wide.shape[2])


def left_weight(weight):
    high, low = cut(weight)
    return jnp.concatenate(
        [jnp.concatenate([high, high], axis=1), jnp.concatenate([low, low], axis=1)], axis=0
    )


def in_groups(array, axis, groups):
    shape = array.shape
    split = shape[:axis] + (groups, shape[axis] // groups) + shape[axis + 1 :]
    array = array.reshape(split)
    pads = [(0, 0)] * array.ndim
    pads[axis + 1] = (0, GROUP - split[axis + 1])
    return jnp.pad(array, pads).reshape(shape[:axis] + (groups * GROUP,) + shape[axis + 1 :])


def from_groups(array, axis, groups, size):
    shape = array.shape
    array = array.reshape(shape[:axis] + (groups, GROUP) + shape[axis + 1 :])
    array = lax.slice_in_dim(array, 0, size, axis=axis + 1)
    return array.reshape(shape[:axis] + (groups * size,) + shape[axis + 1 :])


def shift_along(value, axis, steps):
    count = lax.axis_size(axis)
    return lax.ppermute(value, axis, [(own, (own + steps) % count) for own in range(count)])


def group_of(value):
    dp, sections = lax.axis_size("dp"), lax.axis_size("section")
    groups = [list(range(2 * dp * pair, 2 * dp * (pair + 1))) for pair in range(sections // 2)]
    wide = jnp.broadcast_to(value[None], (2 * dp,) + value.shape)
    return lax.all_to_all(wide, ("section", "dp"), 0, 0, axis_index_groups=groups)


def micro_sum_direct(value):
    return jnp.sum(group_of(value), axis=0)


def micro_sum(value):
    dp, sections = lax.axis_size("dp"), lax.axis_size("section")
    reach = 1
    while 2 * reach < dp:
        offsets = [1, 2, 3] if 4 * reach <= dp else [1]
        value = value + sum(
            lax.ppermute(value, "dp", [(own, own ^ (offset * reach)) for own in range(dp)])
            for offset in offsets
        )
        reach *= 4
    if reach < dp:
        both = [(own, section) for section in range(sections) for own in range(dp)]
        pairs = lambda flip, jump: [
            (section * dp + own, (section ^ flip) * dp + (own ^ jump)) for own, section in both
        ]
        return value + sum(
            lax.ppermute(value, ("section", "dp"), pairs(flip, jump))
            for flip, jump in ((0, reach), (1, 0), (1, reach))
        )
    return value + lax.ppermute(value, "section", [(own, own ^ 1) for own in range(sections)])


def pick(array, index):
    return lax.dynamic_index_in_dim(array, index, 0, keepdims=False)


def on_device(
    state_start,
    static_maps,
    grouping,
    cotangent,
    w_input,
    b_input,
    w_first,
    gain_first,
    shift_first,
    w_second,
    gain_second,
    shift_second,
    w_query,
    w_key,
    w_value,
    w_mixer,
    w_velocity,
    b_velocity,
):
    segments = lax.axis_size("section")
    segment_rank = lax.axis_index("section")
    micro_count = segments // 2
    per_micro = state_start.shape[0] // micro_count
    cells = state_start.shape[2]
    lon = cells // LAT
    count = float(per_micro * cells * lax.axis_size("dp"))
    step_size = 2.0 / segments
    block_size = ATT_ROWS * lon
    channels = w_first.shape[2]
    quantities = state_start.shape[1] // 3
    moving = 5 * quantities
    local_order = grouping[0]
    cot_local = cotangent[0]
    statics = static_maps.shape[0]

    def place(offset):
        return lax.rem(segment_rank + offset + segments, segments)

    got = [pick(cot_local, local_order[segment_rank])]
    for offset in range(1, segments):
        got.append(shift_along(pick(cot_local, local_order[place(offset)]), "section", offset))
    got = jnp.stack(got)
    cots = jnp.stack([pick(got, place(-step)) for step in range(segments)])
    cots = in_groups(cots, 1, 3)
    state = in_groups(pick(state_start, local_order[segment_rank]), 0, 3)

    w_moving = in_groups(w_input[:, :moving], 1, 5).reshape(3, 3 * 5 * GROUP, channels)
    w_moving = jnp.pad(w_moving, ((0, 0), (0, channels - 3 * 5 * GROUP), (0, 0)))
    w_static = jnp.pad(w_input[:, moving:], ((0, 0), (0, channels - statics), (0, 0)))
    maps = jnp.pad(static_maps, ((0, channels - statics), (0, 0)))
    w_qkv = jnp.concatenate([w_query, w_key, w_value], axis=1)
    w_out = in_groups(w_velocity, 2, 2)
    w_out_rows = jnp.swapaxes(w_out, 1, 2).reshape(-1, channels)
    b_out = in_groups(b_velocity[:, None], 0, 2)
    moving_cat = conv_weight(w_moving)
    moving_back_cat = conv_weight(jnp.swapaxes(w_moving[::-1], 1, 2))
    static_cat = conv_weight(w_static)
    first_cat = conv_weight(w_first)
    first_back_cat = conv_weight(jnp.swapaxes(w_first[::-1], 1, 2))
    second_cat = conv_weight(w_second)
    second_back_cat = conv_weight(jnp.swapaxes(w_second[::-1], 1, 2))
    qkv_cat = left_weight(w_qkv.T)
    qkv_back_cat = left_weight(w_qkv)
    mixer_cat = left_weight(w_mixer.T)
    mixer_back_cat = left_weight(w_mixer)
    out_cat = left_weight(w_out_rows)
    out_back_cat = left_weight(w_out_rows.T)
    gain_one, shift_one = gain_first[None], shift_first[None]
    gain_two, shift_two = gain_second[None], shift_second[None]

    plane = (cells, channels)
    small = (GROUP, channels)
    patches = pltpu.VMEM((cells + 2 * lon, 6 * channels), BF16)
    wide = pltpu.VMEM((3 * channels, cells), F32)
    narrow = pltpu.VMEM((channels, cells), F32)
    state_shape = (3 * GROUP, cells)

    (static_part,) = call(
        functools.partial(static_kernel, lon), [plane], [patches], name="static_inlet"
    )(maps, static_cat, b_input[None])

    inlet = call(
        functools.partial(inlet_kernel, lon), [plane, plane, small], [patches], name="inlet"
    )
    middle = call(
        functools.partial(middle_kernel, lon, count), [plane, small], [patches], name="middle"
    )
    outlet = call(
        functools.partial(outlet_kernel, lon, count, block_size, step_size),
        [state_shape], [wide, narrow], name="outlet",
    )
    outlet_back = call(
        functools.partial(outlet_back_kernel, lon, count, block_size, step_size),
        [state_shape, plane, small, (channels, 3 * channels), (channels, channels),
         (18 * GROUP, channels), (3 * GROUP, channels)],
        [wide, narrow, narrow, wide],
        {12: 3, 13: 4, 14: 5, 15: 6}, name="outlet_back",
    )
    middle_back = call(
        functools.partial(middle_back_kernel, lon, count),
        [plane, small, (9, channels, channels), small], [patches],
        {10: 2, 11: 3}, name="middle_back",
    )
    inlet_back = call(
        functools.partial(inlet_back_kernel, lon, count),
        [state_shape, (9, channels, channels), (3, channels, channels), plane], [patches],
        {11: 1, 12: 2, 13: 3}, name="inlet_back",
    )

    def forward(state_in, unused):
        inner, pre_one, sums_one = inlet(state_in, static_part, moving_cat, first_cat)
        sums_one = micro_sum_direct(sums_one)
        pre_two, sums_two = middle(pre_one, sums_one, gain_one, shift_one, second_cat)
        sums_two = micro_sum_direct(sums_two)
        (state_out,) = outlet(
            state_in, inner, pre_two, sums_two, gain_two, shift_two, qkv_cat, mixer_cat, out_cat, b_out
        )
        return state_out, (state_in, state_out, inner, pre_one, pre_two, sums_one, sums_two)

    unused_last, (entered, path, inners, pres_one, pres_two, all_sums_one, all_sums_two) = lax.scan(
        forward, state, None, length=segments, unroll=min(4, segments)
    )

    def to_steps(values):
        values = from_groups(values, 1, 3, quantities)
        back = [pick(values, segment_rank)]
        for offset in range(1, segments):
            back.append(shift_along(pick(values, place(offset)), "section", offset))
        back = jnp.stack(back)
        senders = local_order[lax.rem(segment_rank - jnp.arange(segments) + segments, segments)]
        return jnp.take(back, jnp.argsort(senders), axis=0)[None]

    path_out = to_steps(path)

    def backward(carry, saved):
        d_state, acc = carry
        cot_now, state_in, inner, pre_one, pre_two, sums_one, sums_two = saved
        seed = d_state + cot_now
        d_partial, d_two, grad_two, qkv, mixer, velocity, small_two = outlet_back(
            state_in, seed, inner, pre_two, sums_two, gain_two, shift_two,
            qkv_cat, mixer_cat, qkv_back_cat, mixer_back_cat, out_back_cat,
            acc["qkv"], acc["mixer"], acc["velocity"], acc["small_two"],
        )
        grad_two = micro_sum(grad_two)
        d_normed, grad_one, second, small_one = middle_back(
            d_two, pre_two, sums_two, grad_two, gain_two,
            pre_one, sums_one, gain_one, shift_one, second_back_cat,
            acc["second"], acc["small_one"],
        )
        grad_one = micro_sum(grad_one)
        d_state, first, moved, inner_sum = inlet_back(
            state_in, d_normed, pre_one, sums_one, grad_one, gain_one,
            inner, d_two, d_partial, first_back_cat, moving_back_cat,
            acc["first"], acc["moving"], acc["inner"],
        )
        acc = dict(
            qkv=qkv, mixer=mixer, velocity=velocity, small_two=small_two, second=second,
            small_one=small_one, first=first, moving=moved, inner=inner_sum,
        )
        return (d_state, acc), d_state

    acc = dict(
        qkv=jnp.zeros((channels, 3 * channels), F32),
        mixer=jnp.zeros((channels, channels), F32),
        velocity=jnp.zeros((18 * GROUP, channels), F32),
        small_two=jnp.zeros((3 * GROUP, channels), F32),
        second=jnp.zeros((9, channels, channels), F32),
        small_one=jnp.zeros(small, F32),
        first=jnp.zeros((9, channels, channels), F32),
        moving=jnp.zeros((3, channels, channels), F32),
        inner=jnp.zeros(plane, F32),
    )
    (unused_start, acc), grads = lax.scan(
        backward,
        (jnp.zeros(state_shape, F32), acc),
        (cots, entered, inners, pres_one, pres_two, all_sums_one, all_sums_two),
        reverse=True,
        unroll=min(4, segments),
    )
    grads_out = to_steps(grads)
    d_static, bias = call(
        functools.partial(static_back_kernel, lon), [(9, channels, channels), small], [patches],
        name="static_back",
    )(maps, acc["inner"])

    sizes = [
        ("first", (9, channels, channels)),
        ("second", (9, channels, channels)),
        ("static", (9, channels, channels)),
        ("moving", (3, channels, channels)),
        ("qkv", (channels, 3 * channels)),
        ("mixer", (channels, channels)),
        ("velocity", (18 * GROUP, channels)),
        ("bias", small),
        ("small_one", small),
        ("small_two", (3 * GROUP, channels)),
    ]
    acc["static"], acc["bias"] = d_static, bias
    names = [name for name, unused_shape in sizes]
    summed = dict(zip(names, final_sum([acc[name] for name in names])))
    d_moving = from_groups(
        summed["moving"][:, : 15 * GROUP].reshape(9, 5 * GROUP, channels), 1, 5, quantities
    )
    d_input = jnp.concatenate([d_moving, summed["static"][:, :statics]], axis=1)
    qkv = summed["qkv"]
    d_out = jnp.swapaxes(summed["velocity"].reshape(9, 2 * GROUP, channels), 1, 2)
    d_out = from_groups(d_out, 2, 2, quantities)
    small_one, small_two = summed["small_one"], summed["small_two"]
    return (
        path_out,
        grads_out,
        d_input,
        summed["bias"][0],
        summed["first"],
        small_one[0],
        small_one[1],
        summed["second"],
        small_two[0],
        small_two[1],
        qkv[:, :channels],
        qkv[:, channels : 2 * channels],
        qkv[:, 2 * channels :],
        summed["mixer"],
        d_out,
        from_groups(small_two[GROUP:, :1], 0, 2, quantities)[:, 0],
    )


def final_sum(values):
    flat = jnp.concatenate([value.reshape(-1, 128) for value in values])
    summed = lax.psum(flat, ("section", "dp"))
    outs = []
    start = 0
    for value in values:
        rows = value.size // flat.shape[1]
        outs.append(summed[start : start + rows].reshape(value.shape))
        start += rows
    return outs


def solution(mesh):
    weights = (P(),) * 14
    return jax.shard_map(
        on_device,
        mesh=mesh,
        in_specs=(P("dp", None, None), P(), P("dp", None), P("section", "dp", None, None)) + weights,
        out_specs=(P("section", "dp", None, None), P("section", "dp", None, None)) + weights,
        check_vma=False,
    )
```

```python
import functools
import math

import jax
import jax.numpy as jnp
from jax import lax
from jax.experimental import pallas as pl
from jax.experimental.pallas import tpu as pltpu
from jax.sharding import PartitionSpec as P

HEADS = 4
LAT = 16
ATT_ROWS = 8
EPSILON = 1e-05
F32 = jnp.float32
BF16 = jnp.bfloat16
GROUP = 8


def dot(left, right, left_dim=1, right_dim=0):
    return lax.dot_general(
        left, right, (((left_dim,), (right_dim,)), ((), ())), preferred_element_type=F32
    )


def halves(value):
    high = value.astype(BF16)
    return high, (value - high.astype(F32)).astype(BF16)


def thirds(value):
    high = value.astype(BF16)
    rest = value - high.astype(F32)
    middle = rest.astype(BF16)
    return high, middle, (rest - middle.astype(F32)).astype(BF16)


def stacked(value):
    return jnp.concatenate(halves(value), axis=0)


def beside(value):
    return jnp.concatenate(halves(value), axis=1)


def folded(value, axis):
    size = value.shape[axis] // 2
    if axis == 0:
        return value[:size] + value[size:]
    return value[:, :size] + value[:, size:]


def cells_of(value):
    return lax.broadcasted_iota(jnp.int32, value.shape, value.ndim - 1)


def lon_moved(value, offset, lon):
    cells = value.shape[1]
    column = lax.rem(cells_of(value), lon)
    near = pltpu.roll(value, (-offset) % cells, 1)
    wrapped = pltpu.roll(value, (offset * (lon - 1)) % cells, 1)
    edge = lon - 1 if offset > 0 else 0
    return jnp.where(column == edge, wrapped, near)


def lat_moved(value, offset, lon):
    cells = value.shape[1]
    moved = pltpu.roll(value, (-offset * lon) % cells, 1)
    cell = cells_of(value)
    if offset > 0:
        return jnp.where(cell < cells - lon, moved, 0.0)
    return jnp.where(cell >= lon, moved, 0.0)


def along_lon(value, lon):
    return 0.5 * (lon_moved(value, 1, lon) - lon_moved(value, -1, lon))


def along_lat(value, lon):
    return 0.5 * (lat_moved(value, 1, lon) - lat_moved(value, -1, lon))


def fill_patches(patches_ref, value, lon):
    cells, channels = value.shape
    planes = value.reshape(cells // lon, lon, channels)
    blank = jnp.zeros((lon, patches_ref.shape[1]), BF16)
    patches_ref[:lon] = blank
    patches_ref[lon + cells :] = blank
    for place, offset in enumerate((-1, 0, 1)):
        moved = value
        if offset:
            moved = pltpu.roll(planes, (-offset) % lon, 1).reshape(cells, channels)
        high, low = halves(moved)
        start = place * 2 * channels
        patches_ref[lon : lon + cells, start : start + channels] = high
        patches_ref[lon : lon + cells, start + channels : start + 2 * channels] = low


def conv_patches(patches_ref, weight_ref, lon):
    cells = patches_ref.shape[0] - 2 * lon
    rows = [patches_ref[lon * place : lon * place + cells] for place in range(3)]
    return folded(dot(jnp.concatenate(rows, axis=1), weight_ref[...]), 1)


def sigmoid(value):
    return 1.0 / (1.0 + jnp.exp(-value))


def norm_of(sums, gain, count):
    mean = sums[0:1] / count
    spread = sums[1:2] / count - mean * mean
    scale = lax.rsqrt(spread + EPSILON)
    return mean, scale, gain * scale


def sums_of(value, other):
    total = jnp.sum(value, axis=0, keepdims=True)
    product = jnp.sum(value * other, axis=0, keepdims=True)
    row = lax.broadcasted_iota(jnp.int32, (GROUP, value.shape[1]), 0)
    return jnp.where(row == 0, total, jnp.where(row == 1, product, 0.0))


def inlet_channels(state, lon):
    amount = state[:GROUP]
    groups = jnp.concatenate([state, along_lon(amount, lon), along_lat(amount, lon)], axis=0)
    blank = jnp.zeros((GROUP, state.shape[1]), F32)
    return jnp.concatenate(
        [lon_moved(groups, -1, lon), groups, lon_moved(groups, 1, lon), blank], axis=0
    )


def advected(state, step_size, lon):
    amount, east, north = state[:GROUP], state[GROUP : 2 * GROUP], state[2 * GROUP :]
    return amount - step_size * (along_lon(amount * east, lon) + along_lat(amount * north, lon))


def attention_scores(key_rows, query_rows):
    key_high, key_mid, key_low = thirds(key_rows)
    query_high, query_mid, query_low = thirds(query_rows)
    left = jnp.concatenate([key_high, key_high, key_mid, key_mid, key_high, key_low], axis=0)
    right = jnp.concatenate(
        [query_high, query_mid, query_high, query_mid, query_low, query_high], axis=0
    )
    return dot(left, right, 0, 0)


def by_halves(left_halves, right):
    high, low = halves(right)
    return folded(dot(left_halves, high) + dot(left_halves, low), 0)


def inlet_kernel(
    lon, state_ref, static_ref, w_input_ref, w_first_ref,
    inner_ref, pre_ref, sums_ref, patches_ref,
):
    cells = state_ref.shape[1]
    moving = inlet_channels(state_ref[...], lon).T
    width = patches_ref.shape[1]
    blank = jnp.zeros((lon, width), BF16)
    patches_ref[:lon] = blank
    patches_ref[lon + cells :] = blank
    patches_ref[lon : lon + cells, :256] = beside(moving)
    rows = [patches_ref[lon * place : lon * place + cells, :256] for place in range(3)]
    inner = folded(dot(jnp.concatenate(rows, axis=1), w_input_ref[...]), 1) + static_ref[...]
    inner_ref[...] = inner
    fill_patches(patches_ref, inner * sigmoid(inner), lon)
    pre = conv_patches(patches_ref, w_first_ref, lon)
    pre_ref[...] = pre
    sums_ref[...] = sums_of(pre, pre)


def middle_kernel(
    lon, count, pre_one_ref, sums_one_ref, gain_ref, shift_ref, w_second_ref,
    pre_ref, sums_ref, patches_ref,
):
    mean, unused_scale, factor = norm_of(sums_one_ref[...], gain_ref[...], count)
    normed = (pre_one_ref[...] - mean) * factor + shift_ref[...]
    fill_patches(patches_ref, normed * sigmoid(normed), lon)
    pre = conv_patches(patches_ref, w_second_ref, lon)
    pre_ref[...] = pre
    sums_ref[...] = sums_of(pre, pre)


def act_two_channels(inner, pre_two, sums, gain, shift, count):
    mean, unused_scale, factor = norm_of(sums, gain, count)
    return (inner * sigmoid(inner) + (pre_two - mean) * factor + shift).T


def project(w_qkv_ref, act_two, head_width, qkv_ref):
    channels = act_two.shape[0]
    rows = folded(dot(w_qkv_ref[...], stacked(act_two)), 0)
    qkv_ref[:channels] = rows[:channels] * (1.0 / math.sqrt(head_width))
    qkv_ref[channels:] = rows[channels:]


def outlet_kernel(
    lon, count, block_size, step_size,
    state_ref, inner_ref, pre_two_ref, sums_two_ref, gain_ref, shift_ref,
    w_qkv_ref, w_mixer_ref, w_velocity_ref, b_velocity_ref,
    out_ref, qkv_ref, mixed_ref,
):
    channels = inner_ref.shape[1]
    cells = inner_ref.shape[0]
    head_width = channels // HEADS
    act_two = act_two_channels(
        inner_ref[...], pre_two_ref[...], sums_two_ref[...], gain_ref[...], shift_ref[...], count
    )
    project(w_qkv_ref, act_two, head_width, qkv_ref)

    def one_head(turn, unused):
        head, block = turn % HEADS, turn // HEADS
        lanes = pl.ds(pl.multiple_of(block * block_size, block_size), block_size)
        start = pl.multiple_of(head * head_width, head_width)
        query = qkv_ref[pl.ds(start, head_width), lanes]
        key = qkv_ref[pl.ds(start + channels, head_width), lanes]
        value = qkv_ref[pl.ds(start + 2 * channels, head_width), lanes]
        scores = attention_scores(key, query)
        top = jnp.max(scores, axis=0, keepdims=True)
        powers = jnp.exp(scores - top)
        total = jnp.sum(powers, axis=0, keepdims=True)
        mixed_ref[pl.ds(start, head_width), lanes] = by_halves(stacked(value), powers) / total
        return unused

    lax.fori_loop(0, HEADS * (cells // block_size), one_head, 0)
    act_three = act_two + folded(dot(w_mixer_ref[...], stacked(mixed_ref[...])), 0)
    parts = folded(dot(w_velocity_ref[...], stacked(act_three)), 0)
    forcing = jnp.zeros((2 * GROUP, cells), F32) + b_velocity_ref[...]
    for column, lon_offset in enumerate((-1, 0, 1)):
        total = None
        for row, lat_offset in enumerate((-1, 0, 1)):
            start = (row * 3 + column) * 2 * GROUP
            part = parts[start : start + 2 * GROUP]
            if lat_offset:
                part = lat_moved(part, lat_offset, lon)
            total = part if total is None else total + part
        forcing = forcing + (lon_moved(total, lon_offset, lon) if lon_offset else total)
    state = state_ref[...]
    flows = state[GROUP:]
    out_ref[:GROUP] = advected(state, step_size, lon)
    out_ref[GROUP:] = flows + step_size * (forcing - flows)


def outlet_back_kernel(
    lon, count, block_size, step_size, sections,
    ids_ref, step_ref,
    state_ref, d_next_ref, cots_ref, inner_ref, pre_two_ref, sums_two_ref, gain_ref, shift_ref,
    w_qkv_ref, w_mixer_ref, w_qkv_back_ref, w_mixer_back_ref, w_velocity_back_ref,
    acc_qkv_ref, acc_mixer_ref, acc_velocity_ref, acc_small_ref,
    d_state_ref, d_two_ref, sums_ref,
    out_qkv_ref, out_mixer_ref, out_velocity_ref, out_small_ref,
    qkv_ref, mixed_ref, d_mixed_ref, d_qkv_ref,
):
    channels = inner_ref.shape[1]
    cells = inner_ref.shape[0]
    head_width = channels // HEADS
    state = state_ref[...]
    seed = d_next_ref[...] + cots_ref[lax.rem(ids_ref[0] - step_ref[0] + sections, sections)]
    amount, east, north = state[:GROUP], state[GROUP : 2 * GROUP], state[2 * GROUP :]
    d_amount = seed[:GROUP]
    d_lon = step_size * along_lon(d_amount, lon)
    d_lat = step_size * along_lat(d_amount, lon)
    d_state_ref[:GROUP] = d_amount + d_lon * east + d_lat * north
    d_state_ref[GROUP : 2 * GROUP] = (1.0 - step_size) * seed[GROUP : 2 * GROUP] + d_lon * amount
    d_state_ref[2 * GROUP :] = (1.0 - step_size) * seed[2 * GROUP :] + d_lat * amount
    d_forcing = step_size * seed[GROUP:]
    pieces = []
    for lat_offset in (-1, 0, 1):
        rows = lat_moved(d_forcing, -lat_offset, lon) if lat_offset else d_forcing
        for lon_offset in (-1, 0, 1):
            pieces.append(lon_moved(rows, -lon_offset, lon) if lon_offset else rows)
    d_parts = stacked(jnp.concatenate(pieces, axis=0))
    d_three = folded(dot(w_velocity_back_ref[...], d_parts), 0)
    d_three_halves = stacked(d_three)
    d_mixed_ref[...] = folded(dot(w_mixer_back_ref[...], d_three_halves), 0)
    act_two = act_two_channels(
        inner_ref[...], pre_two_ref[...], sums_two_ref[...], gain_ref[...], shift_ref[...], count
    )
    act_two_halves = stacked(act_two)
    project(w_qkv_ref, act_two, head_width, qkv_ref)

    def one_head(turn, unused):
        head, block = turn % HEADS, turn // HEADS
        lanes = pl.ds(pl.multiple_of(block * block_size, block_size), block_size)
        start = pl.multiple_of(head * head_width, head_width)
        query = qkv_ref[pl.ds(start, head_width), lanes]
        key = qkv_ref[pl.ds(start + channels, head_width), lanes]
        value = qkv_ref[pl.ds(start + 2 * channels, head_width), lanes]
        scores = attention_scores(key, query)
        top = jnp.max(scores, axis=0, keepdims=True)
        powers = jnp.exp(scores - top)
        weight = 1.0 / jnp.sum(powers, axis=0, keepdims=True)
        power_high, power_low = halves(powers)
        value_halves = stacked(value)
        mixed = folded(dot(value_halves, power_high) + dot(value_halves, power_low), 0) * weight
        mixed_ref[pl.ds(start, head_width), lanes] = mixed
        d_mixed = d_mixed_ref[pl.ds(start, head_width), lanes] * weight
        inner_sum = jnp.sum(d_mixed * mixed, axis=0, keepdims=True)
        d_mixed_cells = beside(d_mixed.T)
        d_value = folded(dot(power_high, d_mixed_cells) + dot(power_low, d_mixed_cells), 1)
        d_powers = attention_scores(value, d_mixed)
        d_high, d_low = halves(powers * (d_powers - inner_sum))
        query_cells = beside(query.T)
        d_key = folded(dot(d_high, query_cells) + dot(d_low, query_cells), 1)
        key_halves = stacked(key)
        d_query = folded(dot(key_halves, d_high) + dot(key_halves, d_low), 0)
        d_qkv_ref[pl.ds(start, head_width), lanes] = d_query * (1.0 / math.sqrt(head_width))
        d_qkv_ref[pl.ds(start + channels, head_width), lanes] = d_key.T
        d_qkv_ref[pl.ds(start + 2 * channels, head_width), lanes] = d_value.T
        return unused

    lax.fori_loop(0, HEADS * (cells // block_size), one_head, 0)
    mixed_halves = stacked(mixed_ref[...])
    act_three = act_two + folded(dot(w_mixer_ref[...], mixed_halves), 0)
    d_qkv_halves = stacked(d_qkv_ref[...])
    d_two = (d_three + folded(dot(w_qkv_back_ref[...], d_qkv_halves), 0)).T
    d_two_ref[...] = d_two
    mean, scale, unused_factor = norm_of(sums_two_ref[...], gain_ref[...], count)
    sums = sums_of(d_two, pre_two_ref[...] - mean)
    sums_ref[...] = sums
    def pairs(left, right):
        return folded(folded(dot(left, right, 1, 1), 0), 1)

    out_velocity_ref[...] = acc_velocity_ref[...] + pairs(d_parts, stacked(act_three))
    out_mixer_ref[...] = acc_mixer_ref[...] + pairs(mixed_halves, d_three_halves)
    out_qkv_ref[...] = acc_qkv_ref[...] + pairs(act_two_halves, d_qkv_halves)
    bias = jnp.sum(d_forcing, axis=1, keepdims=True)
    row = lax.broadcasted_iota(jnp.int32, (GROUP, channels), 0)
    small = jnp.where(row == 0, sums[1:2] * scale, jnp.where(row == 1, sums[0:1], 0.0))
    out_small_ref[:GROUP] = acc_small_ref[:GROUP] + small
    out_small_ref[GROUP:] = acc_small_ref[GROUP:] + bias


def d_pre_of(d_normed, centred, sums, all_grad_sums, gain, count):
    unused_mean, scale, factor = norm_of(sums, gain, count)
    d_spread = -0.5 * gain * scale * scale * scale * all_grad_sums[1:2]
    return factor * (d_normed - all_grad_sums[0:1] / count) + (2.0 * d_spread / count) * centred


def weight_pairs(acc_ref, out_ref, left_halves, patches_ref, lon):
    cells = patches_ref.shape[0] - 2 * lon
    width = patches_ref.shape[1] // 3
    for tap in range(9):
        row, column = divmod(8 - tap, 3)
        right = patches_ref[lon * row : lon * row + cells, column * width : (column + 1) * width]
        out_ref[tap] = acc_ref[tap] + folded(folded(dot(left_halves, right), 0), 1)


def middle_back_kernel(
    lon, count,
    d_two_ref, pre_two_ref, sums_two_ref, all_two_ref, gain_two_ref,
    pre_one_ref, sums_one_ref, gain_ref, shift_ref, w_second_back_ref,
    acc_weight_ref, acc_small_ref,
    d_normed_ref, sums_ref, out_weight_ref, out_small_ref,
    patches_ref,
):
    sums_two = sums_two_ref[...]
    d_pre = d_pre_of(
        d_two_ref[...], pre_two_ref[...] - sums_two[0:1] / count, sums_two, all_two_ref[...],
        gain_two_ref[...], count,
    )
    fill_patches(patches_ref, d_pre, lon)
    d_act = conv_patches(patches_ref, w_second_back_ref, lon)
    mean, scale, factor = norm_of(sums_one_ref[...], gain_ref[...], count)
    centred = pre_one_ref[...] - mean
    normed = centred * factor + shift_ref[...]
    gate = sigmoid(normed)
    d_normed = d_act * gate * (1.0 + normed * (1.0 - gate))
    d_normed_ref[...] = d_normed
    sums = sums_of(d_normed, centred)
    sums_ref[...] = sums
    weight_pairs(acc_weight_ref, out_weight_ref, stacked((normed * gate).T), patches_ref, lon)
    row = lax.broadcasted_iota(jnp.int32, sums.shape, 0)
    small = jnp.where(row == 0, sums[1:2] * scale, jnp.where(row == 1, sums[0:1], 0.0))
    out_small_ref[...] = acc_small_ref[...] + small


def inlet_back_kernel(
    lon, count,
    state_ref, d_normed_ref, pre_one_ref, sums_one_ref, all_one_ref, gain_ref,
    inner_ref, d_two_ref, d_state_in_ref, w_first_back_ref, w_input_back_ref,
    acc_first_ref, acc_input_ref, acc_inner_ref,
    d_state_ref, out_first_ref, out_input_ref, out_inner_ref,
    patches_ref,
):
    cells = inner_ref.shape[0]
    sums_one = sums_one_ref[...]
    d_pre = d_pre_of(
        d_normed_ref[...], pre_one_ref[...] - sums_one[0:1] / count, sums_one, all_one_ref[...],
        gain_ref[...], count,
    )
    fill_patches(patches_ref, d_pre, lon)
    d_act = conv_patches(patches_ref, w_first_back_ref, lon) + d_two_ref[...]
    inner = inner_ref[...]
    gate = sigmoid(inner)
    d_inner = d_act * gate * (1.0 + inner * (1.0 - gate))
    weight_pairs(acc_first_ref, out_first_ref, stacked((inner * gate).T), patches_ref, lon)
    out_inner_ref[...] = acc_inner_ref[...] + d_inner
    patches_ref[lon : lon + cells, :256] = beside(d_inner)
    rows = [patches_ref[lon * place : lon * place + cells, :256] for place in range(3)]
    d_moving = folded(dot(jnp.concatenate(rows, axis=1), w_input_back_ref[...]), 1).T
    state = state_ref[...]
    moving_halves = stacked(inlet_channels(state, lon))
    for place in range(3):
        out_input_ref[place] = acc_input_ref[place] + folded(
            folded(dot(moving_halves, rows[2 - place]), 0), 1
        )
    size = 5 * GROUP
    d_groups = (
        lon_moved(d_moving[:size], 1, lon)
        + d_moving[size : 2 * size]
        + lon_moved(d_moving[2 * size : 3 * size], -1, lon)
    )
    d_state = d_state_in_ref[...] + d_groups[: 3 * GROUP]
    d_state_ref[:GROUP] = (
        d_state[:GROUP]
        - along_lon(d_groups[3 * GROUP : 4 * GROUP], lon)
        - along_lat(d_groups[4 * GROUP :], lon)
    )
    d_state_ref[GROUP:] = d_state[GROUP:]


def spread(groups, array, size):
    pad = jnp.zeros((GROUP - size, array.shape[1]), F32)
    pieces = []
    for group in range(groups):
        pieces += [array[group * size : (group + 1) * size], pad]
    return jnp.concatenate(pieces, axis=0)


def enter_kernel(plan, ids_ref, order_ref, state_ref, cot_ref, *out_refs):
    section, dp = ids_ref[0], ids_ref[1]
    size = state_ref.shape[1] // 3
    out_refs[0][...] = spread(3, state_ref[order_ref[0, plan.slot(section, dp)]], size)
    for steps, out_ref in enumerate(out_refs[1:]):
        target = lax.rem(section + steps, plan.sections)
        out_ref[...] = spread(3, cot_ref[0, order_ref[0, plan.slot(target, dp)]], size)


def leave_kernel(plan, ids_ref, values_ref, *out_refs):
    for steps, out_ref in enumerate(out_refs):
        out_ref[...] = values_ref[lax.rem(ids_ref[0] + steps, plan.sections)]


def arrive_kernel(plan, ids_ref, order_ref, *refs):
    section, dp = ids_ref[0], ids_ref[1]
    out_ref = refs[-1]
    size = out_ref.shape[2] // 3
    for steps, ref in enumerate(refs[:-1]):
        source = lax.rem(section - steps + plan.sections, plan.sections)
        place = order_ref[0, plan.slot(source, dp)]
        for group in range(3):
            out_ref[0, place, group * size : (group + 1) * size] = ref[group * GROUP : group * GROUP + size]


def put_conv_weight(out_ref, taps):
    for tap, weight in enumerate(taps):
        wide = beside(weight)
        rows = weight.shape[0]
        out_ref[2 * tap * rows : (2 * tap + 1) * rows] = wide
        out_ref[(2 * tap + 1) * rows : (2 * tap + 2) * rows] = wide


def put_left_weight(out_ref, weight):
    rows = weight.shape[0]
    for place, half in enumerate(halves(weight)):
        out_ref[place * rows : (place + 1) * rows] = jnp.concatenate([half, half], axis=1)


def first_weights_kernel(
    lon, quantities, w_input_ref, w_first_ref, b_input_ref, maps_ref,
    static_part_ref, moving_cat_ref, moving_back_ref, first_cat_ref,
    patches_ref, weight_ref, taps_ref,
):
    channels = w_input_ref.shape[2]
    moving = 5 * quantities
    statics = maps_ref.shape[0]
    taps_ref[...] = jnp.zeros(taps_ref.shape, F32)
    for tap in range(9):
        row, column = divmod(tap, 3)
        for group in range(5):
            start = (column * 5 + group) * GROUP
            taps_ref[9 + row, start : start + quantities] = w_input_ref[
                tap, group * quantities : (group + 1) * quantities
            ]
        taps_ref[tap, :statics] = w_input_ref[tap, moving:]
    put_conv_weight(moving_cat_ref, [taps_ref[9 + row] for row in range(3)])
    put_conv_weight(moving_back_ref, [taps_ref[11 - row].T for row in range(3)])
    put_conv_weight(weight_ref, [taps_ref[tap] for tap in range(9)])
    maps = jnp.concatenate(
        [maps_ref[...], jnp.zeros((channels - statics, maps_ref.shape[1]), F32)], axis=0
    )
    fill_patches(patches_ref, maps.T, lon)
    static_part_ref[...] = conv_patches(patches_ref, weight_ref, lon) + b_input_ref[...]
    put_conv_weight(first_cat_ref, [w_first_ref[tap] for tap in range(9)])


def second_weights_kernel(w_second_ref, out_ref):
    put_conv_weight(out_ref, [w_second_ref[tap] for tap in range(9)])


def outlet_weights_kernel(
    quantities, w_query_ref, w_key_ref, w_value_ref, w_mixer_ref, w_velocity_ref,
    qkv_ref, qkv_back_ref, mixer_ref, mixer_back_ref, velocity_ref, velocity_back_ref,
    rows_ref,
):
    parts = [ref[...] for ref in (w_query_ref, w_key_ref, w_value_ref)]
    put_left_weight(qkv_ref, jnp.concatenate([part.T for part in parts], axis=0))
    put_left_weight(qkv_back_ref, jnp.concatenate(parts, axis=1))
    put_left_weight(mixer_ref, w_mixer_ref[...].T)
    put_left_weight(mixer_back_ref, w_mixer_ref[...])
    channels = w_mixer_ref.shape[0]
    rows_ref[...] = jnp.zeros(rows_ref.shape, F32)
    for tap in range(9):
        for group in range(2):
            start = (tap * 2 + group) * GROUP
            rows_ref[start : start + quantities] = w_velocity_ref[
                tap, group * quantities : (group + 1) * quantities
            ]
    size = 18 * GROUP
    put_left_weight(velocity_ref, rows_ref[:size])
    put_left_weight(velocity_back_ref, rows_ref[...].T[:, :size])


def back_weights_kernel(w_first_ref, w_second_ref, first_ref, second_ref):
    put_conv_weight(first_ref, [w_first_ref[8 - tap].T for tap in range(9)])
    put_conv_weight(second_ref, [w_second_ref[8 - tap].T for tap in range(9)])


def index_of(ids_ref, plan, bits):
    own = ids_ref[0] * plan.dp + ids_ref[1]
    return sum(lax.rem(own // bit, 2) << place for place, bit in enumerate(bits))


def deal(total_ref, own, out_refs):
    rows = out_refs[0].shape[0]
    for turn, out_ref in enumerate(out_refs):
        out_ref[...] = total_ref[pl.ds(pl.multiple_of((own ^ turn) * rows, GROUP), rows)]


def pack_kernel(
    plan, bits, lon, statics, ids_ref, maps_ref, inner_ref, first_ref, second_ref, moving_ref,
    qkv_ref, mixer_ref, velocity_ref, small_one_ref, small_two_ref, *refs,
):
    out_refs, total_ref, patches_ref = refs[:-2], refs[-2], refs[-1]
    cells, channels = inner_ref.shape
    d_inner = inner_ref[...]
    fill_patches(patches_ref, d_inner, lon)
    width = patches_ref.shape[1] // 3
    maps = maps_ref[...]
    blank = jnp.zeros((-statics % GROUP, cells), F32)
    maps = jnp.concatenate([maps, blank], axis=0)
    rows = maps.shape[0]
    left = jnp.concatenate(halves(maps), axis=0)
    start = 0

    def put(value):
        nonlocal start
        total_ref[start : start + value.shape[0]] = value
        start += value.shape[0]

    for tap in range(9):
        put(first_ref[tap])
    for tap in range(9):
        put(second_ref[tap])
    for tap in range(9):
        row, column = divmod(8 - tap, 3)
        right = patches_ref[lon * row : lon * row + cells, column * width : (column + 1) * width]
        put(folded(folded(dot(left, right), 0), 1))
    for place in range(3):
        put(moving_ref[place, : 15 * GROUP])
    for part in range(3):
        put(qkv_ref[:, part * channels : (part + 1) * channels])
    put(mixer_ref[...])
    put(velocity_ref[...])
    put(small_one_ref[...])
    put(small_two_ref[...])
    put(jnp.zeros((GROUP, channels), F32) + jnp.sum(d_inner, axis=0, keepdims=True))
    total_ref[start:] = jnp.zeros((total_ref.shape[0] - start, channels), F32)
    deal(total_ref, index_of(ids_ref, plan, bits), out_refs)


def reduce_kernel(plan, bits, count, ids_ref, *refs):
    total_ref = refs[-1]
    total = refs[0][...]
    for ref in refs[1:count]:
        total = total + ref[...]
    if not bits:
        refs[count][...] = total
        return
    total_ref[...] = total
    deal(total_ref, index_of(ids_ref, plan, bits), refs[count:-1])


def gather_rows(plan, bits, ids_ref, part_refs, out_ref):
    own = index_of(ids_ref, plan, bits)
    rows = part_refs[0].shape[0]
    for turn, ref in enumerate(part_refs):
        out_ref[pl.ds(pl.multiple_of((own ^ turn) * rows, GROUP), rows)] = ref[...]


def gather_kernel(plan, bits, ids_ref, *refs):
    gather_rows(plan, bits, ids_ref, refs[:-1], refs[-1])


def unpack_kernel(
    plan, bits, quantities, statics, ids_ref, *refs,
):
    count = 1 << len(bits)
    (
        input_ref, bias_ref, first_ref, gain_one_ref, shift_one_ref, second_ref, gain_two_ref, shift_two_ref,
        query_ref, key_ref, value_ref, mixer_ref, velocity_ref, velocity_bias_ref, total_ref,
    ) = refs[count:]
    gather_rows(plan, bits, ids_ref, refs[:count], total_ref)
    channels = mixer_ref.shape[0]
    moving = 5 * quantities
    start = 0

    def take(rows):
        nonlocal start
        start += rows
        return total_ref[start - rows : start]

    for tap in range(9):
        first_ref[tap] = take(channels)
    for tap in range(9):
        second_ref[tap] = take(channels)
    for tap in range(9):
        input_ref[tap, moving:] = take(statics + -statics % GROUP)[:statics]
    for row in range(3):
        for column in range(3):
            for group in range(5):
                rows = take(GROUP)
                input_ref[row * 3 + column, group * quantities : (group + 1) * quantities] = rows[:quantities]
    query_ref[...] = take(channels)
    key_ref[...] = take(channels)
    value_ref[...] = take(channels)
    mixer_ref[...] = take(channels)
    for tap in range(9):
        for group in range(2):
            velocity_ref[tap, group * quantities : (group + 1) * quantities] = take(GROUP)[:quantities]
    small = take(GROUP)
    gain_one_ref[...], shift_one_ref[...] = small[0:1], small[1:2]
    small = take(GROUP)
    gain_two_ref[...], shift_two_ref[...] = small[0:1], small[1:2]
    velocity_bias_ref[...] = take(2 * GROUP)
    bias_ref[...] = take(GROUP)[0:1]


def call(kernel, outs, scratch=(), aliases=None, name=None, scalars=0, kinds=None):
    kinds = kinds or [F32] * len(outs)

    def run(*operands):
        places = [pltpu.SMEM] * scalars + [pltpu.VMEM] * (len(operands) - scalars)
        return pl.pallas_call(
            kernel,
            out_shape=tuple(jax.ShapeDtypeStruct(shape, kind) for shape, kind in zip(outs, kinds)),
            in_specs=[pl.BlockSpec(memory_space=place) for place in places],
            out_specs=tuple(pl.BlockSpec(memory_space=pltpu.VMEM) for unused in outs),
            scratch_shapes=scratch,
            input_output_aliases=aliases or {},
            compiler_params=pltpu.CompilerParams(vmem_limit_bytes=VMEM_LIMIT),
            name=name,
        )(*operands)

    return run


VMEM_LIMIT = 24 * 1024 * 1024


def in_groups(array, axis, groups):
    shape = array.shape
    split = shape[:axis] + (groups, shape[axis] // groups) + shape[axis + 1 :]
    array = array.reshape(split)
    pads = [(0, 0)] * array.ndim
    pads[axis + 1] = (0, GROUP - split[axis + 1])
    return jnp.pad(array, pads).reshape(shape[:axis] + (groups * GROUP,) + shape[axis + 1 :])


def from_groups(array, axis, groups, size):
    shape = array.shape
    array = array.reshape(shape[:axis] + (groups, GROUP) + shape[axis + 1 :])
    array = lax.slice_in_dim(array, 0, size, axis=axis + 1)
    return array.reshape(shape[:axis] + (groups * size,) + shape[axis + 1 :])


class Plan:
    def __init__(self, sections, dp):
        self.sections, self.dp = sections, dp
        self.halved = sections == 4 and dp >= 4
        self.half = dp // 2
        bits = [1 << place for place in range((sections * dp).bit_length() - 1)]
        dp_bits = [bit for bit in bits if bit < dp]
        section_bits = [bit for bit in bits if bit >= dp]
        if self.halved:
            self.sum_rounds = in_pairs(dp_bits[:-1]) + in_pairs(section_bits)
        else:
            self.sum_rounds = in_pairs(dp_bits) + [section_bits[:1]]
        self.all_rounds = [dp_bits[:1]] + in_pairs(section_bits) + in_pairs(dp_bits[1:])

    def slot(self, section, home):
        if not self.halved:
            return section
        return lax.rem(home // self.half + section // 2, 2) * 2 + lax.rem(section, 2)

    def other(self, section, dp):
        return dp ^ self.half if self.halved and section >= 2 else dp

    def to_workers(self, steps):
        return [
            (section * self.dp + home, self.joint((section + steps) % self.sections, home))
            for section in range(self.sections)
            for home in range(self.dp)
        ]

    def to_homes(self, steps):
        return [
            (section * self.dp + own, (section + steps) % self.sections * self.dp + self.other(section, own))
            for section in range(self.sections)
            for own in range(self.dp)
        ]

    def joint(self, section, home):
        return section * self.dp + self.other(section, home)


def in_pairs(bits):
    return [bits[start : start + 2] for start in range(0, len(bits), 2)]


def masks_of(bits):
    return [sum(bit for place, bit in enumerate(bits) if turn >> place & 1) for turn in range(1, 1 << len(bits))]


def exchanged(value, mask):
    size = lax.axis_size("section") * lax.axis_size("dp")
    return lax.ppermute(value, ("section", "dp"), [(own, own ^ mask) for own in range(size)])


def moved(value, pairs):
    going = [(source, target) for source, target in pairs if source != target]
    if not going:
        return value
    arrived = lax.ppermute(value, ("section", "dp"), going)
    if len(going) == len(pairs):
        return arrived
    stays = jnp.array([source == target for source, target in sorted(pairs)])
    own = lax.axis_index("section") * lax.axis_size("dp") + lax.axis_index("dp")
    return jnp.where(stays[own], value, arrived)


def micro_sum(plan, value):
    for bits in plan.sum_rounds:
        value = value + sum(exchanged(value, mask) for mask in masks_of(bits))
    return value


def on_device(
    state_start,
    static_maps,
    grouping,
    cotangent,
    w_input,
    b_input,
    w_first,
    gain_first,
    shift_first,
    w_second,
    gain_second,
    shift_second,
    w_query,
    w_key,
    w_value,
    w_mixer,
    w_velocity,
    b_velocity,
):
    segments = lax.axis_size("section")
    plan = Plan(segments, lax.axis_size("dp"))
    micro_count = segments // 2
    per_micro = state_start.shape[0] // micro_count
    cells = state_start.shape[2]
    lon = cells // LAT
    count = float(per_micro * cells * plan.dp)
    step_size = 2.0 / segments
    block_size = ATT_ROWS * lon
    channels = w_first.shape[2]
    quantities = state_start.shape[1] // 3
    statics = static_maps.shape[0]
    ids = jnp.stack([lax.axis_index("section"), lax.axis_index("dp")]).astype(jnp.int32)

    plane = (cells, channels)
    small = (GROUP, channels)
    conv = (9 * 2 * channels, 2 * channels)
    patches = pltpu.VMEM((cells + 2 * lon, 6 * channels), BF16)
    wide = pltpu.VMEM((3 * channels, cells), F32)
    narrow = pltpu.VMEM((channels, cells), F32)
    state_shape = (3 * GROUP, cells)

    state, *cots = call(
        functools.partial(enter_kernel, plan), [state_shape] * (segments + 1), name="enter", scalars=2
    )(ids, grouping, state_start, cotangent)
    state = moved(state, plan.to_workers(0))
    cots = jnp.stack([moved(cot, plan.to_workers(steps)) for steps, cot in enumerate(cots)])

    static_part, moving_cat, moving_back_cat, first_cat = call(
        functools.partial(first_weights_kernel, lon, quantities),
        [plane, (6 * channels, 2 * channels), (6 * channels, 2 * channels), conv],
        [patches, pltpu.VMEM(conv, BF16), pltpu.VMEM((12, channels, channels), F32)],
        name="first_weights", kinds=[F32, BF16, BF16, BF16],
    )(w_input, w_first, b_input[None], static_maps)
    (second_cat,) = call(second_weights_kernel, [conv], name="second_weights", kinds=[BF16])(w_second)
    qkv_cat, qkv_back_cat, mixer_cat, mixer_back_cat, out_cat, out_back_cat = call(
        functools.partial(outlet_weights_kernel, quantities),
        [(6 * channels, 2 * channels), (2 * channels, 6 * channels), (2 * channels, 2 * channels),
         (2 * channels, 2 * channels), (36 * GROUP, 2 * channels), (2 * channels, 36 * GROUP)],
        [pltpu.VMEM((2 * channels, channels), F32)], name="outlet_weights", kinds=[BF16] * 6,
    )(w_query, w_key, w_value, w_mixer, jnp.swapaxes(w_velocity, 1, 2))
    first_back_cat, second_back_cat = call(
        back_weights_kernel, [conv, conv], name="back_weights", kinds=[BF16, BF16]
    )(w_first, w_second)
    b_out = in_groups(b_velocity[:, None], 0, 2)
    gain_one, shift_one = gain_first[None], shift_first[None]
    gain_two, shift_two = gain_second[None], shift_second[None]

    inlet = call(
        functools.partial(inlet_kernel, lon), [plane, plane, small], [patches], name="inlet"
    )
    middle = call(
        functools.partial(middle_kernel, lon, count), [plane, small], [patches], name="middle"
    )
    outlet = call(
        functools.partial(outlet_kernel, lon, count, block_size, step_size),
        [state_shape], [wide, narrow], name="outlet",
    )
    outlet_back = call(
        functools.partial(outlet_back_kernel, lon, count, block_size, step_size, segments),
        [state_shape, plane, small, (channels, 3 * channels), (channels, channels),
         (18 * GROUP, channels), (3 * GROUP, channels)],
        [wide, narrow, narrow, wide],
        {15: 3, 16: 4, 17: 5, 18: 6}, name="outlet_back", scalars=2,
    )
    middle_back = call(
        functools.partial(middle_back_kernel, lon, count),
        [plane, small, (9, channels, channels), small], [patches],
        {10: 2, 11: 3}, name="middle_back",
    )
    inlet_back = call(
        functools.partial(inlet_back_kernel, lon, count),
        [state_shape, (9, channels, channels), (3, channels, channels), plane], [patches],
        {11: 1, 12: 2, 13: 3}, name="inlet_back",
    )

    def forward(state_in, unused):
        inner, pre_one, sums_one = inlet(state_in, static_part, moving_cat, first_cat)
        sums_one = micro_sum(plan, sums_one)
        pre_two, sums_two = middle(pre_one, sums_one, gain_one, shift_one, second_cat)
        sums_two = micro_sum(plan, sums_two)
        (state_out,) = outlet(
            state_in, inner, pre_two, sums_two, gain_two, shift_two, qkv_cat, mixer_cat, out_cat, b_out
        )
        return state_out, (state_in, state_out, inner, pre_one, pre_two, sums_one, sums_two)

    unused_last, (entered, path, inners, pres_one, pres_two, all_sums_one, all_sums_two) = lax.scan(
        forward, state, None, length=segments, unroll=min(4, segments)
    )

    def to_steps(values):
        parts = call(
            functools.partial(leave_kernel, plan), [state_shape] * segments, name="leave", scalars=1
        )(ids, values)
        parts = [moved(part, plan.to_homes(steps)) for steps, part in enumerate(parts)]
        (out,) = call(
            functools.partial(arrive_kernel, plan), [(1,) + state_start.shape], name="arrive", scalars=2
        )(ids, grouping, *parts)
        return out

    path_out = to_steps(path)

    def backward(carry, saved):
        d_state, acc = carry
        step, state_in, inner, pre_one, pre_two, sums_one, sums_two = saved
        d_partial, d_two, grad_two, qkv, mixer, velocity, small_two = outlet_back(
            ids, step, state_in, d_state, cots, inner, pre_two, sums_two, gain_two, shift_two,
            qkv_cat, mixer_cat, qkv_back_cat, mixer_back_cat, out_back_cat,
            acc["qkv"], acc["mixer"], acc["velocity"], acc["small_two"],
        )
        grad_two = micro_sum(plan, grad_two)
        d_normed, grad_one, second, small_one = middle_back(
            d_two, pre_two, sums_two, grad_two, gain_two,
            pre_one, sums_one, gain_one, shift_one, second_back_cat,
            acc["second"], acc["small_one"],
        )
        grad_one = micro_sum(plan, grad_one)
        d_state, first, moving, inner_sum = inlet_back(
            state_in, d_normed, pre_one, sums_one, grad_one, gain_one,
            inner, d_two, d_partial, first_back_cat, moving_back_cat,
            acc["first"], acc["moving"], acc["inner"],
        )
        acc = dict(
            qkv=qkv, mixer=mixer, velocity=velocity, small_two=small_two, second=second,
            small_one=small_one, first=first, moving=moving, inner=inner_sum,
        )
        return (d_state, acc), d_state

    acc = dict(
        qkv=jnp.zeros((channels, 3 * channels), F32),
        mixer=jnp.zeros((channels, channels), F32),
        velocity=jnp.zeros((18 * GROUP, channels), F32),
        small_two=jnp.zeros((3 * GROUP, channels), F32),
        second=jnp.zeros((9, channels, channels), F32),
        small_one=jnp.zeros(small, F32),
        first=jnp.zeros((9, channels, channels), F32),
        moving=jnp.zeros((3, channels, channels), F32),
        inner=jnp.zeros(plane, F32),
    )
    steps = jnp.arange(segments, dtype=jnp.int32)[:, None]
    (unused_start, acc), grads = lax.scan(
        backward,
        (jnp.zeros(state_shape, F32), acc),
        (steps, entered, inners, pres_one, pres_two, all_sums_one, all_sums_two),
        reverse=True,
        unroll=min(4, segments),
    )
    grads_out = to_steps(grads)

    rounds = plan.all_rounds
    rows = 2 * 9 * channels + 9 * (statics + -statics % GROUP) + 45 * GROUP + 4 * channels + 23 * GROUP
    unit = GROUP * segments * plan.dp
    rows = -(-rows // unit) * unit

    def shares(rows, bits):
        return [(rows >> len(bits), channels)] * (1 << len(bits))

    def swap(parts, bits):
        return [parts[0]] + [exchanged(part, mask) for part, mask in zip(parts[1:], masks_of(bits))]

    parts = call(
        functools.partial(pack_kernel, plan, rounds[0], lon, statics), shares(rows, rounds[0]),
        [pltpu.VMEM((rows, channels), F32), patches], name="pack", scalars=1,
    )(
        ids, static_maps, acc["inner"], acc["first"], acc["second"], acc["moving"], acc["qkv"], acc["mixer"],
        acc["velocity"], acc["small_one"], acc["small_two"],
    )
    for bits, later in zip(rounds, rounds[1:] + [[]]):
        parts = swap(parts, bits)
        rows >>= len(bits)
        parts = call(
            functools.partial(reduce_kernel, plan, later, len(parts)), shares(rows, later),
            [pltpu.VMEM((rows, channels), F32)], name="reduce_part", scalars=1,
        )(ids, *parts)
    for bits in rounds[::-1]:
        parts = swap([parts[0]] * (1 << len(bits)), bits)
        rows <<= len(bits)
        if bits is rounds[0]:
            break
        parts = call(
            functools.partial(gather_kernel, plan, bits), [(rows, channels)], name="gather_part", scalars=1
        )(ids, *parts)
    row = (1, channels)
    square = (channels, channels)
    grads_all = call(
        functools.partial(unpack_kernel, plan, rounds[0], quantities, statics),
        [w_input.shape, row, w_first.shape, row, row, w_second.shape, row, row, square, square, square, square,
         (9, 2 * quantities, channels), (2 * GROUP, channels)],
        [pltpu.VMEM((rows, channels), F32)], name="unpack", scalars=1,
    )(ids, *parts)
    grads_all = [grad[0] if grad.shape == row else grad for grad in grads_all]
    grads_all[-2] = jnp.swapaxes(grads_all[-2], 1, 2)
    grads_all[-1] = from_groups(grads_all[-1][:, :1], 0, 2, quantities)[:, 0]
    return (path_out, grads_out) + tuple(grads_all)


def solution(mesh):
    weights = (P(),) * 14
    return jax.shard_map(
        on_device,
        mesh=mesh,
        in_specs=(P("dp", None, None), P(), P("dp", None), P("section", "dp", None, None)) + weights,
        out_specs=(P("section", "dp", None, None), P("section", "dp", None, None)) + weights,
        check_vma=False,
    )
```

```python
import functools
import math

import jax
import jax.numpy as jnp
from jax import lax
from jax.experimental import pallas as pl
from jax.experimental.pallas import tpu as pltpu
from jax.sharding import PartitionSpec as P

HEADS = 4
LAT = 16
ATT_ROWS = 8
EPSILON = 1e-05
LOG2_E = 1.0 / math.log(2.0)
F32 = jnp.float32
BF16 = jnp.bfloat16
GROUP = 8


def dot(left, right, left_dim=1, right_dim=0):
    return lax.dot_general(
        left, right, (((left_dim,), (right_dim,)), ((), ())), preferred_element_type=F32
    )


def halves(value):
    high = value.astype(BF16)
    return high, (value - high.astype(F32)).astype(BF16)


def thirds(value):
    high = value.astype(BF16)
    rest = value - high.astype(F32)
    middle = rest.astype(BF16)
    return high, middle, (rest - middle.astype(F32)).astype(BF16)


def stacked(value):
    return jnp.concatenate(halves(value), axis=0)


def beside(value):
    return jnp.concatenate(halves(value), axis=1)


def folded(value, axis):
    size = value.shape[axis] // 2
    if axis == 0:
        return value[:size] + value[size:]
    return value[:, :size] + value[:, size:]


def cells_of(value):
    return lax.broadcasted_iota(jnp.int32, value.shape, value.ndim - 1)


def lon_moved(value, offset, lon):
    cells = value.shape[1]
    column = lax.rem(cells_of(value), lon)
    near = pltpu.roll(value, (-offset) % cells, 1)
    wrapped = pltpu.roll(value, (offset * (lon - 1)) % cells, 1)
    edge = lon - 1 if offset > 0 else 0
    return jnp.where(column == edge, wrapped, near)


def lat_moved(value, offset, lon):
    cells = value.shape[1]
    moved = pltpu.roll(value, (-offset * lon) % cells, 1)
    cell = cells_of(value)
    if offset > 0:
        return jnp.where(cell < cells - lon, moved, 0.0)
    return jnp.where(cell >= lon, moved, 0.0)


def along_lon(value, lon):
    return 0.5 * (lon_moved(value, 1, lon) - lon_moved(value, -1, lon))


def along_lat(value, lon):
    return 0.5 * (lat_moved(value, 1, lon) - lat_moved(value, -1, lon))


def fill_patches(patches_ref, value, lon):
    cells, channels = value.shape
    planes = value.reshape(cells // lon, lon, channels)
    blank = jnp.zeros((lon, patches_ref.shape[1]), BF16)
    patches_ref[:lon] = blank
    patches_ref[lon + cells :] = blank
    for place, offset in enumerate((-1, 0, 1)):
        moved = value
        if offset:
            moved = pltpu.roll(planes, (-offset) % lon, 1).reshape(cells, channels)
        high, low = halves(moved)
        start = place * 2 * channels
        patches_ref[lon : lon + cells, start : start + channels] = high
        patches_ref[lon : lon + cells, start + channels : start + 2 * channels] = low


def conv_patches(patches_ref, weight_ref, lon):
    cells = patches_ref.shape[0] - 2 * lon
    rows = [patches_ref[lon * place : lon * place + cells] for place in range(3)]
    return folded(dot(jnp.concatenate(rows, axis=1), weight_ref[...]), 1)


def sigmoid(value):
    return 1.0 / (1.0 + jnp.exp(-value))


def norm_of(sums, gain, count):
    mean = sums[0:1] / count
    spread = sums[1:2] / count - mean * mean
    scale = lax.rsqrt(spread + EPSILON)
    return mean, scale, gain * scale


def sums_of(value, other):
    total = jnp.sum(value, axis=0, keepdims=True)
    product = jnp.sum(value * other, axis=0, keepdims=True)
    row = lax.broadcasted_iota(jnp.int32, (GROUP, value.shape[1]), 0)
    return jnp.where(row == 0, total, jnp.where(row == 1, product, 0.0))


def inlet_channels(state, lon):
    amount = state[:GROUP]
    groups = jnp.concatenate([state, along_lon(amount, lon), along_lat(amount, lon)], axis=0)
    blank = jnp.zeros((GROUP, state.shape[1]), F32)
    return jnp.concatenate(
        [lon_moved(groups, -1, lon), groups, lon_moved(groups, 1, lon), blank], axis=0
    )


def advected(state, step_size, lon):
    amount, east, north = state[:GROUP], state[GROUP : 2 * GROUP], state[2 * GROUP :]
    return amount - step_size * (along_lon(amount * east, lon) + along_lat(amount * north, lon))


def row_products(left_rows, right_rows):
    left_high, left_low = halves(left_rows)
    right_high, right_low = halves(right_rows)
    left = jnp.concatenate([left_high, left_high, left_low, left_low], axis=0)
    right = jnp.concatenate([right_high, right_low, right_high, right_low], axis=0)
    return dot(left, right, 0, 0)


def attention_scores(key_rows, query_rows):
    key_high, key_mid, key_low = thirds(key_rows)
    query_high, query_mid, query_low = thirds(query_rows)
    left = jnp.concatenate([key_high, key_high, key_mid, key_mid, key_high, key_low], axis=0)
    right = jnp.concatenate(
        [query_high, query_mid, query_high, query_mid, query_low, query_high], axis=0
    )
    return dot(left, right, 0, 0)


def heads_of(channels, cells, block_size):
    width = channels // HEADS
    return [
        (slice(head * width, (head + 1) * width), slice(start, start + block_size))
        for start in range(0, cells, block_size)
        for head in range(HEADS)
    ]


def below(rows, offset):
    return slice(rows.start + offset, rows.stop + offset)


def entered_inlet_kernel(lon, ids_ref, own_ref, arrived_ref, *refs):
    state_ref = refs[3]
    state_ref[...] = jnp.where(ids_ref[0] < 2, own_ref[...], arrived_ref[...])
    inlet_kernel(lon, state_ref, *refs[:3], *refs[4:])


def inlet_kernel(
    lon, state_ref, static_ref, w_input_ref, w_first_ref,
    inner_ref, pre_ref, sums_ref, patches_ref,
):
    cells = state_ref.shape[1]
    moving = inlet_channels(state_ref[...], lon).T
    width = patches_ref.shape[1]
    blank = jnp.zeros((lon, width), BF16)
    patches_ref[:lon] = blank
    patches_ref[lon + cells :] = blank
    patches_ref[lon : lon + cells, :256] = beside(moving)
    rows = [patches_ref[lon * place : lon * place + cells, :256] for place in range(3)]
    inner = folded(dot(jnp.concatenate(rows, axis=1), w_input_ref[...]), 1) + static_ref[...]
    inner_ref[...] = inner
    fill_patches(patches_ref, inner * sigmoid(inner), lon)
    pre = conv_patches(patches_ref, w_first_ref, lon)
    pre_ref[...] = pre
    sums_ref[...] = sums_of(pre, pre)


def middle_kernel(
    lon, count, pre_one_ref, sums_one_ref, gain_ref, shift_ref, w_second_ref,
    pre_ref, sums_ref, patches_ref,
):
    mean, unused_scale, factor = norm_of(sums_one_ref[...], gain_ref[...], count)
    normed = (pre_one_ref[...] - mean) * factor + shift_ref[...]
    fill_patches(patches_ref, normed * sigmoid(normed), lon)
    pre = conv_patches(patches_ref, w_second_ref, lon)
    pre_ref[...] = pre
    sums_ref[...] = sums_of(pre, pre)


def act_two_channels(inner, pre_two, sums, gain, shift, count):
    mean, unused_scale, factor = norm_of(sums, gain, count)
    return (inner * sigmoid(inner) + (pre_two - mean) * factor + shift).T


def project(w_qkv_ref, act_two, head_width, qkv_ref):
    channels = act_two.shape[0]
    rows = folded(dot(w_qkv_ref[...], stacked(act_two)), 0)
    qkv_ref[:channels] = rows[:channels] * (LOG2_E / math.sqrt(head_width))
    qkv_ref[channels:] = rows[channels:]


def outlet_kernel(
    lon, count, block_size, step_size,
    state_ref, inner_ref, pre_two_ref, sums_two_ref, gain_ref, shift_ref,
    w_qkv_ref, w_mixer_ref, w_velocity_ref, b_velocity_ref,
    out_ref, qkv_ref, mixed_ref, weight_ref, powers_ref,
    slots_ref, done_ref,
):
    channels = inner_ref.shape[1]
    cells = inner_ref.shape[0]
    act_two = act_two_channels(
        inner_ref[...], pre_two_ref[...], sums_two_ref[...], gain_ref[...], shift_ref[...], count
    )
    project(w_qkv_ref, act_two, channels // HEADS, qkv_ref)
    heads = heads_of(channels, cells, block_size)

    def scores_of(turn):
        rows, lanes = heads[turn]
        return attention_scores(qkv_ref[below(rows, channels), lanes], qkv_ref[rows, lanes])

    def keep(turn):
        return pltpu.make_async_copy(
            slots_ref.at[turn % 2], powers_ref.at[turn], done_ref.at[turn % 2]
        )

    following = scores_of(0)
    for turn, (rows, lanes) in enumerate(heads):
        scores = following
        if turn + 1 < len(heads):
            following = scores_of(turn + 1)
        top = jnp.max(scores, axis=0, keepdims=True)
        powers = jnp.exp2(scores - top)
        weight = 1.0 / jnp.sum(powers, axis=0, keepdims=True)
        weight_ref[turn : turn + 1] = weight
        high, low = halves(powers)
        if turn >= 2:
            keep(turn - 2).wait()
        slots_ref[turn % 2, 0] = high
        slots_ref[turn % 2, 1] = low
        keep(turn).start()
        value = stacked(qkv_ref[below(rows, 2 * channels), lanes])
        mixed_ref[rows, lanes] = folded(dot(value, high) + dot(value, low), 0) * weight
    act_three = act_two + folded(dot(w_mixer_ref[...], stacked(mixed_ref[...])), 0)
    parts = folded(dot(w_velocity_ref[...], stacked(act_three)), 0)
    forcing = jnp.zeros((2 * GROUP, cells), F32) + b_velocity_ref[...]
    for column, lon_offset in enumerate((-1, 0, 1)):
        total = None
        for row, lat_offset in enumerate((-1, 0, 1)):
            start = (row * 3 + column) * 2 * GROUP
            part = parts[start : start + 2 * GROUP]
            if lat_offset:
                part = lat_moved(part, lat_offset, lon)
            total = part if total is None else total + part
        forcing = forcing + (lon_moved(total, lon_offset, lon) if lon_offset else total)
    state = state_ref[...]
    flows = state[GROUP:]
    out_ref[:GROUP] = advected(state, step_size, lon)
    out_ref[GROUP:] = flows + step_size * (forcing - flows)
    for turn in range(max(0, len(heads) - 2), len(heads)):
        keep(turn).wait()


def outlet_back_kernel(
    lon, count, block_size, step_size, sections, step,
    ids_ref,
    state_ref, d_next_ref, cots_ref, inner_ref, pre_two_ref, sums_two_ref, gain_ref, shift_ref,
    qkv_ref, mixed_ref, weight_ref, powers_ref,
    w_mixer_ref, w_qkv_back_ref, w_mixer_back_ref, w_velocity_back_ref,
    acc_qkv_ref, acc_mixer_ref, acc_velocity_ref, acc_small_ref,
    d_state_ref, d_two_ref, sums_ref,
    out_qkv_ref, out_mixer_ref, out_velocity_ref, out_small_ref,
    d_mixed_ref, d_qkv_ref, slots_ref, done_ref,
):
    channels = inner_ref.shape[1]
    cells = inner_ref.shape[0]
    heads = heads_of(channels, cells, block_size)

    def fetch(turn):
        return pltpu.make_async_copy(
            powers_ref.at[turn], slots_ref.at[turn % 2], done_ref.at[turn % 2]
        )

    for turn in range(min(2, len(heads))):
        fetch(turn).start()
    state = state_ref[...]
    seed = d_next_ref[...] + cots_ref[lax.rem(ids_ref[0] - step + sections, sections)]
    amount, east, north = state[:GROUP], state[GROUP : 2 * GROUP], state[2 * GROUP :]
    d_amount = seed[:GROUP]
    d_lon = step_size * along_lon(d_amount, lon)
    d_lat = step_size * along_lat(d_amount, lon)
    d_state_ref[:GROUP] = d_amount + d_lon * east + d_lat * north
    d_state_ref[GROUP : 2 * GROUP] = (1.0 - step_size) * seed[GROUP : 2 * GROUP] + d_lon * amount
    d_state_ref[2 * GROUP :] = (1.0 - step_size) * seed[2 * GROUP :] + d_lat * amount
    d_forcing = step_size * seed[GROUP:]
    pieces = []
    for lat_offset in (-1, 0, 1):
        moved_rows = lat_moved(d_forcing, -lat_offset, lon) if lat_offset else d_forcing
        for lon_offset in (-1, 0, 1):
            pieces.append(lon_moved(moved_rows, -lon_offset, lon) if lon_offset else moved_rows)
    d_parts = stacked(jnp.concatenate(pieces, axis=0))
    d_three = folded(dot(w_velocity_back_ref[...], d_parts), 0)
    d_three_halves = stacked(d_three)
    d_mixed_ref[...] = folded(dot(w_mixer_back_ref[...], d_three_halves), 0)

    def d_powers_of(turn):
        rows, lanes = heads[turn]
        d_mixed = d_mixed_ref[rows, lanes] * weight_ref[turn : turn + 1]
        return d_mixed, row_products(qkv_ref[below(rows, 2 * channels), lanes], d_mixed)

    following = d_powers_of(0)
    for turn, (rows, lanes) in enumerate(heads):
        d_mixed, d_powers = following
        if turn + 1 < len(heads):
            following = d_powers_of(turn + 1)
        inner_sum = jnp.sum(d_mixed * mixed_ref[rows, lanes], axis=0, keepdims=True)
        fetch(turn).wait()
        power_high, power_low = slots_ref[turn % 2, 0], slots_ref[turn % 2, 1]
        powers = power_high.astype(F32) + power_low.astype(F32)
        d_high, d_low = halves(powers * (d_powers - inner_sum))
        d_mixed_cells = beside(d_mixed.T)
        d_value = folded(dot(power_high, d_mixed_cells) + dot(power_low, d_mixed_cells), 1)
        query_cells = beside(qkv_ref[rows, lanes].T)
        d_key = folded(dot(d_high, query_cells) + dot(d_low, query_cells), 1)
        key_halves = stacked(qkv_ref[below(rows, channels), lanes])
        d_query = folded(dot(key_halves, d_high) + dot(key_halves, d_low), 0)
        if turn + 2 < len(heads):
            fetch(turn + 2).start()
        d_qkv_ref[rows, lanes] = d_query * (1.0 / math.sqrt(channels // HEADS))
        d_qkv_ref[below(rows, channels), lanes] = d_key.T * (1.0 / LOG2_E)
        d_qkv_ref[below(rows, 2 * channels), lanes] = d_value.T
    d_qkv_halves = stacked(d_qkv_ref[...])
    d_two = (d_three + folded(dot(w_qkv_back_ref[...], d_qkv_halves), 0)).T
    d_two_ref[...] = d_two
    mean, scale, unused_factor = norm_of(sums_two_ref[...], gain_ref[...], count)
    sums = sums_of(d_two, pre_two_ref[...] - mean)
    sums_ref[...] = sums

    def pairs(left, right):
        return folded(folded(dot(left, right, 1, 1), 0), 1)

    act_two = act_two_channels(
        inner_ref[...], pre_two_ref[...], sums_two_ref[...], gain_ref[...], shift_ref[...], count
    )
    mixed_halves = stacked(mixed_ref[...])
    act_three = act_two + folded(dot(w_mixer_ref[...], mixed_halves), 0)
    out_velocity_ref[...] = acc_velocity_ref[...] + pairs(d_parts, stacked(act_three))
    out_mixer_ref[...] = acc_mixer_ref[...] + pairs(mixed_halves, d_three_halves)
    out_qkv_ref[...] = acc_qkv_ref[...] + pairs(stacked(act_two), d_qkv_halves)
    bias = jnp.sum(d_forcing, axis=1, keepdims=True)
    row = lax.broadcasted_iota(jnp.int32, (GROUP, channels), 0)
    small = jnp.where(row == 0, sums[1:2] * scale, jnp.where(row == 1, sums[0:1], 0.0))
    out_small_ref[:GROUP] = acc_small_ref[:GROUP] + small
    out_small_ref[GROUP:] = acc_small_ref[GROUP:] + bias


def d_pre_of(d_normed, centred, sums, all_grad_sums, gain, count):
    unused_mean, scale, factor = norm_of(sums, gain, count)
    d_spread = -0.5 * gain * scale * scale * scale * all_grad_sums[1:2]
    return factor * (d_normed - all_grad_sums[0:1] / count) + (2.0 * d_spread / count) * centred


def weight_pairs(acc_ref, out_ref, left_halves, patches_ref, lon):
    cells = patches_ref.shape[0] - 2 * lon
    width = patches_ref.shape[1] // 3
    for tap in range(9):
        row, column = divmod(8 - tap, 3)
        right = patches_ref[lon * row : lon * row + cells, column * width : (column + 1) * width]
        out_ref[tap] = acc_ref[tap] + folded(folded(dot(left_halves, right), 0), 1)


def middle_back_kernel(
    lon, count,
    d_two_ref, pre_two_ref, sums_two_ref, all_two_ref, gain_two_ref,
    pre_one_ref, sums_one_ref, gain_ref, shift_ref, w_second_back_ref,
    acc_weight_ref, acc_small_ref,
    d_normed_ref, sums_ref, out_weight_ref, out_small_ref,
    patches_ref,
):
    sums_two = sums_two_ref[...]
    d_pre = d_pre_of(
        d_two_ref[...], pre_two_ref[...] - sums_two[0:1] / count, sums_two, all_two_ref[...],
        gain_two_ref[...], count,
    )
    fill_patches(patches_ref, d_pre, lon)
    d_act = conv_patches(patches_ref, w_second_back_ref, lon)
    mean, scale, factor = norm_of(sums_one_ref[...], gain_ref[...], count)
    centred = pre_one_ref[...] - mean
    normed = centred * factor + shift_ref[...]
    gate = sigmoid(normed)
    d_normed = d_act * gate * (1.0 + normed * (1.0 - gate))
    d_normed_ref[...] = d_normed
    sums = sums_of(d_normed, centred)
    sums_ref[...] = sums
    weight_pairs(acc_weight_ref, out_weight_ref, stacked((normed * gate).T), patches_ref, lon)
    row = lax.broadcasted_iota(jnp.int32, sums.shape, 0)
    small = jnp.where(row == 0, sums[1:2] * scale, jnp.where(row == 1, sums[0:1], 0.0))
    out_small_ref[...] = acc_small_ref[...] + small


def inlet_back_kernel(
    lon, count,
    state_ref, d_normed_ref, pre_one_ref, sums_one_ref, all_one_ref, gain_ref,
    inner_ref, d_two_ref, d_state_in_ref, w_first_back_ref, w_input_back_ref,
    acc_first_ref, acc_input_ref, acc_inner_ref,
    d_state_ref, out_first_ref, out_input_ref, out_inner_ref,
    patches_ref,
):
    cells = inner_ref.shape[0]
    sums_one = sums_one_ref[...]
    d_pre = d_pre_of(
        d_normed_ref[...], pre_one_ref[...] - sums_one[0:1] / count, sums_one, all_one_ref[...],
        gain_ref[...], count,
    )
    fill_patches(patches_ref, d_pre, lon)
    d_act = conv_patches(patches_ref, w_first_back_ref, lon) + d_two_ref[...]
    inner = inner_ref[...]
    gate = sigmoid(inner)
    d_inner = d_act * gate * (1.0 + inner * (1.0 - gate))
    weight_pairs(acc_first_ref, out_first_ref, stacked((inner * gate).T), patches_ref, lon)
    out_inner_ref[...] = acc_inner_ref[...] + d_inner
    patches_ref[lon : lon + cells, :256] = beside(d_inner)
    rows = [patches_ref[lon * place : lon * place + cells, :256] for place in range(3)]
    d_moving = folded(dot(jnp.concatenate(rows, axis=1), w_input_back_ref[...]), 1).T
    state = state_ref[...]
    moving_halves = stacked(inlet_channels(state, lon))
    for place in range(3):
        out_input_ref[place] = acc_input_ref[place] + folded(
            folded(dot(moving_halves, rows[2 - place]), 0), 1
        )
    size = 5 * GROUP
    d_groups = (
        lon_moved(d_moving[:size], 1, lon)
        + d_moving[size : 2 * size]
        + lon_moved(d_moving[2 * size : 3 * size], -1, lon)
    )
    d_state = d_state_in_ref[...] + d_groups[: 3 * GROUP]
    d_state_ref[:GROUP] = (
        d_state[:GROUP]
        - along_lon(d_groups[3 * GROUP : 4 * GROUP], lon)
        - along_lat(d_groups[4 * GROUP :], lon)
    )
    d_state_ref[GROUP:] = d_state[GROUP:]


def put_sample(out_ref, from_ref, place):
    size = from_ref.shape[0] // 3
    out_ref[...] = jnp.zeros(out_ref.shape, F32)
    for row in range(from_ref.shape[0]):
        target = row // size * GROUP + row % size
        out_ref[target : target + 1] = from_ref[row, pl.ds(place, 1)]


def enter_kernel(plan, ids_ref, order_ref, state_ref, out_ref):
    put_sample(out_ref, state_ref, order_ref[0, plan.slot(ids_ref[0], ids_ref[1])])


def seeds_kernel(plan, ids_ref, order_ref, cot_ref, *out_refs):
    for steps, out_ref in enumerate(out_refs):
        target = lax.rem(ids_ref[0] + steps, plan.sections)
        put_sample(out_ref, cot_ref, order_ref[0, plan.slot(target, ids_ref[1])])


def leave_kernel(plan, ids_ref, *refs):
    values_ref = refs[-1]
    for step in range(plan.sections):
        values_ref[step] = refs[step][...]
    for steps, out_ref in enumerate(refs[plan.sections : -1]):
        out_ref[...] = values_ref[lax.rem(ids_ref[0] + steps, plan.sections)]


def arrive_kernel(plan, ids_ref, order_ref, kept_ref, *refs):
    section, dp = ids_ref[0], ids_ref[1]
    out_ref = refs[-1]
    size = out_ref.shape[0] // 3
    for steps, ref in enumerate(refs[:-1]):
        source = lax.rem(section - steps + plan.sections, plan.sections)
        place = order_ref[0, plan.slot(source, dp)]
        value = ref[...]
        if plan.halved and not steps:
            value = jnp.where(section < 2, kept_ref[...], value)
        for row in range(out_ref.shape[0]):
            start = row // size * GROUP + row % size
            out_ref[row, pl.ds(place, 1)] = value[start : start + 1]


def put_conv_weight(out_ref, taps):
    for tap, weight in enumerate(taps):
        wide = beside(weight)
        rows = weight.shape[0]
        out_ref[2 * tap * rows : (2 * tap + 1) * rows] = wide
        out_ref[(2 * tap + 1) * rows : (2 * tap + 2) * rows] = wide


def put_left_weight(out_ref, weight):
    rows = weight.shape[0]
    for place, half in enumerate(halves(weight)):
        out_ref[place * rows : (place + 1) * rows] = jnp.concatenate([half, half], axis=1)


def first_weights_kernel(
    lon, quantities, w_input_ref, w_first_ref, b_input_ref, maps_ref,
    static_part_ref, moving_cat_ref, moving_back_ref, first_cat_ref,
    patches_ref, weight_ref, taps_ref,
):
    channels = w_input_ref.shape[2]
    moving = 5 * quantities
    statics = maps_ref.shape[0]
    taps_ref[...] = jnp.zeros(taps_ref.shape, F32)
    for tap in range(9):
        row, column = divmod(tap, 3)
        for group in range(5):
            start = (column * 5 + group) * GROUP
            taps_ref[9 + row, start : start + quantities] = w_input_ref[
                tap, group * quantities : (group + 1) * quantities
            ]
        taps_ref[tap, :statics] = w_input_ref[tap, moving:]
    put_conv_weight(moving_cat_ref, [taps_ref[9 + row] for row in range(3)])
    put_conv_weight(moving_back_ref, [taps_ref[11 - row].T for row in range(3)])
    put_conv_weight(weight_ref, [taps_ref[tap] for tap in range(9)])
    maps = jnp.concatenate(
        [maps_ref[...], jnp.zeros((channels - statics, maps_ref.shape[1]), F32)], axis=0
    )
    fill_patches(patches_ref, maps.T, lon)
    static_part_ref[...] = conv_patches(patches_ref, weight_ref, lon) + b_input_ref[...]
    put_conv_weight(first_cat_ref, [w_first_ref[tap] for tap in range(9)])


def second_weights_kernel(w_second_ref, out_ref):
    put_conv_weight(out_ref, [w_second_ref[tap] for tap in range(9)])


def outlet_weights_kernel(
    quantities, w_query_ref, w_key_ref, w_value_ref, w_mixer_ref, w_velocity_ref,
    qkv_ref, qkv_back_ref, mixer_ref, mixer_back_ref, velocity_ref, velocity_back_ref,
    rows_ref,
):
    parts = [ref[...] for ref in (w_query_ref, w_key_ref, w_value_ref)]
    put_left_weight(qkv_ref, jnp.concatenate([part.T for part in parts], axis=0))
    put_left_weight(qkv_back_ref, jnp.concatenate(parts, axis=1))
    put_left_weight(mixer_ref, w_mixer_ref[...].T)
    put_left_weight(mixer_back_ref, w_mixer_ref[...])
    channels = w_mixer_ref.shape[0]
    rows_ref[...] = jnp.zeros(rows_ref.shape, F32)
    for tap in range(9):
        for group in range(2):
            start = (tap * 2 + group) * GROUP
            rows_ref[start : start + quantities] = w_velocity_ref[
                tap, group * quantities : (group + 1) * quantities
            ]
    size = 18 * GROUP
    put_left_weight(velocity_ref, rows_ref[:size])
    put_left_weight(velocity_back_ref, rows_ref[...].T[:, :size])


def back_weights_kernel(w_first_ref, w_second_ref, first_ref, second_ref):
    put_conv_weight(first_ref, [w_first_ref[8 - tap].T for tap in range(9)])
    put_conv_weight(second_ref, [w_second_ref[8 - tap].T for tap in range(9)])


def index_of(ids_ref, plan, bits):
    own = ids_ref[0] * plan.dp + ids_ref[1]
    return sum(lax.rem(own // bit, 2) << place for place, bit in enumerate(bits))


def deal(total_ref, own, out_refs):
    rows = out_refs[0].shape[0]
    for turn, out_ref in enumerate(out_refs):
        out_ref[...] = total_ref[pl.ds(pl.multiple_of((own ^ turn) * rows, GROUP), rows)]


def pack_kernel(
    plan, bits, lon, statics, ids_ref, maps_ref, inner_ref, first_ref, second_ref, moving_ref,
    qkv_ref, mixer_ref, velocity_ref, small_one_ref, small_two_ref, *refs,
):
    out_refs, total_ref, patches_ref = refs[:-2], refs[-2], refs[-1]
    cells, channels = inner_ref.shape
    d_inner = inner_ref[...]
    fill_patches(patches_ref, d_inner, lon)
    width = patches_ref.shape[1] // 3
    maps = maps_ref[...]
    blank = jnp.zeros((-statics % GROUP, cells), F32)
    maps = jnp.concatenate([maps, blank], axis=0)
    rows = maps.shape[0]
    left = jnp.concatenate(halves(maps), axis=0)
    start = 0

    def put(value):
        nonlocal start
        total_ref[start : start + value.shape[0]] = value
        start += value.shape[0]

    for tap in range(9):
        put(first_ref[tap])
    for tap in range(9):
        put(second_ref[tap])
    for tap in range(9):
        row, column = divmod(8 - tap, 3)
        right = patches_ref[lon * row : lon * row + cells, column * width : (column + 1) * width]
        put(folded(folded(dot(left, right), 0), 1))
    for place in range(3):
        put(moving_ref[place, : 15 * GROUP])
    for part in range(3):
        put(qkv_ref[:, part * channels : (part + 1) * channels])
    put(mixer_ref[...])
    put(velocity_ref[...])
    put(small_one_ref[...])
    put(small_two_ref[...])
    put(jnp.zeros((GROUP, channels), F32) + jnp.sum(d_inner, axis=0, keepdims=True))
    total_ref[start:] = jnp.zeros((total_ref.shape[0] - start, channels), F32)
    deal(total_ref, index_of(ids_ref, plan, bits), out_refs)


def reduce_kernel(plan, bits, count, ids_ref, *refs):
    total_ref = refs[-1]
    total = refs[0][...]
    for ref in refs[1:count]:
        total = total + ref[...]
    if not bits:
        refs[count][...] = total
        return
    total_ref[...] = total
    deal(total_ref, index_of(ids_ref, plan, bits), refs[count:-1])


def gather_rows(plan, bits, ids_ref, part_refs, out_ref):
    own = index_of(ids_ref, plan, bits)
    rows = part_refs[0].shape[0]
    for turn, ref in enumerate(part_refs):
        out_ref[pl.ds(pl.multiple_of((own ^ turn) * rows, GROUP), rows)] = ref[...]


def gather_kernel(plan, bits, ids_ref, *refs):
    gather_rows(plan, bits, ids_ref, refs[:-1], refs[-1])


def unpack_kernel(
    plan, bits, quantities, statics, ids_ref, *refs,
):
    count = 1 << len(bits)
    (
        input_ref, bias_ref, first_ref, gain_one_ref, shift_one_ref, second_ref, gain_two_ref, shift_two_ref,
        query_ref, key_ref, value_ref, mixer_ref, velocity_ref, velocity_bias_ref, total_ref,
    ) = refs[count:]
    gather_rows(plan, bits, ids_ref, refs[:count], total_ref)
    channels = mixer_ref.shape[0]
    moving = 5 * quantities
    start = 0

    def take(rows):
        nonlocal start
        start += rows
        return total_ref[start - rows : start]

    for tap in range(9):
        first_ref[tap] = take(channels)
    for tap in range(9):
        second_ref[tap] = take(channels)
    for tap in range(9):
        input_ref[tap, moving:] = take(statics + -statics % GROUP)[:statics]
    for row in range(3):
        for column in range(3):
            for group in range(5):
                rows = take(GROUP)
                input_ref[row * 3 + column, group * quantities : (group + 1) * quantities] = rows[:quantities]
    query_ref[...] = take(channels)
    key_ref[...] = take(channels)
    value_ref[...] = take(channels)
    mixer_ref[...] = take(channels)
    for tap in range(9):
        for group in range(2):
            velocity_ref[tap, group * quantities : (group + 1) * quantities] = take(GROUP)[:quantities]
    small = take(GROUP)
    gain_one_ref[...], shift_one_ref[...] = small[0:1], small[1:2]
    small = take(GROUP)
    gain_two_ref[...], shift_two_ref[...] = small[0:1], small[1:2]
    velocity_bias_ref[...] = take(2 * GROUP)
    bias_ref[...] = take(GROUP)[0:1]


def call(kernel, outs, scratch=(), aliases=None, name=None, scalars=0, kinds=None, far_in=(), far_out=()):
    kinds = kinds or [F32] * len(outs)

    def run(*operands):
        places = [pltpu.SMEM] * scalars + [pltpu.VMEM] * (len(operands) - scalars)
        for place in far_in:
            places[place] = pl.ANY
        out_places = [pl.ANY if place in far_out else pltpu.VMEM for place in range(len(outs))]
        return pl.pallas_call(
            kernel,
            out_shape=tuple(jax.ShapeDtypeStruct(shape, kind) for shape, kind in zip(outs, kinds)),
            in_specs=[pl.BlockSpec(memory_space=place) for place in places],
            out_specs=tuple(pl.BlockSpec(memory_space=place) for place in out_places),
            scratch_shapes=scratch,
            input_output_aliases=aliases or {},
            compiler_params=pltpu.CompilerParams(vmem_limit_bytes=VMEM_LIMIT),
            name=name,
        )(*operands)

    return run


KEPT_STEPS = 4
VMEM_LIMIT = 24 * 1024 * 1024


def in_groups(array, axis, groups):
    shape = array.shape
    split = shape[:axis] + (groups, shape[axis] // groups) + shape[axis + 1 :]
    array = array.reshape(split)
    pads = [(0, 0)] * array.ndim
    pads[axis + 1] = (0, GROUP - split[axis + 1])
    return jnp.pad(array, pads).reshape(shape[:axis] + (groups * GROUP,) + shape[axis + 1 :])


def from_groups(array, axis, groups, size):
    shape = array.shape
    array = array.reshape(shape[:axis] + (groups, GROUP) + shape[axis + 1 :])
    array = lax.slice_in_dim(array, 0, size, axis=axis + 1)
    return array.reshape(shape[:axis] + (groups * size,) + shape[axis + 1 :])


class Plan:
    def __init__(self, sections, dp):
        self.sections, self.dp = sections, dp
        self.halved = sections == 4 and dp >= 4
        self.half = dp // 2
        bits = [1 << place for place in range((sections * dp).bit_length() - 1)]
        dp_bits = [bit for bit in bits if bit < dp]
        section_bits = [bit for bit in bits if bit >= dp]
        if self.halved:
            self.sum_rounds = in_pairs(dp_bits[:-1]) + in_pairs(section_bits)
        else:
            self.sum_rounds = in_pairs(dp_bits) + [section_bits[:1]]
        self.all_rounds = [dp_bits[:1]] + in_pairs(section_bits) + in_pairs(dp_bits[1:])

    def slot(self, section, home):
        if not self.halved:
            return section
        return lax.rem(home // self.half + section // 2, 2) * 2 + lax.rem(section, 2)

    def other(self, section, dp):
        return dp ^ self.half if self.halved and section >= 2 else dp

    def to_workers(self, steps):
        return [
            (section * self.dp + home, self.joint((section + steps) % self.sections, home))
            for section in range(self.sections)
            for home in range(self.dp)
        ]

    def to_homes(self, steps):
        return [
            (section * self.dp + own, (section + steps) % self.sections * self.dp + self.other(section, own))
            for section in range(self.sections)
            for own in range(self.dp)
        ]

    def joint(self, section, home):
        return section * self.dp + self.other(section, home)


def in_pairs(bits):
    return [bits[start : start + 2] for start in range(0, len(bits), 2)]


def masks_of(bits):
    return [sum(bit for place, bit in enumerate(bits) if turn >> place & 1) for turn in range(1, 1 << len(bits))]


def exchanged(value, mask):
    size = lax.axis_size("section") * lax.axis_size("dp")
    return lax.ppermute(value, ("section", "dp"), [(own, own ^ mask) for own in range(size)])


def moved(value, pairs):
    going = [(source, target) for source, target in pairs if source != target]
    if not going:
        return value
    return lax.ppermute(value, ("section", "dp"), going)


def micro_sum(plan, value):
    for bits in plan.sum_rounds:
        value = value + sum(exchanged(value, mask) for mask in masks_of(bits))
    return value


def on_device(
    state_start,
    static_maps,
    grouping,
    cotangent,
    w_input,
    b_input,
    w_first,
    gain_first,
    shift_first,
    w_second,
    gain_second,
    shift_second,
    w_query,
    w_key,
    w_value,
    w_mixer,
    w_velocity,
    b_velocity,
):
    segments = lax.axis_size("section")
    plan = Plan(segments, lax.axis_size("dp"))
    micro_count = segments // 2
    per_micro = state_start.shape[0] // micro_count
    cells = state_start.shape[2]
    lon = cells // LAT
    count = float(per_micro * cells * plan.dp)
    step_size = 2.0 / segments
    block_size = ATT_ROWS * lon
    channels = w_first.shape[2]
    quantities = state_start.shape[1] // 3
    statics = static_maps.shape[0]
    ids = jnp.stack([lax.axis_index("section"), lax.axis_index("dp")]).astype(jnp.int32)

    plane = (cells, channels)
    small = (GROUP, channels)
    conv = (9 * 2 * channels, 2 * channels)
    patches = pltpu.VMEM((cells + 2 * lon, 6 * channels), BF16)
    wide = pltpu.VMEM((3 * channels, cells), F32)
    narrow = pltpu.VMEM((channels, cells), F32)
    state_shape = (3 * GROUP, cells)

    (own_state,) = call(functools.partial(enter_kernel, plan), [state_shape], name="enter", scalars=2)(
        ids, grouping, jnp.swapaxes(state_start, 0, 1)
    )
    arrived_state = moved(own_state, plan.to_workers(0))

    static_part, moving_cat, moving_back_cat, first_cat = call(
        functools.partial(first_weights_kernel, lon, quantities),
        [plane, (6 * channels, 2 * channels), (6 * channels, 2 * channels), conv],
        [patches, pltpu.VMEM(conv, BF16), pltpu.VMEM((12, channels, channels), F32)],
        name="first_weights", kinds=[F32, BF16, BF16, BF16],
    )(w_input, w_first, b_input[None], static_maps)
    (second_cat,) = call(second_weights_kernel, [conv], name="second_weights", kinds=[BF16])(w_second)
    qkv_cat, qkv_back_cat, mixer_cat, mixer_back_cat, out_cat, out_back_cat = call(
        functools.partial(outlet_weights_kernel, quantities),
        [(6 * channels, 2 * channels), (2 * channels, 6 * channels), (2 * channels, 2 * channels),
         (2 * channels, 2 * channels), (36 * GROUP, 2 * channels), (2 * channels, 36 * GROUP)],
        [pltpu.VMEM((2 * channels, channels), F32)], name="outlet_weights", kinds=[BF16] * 6,
    )(w_query, w_key, w_value, w_mixer, jnp.swapaxes(w_velocity, 1, 2))
    first_back_cat, second_back_cat = call(
        back_weights_kernel, [conv, conv], name="back_weights", kinds=[BF16, BF16]
    )(w_first, w_second)
    b_out = in_groups(b_velocity[:, None], 0, 2)
    gain_one, shift_one = gain_first[None], shift_first[None]
    gain_two, shift_two = gain_second[None], shift_second[None]

    inlet = call(
        functools.partial(inlet_kernel, lon), [plane, plane, small], [patches], name="inlet"
    )
    middle = call(
        functools.partial(middle_kernel, lon, count), [plane, small], [patches], name="middle"
    )
    heads = HEADS * (cells // block_size)
    powers = (heads, 2, block_size, block_size)
    slots = [pltpu.VMEM((2,) + powers[1:], BF16), pltpu.SemaphoreType.DMA((2,))]
    outlet = call(
        functools.partial(outlet_kernel, lon, count, block_size, step_size),
        [state_shape, (3 * channels, cells), (channels, cells), (heads, block_size), powers],
        slots, name="outlet", kinds=[F32] * 4 + [BF16], far_out=[4],
    )

    def outlet_back(step):
        return call(
            functools.partial(outlet_back_kernel, lon, count, block_size, step_size, segments, step),
            [state_shape, plane, small, (channels, 3 * channels), (channels, channels),
             (18 * GROUP, channels), (3 * GROUP, channels)],
            [narrow, wide] + slots,
            {17: 3, 18: 4, 19: 5, 20: 6}, name="outlet_back", scalars=1, far_in=[12],
        )

    middle_back = call(
        functools.partial(middle_back_kernel, lon, count),
        [plane, small, (9, channels, channels), small], [patches],
        {10: 2, 11: 3}, name="middle_back",
    )
    inlet_back = call(
        functools.partial(inlet_back_kernel, lon, count),
        [state_shape, (9, channels, channels), (3, channels, channels), plane], [patches],
        {11: 1, 12: 2, 13: 3}, name="inlet_back",
    )

    state = own_state
    path, saved = [], []
    cots = None
    for step in range(segments):
        if plan.halved and not step:
            state, inner, pre_one, sums_one = call(
                functools.partial(entered_inlet_kernel, lon), [state_shape, plane, plane, small], [patches],
                name="inlet", scalars=1,
            )(ids, own_state, arrived_state, static_part, moving_cat, first_cat)
        else:
            inner, pre_one, sums_one = inlet(state, static_part, moving_cat, first_cat)
        sums_one = micro_sum(plan, sums_one)
        pre_two, sums_two = middle(pre_one, sums_one, gain_one, shift_one, second_cat)
        sums_two = micro_sum(plan, sums_two)
        state_out, qkv, mixed, weight, powers_kept = outlet(
            state, inner, pre_two, sums_two, gain_two, shift_two, qkv_cat, mixer_cat, out_cat, b_out
        )
        kept = (qkv, mixed, weight, powers_kept) if step >= segments - KEPT_STEPS else None
        saved.append((state, inner, pre_one, pre_two, sums_one, sums_two, kept))
        path.append(state_out)
        state = state_out
        if not step:
            state, cot_local = lax.optimization_barrier((state, cotangent))
            sent = call(
                functools.partial(seeds_kernel, plan), [state_shape] * segments, name="seeds", scalars=2
            )(ids, grouping, jnp.swapaxes(cot_local[0], 0, 1))
            cots = [moved(cot, plan.to_workers(steps)) for steps, cot in enumerate(sent)]
            if plan.halved:
                cots[0] = jnp.where(lax.axis_index("section") < 2, sent[0], cots[0])
    cots = jnp.stack(cots)

    def sent_home(values):
        parts = call(
            functools.partial(leave_kernel, plan), [state_shape] * segments,
            [pltpu.VMEM((segments,) + state_shape, F32)], name="leave", scalars=1,
        )(ids, *values)
        return [parts[0]] + [moved(part, plan.to_homes(steps)) for steps, part in enumerate(parts)]

    def put_home(parts):
        rows, samples = state_start.shape[1], state_start.shape[0]
        (out,) = call(
            functools.partial(arrive_kernel, plan), [(rows, samples, cells)], name="arrive", scalars=2
        )(ids, grouping, *parts)
        return jnp.swapaxes(out, 0, 1)[None]

    path_parts = sent_home(path)

    acc = dict(
        qkv=jnp.zeros((channels, 3 * channels), F32),
        mixer=jnp.zeros((channels, channels), F32),
        velocity=jnp.zeros((18 * GROUP, channels), F32),
        small_two=jnp.zeros((3 * GROUP, channels), F32),
        second=jnp.zeros((9, channels, channels), F32),
        small_one=jnp.zeros(small, F32),
        first=jnp.zeros((9, channels, channels), F32),
        moving=jnp.zeros((3, channels, channels), F32),
        inner=jnp.zeros(plane, F32),
    )
    d_state = jnp.zeros(state_shape, F32)
    grads = [None] * segments
    path_out = None
    for step in reversed(range(segments)):
        state, inner, pre_one, pre_two, sums_one, sums_two, kept = saved[step]
        if kept is None:
            state, d_state = lax.optimization_barrier((state, d_state))
            kept = outlet(
                state, inner, pre_two, sums_two, gain_two, shift_two, qkv_cat, mixer_cat, out_cat, b_out
            )[1:]
        qkv, mixed, weight, powers_kept = kept
        d_partial, d_two, grad_two, acc["qkv"], acc["mixer"], acc["velocity"], acc["small_two"] = outlet_back(step)(
            ids, state, d_state, cots, inner, pre_two, sums_two, gain_two, shift_two,
            qkv, mixed, weight, powers_kept,
            mixer_cat, qkv_back_cat, mixer_back_cat, out_back_cat,
            acc["qkv"], acc["mixer"], acc["velocity"], acc["small_two"],
        )
        grad_two = micro_sum(plan, grad_two)
        d_normed, grad_one, acc["second"], acc["small_one"] = middle_back(
            d_two, pre_two, sums_two, grad_two, gain_two,
            pre_one, sums_one, gain_one, shift_one, second_back_cat,
            acc["second"], acc["small_one"],
        )
        grad_one = micro_sum(plan, grad_one)
        d_state, acc["first"], acc["moving"], acc["inner"] = inlet_back(
            state, d_normed, pre_one, sums_one, grad_one, gain_one,
            inner, d_two, d_partial, first_back_cat, moving_back_cat,
            acc["first"], acc["moving"], acc["inner"],
        )
        grads[step] = d_state
        if path_out is None:
            d_state, *path_parts = lax.optimization_barrier((d_state, *path_parts))
            path_out = put_home(path_parts)
            d_state, path_out = lax.optimization_barrier((d_state, path_out))
    grad_parts = sent_home(grads)

    rounds = plan.all_rounds
    rows = 2 * 9 * channels + 9 * (statics + -statics % GROUP) + 45 * GROUP + 4 * channels + 23 * GROUP
    unit = GROUP * segments * plan.dp
    rows = -(-rows // unit) * unit

    def shares(rows, bits):
        return [(rows >> len(bits), channels)] * (1 << len(bits))

    def swap(parts, bits):
        return [parts[0]] + [exchanged(part, mask) for part, mask in zip(parts[1:], masks_of(bits))]

    parts = call(
        functools.partial(pack_kernel, plan, rounds[0], lon, statics), shares(rows, rounds[0]),
        [pltpu.VMEM((rows, channels), F32), patches], name="pack", scalars=1,
    )(
        ids, static_maps, acc["inner"], acc["first"], acc["second"], acc["moving"], acc["qkv"], acc["mixer"],
        acc["velocity"], acc["small_one"], acc["small_two"],
    )
    grads_out = None
    for bits, later in zip(rounds, rounds[1:] + [[]]):
        parts = swap(parts, bits)
        if grads_out is None:
            parts, grad_parts = lax.optimization_barrier((parts, grad_parts))
            grads_out = put_home(grad_parts)
        rows >>= len(bits)
        parts = call(
            functools.partial(reduce_kernel, plan, later, len(parts)), shares(rows, later),
            [pltpu.VMEM((rows, channels), F32)], name="reduce_part", scalars=1,
        )(ids, *parts)
    for bits in rounds[::-1]:
        parts = swap([parts[0]] * (1 << len(bits)), bits)
        rows <<= len(bits)
        if bits is rounds[0]:
            break
        parts = call(
            functools.partial(gather_kernel, plan, bits), [(rows, channels)], name="gather_part", scalars=1
        )(ids, *parts)
    row = (1, channels)
    square = (channels, channels)
    grads_all = call(
        functools.partial(unpack_kernel, plan, rounds[0], quantities, statics),
        [w_input.shape, row, w_first.shape, row, row, w_second.shape, row, row, square, square, square, square,
         (9, 2 * quantities, channels), (2 * GROUP, channels)],
        [pltpu.VMEM((rows, channels), F32)], name="unpack", scalars=1,
    )(ids, *parts)
    grads_all = [grad[0] if grad.shape == row else grad for grad in grads_all]
    grads_all[-2] = jnp.swapaxes(grads_all[-2], 1, 2)
    grads_all[-1] = from_groups(grads_all[-1][:, :1], 0, 2, quantities)[:, 0]
    return (path_out, grads_out) + tuple(grads_all)


def solution(mesh):
    weights = (P(),) * 14
    return jax.shard_map(
        on_device,
        mesh=mesh,
        in_specs=(P("dp", None, None), P(), P("dp", None), P("section", "dp", None, None)) + weights,
        out_specs=(P("section", "dp", None, None), P("section", "dp", None, None)) + weights,
        check_vma=False,
    )
```

```python
import functools
import math

import jax
import jax.numpy as jnp
from jax import lax
from jax.experimental import pallas as pl
from jax.experimental.pallas import tpu as pltpu
from jax.sharding import PartitionSpec as P

HEADS = 4
LAT = 16
ATT_ROWS = 8
EPSILON = 1e-05
LOG2_E = 1.0 / math.log(2.0)
F32 = jnp.float32
BF16 = jnp.bfloat16
GROUP = 8


def dot(left, right, left_dim=1, right_dim=0):
    return lax.dot_general(
        left, right, (((left_dim,), (right_dim,)), ((), ())), preferred_element_type=F32
    )


def halves(value):
    high = value.astype(BF16)
    return high, (value - high.astype(F32)).astype(BF16)


def thirds(value):
    high = value.astype(BF16)
    rest = value - high.astype(F32)
    middle = rest.astype(BF16)
    return high, middle, (rest - middle.astype(F32)).astype(BF16)


def stacked(value):
    return jnp.concatenate(halves(value), axis=0)


def beside(value):
    return jnp.concatenate(halves(value), axis=1)


def folded(value, axis):
    size = value.shape[axis] // 2
    if axis == 0:
        return value[:size] + value[size:]
    return value[:, :size] + value[:, size:]


def cells_of(value):
    return lax.broadcasted_iota(jnp.int32, value.shape, value.ndim - 1)


def lon_moved(value, offset, lon):
    cells = value.shape[1]
    column = lax.rem(cells_of(value), lon)
    near = pltpu.roll(value, (-offset) % cells, 1)
    wrapped = pltpu.roll(value, (offset * (lon - 1)) % cells, 1)
    edge = lon - 1 if offset > 0 else 0
    return jnp.where(column == edge, wrapped, near)


def lat_moved(value, offset, lon):
    cells = value.shape[1]
    moved = pltpu.roll(value, (-offset * lon) % cells, 1)
    cell = cells_of(value)
    if offset > 0:
        return jnp.where(cell < cells - lon, moved, 0.0)
    return jnp.where(cell >= lon, moved, 0.0)


def along_lon(value, lon):
    return 0.5 * (lon_moved(value, 1, lon) - lon_moved(value, -1, lon))


def along_lat(value, lon):
    return 0.5 * (lat_moved(value, 1, lon) - lat_moved(value, -1, lon))


def fill_patches(patches_ref, value, lon):
    cells, channels = value.shape
    planes = value.reshape(cells // lon, lon, channels)
    blank = jnp.zeros((lon, patches_ref.shape[1]), BF16)
    patches_ref[:lon] = blank
    patches_ref[lon + cells :] = blank
    for place, offset in enumerate((-1, 0, 1)):
        moved = value
        if offset:
            moved = pltpu.roll(planes, (-offset) % lon, 1).reshape(cells, channels)
        high, low = halves(moved)
        start = place * 2 * channels
        patches_ref[lon : lon + cells, start : start + channels] = high
        patches_ref[lon : lon + cells, start + channels : start + 2 * channels] = low


def conv_patches(patches_ref, weight_ref, lon):
    cells = patches_ref.shape[0] - 2 * lon
    rows = [patches_ref[lon * place : lon * place + cells] for place in range(3)]
    return folded(dot(jnp.concatenate(rows, axis=1), weight_ref[...]), 1)


def sigmoid(value):
    return 1.0 / (1.0 + jnp.exp(-value))


def norm_of(sums, gain, count):
    mean = sums[0:1] / count
    spread = sums[1:2] / count - mean * mean
    scale = lax.rsqrt(spread + EPSILON)
    return mean, scale, gain * scale


def sums_of(value, other):
    total = jnp.sum(value, axis=0, keepdims=True)
    product = jnp.sum(value * other, axis=0, keepdims=True)
    row = lax.broadcasted_iota(jnp.int32, (GROUP, value.shape[1]), 0)
    return jnp.where(row == 0, total, jnp.where(row == 1, product, 0.0))


def inlet_channels(state, lon):
    amount = state[:GROUP]
    groups = jnp.concatenate([state, along_lon(amount, lon), along_lat(amount, lon)], axis=0)
    blank = jnp.zeros((GROUP, state.shape[1]), F32)
    return jnp.concatenate(
        [lon_moved(groups, -1, lon), groups, lon_moved(groups, 1, lon), blank], axis=0
    )


def advected(state, step_size, lon):
    amount, east, north = state[:GROUP], state[GROUP : 2 * GROUP], state[2 * GROUP :]
    return amount - step_size * (along_lon(amount * east, lon) + along_lat(amount * north, lon))


def row_products(left_rows, right_rows):
    left_high, left_low = halves(left_rows)
    right_high, right_low = halves(right_rows)
    left = jnp.concatenate([left_high, left_high, left_low, left_low], axis=0)
    right = jnp.concatenate([right_high, right_low, right_high, right_low], axis=0)
    return dot(left, right, 0, 0)


def attention_scores(key_rows, query_rows):
    key_high, key_mid, key_low = thirds(key_rows)
    query_high, query_mid, query_low = thirds(query_rows)
    left = jnp.concatenate([key_high, key_high, key_mid, key_mid, key_high, key_low], axis=0)
    right = jnp.concatenate(
        [query_high, query_mid, query_high, query_mid, query_low, query_high], axis=0
    )
    return dot(left, right, 0, 0)


def heads_of(channels, cells, block_size):
    width = channels // HEADS
    return [
        (slice(head * width, (head + 1) * width), slice(start, start + block_size))
        for start in range(0, cells, block_size)
        for head in range(HEADS)
    ]


def of_head(value, rows):
    channel = lax.broadcasted_iota(jnp.int32, value.shape, 1)
    return jnp.where((channel >= rows.start) & (channel < rows.stop), value, 0.0)


def below(rows, offset):
    return slice(rows.start + offset, rows.stop + offset)


def entered_inlet_kernel(lon, ids_ref, own_ref, arrived_ref, *refs):
    state_ref = refs[3]
    state_ref[...] = jnp.where(ids_ref[0] < 2, own_ref[...], arrived_ref[...])
    inlet_kernel(lon, state_ref, *refs[:3], *refs[4:])


def inlet_kernel(
    lon, state_ref, static_ref, w_input_ref, w_first_ref,
    inner_ref, pre_ref, sums_ref, patches_ref,
):
    cells = state_ref.shape[1]
    moving = inlet_channels(state_ref[...], lon).T
    width = patches_ref.shape[1]
    blank = jnp.zeros((lon, width), BF16)
    patches_ref[:lon] = blank
    patches_ref[lon + cells :] = blank
    patches_ref[lon : lon + cells, :256] = beside(moving)
    rows = [patches_ref[lon * place : lon * place + cells, :256] for place in range(3)]
    inner = folded(dot(jnp.concatenate(rows, axis=1), w_input_ref[...]), 1) + static_ref[...]
    inner_ref[...] = inner
    fill_patches(patches_ref, inner * sigmoid(inner), lon)
    pre = conv_patches(patches_ref, w_first_ref, lon)
    pre_ref[...] = pre
    sums_ref[...] = sums_of(pre, pre)


def middle_kernel(
    lon, count, pre_one_ref, sums_one_ref, gain_ref, shift_ref, w_second_ref,
    pre_ref, sums_ref, patches_ref,
):
    mean, unused_scale, factor = norm_of(sums_one_ref[...], gain_ref[...], count)
    normed = (pre_one_ref[...] - mean) * factor + shift_ref[...]
    fill_patches(patches_ref, normed * sigmoid(normed), lon)
    pre = conv_patches(patches_ref, w_second_ref, lon)
    pre_ref[...] = pre
    sums_ref[...] = sums_of(pre, pre)


def act_two_channels(inner, pre_two, sums, gain, shift, count):
    mean, unused_scale, factor = norm_of(sums, gain, count)
    return (inner * sigmoid(inner) + (pre_two - mean) * factor + shift).T


def project(w_qkv_ref, act_two, head_width, qkv_ref):
    channels = act_two.shape[0]
    rows = folded(dot(w_qkv_ref[...], stacked(act_two)), 0)
    qkv_ref[:channels] = rows[:channels] * (LOG2_E / math.sqrt(head_width))
    qkv_ref[channels:] = rows[channels:]


def outlet_kernel(
    lon, count, block_size, step_size, quantities,
    state_ref, inner_ref, pre_two_ref, sums_two_ref, gain_ref, shift_ref,
    w_qkv_ref, w_mixer_ref, w_velocity_ref, b_velocity_ref,
    out_ref, packed_ref, qkv_ref, mixed_ref, weight_ref, powers_ref,
    slots_ref, done_ref,
):
    channels = inner_ref.shape[1]
    cells = inner_ref.shape[0]
    act_two = act_two_channels(
        inner_ref[...], pre_two_ref[...], sums_two_ref[...], gain_ref[...], shift_ref[...], count
    )
    project(w_qkv_ref, act_two, channels // HEADS, qkv_ref)
    heads = heads_of(channels, cells, block_size)

    def scores_of(turn):
        rows, lanes = heads[turn]
        return attention_scores(qkv_ref[below(rows, channels), lanes], qkv_ref[rows, lanes])

    def keep(turn):
        return pltpu.make_async_copy(
            slots_ref.at[turn % 2], powers_ref.at[turn], done_ref.at[turn % 2]
        )

    following = scores_of(0)
    value_cells = qkv_ref[2 * channels :].T
    for turn, (rows, lanes) in enumerate(heads):
        scores = following
        if turn + 1 < len(heads):
            following = scores_of(turn + 1)
        top = jnp.max(scores, axis=0, keepdims=True)
        powers = jnp.exp2(scores - top)
        weight = 1.0 / jnp.sum(powers, axis=0, keepdims=True)
        weight_ref[turn : turn + 1] = weight
        high, low = halves(powers)
        if turn >= 2:
            keep(turn - 2).wait()
        slots_ref[turn % 2, 0] = high
        slots_ref[turn % 2, 1] = low
        keep(turn).start()
        value = beside(of_head(value_cells[lanes], rows))
        part = dot(high, value, 0, 0) + dot(low, value, 0, 0)
        mixed = part if rows.start == 0 else mixed + part
        if rows.stop == channels:
            mixed_ref[:, lanes] = folded(mixed, 1).T
            first = turn + 1 - HEADS
            for head in range(HEADS):
                own_rows = heads[head][0]
                mixed_ref[own_rows, lanes] = (
                    mixed_ref[own_rows, lanes] * weight_ref[first + head : first + head + 1]
                )
    act_three = act_two + folded(dot(w_mixer_ref[...], stacked(mixed_ref[...])), 0)
    parts = folded(dot(w_velocity_ref[...], stacked(act_three)), 0)
    forcing = jnp.zeros((2 * GROUP, cells), F32) + b_velocity_ref[...]
    for column, lon_offset in enumerate((-1, 0, 1)):
        total = None
        for row, lat_offset in enumerate((-1, 0, 1)):
            start = (row * 3 + column) * 2 * GROUP
            part = parts[start : start + 2 * GROUP]
            if lat_offset:
                part = lat_moved(part, lat_offset, lon)
            total = part if total is None else total + part
        forcing = forcing + (lon_moved(total, lon_offset, lon) if lon_offset else total)
    state = state_ref[...]
    flows = state[GROUP:]
    out_ref[:GROUP] = advected(state, step_size, lon)
    out_ref[GROUP:] = flows + step_size * (forcing - flows)
    put_packed(packed_ref, out_ref[...], quantities)
    for turn in range(max(0, len(heads) - 2), len(heads)):
        keep(turn).wait()


def outlet_back_kernel(
    lon, count, block_size, step_size, quantities, sections, step,
    ids_ref,
    state_ref, d_next_ref, cots_ref, inner_ref, pre_two_ref, sums_two_ref, gain_ref, shift_ref,
    qkv_ref, mixed_ref, weight_ref, powers_ref,
    w_mixer_ref, w_qkv_back_ref, w_mixer_back_ref, w_velocity_back_ref,
    acc_qkv_ref, acc_mixer_ref, acc_velocity_ref, acc_small_ref,
    d_state_ref, d_two_ref, sums_ref,
    out_qkv_ref, out_mixer_ref, out_velocity_ref, out_small_ref,
    d_mixed_ref, d_qkv_ref, seed_ref, slots_ref, done_ref,
):
    channels = inner_ref.shape[1]
    cells = inner_ref.shape[0]
    heads = heads_of(channels, cells, block_size)

    def fetch(turn):
        return pltpu.make_async_copy(
            powers_ref.at[turn], slots_ref.at[turn % 2], done_ref.at[turn % 2]
        )

    for turn in range(min(2, len(heads))):
        fetch(turn).start()
    state = state_ref[...]
    packed = cots_ref[lax.rem(ids_ref[0] - step + sections, sections)]
    put_groups(seed_ref, packed[: 3 * quantities])
    seed = seed_ref[...] + d_next_ref[...]
    amount, east, north = state[:GROUP], state[GROUP : 2 * GROUP], state[2 * GROUP :]
    d_amount = seed[:GROUP]
    d_lon = step_size * along_lon(d_amount, lon)
    d_lat = step_size * along_lat(d_amount, lon)
    d_state_ref[:GROUP] = d_amount + d_lon * east + d_lat * north
    d_state_ref[GROUP : 2 * GROUP] = (1.0 - step_size) * seed[GROUP : 2 * GROUP] + d_lon * amount
    d_state_ref[2 * GROUP :] = (1.0 - step_size) * seed[2 * GROUP :] + d_lat * amount
    d_forcing = step_size * seed[GROUP:]
    pieces = []
    for lat_offset in (-1, 0, 1):
        moved_rows = lat_moved(d_forcing, -lat_offset, lon) if lat_offset else d_forcing
        for lon_offset in (-1, 0, 1):
            pieces.append(lon_moved(moved_rows, -lon_offset, lon) if lon_offset else moved_rows)
    d_parts = stacked(jnp.concatenate(pieces, axis=0))
    d_three = folded(dot(w_velocity_back_ref[...], d_parts), 0)
    d_three_halves = stacked(d_three)
    d_mixed_ref[...] = folded(dot(w_mixer_back_ref[...], d_three_halves), 0)
    for turn, (rows, lanes) in enumerate(heads):
        d_mixed_ref[rows, lanes] = d_mixed_ref[rows, lanes] * weight_ref[turn : turn + 1]
    d_mixed_cells = d_mixed_ref[...].T
    query_cells = qkv_ref[:channels].T

    def d_powers_of(turn):
        rows, lanes = heads[turn]
        d_mixed = d_mixed_ref[rows, lanes]
        return d_mixed, row_products(qkv_ref[below(rows, 2 * channels), lanes], d_mixed)

    following = d_powers_of(0)
    for turn, (rows, lanes) in enumerate(heads):
        d_mixed, d_powers = following
        if turn + 1 < len(heads):
            following = d_powers_of(turn + 1)
        inner_sum = jnp.sum(d_mixed * mixed_ref[rows, lanes], axis=0, keepdims=True)
        fetch(turn).wait()
        power_high, power_low = slots_ref[turn % 2, 0], slots_ref[turn % 2, 1]
        powers = power_high.astype(F32) + power_low.astype(F32)
        d_high, d_low = halves(powers * (d_powers - inner_sum))
        right = beside(of_head(d_mixed_cells[lanes], rows))
        d_value = dot(power_high, right) + dot(power_low, right) + (d_value if rows.start else 0.0)
        right = beside(of_head(query_cells[lanes], rows))
        d_key = dot(d_high, right) + dot(d_low, right) + (d_key if rows.start else 0.0)
        key_halves = stacked(qkv_ref[below(rows, channels), lanes])
        d_query = folded(dot(key_halves, d_high) + dot(key_halves, d_low), 0)
        if turn + 2 < len(heads):
            fetch(turn + 2).start()
        d_qkv_ref[rows, lanes] = d_query * (1.0 / math.sqrt(channels // HEADS))
        if rows.stop == channels:
            d_qkv_ref[channels : 2 * channels, lanes] = folded(d_key, 1).T * (1.0 / LOG2_E)
            d_qkv_ref[2 * channels :, lanes] = folded(d_value, 1).T
    d_qkv_halves = stacked(d_qkv_ref[...])
    d_two = (d_three + folded(dot(w_qkv_back_ref[...], d_qkv_halves), 0)).T
    d_two_ref[...] = d_two
    mean, scale, unused_factor = norm_of(sums_two_ref[...], gain_ref[...], count)
    sums = sums_of(d_two, pre_two_ref[...] - mean)
    sums_ref[...] = sums

    def pairs(left, right):
        return folded(folded(dot(left, right, 1, 1), 0), 1)

    act_two = act_two_channels(
        inner_ref[...], pre_two_ref[...], sums_two_ref[...], gain_ref[...], shift_ref[...], count
    )
    mixed_halves = stacked(mixed_ref[...])
    act_three = act_two + folded(dot(w_mixer_ref[...], mixed_halves), 0)
    out_velocity_ref[...] = acc_velocity_ref[...] + pairs(d_parts, stacked(act_three))
    out_mixer_ref[...] = acc_mixer_ref[...] + pairs(mixed_halves, d_three_halves)
    out_qkv_ref[...] = acc_qkv_ref[...] + pairs(stacked(act_two), d_qkv_halves)
    bias = jnp.sum(d_forcing, axis=1, keepdims=True)
    row = lax.broadcasted_iota(jnp.int32, (GROUP, channels), 0)
    small = jnp.where(row == 0, sums[1:2] * scale, jnp.where(row == 1, sums[0:1], 0.0))
    out_small_ref[:GROUP] = acc_small_ref[:GROUP] + small
    out_small_ref[GROUP:] = acc_small_ref[GROUP:] + bias


def d_pre_of(d_normed, centred, sums, all_grad_sums, gain, count):
    unused_mean, scale, factor = norm_of(sums, gain, count)
    d_spread = -0.5 * gain * scale * scale * scale * all_grad_sums[1:2]
    return factor * (d_normed - all_grad_sums[0:1] / count) + (2.0 * d_spread / count) * centred


def weight_pairs(acc_ref, out_ref, left_halves, patches_ref, lon):
    cells = patches_ref.shape[0] - 2 * lon
    width = patches_ref.shape[1] // 3
    for tap in range(9):
        row, column = divmod(8 - tap, 3)
        right = patches_ref[lon * row : lon * row + cells, column * width : (column + 1) * width]
        out_ref[tap] = acc_ref[tap] + folded(folded(dot(left_halves, right), 0), 1)


def middle_back_kernel(
    lon, count,
    d_two_ref, pre_two_ref, sums_two_ref, all_two_ref, gain_two_ref,
    pre_one_ref, sums_one_ref, gain_ref, shift_ref, w_second_back_ref,
    acc_weight_ref, acc_small_ref,
    d_normed_ref, sums_ref, out_weight_ref, out_small_ref,
    patches_ref,
):
    sums_two = sums_two_ref[...]
    d_pre = d_pre_of(
        d_two_ref[...], pre_two_ref[...] - sums_two[0:1] / count, sums_two, all_two_ref[...],
        gain_two_ref[...], count,
    )
    fill_patches(patches_ref, d_pre, lon)
    d_act = conv_patches(patches_ref, w_second_back_ref, lon)
    mean, scale, factor = norm_of(sums_one_ref[...], gain_ref[...], count)
    centred = pre_one_ref[...] - mean
    normed = centred * factor + shift_ref[...]
    gate = sigmoid(normed)
    d_normed = d_act * gate * (1.0 + normed * (1.0 - gate))
    d_normed_ref[...] = d_normed
    sums = sums_of(d_normed, centred)
    sums_ref[...] = sums
    weight_pairs(acc_weight_ref, out_weight_ref, stacked((normed * gate).T), patches_ref, lon)
    row = lax.broadcasted_iota(jnp.int32, sums.shape, 0)
    small = jnp.where(row == 0, sums[1:2] * scale, jnp.where(row == 1, sums[0:1], 0.0))
    out_small_ref[...] = acc_small_ref[...] + small


def inlet_back_kernel(
    lon, count, quantities,
    state_ref, d_normed_ref, pre_one_ref, sums_one_ref, all_one_ref, gain_ref,
    inner_ref, d_two_ref, d_state_in_ref, w_first_back_ref, w_input_back_ref,
    acc_first_ref, acc_input_ref, acc_inner_ref,
    d_state_ref, packed_ref, out_first_ref, out_input_ref, out_inner_ref,
    patches_ref,
):
    cells = inner_ref.shape[0]
    sums_one = sums_one_ref[...]
    d_pre = d_pre_of(
        d_normed_ref[...], pre_one_ref[...] - sums_one[0:1] / count, sums_one, all_one_ref[...],
        gain_ref[...], count,
    )
    fill_patches(patches_ref, d_pre, lon)
    d_act = conv_patches(patches_ref, w_first_back_ref, lon) + d_two_ref[...]
    inner = inner_ref[...]
    gate = sigmoid(inner)
    d_inner = d_act * gate * (1.0 + inner * (1.0 - gate))
    weight_pairs(acc_first_ref, out_first_ref, stacked((inner * gate).T), patches_ref, lon)
    out_inner_ref[...] = acc_inner_ref[...] + d_inner
    patches_ref[lon : lon + cells, :256] = beside(d_inner)
    rows = [patches_ref[lon * place : lon * place + cells, :256] for place in range(3)]
    d_moving = folded(dot(jnp.concatenate(rows, axis=1), w_input_back_ref[...]), 1).T
    state = state_ref[...]
    moving_halves = stacked(inlet_channels(state, lon))
    for place in range(3):
        out_input_ref[place] = acc_input_ref[place] + folded(
            folded(dot(moving_halves, rows[2 - place]), 0), 1
        )
    size = 5 * GROUP
    d_groups = (
        lon_moved(d_moving[:size], 1, lon)
        + d_moving[size : 2 * size]
        + lon_moved(d_moving[2 * size : 3 * size], -1, lon)
    )
    d_state = d_state_in_ref[...] + d_groups[: 3 * GROUP]
    d_state_ref[:GROUP] = (
        d_state[:GROUP]
        - along_lon(d_groups[3 * GROUP : 4 * GROUP], lon)
        - along_lat(d_groups[4 * GROUP :], lon)
    )
    d_state_ref[GROUP:] = d_state[GROUP:]
    put_packed(packed_ref, d_state_ref[...], quantities)


def put_groups(out_ref, rows):
    size = rows.shape[0] // 3
    out_ref[...] = jnp.zeros(out_ref.shape, F32)
    for group in range(3):
        out_ref[group * GROUP : group * GROUP + size] = rows[group * size : (group + 1) * size]


def put_packed(out_ref, grouped, size):
    out_ref[...] = jnp.zeros(out_ref.shape, F32)
    for group in range(3):
        out_ref[group * size : (group + 1) * size] = grouped[group * GROUP : group * GROUP + size]


def fetched(far_refs, near_refs, done_ref):
    copies = [
        pltpu.make_async_copy(far_ref, near_ref, done_ref.at[place])
        for place, (far_ref, near_ref) in enumerate(zip(far_refs, near_refs))
    ]
    for copy in copies:
        copy.start()
    return copies


def enter_kernel(plan, ids_ref, order_ref, state_ref, out_ref, near_ref, rows_ref, done_ref):
    (copy,) = fetched([state_ref], [near_ref], done_ref)
    copy.wait()
    place = order_ref[0, plan.slot(ids_ref[0], ids_ref[1])]
    for row in range(rows_ref.shape[0]):
        rows_ref[row : row + 1] = near_ref[row, pl.ds(place, 1)]
    put_groups(out_ref, rows_ref[...])


def seeds_kernel(plan, ids_ref, order_ref, cot_ref, *refs):
    out_refs, near_ref, done_ref = refs[:-2], refs[-2], refs[-1]
    (copy,) = fetched([cot_ref], [near_ref], done_ref)
    copy.wait()
    for steps, out_ref in enumerate(out_refs):
        target = lax.rem(ids_ref[0] + steps, plan.sections)
        place = order_ref[0, plan.slot(target, ids_ref[1])]
        out_ref[...] = jnp.zeros(out_ref.shape, F32)
        for row in range(near_ref.shape[0]):
            out_ref[row : row + 1] = near_ref[row, pl.ds(place, 1)]


def leave_kernel(plan, ids_ref, *refs):
    values_ref = refs[-1]
    size = refs[0].shape[0]
    for step in range(plan.sections):
        values_ref[step, :size] = refs[step][...]
        if step:
            values_ref[step, size:] = refs[plan.sections + step - 1][...]
        else:
            values_ref[step, size:] = jnp.zeros(refs[0].shape, F32)
    for steps, out_ref in enumerate(refs[2 * plan.sections - 1 : -1]):
        out_ref[...] = values_ref[lax.rem(ids_ref[0] + steps, plan.sections)]


def arrive_kernel(plan, start, ids_ref, order_ref, kept_ref, *refs):
    section, dp = ids_ref[0], ids_ref[1]
    out_ref = refs[-1]
    size = kept_ref.shape[0] // 2
    early, late = refs[: plan.sections], refs[plan.sections : -1]
    for steps, ref in enumerate(early):
        source = lax.rem(section - steps + plan.sections, plan.sections)
        place = order_ref[0, plan.slot(source, dp)]
        value = ref[start : start + size]
        if plan.halved and not steps:
            value = jnp.where(section < 2, kept_ref[start : start + size], value)
        if late:
            value = jnp.where(section == 0, late[steps][...], value)
        for row in range(out_ref.shape[0]):
            out_ref[row, pl.ds(place, 1)] = value[row : row + 1]


def put_conv_weight(out_ref, taps):
    for tap, weight in enumerate(taps):
        wide = beside(weight)
        rows = weight.shape[0]
        out_ref[2 * tap * rows : (2 * tap + 1) * rows] = wide
        out_ref[(2 * tap + 1) * rows : (2 * tap + 2) * rows] = wide


def put_left_weight(out_ref, weight):
    rows = weight.shape[0]
    for place, half in enumerate(halves(weight)):
        out_ref[place * rows : (place + 1) * rows] = jnp.concatenate([half, half], axis=1)


def first_weights_kernel(
    lon, quantities, w_input_ref, w_first_ref, b_input_ref, maps_ref,
    static_part_ref, moving_cat_ref, moving_back_ref, first_cat_ref,
    patches_ref, weight_ref, taps_ref, *near_refs,
):
    near_refs, done_ref = near_refs[:-1], near_refs[-1]
    copies = fetched([w_input_ref, maps_ref, b_input_ref, w_first_ref], near_refs, done_ref)
    w_input_ref, maps_ref, b_input_ref, w_first_ref = near_refs
    copies[0].wait()
    channels = w_input_ref.shape[2]
    moving = 5 * quantities
    statics = maps_ref.shape[0]
    taps_ref[...] = jnp.zeros(taps_ref.shape, F32)
    for tap in range(9):
        row, column = divmod(tap, 3)
        for group in range(5):
            start = (column * 5 + group) * GROUP
            taps_ref[9 + row, start : start + quantities] = w_input_ref[
                tap, group * quantities : (group + 1) * quantities
            ]
        taps_ref[tap, :statics] = w_input_ref[tap, moving:]
    put_conv_weight(moving_cat_ref, [taps_ref[9 + row] for row in range(3)])
    put_conv_weight(moving_back_ref, [taps_ref[11 - row].T for row in range(3)])
    put_conv_weight(weight_ref, [taps_ref[tap] for tap in range(9)])
    copies[1].wait()
    copies[2].wait()
    maps = jnp.concatenate(
        [maps_ref[...], jnp.zeros((channels - statics, maps_ref.shape[1]), F32)], axis=0
    )
    fill_patches(patches_ref, maps.T, lon)
    static_part_ref[...] = conv_patches(patches_ref, weight_ref, lon) + b_input_ref[...]
    copies[3].wait()
    put_conv_weight(first_cat_ref, [w_first_ref[tap] for tap in range(9)])


def second_weights_kernel(far_ref, out_ref, w_second_ref, done_ref):
    fetched([far_ref], [w_second_ref], done_ref)[0].wait()
    put_conv_weight(out_ref, [w_second_ref[tap] for tap in range(9)])


def outlet_weights_kernel(
    quantities, w_query_ref, w_key_ref, w_value_ref, w_mixer_ref, w_velocity_ref,
    qkv_ref, qkv_back_ref, mixer_ref, mixer_back_ref, velocity_ref, velocity_back_ref,
    rows_ref, *near_refs,
):
    near_refs, done_ref = near_refs[:-1], near_refs[-1]
    copies = fetched([w_query_ref, w_key_ref, w_value_ref, w_mixer_ref, w_velocity_ref], near_refs, done_ref)
    w_query_ref, w_key_ref, w_value_ref, w_mixer_ref, w_velocity_ref = near_refs
    for copy in copies:
        copy.wait()
    parts = [ref[...] for ref in (w_query_ref, w_key_ref, w_value_ref)]
    put_left_weight(qkv_ref, jnp.concatenate([part.T for part in parts], axis=0))
    put_left_weight(qkv_back_ref, jnp.concatenate(parts, axis=1))
    put_left_weight(mixer_ref, w_mixer_ref[...].T)
    put_left_weight(mixer_back_ref, w_mixer_ref[...])
    channels = w_mixer_ref.shape[0]
    rows_ref[...] = jnp.zeros(rows_ref.shape, F32)
    for tap in range(9):
        for group in range(2):
            start = (tap * 2 + group) * GROUP
            rows_ref[start : start + quantities] = w_velocity_ref[
                tap, group * quantities : (group + 1) * quantities
            ]
    size = 18 * GROUP
    put_left_weight(velocity_ref, rows_ref[:size])
    put_left_weight(velocity_back_ref, rows_ref[...].T[:, :size])


def back_weights_kernel(far_first_ref, far_second_ref, first_ref, second_ref, w_first_ref, w_second_ref, done_ref):
    for copy in fetched([far_first_ref, far_second_ref], [w_first_ref, w_second_ref], done_ref):
        copy.wait()
    put_conv_weight(first_ref, [w_first_ref[8 - tap].T for tap in range(9)])
    put_conv_weight(second_ref, [w_second_ref[8 - tap].T for tap in range(9)])


def index_of(ids_ref, plan, bits):
    own = ids_ref[0] * plan.dp + ids_ref[1]
    return sum(lax.rem(own // bit, 2) << place for place, bit in enumerate(bits))


def deal(total_ref, own, out_refs):
    rows = out_refs[0].shape[0]
    for turn, out_ref in enumerate(out_refs):
        out_ref[...] = total_ref[pl.ds(pl.multiple_of((own ^ turn) * rows, GROUP), rows)]


def pack_kernel(
    plan, bits, lon, statics, ids_ref, maps_ref, inner_ref, first_ref, second_ref, moving_ref,
    qkv_ref, mixer_ref, velocity_ref, small_one_ref, small_two_ref, *refs,
):
    out_refs, total_ref, patches_ref = refs[:-2], refs[-2], refs[-1]
    cells, channels = inner_ref.shape
    d_inner = inner_ref[...]
    fill_patches(patches_ref, d_inner, lon)
    width = patches_ref.shape[1] // 3
    maps = maps_ref[...]
    blank = jnp.zeros((-statics % GROUP, cells), F32)
    maps = jnp.concatenate([maps, blank], axis=0)
    rows = maps.shape[0]
    left = jnp.concatenate(halves(maps), axis=0)
    start = 0

    def put(value):
        nonlocal start
        total_ref[start : start + value.shape[0]] = value
        start += value.shape[0]

    for tap in range(9):
        put(first_ref[tap])
    for tap in range(9):
        put(second_ref[tap])
    for tap in range(9):
        row, column = divmod(8 - tap, 3)
        right = patches_ref[lon * row : lon * row + cells, column * width : (column + 1) * width]
        put(folded(folded(dot(left, right), 0), 1))
    for place in range(3):
        put(moving_ref[place, : 15 * GROUP])
    for part in range(3):
        put(qkv_ref[:, part * channels : (part + 1) * channels])
    put(mixer_ref[...])
    put(velocity_ref[...])
    put(small_one_ref[...])
    put(small_two_ref[...])
    put(jnp.zeros((GROUP, channels), F32) + jnp.sum(d_inner, axis=0, keepdims=True))
    total_ref[start:] = jnp.zeros((total_ref.shape[0] - start, channels), F32)
    deal(total_ref, index_of(ids_ref, plan, bits), out_refs)


def reduce_kernel(plan, bits, count, ids_ref, *refs):
    total_ref = refs[-1]
    total = refs[0][...]
    for ref in refs[1:count]:
        total = total + ref[...]
    if not bits:
        refs[count][...] = total
        return
    total_ref[...] = total
    deal(total_ref, index_of(ids_ref, plan, bits), refs[count:-1])


def gather_rows(plan, bits, ids_ref, part_refs, out_ref):
    own = index_of(ids_ref, plan, bits)
    rows = part_refs[0].shape[0]
    for turn, ref in enumerate(part_refs):
        out_ref[pl.ds(pl.multiple_of((own ^ turn) * rows, GROUP), rows)] = ref[...]


def gather_kernel(plan, bits, ids_ref, *refs):
    gather_rows(plan, bits, ids_ref, refs[:-1], refs[-1])


def unpack_kernel(
    plan, bits, quantities, statics, ids_ref, *refs,
):
    count = 1 << len(bits)
    (
        input_ref, bias_ref, first_ref, gain_one_ref, shift_one_ref, second_ref, gain_two_ref, shift_two_ref,
        query_ref, key_ref, value_ref, mixer_ref, velocity_ref, velocity_bias_ref, total_ref,
    ) = refs[count:]
    gather_rows(plan, bits, ids_ref, refs[:count], total_ref)
    channels = mixer_ref.shape[0]
    moving = 5 * quantities
    start = 0

    def take(rows):
        nonlocal start
        start += rows
        return total_ref[start - rows : start]

    for tap in range(9):
        first_ref[tap] = take(channels)
    for tap in range(9):
        second_ref[tap] = take(channels)
    for tap in range(9):
        input_ref[tap, moving:] = take(statics + -statics % GROUP)[:statics]
    for row in range(3):
        for column in range(3):
            for group in range(5):
                rows = take(GROUP)
                input_ref[row * 3 + column, group * quantities : (group + 1) * quantities] = rows[:quantities]
    query_ref[...] = take(channels)
    key_ref[...] = take(channels)
    value_ref[...] = take(channels)
    mixer_ref[...] = take(channels)
    for tap in range(9):
        for group in range(2):
            velocity_ref[tap, group * quantities : (group + 1) * quantities] = take(GROUP)[:quantities]
    small = take(GROUP)
    gain_one_ref[...], shift_one_ref[...] = small[0:1], small[1:2]
    small = take(GROUP)
    gain_two_ref[...], shift_two_ref[...] = small[0:1], small[1:2]
    velocity_bias_ref[...] = take(2 * GROUP)
    bias_ref[...] = take(GROUP)[0:1]


def call(kernel, outs, scratch=(), aliases=None, name=None, scalars=0, kinds=None, far_in=(), far_out=()):
    kinds = kinds or [F32] * len(outs)

    def run(*operands):
        places = [pltpu.SMEM] * scalars + [pltpu.VMEM] * (len(operands) - scalars)
        for place in far_in:
            places[place] = pltpu.HBM
        out_places = [pltpu.HBM if place in far_out else pltpu.VMEM for place in range(len(outs))]
        return pl.pallas_call(
            kernel,
            out_shape=tuple(jax.ShapeDtypeStruct(shape, kind) for shape, kind in zip(outs, kinds)),
            in_specs=[pl.BlockSpec(memory_space=place) for place in places],
            out_specs=tuple(pl.BlockSpec(memory_space=place) for place in out_places),
            scratch_shapes=scratch,
            input_output_aliases=aliases or {},
            compiler_params=pltpu.CompilerParams(vmem_limit_bytes=VMEM_LIMIT),
            name=name,
        )(*operands)

    return run


KEPT_STEPS = 4
VMEM_LIMIT = 24 * 1024 * 1024


def in_groups(array, axis, groups):
    shape = array.shape
    split = shape[:axis] + (groups, shape[axis] // groups) + shape[axis + 1 :]
    array = array.reshape(split)
    pads = [(0, 0)] * array.ndim
    pads[axis + 1] = (0, GROUP - split[axis + 1])
    return jnp.pad(array, pads).reshape(shape[:axis] + (groups * GROUP,) + shape[axis + 1 :])


def from_groups(array, axis, groups, size):
    shape = array.shape
    array = array.reshape(shape[:axis] + (groups, GROUP) + shape[axis + 1 :])
    array = lax.slice_in_dim(array, 0, size, axis=axis + 1)
    return array.reshape(shape[:axis] + (groups * size,) + shape[axis + 1 :])


class Plan:
    def __init__(self, sections, dp):
        self.sections, self.dp = sections, dp
        self.halved = sections == 4 and dp >= 4
        self.half = dp // 2
        bits = [1 << place for place in range((sections * dp).bit_length() - 1)]
        dp_bits = [bit for bit in bits if bit < dp]
        section_bits = [bit for bit in bits if bit >= dp]
        if self.halved:
            self.sum_rounds = in_pairs(dp_bits[:-1]) + in_pairs(section_bits)
        else:
            self.sum_rounds = in_pairs(dp_bits) + [section_bits[:1]]
        self.all_rounds = [dp_bits[:1]] + in_pairs(section_bits) + in_pairs(dp_bits[1:])

    def slot(self, section, home):
        if not self.halved:
            return section
        return lax.rem(home // self.half + section // 2, 2) * 2 + lax.rem(section, 2)

    def other(self, section, dp):
        return dp ^ self.half if self.halved and section >= 2 else dp

    def to_workers(self, steps):
        return [
            (section * self.dp + home, self.joint((section + steps) % self.sections, home))
            for section in range(self.sections)
            for home in range(self.dp)
        ]

    def to_homes(self, steps):
        return [
            (section * self.dp + own, (section + steps) % self.sections * self.dp + self.other(section, own))
            for section in range(self.sections)
            for own in range(self.dp)
        ]

    def to_first_home(self, steps):
        return [(source, target) for source, target in self.to_homes(steps) if target < self.dp]

    def joint(self, section, home):
        return section * self.dp + self.other(section, home)


def in_pairs(bits):
    return [bits[start : start + 2] for start in range(0, len(bits), 2)]


def masks_of(bits):
    return [sum(bit for place, bit in enumerate(bits) if turn >> place & 1) for turn in range(1, 1 << len(bits))]


def exchanged(value, mask):
    size = lax.axis_size("section") * lax.axis_size("dp")
    return lax.ppermute(value, ("section", "dp"), [(own, own ^ mask) for own in range(size)])


def moved(value, pairs):
    going = [(source, target) for source, target in pairs if source != target]
    if not going:
        return value
    return lax.ppermute(value, ("section", "dp"), going)


def micro_sum(plan, value, paired=False):
    for bits in [[bit] for bits in plan.sum_rounds for bit in bits] if paired else plan.sum_rounds:
        value = value + sum(exchanged(value, mask) for mask in masks_of(bits))
    return value


def on_device(
    state_start,
    static_maps,
    grouping,
    cotangent,
    w_input,
    b_input,
    w_first,
    gain_first,
    shift_first,
    w_second,
    gain_second,
    shift_second,
    w_query,
    w_key,
    w_value,
    w_mixer,
    w_velocity,
    b_velocity,
):
    segments = lax.axis_size("section")
    plan = Plan(segments, lax.axis_size("dp"))
    micro_count = segments // 2
    per_micro = state_start.shape[0] // micro_count
    cells = state_start.shape[2]
    lon = cells // LAT
    count = float(per_micro * cells * plan.dp)
    step_size = 2.0 / segments
    block_size = ATT_ROWS * lon
    channels = w_first.shape[2]
    quantities = state_start.shape[1] // 3
    statics = static_maps.shape[0]
    ids = jnp.stack([lax.axis_index("section"), lax.axis_index("dp")]).astype(jnp.int32)

    plane = (cells, channels)
    small = (GROUP, channels)
    conv = (9 * 2 * channels, 2 * channels)
    patches = pltpu.VMEM((cells + 2 * lon, 6 * channels), BF16)
    wide = pltpu.VMEM((3 * channels, cells), F32)
    narrow = pltpu.VMEM((channels, cells), F32)
    state_shape = (3 * GROUP, cells)

    packed = (2 * GROUP, cells)

    def near(*arrays):
        return [pltpu.VMEM(array.shape, F32) for array in arrays] + [pltpu.SemaphoreType.DMA((len(arrays),))]

    state_rows = jnp.swapaxes(state_start, 0, 1)
    (own_state,) = call(
        functools.partial(enter_kernel, plan), [state_shape],
        [pltpu.VMEM(state_rows.shape, F32), pltpu.VMEM((3 * quantities, cells), F32), pltpu.SemaphoreType.DMA((1,))],
        name="enter", scalars=2, far_in=[2],
    )(ids, grouping, state_rows)
    arrived_state = moved(own_state, plan.to_workers(0))

    static_part, moving_cat, moving_back_cat, first_cat = call(
        functools.partial(first_weights_kernel, lon, quantities),
        [plane, (6 * channels, 2 * channels), (6 * channels, 2 * channels), conv],
        [patches, pltpu.VMEM(conv, BF16), pltpu.VMEM((12, channels, channels), F32)]
        + near(w_input, static_maps, b_input[None], w_first),
        name="first_weights", kinds=[F32, BF16, BF16, BF16], far_in=range(4),
    )(w_input, w_first, b_input[None], static_maps)
    (second_cat,) = call(
        second_weights_kernel, [conv], near(w_second), name="second_weights", kinds=[BF16], far_in=[0]
    )(w_second)
    w_velocity_rows = jnp.swapaxes(w_velocity, 1, 2)
    qkv_cat, qkv_back_cat, mixer_cat, mixer_back_cat, out_cat, out_back_cat = call(
        functools.partial(outlet_weights_kernel, quantities),
        [(6 * channels, 2 * channels), (2 * channels, 6 * channels), (2 * channels, 2 * channels),
         (2 * channels, 2 * channels), (36 * GROUP, 2 * channels), (2 * channels, 36 * GROUP)],
        [pltpu.VMEM((2 * channels, channels), F32)]
        + near(w_query, w_key, w_value, w_mixer, w_velocity_rows),
        name="outlet_weights", kinds=[BF16] * 6, far_in=range(5),
    )(w_query, w_key, w_value, w_mixer, w_velocity_rows)
    first_back_cat, second_back_cat = call(
        back_weights_kernel, [conv, conv], near(w_first, w_second), name="back_weights", kinds=[BF16, BF16],
        far_in=range(2),
    )(w_first, w_second)
    b_out = in_groups(b_velocity[:, None], 0, 2)
    gain_one, shift_one = gain_first[None], shift_first[None]
    gain_two, shift_two = gain_second[None], shift_second[None]

    inlet = call(
        functools.partial(inlet_kernel, lon), [plane, plane, small], [patches], name="inlet"
    )
    middle = call(
        functools.partial(middle_kernel, lon, count), [plane, small], [patches], name="middle"
    )
    heads = HEADS * (cells // block_size)
    powers = (heads, 2, block_size, block_size)
    slots = [pltpu.VMEM((2,) + powers[1:], BF16), pltpu.SemaphoreType.DMA((2,))]
    outlet = call(
        functools.partial(outlet_kernel, lon, count, block_size, step_size, quantities),
        [state_shape, packed, (3 * channels, cells), (channels, cells), (heads, block_size), powers],
        slots, name="outlet", kinds=[F32] * 5 + [BF16], far_out=[5],
    )

    def outlet_back(step):
        return call(
            functools.partial(outlet_back_kernel, lon, count, block_size, step_size, quantities, segments, step),
            [state_shape, plane, small, (channels, 3 * channels), (channels, channels),
             (18 * GROUP, channels), (3 * GROUP, channels)],
            [narrow, wide, pltpu.VMEM(state_shape, F32)] + slots,
            {17: 3, 18: 4, 19: 5, 20: 6}, name="outlet_back", scalars=1, far_in=[12],
        )

    middle_back = call(
        functools.partial(middle_back_kernel, lon, count),
        [plane, small, (9, channels, channels), small], [patches],
        {10: 2, 11: 3}, name="middle_back",
    )
    inlet_back = call(
        functools.partial(inlet_back_kernel, lon, count, quantities),
        [state_shape, packed, (9, channels, channels), (3, channels, channels), plane], [patches],
        {11: 2, 12: 3, 13: 4}, name="inlet_back",
    )

    state = own_state
    path, saved = [], []
    cots = None
    for step in range(segments):
        if plan.halved and not step:
            state, inner, pre_one, sums_one = call(
                functools.partial(entered_inlet_kernel, lon), [state_shape, plane, plane, small], [patches],
                name="inlet", scalars=1,
            )(ids, own_state, arrived_state, static_part, moving_cat, first_cat)
        else:
            inner, pre_one, sums_one = inlet(state, static_part, moving_cat, first_cat)
        sums_one = micro_sum(plan, sums_one, True)
        pre_two, sums_two = middle(pre_one, sums_one, gain_one, shift_one, second_cat)
        sums_two = micro_sum(plan, sums_two, True)
        state_out, state_packed, qkv, mixed, weight, powers_kept = outlet(
            state, inner, pre_two, sums_two, gain_two, shift_two, qkv_cat, mixer_cat, out_cat, b_out
        )
        kept = (qkv, mixed, weight, powers_kept) if step >= segments - KEPT_STEPS else None
        saved.append((state, inner, pre_one, pre_two, sums_one, sums_two, kept))
        path.append(state_packed)
        state = state_out
        if not step:
            state, cot_local = lax.optimization_barrier((state, cotangent))
            sent = call(
                functools.partial(seeds_kernel, plan), [packed] * segments,
                [pltpu.VMEM(state_rows.shape, F32), pltpu.SemaphoreType.DMA((1,))],
                name="seeds", scalars=2, far_in=[2],
            )(ids, grouping, jnp.swapaxes(cot_local[0], 0, 1))
            cots = [moved(cot, plan.to_workers(steps)) for steps, cot in enumerate(sent)]
            if plan.halved:
                cots[0] = jnp.where(lax.axis_index("section") < 2, sent[0], cots[0])
    cots = jnp.stack(cots)

    def put_home(start, parts):
        (out,) = call(
            functools.partial(arrive_kernel, plan, start), [state_rows.shape], name="arrive", scalars=2
        )(ids, grouping, *parts)
        return jnp.swapaxes(out, 0, 1)[None]

    acc = dict(
        qkv=jnp.zeros((channels, 3 * channels), F32),
        mixer=jnp.zeros((channels, channels), F32),
        velocity=jnp.zeros((18 * GROUP, channels), F32),
        small_two=jnp.zeros((3 * GROUP, channels), F32),
        second=jnp.zeros((9, channels, channels), F32),
        small_one=jnp.zeros(small, F32),
        first=jnp.zeros((9, channels, channels), F32),
        moving=jnp.zeros((3, channels, channels), F32),
        inner=jnp.zeros(plane, F32),
    )
    d_state = jnp.zeros(state_shape, F32)
    grads = [None] * segments
    path_out = None
    for step in reversed(range(segments)):
        if not step:
            sent = call(
                functools.partial(leave_kernel, plan), [(4 * GROUP, cells)] * segments,
                [pltpu.VMEM((segments, 4 * GROUP, cells), F32)], name="leave", scalars=1,
            )(ids, *path, *grads[1:])
            early = [sent[0]] + [moved(part, plan.to_homes(steps)) for steps, part in enumerate(sent)]
        state, inner, pre_one, pre_two, sums_one, sums_two, kept = saved[step]
        if kept is None:
            state, d_state = lax.optimization_barrier((state, d_state))
            kept = outlet(
                state, inner, pre_two, sums_two, gain_two, shift_two, qkv_cat, mixer_cat, out_cat, b_out
            )[2:]
        qkv, mixed, weight, powers_kept = kept
        d_partial, d_two, grad_two, acc["qkv"], acc["mixer"], acc["velocity"], acc["small_two"] = outlet_back(step)(
            ids, state, d_state, cots, inner, pre_two, sums_two, gain_two, shift_two,
            qkv, mixed, weight, powers_kept,
            mixer_cat, qkv_back_cat, mixer_back_cat, out_back_cat,
            acc["qkv"], acc["mixer"], acc["velocity"], acc["small_two"],
        )
        if not step:
            d_two, grad_two, early = lax.optimization_barrier((d_two, grad_two, early))
            path_out = put_home(0, early)
        grad_two = micro_sum(plan, grad_two)
        d_normed, grad_one, acc["second"], acc["small_one"] = middle_back(
            d_two, pre_two, sums_two, grad_two, gain_two,
            pre_one, sums_one, gain_one, shift_one, second_back_cat,
            acc["second"], acc["small_one"],
        )
        grad_one = micro_sum(plan, grad_one)
        d_state, grads[step], acc["first"], acc["moving"], acc["inner"] = inlet_back(
            state, d_normed, pre_one, sums_one, grad_one, gain_one,
            inner, d_two, d_partial, first_back_cat, moving_back_cat,
            acc["first"], acc["moving"], acc["inner"],
        )
    late = [grads[0]] + [
        lax.ppermute(grads[0], ("section", "dp"), plan.to_first_home(steps)) for steps in range(1, segments)
    ]

    rounds = plan.all_rounds
    rows = 2 * 9 * channels + 9 * (statics + -statics % GROUP) + 45 * GROUP + 4 * channels + 23 * GROUP
    unit = GROUP * segments * plan.dp
    rows = -(-rows // unit) * unit

    def shares(rows, bits):
        return [(rows >> len(bits), channels)] * (1 << len(bits))

    def swap(parts, bits):
        return [parts[0]] + [exchanged(part, mask) for part, mask in zip(parts[1:], masks_of(bits))]

    parts = call(
        functools.partial(pack_kernel, plan, rounds[0], lon, statics), shares(rows, rounds[0]),
        [pltpu.VMEM((rows, channels), F32), patches], name="pack", scalars=1,
    )(
        ids, static_maps, acc["inner"], acc["first"], acc["second"], acc["moving"], acc["qkv"], acc["mixer"],
        acc["velocity"], acc["small_one"], acc["small_two"],
    )
    grads_out = None
    for bits, later in zip(rounds, rounds[1:] + [[]]):
        parts = swap(parts, bits)
        if grads_out is None:
            parts, late = lax.optimization_barrier((parts, late))
            grads_out = put_home(2 * GROUP, early + late)
        rows >>= len(bits)
        parts = call(
            functools.partial(reduce_kernel, plan, later, len(parts)), shares(rows, later),
            [pltpu.VMEM((rows, channels), F32)], name="reduce_part", scalars=1,
        )(ids, *parts)
    for bits in rounds[::-1]:
        parts = swap([parts[0]] * (1 << len(bits)), bits)
        rows <<= len(bits)
        if bits is rounds[0]:
            break
        parts = call(
            functools.partial(gather_kernel, plan, bits), [(rows, channels)], name="gather_part", scalars=1
        )(ids, *parts)
    row = (1, channels)
    square = (channels, channels)
    grads_all = call(
        functools.partial(unpack_kernel, plan, rounds[0], quantities, statics),
        [w_input.shape, row, w_first.shape, row, row, w_second.shape, row, row, square, square, square, square,
         (9, 2 * quantities, channels), (2 * GROUP, channels)],
        [pltpu.VMEM((rows, channels), F32)], name="unpack", scalars=1,
    )(ids, *parts)
    grads_all = [grad[0] if grad.shape == row else grad for grad in grads_all]
    grads_all[-2] = jnp.swapaxes(grads_all[-2], 1, 2)
    grads_all[-1] = from_groups(grads_all[-1][:, :1], 0, 2, quantities)[:, 0]
    return (path_out, grads_out) + tuple(grads_all)


def solution(mesh):
    weights = (P(),) * 14
    return jax.shard_map(
        on_device,
        mesh=mesh,
        in_specs=(P("dp", None, None), P(), P("dp", None), P("section", "dp", None, None)) + weights,
        out_specs=(P("section", "dp", None, None), P("section", "dp", None, None)) + weights,
        check_vma=False,
    )
```

```python
import functools
import math

import jax
import jax.numpy as jnp
from jax import lax
from jax.experimental import pallas as pl
from jax.experimental.pallas import tpu as pltpu
from jax.sharding import PartitionSpec as P

HEADS = 4
LAT = 16
ATT_ROWS = 8
EPSILON = 1e-05
LOG2_E = 1.0 / math.log(2.0)
F32 = jnp.float32
BF16 = jnp.bfloat16
GROUP = 8


def dot(left, right, left_dim=1, right_dim=0):
    return lax.dot_general(
        left, right, (((left_dim,), (right_dim,)), ((), ())), preferred_element_type=F32
    )


def halves(value):
    high = value.astype(BF16)
    return high, (value - high.astype(F32)).astype(BF16)


def stacked(value):
    return jnp.concatenate(halves(value), axis=0)


def beside(value):
    return jnp.concatenate(halves(value), axis=1)


def folded(value, axis):
    size = value.shape[axis] // 2
    if axis == 0:
        return value[:size] + value[size:]
    return value[:, :size] + value[:, size:]


def cells_of(value):
    return lax.broadcasted_iota(jnp.int32, value.shape, value.ndim - 1)


def lon_moved(value, offset, lon):
    cells = value.shape[1]
    column = lax.rem(cells_of(value), lon)
    near = pltpu.roll(value, (-offset) % cells, 1)
    wrapped = pltpu.roll(value, (offset * (lon - 1)) % cells, 1)
    edge = lon - 1 if offset > 0 else 0
    return jnp.where(column == edge, wrapped, near)


def lat_moved(value, offset, lon):
    cells = value.shape[1]
    moved = pltpu.roll(value, (-offset * lon) % cells, 1)
    cell = cells_of(value)
    if offset > 0:
        return jnp.where(cell < cells - lon, moved, 0.0)
    return jnp.where(cell >= lon, moved, 0.0)


def along_lon(value, lon):
    return 0.5 * (lon_moved(value, 1, lon) - lon_moved(value, -1, lon))


def along_lat(value, lon):
    return 0.5 * (lat_moved(value, 1, lon) - lat_moved(value, -1, lon))


def fill_patches(patches_ref, value, lon):
    cells, channels = value.shape
    planes = value.reshape(cells // lon, lon, channels)
    blank = jnp.zeros((lon, patches_ref.shape[1]), BF16)
    patches_ref[:lon] = blank
    patches_ref[lon + cells :] = blank
    for place, offset in enumerate((-1, 0, 1)):
        moved = value
        if offset:
            moved = pltpu.roll(planes, (-offset) % lon, 1).reshape(cells, channels)
        high, low = halves(moved)
        start = place * 2 * channels
        patches_ref[lon : lon + cells, start : start + channels] = high
        patches_ref[lon : lon + cells, start + channels : start + 2 * channels] = low


def conv_patches(patches_ref, weight_ref, lon):
    cells = patches_ref.shape[0] - 2 * lon
    rows = [patches_ref[lon * place : lon * place + cells] for place in range(3)]
    return folded(dot(jnp.concatenate(rows, axis=1), weight_ref[...]), 1)


def sigmoid(value):
    return 1.0 / (1.0 + jnp.exp(-value))


def norm_of(sums, gain, count):
    mean = sums[0:1] / count
    spread = sums[1:2] / count - mean * mean
    scale = lax.rsqrt(spread + EPSILON)
    return mean, scale, gain * scale


def sums_of(value, other):
    total = jnp.sum(value, axis=0, keepdims=True)
    product = jnp.sum(value * other, axis=0, keepdims=True)
    row = lax.broadcasted_iota(jnp.int32, (GROUP, value.shape[1]), 0)
    return jnp.where(row == 0, total, jnp.where(row == 1, product, 0.0))


def inlet_channels(state, lon):
    amount = state[:GROUP]
    groups = jnp.concatenate([state, along_lon(amount, lon), along_lat(amount, lon)], axis=0)
    blank = jnp.zeros((GROUP, state.shape[1]), F32)
    return jnp.concatenate(
        [lon_moved(groups, -1, lon), groups, lon_moved(groups, 1, lon), blank], axis=0
    )


def advected(state, step_size, lon):
    amount, east, north = state[:GROUP], state[GROUP : 2 * GROUP], state[2 * GROUP :]
    return amount - step_size * (along_lon(amount * east, lon) + along_lat(amount * north, lon))


def row_products(left_rows, right_rows):
    left_high, left_low = halves(left_rows)
    right_high, right_low = halves(right_rows)
    left = jnp.concatenate([left_high, left_high, left_low, left_low], axis=0)
    right = jnp.concatenate([right_high, right_low, right_high, right_low], axis=0)
    return dot(left, right, 0, 0)


def heads_of(channels, cells, block_size):
    width = channels // HEADS
    return [
        (slice(head * width, (head + 1) * width), slice(start, start + block_size))
        for start in range(0, cells, block_size)
        for head in range(HEADS)
    ]


def of_head(value, rows, other=0.0):
    channel = lax.broadcasted_iota(jnp.int32, value.shape, 1)
    return jnp.where((channel >= rows.start) & (channel < rows.stop), value, other)


def below(rows, offset):
    return slice(rows.start + offset, rows.stop + offset)


def entered_inlet_kernel(lon, ids_ref, own_ref, arrived_ref, *refs):
    state_ref, cot_ref = refs[3], refs[4]
    size = state_ref.shape[0]
    state_ref[...] = jnp.where(ids_ref[0] < 2, own_ref[:size], arrived_ref[:size])
    cot_ref[...] = jnp.where(ids_ref[0] < 2, own_ref[size:], arrived_ref[size:])
    inlet_kernel(lon, state_ref, *refs[:3], *refs[5:])


def inlet_kernel(
    lon, state_ref, static_ref, w_input_ref, w_first_ref,
    inner_ref, pre_ref, sums_ref, patches_ref,
):
    cells = state_ref.shape[1]
    moving = inlet_channels(state_ref[...], lon).T
    width = patches_ref.shape[1]
    blank = jnp.zeros((lon, width), BF16)
    patches_ref[:lon] = blank
    patches_ref[lon + cells :] = blank
    patches_ref[lon : lon + cells, :256] = beside(moving)
    rows = [patches_ref[lon * place : lon * place + cells, :256] for place in range(3)]
    inner = folded(dot(jnp.concatenate(rows, axis=1), w_input_ref[...]), 1) + static_ref[...]
    inner_ref[...] = inner
    fill_patches(patches_ref, inner * sigmoid(inner), lon)
    pre = conv_patches(patches_ref, w_first_ref, lon)
    pre_ref[...] = pre
    sums_ref[...] = sums_of(pre, pre)


def middle_kernel(
    lon, count, pre_one_ref, sums_one_ref, gain_ref, shift_ref, w_second_ref,
    pre_ref, sums_ref, patches_ref,
):
    mean, unused_scale, factor = norm_of(sums_one_ref[...], gain_ref[...], count)
    normed = (pre_one_ref[...] - mean) * factor + shift_ref[...]
    fill_patches(patches_ref, normed * sigmoid(normed), lon)
    pre = conv_patches(patches_ref, w_second_ref, lon)
    pre_ref[...] = pre
    sums_ref[...] = sums_of(pre, pre)


def act_two_of(inner, pre_two, sums, gain, shift, count):
    mean, unused_scale, factor = norm_of(sums, gain, count)
    return inner * sigmoid(inner) + (pre_two - mean) * factor + shift


def project(w_qkv_ref, act_two_halves, head_width, qkv_ref):
    channels = act_two_halves.shape[0] // 2
    rows = folded(dot(w_qkv_ref[...], act_two_halves), 0)
    qkv_ref[:channels] = rows[:channels] * (LOG2_E / math.sqrt(head_width))
    qkv_ref[channels:] = rows[channels:]


def outlet_kernel(
    lon, count, block_size, step_size, quantities,
    state_ref, inner_ref, pre_two_ref, sums_two_ref, gain_ref, shift_ref,
    w_heads_ref, w_mixer_ref, w_velocity_ref, b_velocity_ref,
    out_ref, packed_ref, mixed_ref, top_ref, weight_ref,
    query_ref,
):
    cells, channels = inner_ref.shape
    act_two = act_two_of(
        inner_ref[...], pre_two_ref[...], sums_two_ref[...], gain_ref[...], shift_ref[...], count
    )
    projected = folded(dot(beside(act_two), w_heads_ref[...]), 1)
    query = projected[:, : HEADS * channels]
    query_high = query.astype(BF16).astype(F32)
    channel = lax.rem(lax.broadcasted_iota(jnp.int32, query.shape, 1), channels)
    query_ref[...] = jnp.where(channel < channels // 2, query_high, query - query_high).astype(BF16)
    key = projected[:, HEADS * channels : (HEADS + 1) * channels]
    key_high, key_low = halves((key * (LOG2_E / math.sqrt(channels // HEADS))).T)
    value = projected[:, (HEADS + 1) * channels :]
    heads = heads_of(channels, cells, block_size)

    def scores_of(turn):
        rows, lanes = heads[turn]
        right = [half[rows, lanes] for half in (key_high, key_low, key_high, key_low)]
        start = turn % HEADS * channels
        return dot(query_ref[lanes, start : start + channels], jnp.concatenate(right, axis=0))

    following = scores_of(0)
    for turn, (rows, lanes) in enumerate(heads):
        scores = following
        if turn + 1 < len(heads):
            following = scores_of(turn + 1)
        top = jnp.max(scores, axis=1, keepdims=True)
        powers = jnp.exp2(scores - top)
        weight = 1.0 / jnp.sum(powers, axis=1, keepdims=True)
        high, low = halves(powers)
        right = beside(of_head(value[lanes], rows))
        own = folded(dot(high, right) + dot(low, right), 1) * weight
        all_top, all_weight = [jnp.broadcast_to(part, own.shape) for part in (top, weight)]
        if rows.start:
            own = own + mixed
            all_top, all_weight = of_head(all_top, rows, tops), of_head(all_weight, rows, weights)
        mixed, tops, weights = own, all_top, all_weight
        if rows.stop == channels:
            mixed_ref[lanes], top_ref[lanes], weight_ref[lanes] = mixed, tops, weights
    act_three = act_two + folded(dot(beside(mixed_ref[...]), w_mixer_ref[...]), 1)
    parts = folded(dot(w_velocity_ref[...], stacked(act_three.T)), 0)
    forcing = jnp.zeros((2 * GROUP, cells), F32) + b_velocity_ref[...]
    for column, lon_offset in enumerate((-1, 0, 1)):
        total = None
        for row, lat_offset in enumerate((-1, 0, 1)):
            start = (row * 3 + column) * 2 * GROUP
            part = parts[start : start + 2 * GROUP]
            if lat_offset:
                part = lat_moved(part, lat_offset, lon)
            total = part if total is None else total + part
        forcing = forcing + (lon_moved(total, lon_offset, lon) if lon_offset else total)
    state = state_ref[...]
    flows = state[GROUP:]
    out_ref[:GROUP] = advected(state, step_size, lon)
    out_ref[GROUP:] = flows + step_size * (forcing - flows)
    put_packed(packed_ref, out_ref[...], quantities)


def outlet_back_kernel(
    lon, count, block_size, step_size, quantities, sections, step,
    ids_ref,
    state_ref, d_next_ref, cots_ref, inner_ref, pre_two_ref, sums_two_ref, gain_ref, shift_ref,
    mixed_ref, top_ref, weight_ref,
    w_qkv_ref, w_mixer_ref, w_qkv_back_ref, w_mixer_back_ref, w_velocity_back_ref,
    acc_qkv_ref, acc_mixer_ref, acc_velocity_ref, acc_small_ref,
    d_state_ref, d_two_ref, sums_ref,
    out_qkv_ref, out_mixer_ref, out_velocity_ref, out_small_ref,
    d_mixed_ref, d_qkv_ref, seed_ref, qkv_ref, mixed_rows_ref, top_rows_ref,
):
    channels = inner_ref.shape[1]
    cells = inner_ref.shape[0]
    heads = heads_of(channels, cells, block_size)

    state = state_ref[...]
    packed = cots_ref[lax.rem(ids_ref[0] - step + sections, sections)]
    put_groups(seed_ref, packed[: 3 * quantities])
    seed = seed_ref[...] + d_next_ref[...]
    amount, east, north = state[:GROUP], state[GROUP : 2 * GROUP], state[2 * GROUP :]
    d_amount = seed[:GROUP]
    d_lon = step_size * along_lon(d_amount, lon)
    d_lat = step_size * along_lat(d_amount, lon)
    d_state_ref[:GROUP] = d_amount + d_lon * east + d_lat * north
    d_state_ref[GROUP : 2 * GROUP] = (1.0 - step_size) * seed[GROUP : 2 * GROUP] + d_lon * amount
    d_state_ref[2 * GROUP :] = (1.0 - step_size) * seed[2 * GROUP :] + d_lat * amount
    d_forcing = step_size * seed[GROUP:]
    pieces = []
    for lat_offset in (-1, 0, 1):
        moved_rows = lat_moved(d_forcing, -lat_offset, lon) if lat_offset else d_forcing
        for lon_offset in (-1, 0, 1):
            pieces.append(lon_moved(moved_rows, -lon_offset, lon) if lon_offset else moved_rows)
    d_parts = stacked(jnp.concatenate(pieces, axis=0))
    d_three = folded(dot(w_velocity_back_ref[...], d_parts), 0)
    d_three_halves = stacked(d_three)
    d_mixed_ref[...] = folded(dot(w_mixer_back_ref[...], d_three_halves), 0) * weight_ref[...].T
    mixed_rows_ref[...] = mixed_ref[...].T
    top_rows_ref[...] = top_ref[...].T
    act_two = act_two_of(
        inner_ref[...], pre_two_ref[...], sums_two_ref[...], gain_ref[...], shift_ref[...], count
    ).T
    act_two_halves = stacked(act_two)
    project(w_qkv_ref, act_two_halves, channels // HEADS, qkv_ref)
    d_mixed_cells = d_mixed_ref[...].T
    query_cells = qkv_ref[:channels].T

    def products_of(turn):
        rows, lanes = heads[turn]
        scores = row_products(qkv_ref[below(rows, channels), lanes], qkv_ref[rows, lanes])
        return scores, row_products(qkv_ref[below(rows, 2 * channels), lanes], d_mixed_ref[rows, lanes])

    following = products_of(0)
    for turn, (rows, lanes) in enumerate(heads):
        scores, d_powers = following
        if turn + 1 < len(heads):
            following = products_of(turn + 1)
        inner_sum = jnp.sum(d_mixed_ref[rows, lanes] * mixed_rows_ref[rows, lanes], axis=0, keepdims=True)
        powers = jnp.exp2(scores - top_rows_ref[rows.start : rows.start + 1, lanes])
        power_high, power_low = halves(powers)
        d_high, d_low = halves(powers * (d_powers - inner_sum))
        right = beside(of_head(d_mixed_cells[lanes], rows))
        d_value = dot(power_high, right) + dot(power_low, right) + (d_value if rows.start else 0.0)
        right = beside(of_head(query_cells[lanes], rows))
        d_key = dot(d_high, right) + dot(d_low, right) + (d_key if rows.start else 0.0)
        key_halves = stacked(qkv_ref[below(rows, channels), lanes])
        d_query = folded(dot(key_halves, d_high) + dot(key_halves, d_low), 0)
        d_qkv_ref[rows, lanes] = d_query * (1.0 / math.sqrt(channels // HEADS))
        if rows.stop == channels:
            d_qkv_ref[channels : 2 * channels, lanes] = folded(d_key, 1).T * (1.0 / LOG2_E)
            d_qkv_ref[2 * channels :, lanes] = folded(d_value, 1).T
    d_qkv_halves = stacked(d_qkv_ref[...])
    d_two = (d_three + folded(dot(w_qkv_back_ref[...], d_qkv_halves), 0)).T
    d_two_ref[...] = d_two
    mean, scale, unused_factor = norm_of(sums_two_ref[...], gain_ref[...], count)
    sums = sums_of(d_two, pre_two_ref[...] - mean)
    sums_ref[...] = sums

    def pairs(left, right):
        return folded(folded(dot(left, right, 1, 1), 0), 1)

    mixed_halves = stacked(mixed_rows_ref[...])
    act_three = act_two + folded(dot(w_mixer_ref[...], mixed_halves), 0)
    out_velocity_ref[...] = acc_velocity_ref[...] + pairs(d_parts, stacked(act_three))
    out_mixer_ref[...] = acc_mixer_ref[...] + pairs(mixed_halves, d_three_halves)
    out_qkv_ref[...] = acc_qkv_ref[...] + pairs(act_two_halves, d_qkv_halves)
    bias = jnp.sum(d_forcing, axis=1, keepdims=True)
    row = lax.broadcasted_iota(jnp.int32, (GROUP, channels), 0)
    small = jnp.where(row == 0, sums[1:2] * scale, jnp.where(row == 1, sums[0:1], 0.0))
    out_small_ref[:GROUP] = acc_small_ref[:GROUP] + small
    out_small_ref[GROUP:] = acc_small_ref[GROUP:] + bias


def d_pre_of(d_normed, centred, sums, all_grad_sums, gain, count):
    unused_mean, scale, factor = norm_of(sums, gain, count)
    d_spread = -0.5 * gain * scale * scale * scale * all_grad_sums[1:2]
    return factor * (d_normed - all_grad_sums[0:1] / count) + (2.0 * d_spread / count) * centred


def weight_pairs(acc_ref, out_ref, left_halves, patches_ref, lon):
    cells = patches_ref.shape[0] - 2 * lon
    width = patches_ref.shape[1] // 3
    for tap in range(9):
        row, column = divmod(8 - tap, 3)
        right = patches_ref[lon * row : lon * row + cells, column * width : (column + 1) * width]
        out_ref[tap] = acc_ref[tap] + folded(folded(dot(left_halves, right), 0), 1)


def middle_back_kernel(
    lon, count,
    d_two_ref, pre_two_ref, sums_two_ref, all_two_ref, gain_two_ref,
    pre_one_ref, sums_one_ref, gain_ref, shift_ref, w_second_back_ref,
    acc_weight_ref, acc_small_ref,
    d_normed_ref, sums_ref, out_weight_ref, out_small_ref,
    patches_ref,
):
    sums_two = sums_two_ref[...]
    d_pre = d_pre_of(
        d_two_ref[...], pre_two_ref[...] - sums_two[0:1] / count, sums_two, all_two_ref[...],
        gain_two_ref[...], count,
    )
    fill_patches(patches_ref, d_pre, lon)
    d_act = conv_patches(patches_ref, w_second_back_ref, lon)
    mean, scale, factor = norm_of(sums_one_ref[...], gain_ref[...], count)
    centred = pre_one_ref[...] - mean
    normed = centred * factor + shift_ref[...]
    gate = sigmoid(normed)
    d_normed = d_act * gate * (1.0 + normed * (1.0 - gate))
    d_normed_ref[...] = d_normed
    sums = sums_of(d_normed, centred)
    sums_ref[...] = sums
    weight_pairs(acc_weight_ref, out_weight_ref, stacked((normed * gate).T), patches_ref, lon)
    row = lax.broadcasted_iota(jnp.int32, sums.shape, 0)
    small = jnp.where(row == 0, sums[1:2] * scale, jnp.where(row == 1, sums[0:1], 0.0))
    out_small_ref[...] = acc_small_ref[...] + small


def inlet_back_kernel(
    lon, count, quantities,
    state_ref, d_normed_ref, pre_one_ref, sums_one_ref, all_one_ref, gain_ref,
    inner_ref, d_two_ref, d_state_in_ref, w_first_back_ref, w_input_back_ref,
    acc_first_ref, acc_input_ref, acc_inner_ref,
    d_state_ref, packed_ref, out_first_ref, out_input_ref, out_inner_ref,
    patches_ref,
):
    cells = inner_ref.shape[0]
    sums_one = sums_one_ref[...]
    d_pre = d_pre_of(
        d_normed_ref[...], pre_one_ref[...] - sums_one[0:1] / count, sums_one, all_one_ref[...],
        gain_ref[...], count,
    )
    fill_patches(patches_ref, d_pre, lon)
    d_act = conv_patches(patches_ref, w_first_back_ref, lon) + d_two_ref[...]
    inner = inner_ref[...]
    gate = sigmoid(inner)
    d_inner = d_act * gate * (1.0 + inner * (1.0 - gate))
    weight_pairs(acc_first_ref, out_first_ref, stacked((inner * gate).T), patches_ref, lon)
    out_inner_ref[...] = acc_inner_ref[...] + d_inner
    patches_ref[lon : lon + cells, :256] = beside(d_inner)
    rows = [patches_ref[lon * place : lon * place + cells, :256] for place in range(3)]
    d_moving = folded(dot(jnp.concatenate(rows, axis=1), w_input_back_ref[...]), 1).T
    state = state_ref[...]
    moving_halves = stacked(inlet_channels(state, lon))
    for place in range(3):
        out_input_ref[place] = acc_input_ref[place] + folded(
            folded(dot(moving_halves, rows[2 - place]), 0), 1
        )
    size = 5 * GROUP
    d_groups = (
        lon_moved(d_moving[:size], 1, lon)
        + d_moving[size : 2 * size]
        + lon_moved(d_moving[2 * size : 3 * size], -1, lon)
    )
    d_state = d_state_in_ref[...] + d_groups[: 3 * GROUP]
    d_state_ref[:GROUP] = (
        d_state[:GROUP]
        - along_lon(d_groups[3 * GROUP : 4 * GROUP], lon)
        - along_lat(d_groups[4 * GROUP :], lon)
    )
    d_state_ref[GROUP:] = d_state[GROUP:]
    put_packed(packed_ref, d_state_ref[...], quantities)


def put_groups(out_ref, rows):
    size = rows.shape[0] // 3
    out_ref[...] = jnp.zeros(out_ref.shape, F32)
    for group in range(3):
        out_ref[group * GROUP : group * GROUP + size] = rows[group * size : (group + 1) * size]


def put_packed(out_ref, grouped, size):
    out_ref[...] = jnp.zeros(out_ref.shape, F32)
    for group in range(3):
        out_ref[group * size : (group + 1) * size] = grouped[group * GROUP : group * GROUP + size]


def fetched(far_refs, near_refs, done_ref):
    copies = [
        pltpu.make_async_copy(far_ref, near_ref, done_ref.at[place])
        for place, (far_ref, near_ref) in enumerate(zip(far_refs, near_refs))
    ]
    for copy in copies:
        copy.start()
    return copies


def enter_kernel(plan, ids_ref, order_ref, state_ref, cot_ref, *refs):
    out_refs, (near_ref, near_cot_ref, rows_ref, done_ref) = refs[:-4], refs[-4:]
    copies = fetched([state_ref, cot_ref], [near_ref, near_cot_ref], done_ref)
    size = rows_ref.shape[0]
    copies[0].wait()
    place = order_ref[0, plan.slot(ids_ref[0], ids_ref[1])]
    for row in range(size):
        rows_ref[row : row + 1] = near_ref[row, pl.ds(place, 1)]
    put_groups(out_refs[0].at[: 3 * GROUP], rows_ref[...])
    copies[1].wait()
    for steps, out_ref in enumerate(out_refs):
        start = 0 if steps else 3 * GROUP
        target = lax.rem(ids_ref[0] + steps, plan.sections)
        place = order_ref[0, plan.slot(target, ids_ref[1])]
        out_ref[start:] = jnp.zeros((2 * GROUP, out_ref.shape[1]), F32)
        for row in range(size):
            out_ref[start + row : start + row + 1] = near_cot_ref[row, pl.ds(place, 1)]


def leave_kernel(plan, ids_ref, *refs):
    values_ref = refs[-1]
    size = refs[0].shape[0]
    for step in range(plan.sections):
        values_ref[step, :size] = refs[step][...]
        if step:
            values_ref[step, size:] = refs[plan.sections + step - 1][...]
        else:
            values_ref[step, size:] = jnp.zeros(refs[0].shape, F32)
    for steps, out_ref in enumerate(refs[2 * plan.sections - 1 : -1]):
        out_ref[...] = values_ref[lax.rem(ids_ref[0] + steps, plan.sections)]


def arrive_kernel(plan, start, ids_ref, order_ref, kept_ref, *refs):
    section, dp = ids_ref[0], ids_ref[1]
    out_ref = refs[-1]
    size = kept_ref.shape[0] // 2
    early, late = refs[: plan.sections], refs[plan.sections : -1]
    for steps, ref in enumerate(early):
        source = lax.rem(section - steps + plan.sections, plan.sections)
        place = order_ref[0, plan.slot(source, dp)]
        value = ref[start : start + size]
        if plan.halved and not steps:
            value = jnp.where(section < 2, kept_ref[start : start + size], value)
        if late:
            value = jnp.where(section == 0, late[steps][...], value)
        for row in range(out_ref.shape[0]):
            out_ref[row, pl.ds(place, 1)] = value[row : row + 1]


def put_conv_weight(out_ref, taps):
    for tap, weight in enumerate(taps):
        wide = beside(weight)
        rows = weight.shape[0]
        out_ref[2 * tap * rows : (2 * tap + 1) * rows] = wide
        out_ref[(2 * tap + 1) * rows : (2 * tap + 2) * rows] = wide


def put_left_weight(out_ref, weight):
    rows = weight.shape[0]
    for place, half in enumerate(halves(weight)):
        out_ref[place * rows : (place + 1) * rows] = jnp.concatenate([half, half], axis=1)


def weights_kernel(
    lon, quantities,
    w_input_ref, maps_ref, b_input_ref, w_first_ref, w_second_ref,
    w_query_ref, w_key_ref, w_value_ref, w_mixer_ref, w_velocity_ref,
    static_part_ref, moving_cat_ref, moving_back_ref, first_cat_ref, second_cat_ref,
    heads_ref, mixer_cells_ref, qkv_ref, qkv_back_ref, mixer_ref, mixer_back_ref, velocity_ref, velocity_back_ref,
    first_back_ref, second_back_ref,
    patches_ref, weight_ref, taps_ref, rows_ref, *near_refs,
):
    near_refs, done_ref = near_refs[:-1], near_refs[-1]
    copies = fetched(
        [w_input_ref, maps_ref, b_input_ref, w_first_ref, w_second_ref,
         w_query_ref, w_key_ref, w_value_ref, w_mixer_ref, w_velocity_ref],
        near_refs, done_ref,
    )
    (
        w_input_ref, maps_ref, b_input_ref, w_first_ref, w_second_ref,
        w_query_ref, w_key_ref, w_value_ref, w_mixer_ref, w_velocity_ref,
    ) = near_refs
    channels = w_input_ref.shape[2]
    moving = 5 * quantities
    statics = maps_ref.shape[0]
    taps_ref[...] = jnp.zeros(taps_ref.shape, F32)
    rows_ref[...] = jnp.zeros(rows_ref.shape, F32)
    copies[0].wait()
    for tap in range(9):
        row, column = divmod(tap, 3)
        for group in range(5):
            start = (column * 5 + group) * GROUP
            taps_ref[9 + row, start : start + quantities] = w_input_ref[
                tap, group * quantities : (group + 1) * quantities
            ]
        taps_ref[tap, :statics] = w_input_ref[tap, moving:]
    put_conv_weight(moving_cat_ref, [taps_ref[9 + row] for row in range(3)])
    put_conv_weight(moving_back_ref, [taps_ref[11 - row].T for row in range(3)])
    put_conv_weight(weight_ref, [taps_ref[tap] for tap in range(9)])
    copies[1].wait()
    copies[2].wait()
    maps = jnp.concatenate(
        [maps_ref[...], jnp.zeros((channels - statics, maps_ref.shape[1]), F32)], axis=0
    )
    fill_patches(patches_ref, maps.T, lon)
    static_part_ref[...] = conv_patches(patches_ref, weight_ref, lon) + b_input_ref[...]
    for copy in copies[3:]:
        copy.wait()
    put_conv_weight(first_cat_ref, [w_first_ref[tap] for tap in range(9)])
    put_conv_weight(second_cat_ref, [w_second_ref[tap] for tap in range(9)])
    put_conv_weight(first_back_ref, [w_first_ref[8 - tap].T for tap in range(9)])
    put_conv_weight(second_back_ref, [w_second_ref[8 - tap].T for tap in range(9)])
    parts = [ref[...] for ref in (w_query_ref, w_key_ref, w_value_ref)]
    turned = [part.T for part in parts]
    width = channels // HEADS
    repeated = [turned[0][head * width : (head + 1) * width] for head in range(HEADS) for unused in range(HEADS)]
    put_conv_weight(heads_ref, [jnp.concatenate([jnp.concatenate(repeated, axis=0).T, parts[1], parts[2]], axis=1)])
    put_conv_weight(mixer_cells_ref, [w_mixer_ref[...]])
    put_left_weight(qkv_ref, jnp.concatenate(turned, axis=0))
    put_left_weight(qkv_back_ref, jnp.concatenate(parts, axis=1))
    put_left_weight(mixer_ref, w_mixer_ref[...].T)
    put_left_weight(mixer_back_ref, w_mixer_ref[...])
    for tap in range(9):
        for group in range(2):
            start = (tap * 2 + group) * GROUP
            rows_ref[start : start + quantities] = w_velocity_ref[
                tap, group * quantities : (group + 1) * quantities
            ]
    size = 18 * GROUP
    put_left_weight(velocity_ref, rows_ref[:size])
    put_left_weight(velocity_back_ref, rows_ref[...].T[:, :size])


def index_of(ids_ref, plan, bits):
    own = ids_ref[0] * plan.dp + ids_ref[1]
    return sum(lax.rem(own // bit, 2) << place for place, bit in enumerate(bits))


def deal(total_ref, own, out_refs):
    rows = out_refs[0].shape[0]
    for turn, out_ref in enumerate(out_refs):
        out_ref[...] = total_ref[pl.ds(pl.multiple_of((own ^ turn) * rows, GROUP), rows)]


def pack_kernel(
    plan, bits, lon, statics, ids_ref, maps_ref, inner_ref, first_ref, second_ref, moving_ref,
    qkv_ref, mixer_ref, velocity_ref, small_one_ref, small_two_ref, *refs,
):
    out_refs, total_ref, patches_ref = refs[:-2], refs[-2], refs[-1]
    cells, channels = inner_ref.shape
    d_inner = inner_ref[...]
    fill_patches(patches_ref, d_inner, lon)
    width = patches_ref.shape[1] // 3
    maps = maps_ref[...]
    blank = jnp.zeros((-statics % GROUP, cells), F32)
    maps = jnp.concatenate([maps, blank], axis=0)
    rows = maps.shape[0]
    left = jnp.concatenate(halves(maps), axis=0)
    start = 0

    def put(value):
        nonlocal start
        total_ref[start : start + value.shape[0]] = value
        start += value.shape[0]

    for tap in range(9):
        put(first_ref[tap])
    for tap in range(9):
        put(second_ref[tap])
    for tap in range(9):
        row, column = divmod(8 - tap, 3)
        right = patches_ref[lon * row : lon * row + cells, column * width : (column + 1) * width]
        put(folded(folded(dot(left, right), 0), 1))
    for place in range(3):
        put(moving_ref[place, : 15 * GROUP])
    for part in range(3):
        put(qkv_ref[:, part * channels : (part + 1) * channels])
    put(mixer_ref[...])
    put(velocity_ref[...])
    put(small_one_ref[...])
    put(small_two_ref[...])
    put(jnp.zeros((GROUP, channels), F32) + jnp.sum(d_inner, axis=0, keepdims=True))
    total_ref[start:] = jnp.zeros((total_ref.shape[0] - start, channels), F32)
    deal(total_ref, index_of(ids_ref, plan, bits), out_refs)


def reduce_kernel(plan, bits, count, ids_ref, *refs):
    total_ref = refs[-1]
    total = refs[0][...]
    for ref in refs[1:count]:
        total = total + ref[...]
    if not bits:
        refs[count][...] = total
        return
    total_ref[...] = total
    deal(total_ref, index_of(ids_ref, plan, bits), refs[count:-1])


def gather_rows(plan, bits, ids_ref, part_refs, out_ref):
    own = index_of(ids_ref, plan, bits)
    rows = part_refs[0].shape[0]
    for turn, ref in enumerate(part_refs):
        out_ref[pl.ds(pl.multiple_of((own ^ turn) * rows, GROUP), rows)] = ref[...]


def gather_kernel(plan, bits, ids_ref, *refs):
    gather_rows(plan, bits, ids_ref, refs[:-1], refs[-1])


def unpack_kernel(
    plan, bits, quantities, statics, ids_ref, *refs,
):
    count = 1 << len(bits)
    (
        input_ref, bias_ref, first_ref, gain_one_ref, shift_one_ref, second_ref, gain_two_ref, shift_two_ref,
        query_ref, key_ref, value_ref, mixer_ref, velocity_ref, velocity_bias_ref, total_ref,
    ) = refs[count:]
    gather_rows(plan, bits, ids_ref, refs[:count], total_ref)
    channels = mixer_ref.shape[0]
    moving = 5 * quantities
    start = 0

    def take(rows):
        nonlocal start
        start += rows
        return total_ref[start - rows : start]

    for tap in range(9):
        first_ref[tap] = take(channels)
    for tap in range(9):
        second_ref[tap] = take(channels)
    for tap in range(9):
        input_ref[tap, moving:] = take(statics + -statics % GROUP)[:statics]
    for row in range(3):
        for column in range(3):
            for group in range(5):
                rows = take(GROUP)
                input_ref[row * 3 + column, group * quantities : (group + 1) * quantities] = rows[:quantities]
    query_ref[...] = take(channels)
    key_ref[...] = take(channels)
    value_ref[...] = take(channels)
    mixer_ref[...] = take(channels)
    for tap in range(9):
        for group in range(2):
            velocity_ref[tap, group * quantities : (group + 1) * quantities] = take(GROUP)[:quantities]
    small = take(GROUP)
    gain_one_ref[...], shift_one_ref[...] = small[0:1], small[1:2]
    small = take(GROUP)
    gain_two_ref[...], shift_two_ref[...] = small[0:1], small[1:2]
    velocity_bias_ref[...] = take(2 * GROUP)
    bias_ref[...] = take(GROUP)[0:1]


def call(kernel, outs, scratch=(), aliases=None, name=None, scalars=0, kinds=None, far_in=(), limit=None):
    kinds = kinds or [F32] * len(outs)

    def run(*operands):
        places = [pltpu.SMEM] * scalars + [pltpu.VMEM] * (len(operands) - scalars)
        for place in far_in:
            places[place] = pltpu.HBM
        return pl.pallas_call(
            kernel,
            out_shape=tuple(jax.ShapeDtypeStruct(shape, kind) for shape, kind in zip(outs, kinds)),
            in_specs=[pl.BlockSpec(memory_space=place) for place in places],
            out_specs=tuple(pl.BlockSpec(memory_space=pltpu.VMEM) for unused in outs),
            scratch_shapes=scratch,
            input_output_aliases=aliases or {},
            compiler_params=pltpu.CompilerParams(vmem_limit_bytes=limit or VMEM_LIMIT),
            name=name,
        )(*operands)

    return run


VMEM_LIMIT = 24 * 1024 * 1024
ALONE_LIMIT = 56 * 1024 * 1024


def in_groups(array, axis, groups):
    shape = array.shape
    split = shape[:axis] + (groups, shape[axis] // groups) + shape[axis + 1 :]
    array = array.reshape(split)
    pads = [(0, 0)] * array.ndim
    pads[axis + 1] = (0, GROUP - split[axis + 1])
    return jnp.pad(array, pads).reshape(shape[:axis] + (groups * GROUP,) + shape[axis + 1 :])


def from_groups(array, axis, groups, size):
    shape = array.shape
    array = array.reshape(shape[:axis] + (groups, GROUP) + shape[axis + 1 :])
    array = lax.slice_in_dim(array, 0, size, axis=axis + 1)
    return array.reshape(shape[:axis] + (groups * size,) + shape[axis + 1 :])


class Plan:
    def __init__(self, sections, dp):
        self.sections, self.dp = sections, dp
        self.halved = sections == 4 and dp >= 4
        self.half = dp // 2
        bits = [1 << place for place in range((sections * dp).bit_length() - 1)]
        dp_bits = [bit for bit in bits if bit < dp]
        section_bits = [bit for bit in bits if bit >= dp]
        if self.halved:
            self.sum_rounds = in_pairs(dp_bits[:-1]) + in_pairs(section_bits)
        else:
            self.sum_rounds = in_pairs(dp_bits) + [section_bits[:1]]
        self.all_rounds = [dp_bits[:1]] + in_pairs(section_bits) + in_pairs(dp_bits[1:])

    def slot(self, section, home):
        if not self.halved:
            return section
        return lax.rem(home // self.half + section // 2, 2) * 2 + lax.rem(section, 2)

    def other(self, section, dp):
        return dp ^ self.half if self.halved and section >= 2 else dp

    def to_workers(self, steps):
        return [
            (section * self.dp + home, self.joint((section + steps) % self.sections, home))
            for section in range(self.sections)
            for home in range(self.dp)
        ]

    def to_homes(self, steps):
        return [
            (section * self.dp + own, (section + steps) % self.sections * self.dp + self.other(section, own))
            for section in range(self.sections)
            for own in range(self.dp)
        ]

    def to_first_home(self, steps):
        return [(source, target) for source, target in self.to_homes(steps) if target < self.dp]

    def joint(self, section, home):
        return section * self.dp + self.other(section, home)


def in_pairs(bits):
    return [bits[start : start + 2] for start in range(0, len(bits), 2)]


def masks_of(bits):
    return [sum(bit for place, bit in enumerate(bits) if turn >> place & 1) for turn in range(1, 1 << len(bits))]


def exchanged(value, mask):
    size = lax.axis_size("section") * lax.axis_size("dp")
    return lax.ppermute(value, ("section", "dp"), [(own, own ^ mask) for own in range(size)])


def moved(value, pairs):
    going = [(source, target) for source, target in pairs if source != target]
    if not going:
        return value
    return lax.ppermute(value, ("section", "dp"), going)


def micro_sum(plan, value, first_core):
    if not plan.halved or plan.half != 4:
        for bits in plan.sum_rounds:
            value = value + sum(exchanged(value, mask) for mask in masks_of(bits))
        return value
    value = value + exchanged(value, 1)
    plane = masks_of([plan.dp, 2 * plan.dp])
    other = [mask ^ 2 for mask in plane + [0]]
    own = range(plan.sections * plan.dp)
    total = value * first_core
    for turn in range(4):
        pairs = [(device, device ^ other[turn]) for device in own if device & 1]
        if turn < 3:
            pairs += [(device, device ^ plane[turn]) for device in own if not device & 1]
        total = total + lax.ppermute(value, ("section", "dp"), pairs)
    return total + exchanged(total, 1)


def on_device(
    state_start,
    static_maps,
    grouping,
    cotangent,
    w_input,
    b_input,
    w_first,
    gain_first,
    shift_first,
    w_second,
    gain_second,
    shift_second,
    w_query,
    w_key,
    w_value,
    w_mixer,
    w_velocity,
    b_velocity,
):
    segments = lax.axis_size("section")
    plan = Plan(segments, lax.axis_size("dp"))
    micro_count = segments // 2
    per_micro = state_start.shape[0] // micro_count
    cells = state_start.shape[2]
    lon = cells // LAT
    count = float(per_micro * cells * plan.dp)
    step_size = 2.0 / segments
    block_size = ATT_ROWS * lon
    channels = w_first.shape[2]
    quantities = state_start.shape[1] // 3
    statics = static_maps.shape[0]
    ids = jnp.stack([lax.axis_index("section"), lax.axis_index("dp")]).astype(jnp.int32)

    plane = (cells, channels)
    small = (GROUP, channels)
    conv = (9 * 2 * channels, 2 * channels)
    patches = pltpu.VMEM((cells + 2 * lon, 6 * channels), BF16)
    wide = pltpu.VMEM((3 * channels, cells), F32)
    narrow = pltpu.VMEM((channels, cells), F32)
    state_shape = (3 * GROUP, cells)

    packed = (2 * GROUP, cells)

    def near(*arrays):
        return [pltpu.VMEM(array.shape, F32) for array in arrays] + [pltpu.SemaphoreType.DMA((len(arrays),))]

    state_rows, cot_rows = jnp.swapaxes(state_start, 0, 1), jnp.swapaxes(cotangent[0], 0, 1)
    entry, *sent_cots = call(
        functools.partial(enter_kernel, plan), [(5 * GROUP, cells)] + [packed] * (segments - 1),
        [pltpu.VMEM(state_rows.shape, F32)] * 2
        + [pltpu.VMEM((3 * quantities, cells), F32), pltpu.SemaphoreType.DMA((2,))],
        name="enter", scalars=2, far_in=[2, 3], limit=ALONE_LIMIT,
    )(ids, grouping, state_rows, cot_rows)
    arrived = moved(entry, plan.to_workers(0))
    first_core = (1.0 - lax.rem(ids[1], 2).astype(F32)) * jnp.ones(small, F32)
    w_velocity_rows = jnp.swapaxes(w_velocity, 1, 2)
    weights = (
        w_input, static_maps, b_input[None], w_first, w_second, w_query, w_key, w_value, w_mixer, w_velocity_rows
    )
    moving_conv, square_conv = (6 * channels, 2 * channels), (2 * channels, 2 * channels)
    (
        static_part, moving_cat, moving_back_cat, first_cat, second_cat,
        heads_cat, mixer_cells, qkv_cat, qkv_back_cat, mixer_cat, mixer_back_cat, out_cat, out_back_cat,
        first_back_cat, second_back_cat,
    ) = call(
        functools.partial(weights_kernel, lon, quantities),
        [plane, moving_conv, moving_conv, conv, conv,
         (2 * channels, 2 * (HEADS + 2) * channels), square_conv, moving_conv, moving_conv[::-1],
         square_conv, square_conv, (36 * GROUP, 2 * channels), (2 * channels, 36 * GROUP), conv, conv],
        [patches, pltpu.VMEM(conv, BF16), pltpu.VMEM((12, channels, channels), F32),
         pltpu.VMEM((2 * channels, channels), F32)] + near(*weights),
        name="weights", kinds=[F32] + [BF16] * 14, far_in=range(10), limit=ALONE_LIMIT,
    )(*weights)
    b_out = in_groups(b_velocity[:, None], 0, 2)
    gain_one, shift_one = gain_first[None], shift_first[None]
    gain_two, shift_two = gain_second[None], shift_second[None]

    inlet = call(
        functools.partial(inlet_kernel, lon), [plane, plane, small], [patches], name="inlet"
    )
    middle = call(
        functools.partial(middle_kernel, lon, count), [plane, small], [patches], name="middle"
    )
    outlet = call(
        functools.partial(outlet_kernel, lon, count, block_size, step_size, quantities),
        [state_shape, packed, plane, plane, plane],
        [pltpu.VMEM((cells, HEADS * channels), BF16)], name="outlet",
    )

    def outlet_back(step):
        return call(
            functools.partial(outlet_back_kernel, lon, count, block_size, step_size, quantities, segments, step),
            [state_shape, plane, small, (channels, 3 * channels), (channels, channels),
             (18 * GROUP, channels), (3 * GROUP, channels)],
            [narrow, wide, pltpu.VMEM(state_shape, F32), wide, narrow, narrow],
            {17: 3, 18: 4, 19: 5, 20: 6}, name="outlet_back", scalars=1,
        )

    middle_back = call(
        functools.partial(middle_back_kernel, lon, count),
        [plane, small, (9, channels, channels), small], [patches],
        {10: 2, 11: 3}, name="middle_back",
    )
    inlet_back = call(
        functools.partial(inlet_back_kernel, lon, count, quantities),
        [state_shape, packed, (9, channels, channels), (3, channels, channels), plane], [patches],
        {11: 2, 12: 3, 13: 4}, name="inlet_back",
    )

    state = entry[: 3 * GROUP]
    path, saved = [], []
    cots = None
    for step in range(segments):
        if not step:
            if not plan.halved:
                arrived = entry
            state, own_cot, inner, pre_one, sums_one = call(
                functools.partial(entered_inlet_kernel, lon), [state_shape, packed, plane, plane, small], [patches],
                name="inlet", scalars=1,
            )(ids, entry, arrived, static_part, moving_cat, first_cat)
        else:
            inner, pre_one, sums_one = inlet(state, static_part, moving_cat, first_cat)
        sums_one = micro_sum(plan, sums_one, first_core)
        pre_two, sums_two = middle(pre_one, sums_one, gain_one, shift_one, second_cat)
        sums_two = micro_sum(plan, sums_two, first_core)
        state_out, state_packed, mixed, top, weight = outlet(
            state, inner, pre_two, sums_two, gain_two, shift_two, heads_cat, mixer_cells, out_cat, b_out
        )
        saved.append((state, inner, pre_one, pre_two, sums_one, sums_two, mixed, top, weight))
        path.append(state_packed)
        state = state_out
        if not step:
            state, sent_cots = lax.optimization_barrier((state, sent_cots))
            cots = jnp.stack(
                [own_cot] + [moved(cot, plan.to_workers(steps + 1)) for steps, cot in enumerate(sent_cots)]
            )

    def put_home(start, parts):
        (out,) = call(
            functools.partial(arrive_kernel, plan, start), [state_rows.shape], name="arrive", scalars=2
        )(ids, grouping, *parts)
        return jnp.swapaxes(out, 0, 1)[None]

    acc = dict(
        qkv=jnp.zeros((channels, 3 * channels), F32),
        mixer=jnp.zeros((channels, channels), F32),
        velocity=jnp.zeros((18 * GROUP, channels), F32),
        small_two=jnp.zeros((3 * GROUP, channels), F32),
        second=jnp.zeros((9, channels, channels), F32),
        small_one=jnp.zeros(small, F32),
        first=jnp.zeros((9, channels, channels), F32),
        moving=jnp.zeros((3, channels, channels), F32),
        inner=jnp.zeros(plane, F32),
    )
    d_state = jnp.zeros(state_shape, F32)
    grads = [None] * segments
    path_out = None
    for step in reversed(range(segments)):
        if not step:
            sent = call(
                functools.partial(leave_kernel, plan), [(4 * GROUP, cells)] * segments,
                [pltpu.VMEM((segments, 4 * GROUP, cells), F32)], name="leave", scalars=1,
            )(ids, *path, *grads[1:])
            early = [sent[0]] + [moved(part, plan.to_homes(steps)) for steps, part in enumerate(sent)]
        state, inner, pre_one, pre_two, sums_one, sums_two, mixed, top, weight = saved[step]
        d_partial, d_two, grad_two, acc["qkv"], acc["mixer"], acc["velocity"], acc["small_two"] = outlet_back(step)(
            ids, state, d_state, cots, inner, pre_two, sums_two, gain_two, shift_two,
            mixed, top, weight,
            qkv_cat, mixer_cat, qkv_back_cat, mixer_back_cat, out_back_cat,
            acc["qkv"], acc["mixer"], acc["velocity"], acc["small_two"],
        )
        if not step:
            d_two, grad_two, early = lax.optimization_barrier((d_two, grad_two, early))
            path_out = put_home(0, early)
        grad_two = micro_sum(plan, grad_two, first_core)
        d_normed, grad_one, acc["second"], acc["small_one"] = middle_back(
            d_two, pre_two, sums_two, grad_two, gain_two,
            pre_one, sums_one, gain_one, shift_one, second_back_cat,
            acc["second"], acc["small_one"],
        )
        grad_one = micro_sum(plan, grad_one, first_core)
        d_state, grads[step], acc["first"], acc["moving"], acc["inner"] = inlet_back(
            state, d_normed, pre_one, sums_one, grad_one, gain_one,
            inner, d_two, d_partial, first_back_cat, moving_back_cat,
            acc["first"], acc["moving"], acc["inner"],
        )
    late = [grads[0]] + [
        lax.ppermute(grads[0], ("section", "dp"), plan.to_first_home(steps)) for steps in range(1, segments)
    ]

    rounds = plan.all_rounds
    rows = 2 * 9 * channels + 9 * (statics + -statics % GROUP) + 45 * GROUP + 4 * channels + 23 * GROUP
    unit = GROUP * segments * plan.dp
    rows = -(-rows // unit) * unit

    def shares(rows, bits):
        return [(rows >> len(bits), channels)] * (1 << len(bits))

    def swap(parts, bits):
        return [parts[0]] + [exchanged(part, mask) for part, mask in zip(parts[1:], masks_of(bits))]

    parts = call(
        functools.partial(pack_kernel, plan, rounds[0], lon, statics), shares(rows, rounds[0]),
        [pltpu.VMEM((rows, channels), F32), patches], name="pack", scalars=1,
    )(
        ids, static_maps, acc["inner"], acc["first"], acc["second"], acc["moving"], acc["qkv"], acc["mixer"],
        acc["velocity"], acc["small_one"], acc["small_two"],
    )
    for bits, later in zip(rounds, rounds[1:] + [[]]):
        parts = swap(parts, bits)
        rows >>= len(bits)
        parts = call(
            functools.partial(reduce_kernel, plan, later, len(parts)), shares(rows, later),
            [pltpu.VMEM((rows, channels), F32)], name="reduce_part", scalars=1,
        )(ids, *parts)
    parts, late = lax.optimization_barrier((parts, late))
    grads_out = put_home(2 * GROUP, early + late)
    for bits in rounds[::-1]:
        parts = swap([parts[0]] * (1 << len(bits)), bits)
        rows <<= len(bits)
        if bits is rounds[0]:
            break
        parts = call(
            functools.partial(gather_kernel, plan, bits), [(rows, channels)], name="gather_part", scalars=1
        )(ids, *parts)
    row = (1, channels)
    square = (channels, channels)
    grads_all = call(
        functools.partial(unpack_kernel, plan, rounds[0], quantities, statics),
        [w_input.shape, row, w_first.shape, row, row, w_second.shape, row, row, square, square, square, square,
         (9, 2 * quantities, channels), (2 * GROUP, channels)],
        [pltpu.VMEM((rows, channels), F32)], name="unpack", scalars=1,
    )(ids, *parts)
    grads_all = [grad[0] if grad.shape == row else grad for grad in grads_all]
    grads_all[-2] = jnp.swapaxes(grads_all[-2], 1, 2)
    grads_all[-1] = from_groups(grads_all[-1][:, :1], 0, 2, quantities)[:, 0]
    return (path_out, grads_out) + tuple(grads_all)


def solution(mesh):
    weights = (P(),) * 14
    return jax.shard_map(
        on_device,
        mesh=mesh,
        in_specs=(P("dp", None, None), P(), P("dp", None), P("section", "dp", None, None)) + weights,
        out_specs=(P("section", "dp", None, None), P("section", "dp", None, None)) + weights,
        check_vma=False,
    )
```

```python
import functools
import math

import jax
import jax.numpy as jnp
from jax import lax
from jax.experimental import pallas as pl
from jax.experimental.pallas import tpu as pltpu
from jax.sharding import PartitionSpec as P

HEADS = 4
LAT = 16
ATT_ROWS = 8
EPSILON = 1e-05
LOG2_E = 1.0 / math.log(2.0)
F32 = jnp.float32
BF16 = jnp.bfloat16
GROUP = 8


def dot(left, right, left_dim=1, right_dim=0):
    return lax.dot_general(
        left, right, (((left_dim,), (right_dim,)), ((), ())), preferred_element_type=F32
    )


def halves(value):
    high = value.astype(BF16)
    return high, (value - high.astype(F32)).astype(BF16)


def stacked(value):
    return jnp.concatenate(halves(value), axis=0)


def beside(value):
    return jnp.concatenate(halves(value), axis=1)


def folded(value, axis):
    size = value.shape[axis] // 2
    if axis == 0:
        return value[:size] + value[size:]
    return value[:, :size] + value[:, size:]


def cells_of(value):
    return lax.broadcasted_iota(jnp.int32, value.shape, value.ndim - 1)


def lon_moved(value, offset, lon):
    cells = value.shape[1]
    column = lax.rem(cells_of(value), lon)
    near = pltpu.roll(value, (-offset) % cells, 1)
    wrapped = pltpu.roll(value, (offset * (lon - 1)) % cells, 1)
    edge = lon - 1 if offset > 0 else 0
    return jnp.where(column == edge, wrapped, near)


def lat_moved(value, offset, lon):
    cells = value.shape[1]
    moved = pltpu.roll(value, (-offset * lon) % cells, 1)
    cell = cells_of(value)
    if offset > 0:
        return jnp.where(cell < cells - lon, moved, 0.0)
    return jnp.where(cell >= lon, moved, 0.0)


def along_lon(value, lon):
    return 0.5 * (lon_moved(value, 1, lon) - lon_moved(value, -1, lon))


def along_lat(value, lon):
    return 0.5 * (lat_moved(value, 1, lon) - lat_moved(value, -1, lon))


def fill_patches(patches_ref, value, lon):
    cells, channels = value.shape
    planes = value.reshape(cells // lon, lon, channels)
    blank = jnp.zeros((lon, patches_ref.shape[1]), BF16)
    patches_ref[:lon] = blank
    patches_ref[lon + cells :] = blank
    for place, offset in enumerate((-1, 0, 1)):
        moved = value
        if offset:
            moved = pltpu.roll(planes, (-offset) % lon, 1).reshape(cells, channels)
        high, low = halves(moved)
        start = place * 2 * channels
        patches_ref[lon : lon + cells, start : start + channels] = high
        patches_ref[lon : lon + cells, start + channels : start + 2 * channels] = low


def conv_patches(patches_ref, weight_ref, lon):
    cells = patches_ref.shape[0] - 2 * lon
    rows = [patches_ref[lon * place : lon * place + cells] for place in range(3)]
    return folded(dot(jnp.concatenate(rows, axis=1), weight_ref[...]), 1)


def sigmoid(value):
    return 1.0 / (1.0 + jnp.exp(-value))


def norm_of(sums, gain, count):
    mean = sums[0:1] / count
    spread = sums[1:2] / count - mean * mean
    scale = lax.rsqrt(spread + EPSILON)
    return mean, scale, gain * scale


def sums_of(value, other):
    total = jnp.sum(value, axis=0, keepdims=True)
    product = jnp.sum(value * other, axis=0, keepdims=True)
    row = lax.broadcasted_iota(jnp.int32, (GROUP, value.shape[1]), 0)
    return jnp.where(row == 0, total, jnp.where(row == 1, product, 0.0))


def inlet_channels(state, lon):
    amount = state[:GROUP]
    groups = jnp.concatenate([state, along_lon(amount, lon), along_lat(amount, lon)], axis=0)
    blank = jnp.zeros((GROUP, state.shape[1]), F32)
    return jnp.concatenate(
        [lon_moved(groups, -1, lon), groups, lon_moved(groups, 1, lon), blank], axis=0
    )


def advected(state, step_size, lon):
    amount, east, north = state[:GROUP], state[GROUP : 2 * GROUP], state[2 * GROUP :]
    return amount - step_size * (along_lon(amount * east, lon) + along_lat(amount * north, lon))


def row_products(left_rows, right_rows):
    left_high, left_low = halves(left_rows)
    right_high, right_low = halves(right_rows)
    left = jnp.concatenate([left_high, left_high, left_low, left_low], axis=0)
    right = jnp.concatenate([right_high, right_low, right_high, right_low], axis=0)
    return dot(left, right, 0, 0)


def heads_of(channels, cells, block_size):
    width = channels // HEADS
    return [
        (slice(head * width, (head + 1) * width), slice(start, start + block_size))
        for start in range(0, cells, block_size)
        for head in range(HEADS)
    ]


def of_head(value, rows, other=0.0):
    channel = lax.broadcasted_iota(jnp.int32, value.shape, 1)
    return jnp.where((channel >= rows.start) & (channel < rows.stop), value, other)


def below(rows, offset):
    return slice(rows.start + offset, rows.stop + offset)


def entered_inlet_kernel(plan, lon, ids_ref, own_ref, arrived_ref, *refs):
    state_ref, cot_ref = refs[3], refs[4]
    size = state_ref.shape[0]
    stays = plan.stays(ids_ref[0], ids_ref[1])
    state_ref[...] = jnp.where(stays, own_ref[:size], arrived_ref[:size])
    cot_ref[...] = jnp.where(stays, own_ref[size:], arrived_ref[size:])
    inlet_kernel(lon, state_ref, *refs[:3], *refs[5:])


def inlet_kernel(
    lon, state_ref, static_ref, w_input_ref, w_first_ref,
    inner_ref, pre_ref, sums_ref, patches_ref,
):
    cells = state_ref.shape[1]
    moving = inlet_channels(state_ref[...], lon).T
    width = patches_ref.shape[1]
    blank = jnp.zeros((lon, width), BF16)
    patches_ref[:lon] = blank
    patches_ref[lon + cells :] = blank
    patches_ref[lon : lon + cells, :256] = beside(moving)
    rows = [patches_ref[lon * place : lon * place + cells, :256] for place in range(3)]
    inner = folded(dot(jnp.concatenate(rows, axis=1), w_input_ref[...]), 1) + static_ref[...]
    inner_ref[...] = inner
    fill_patches(patches_ref, inner * sigmoid(inner), lon)
    pre = conv_patches(patches_ref, w_first_ref, lon)
    pre_ref[...] = pre
    sums_ref[...] = sums_of(pre, pre)


def middle_kernel(
    lon, count, pre_one_ref, sums_one_ref, gain_ref, shift_ref, w_second_ref,
    pre_ref, sums_ref, patches_ref,
):
    mean, unused_scale, factor = norm_of(sums_one_ref[...], gain_ref[...], count)
    normed = (pre_one_ref[...] - mean) * factor + shift_ref[...]
    fill_patches(patches_ref, normed * sigmoid(normed), lon)
    pre = conv_patches(patches_ref, w_second_ref, lon)
    pre_ref[...] = pre
    sums_ref[...] = sums_of(pre, pre)


def act_two_of(inner, pre_two, sums, gain, shift, count):
    mean, unused_scale, factor = norm_of(sums, gain, count)
    return inner * sigmoid(inner) + (pre_two - mean) * factor + shift


def project(w_qkv_ref, act_two_halves, head_width, qkv_ref):
    channels = act_two_halves.shape[0] // 2
    rows = folded(dot(w_qkv_ref[...], act_two_halves), 0)
    qkv_ref[:channels] = rows[:channels] * (LOG2_E / math.sqrt(head_width))
    qkv_ref[channels:] = rows[channels:]


def outlet_kernel(
    lon, count, block_size, step_size, quantities,
    state_ref, inner_ref, pre_two_ref, sums_two_ref, gain_ref, shift_ref,
    w_heads_ref, w_mixer_ref, w_velocity_ref, b_velocity_ref,
    out_ref, packed_ref, mixed_ref, top_ref, weight_ref,
    query_ref,
):
    cells, channels = inner_ref.shape
    act_two = act_two_of(
        inner_ref[...], pre_two_ref[...], sums_two_ref[...], gain_ref[...], shift_ref[...], count
    )
    projected = folded(dot(beside(act_two), w_heads_ref[...]), 1)
    query = projected[:, : HEADS * channels]
    query_high = query.astype(BF16).astype(F32)
    channel = lax.rem(lax.broadcasted_iota(jnp.int32, query.shape, 1), channels)
    query_ref[...] = jnp.where(channel < channels // 2, query_high, query - query_high).astype(BF16)
    key = projected[:, HEADS * channels : (HEADS + 1) * channels]
    key_high, key_low = halves((key * (LOG2_E / math.sqrt(channels // HEADS))).T)
    value = projected[:, (HEADS + 1) * channels :]
    heads = heads_of(channels, cells, block_size)

    def scores_of(turn):
        rows, lanes = heads[turn]
        right = [half[rows, lanes] for half in (key_high, key_low, key_high, key_low)]
        start = turn % HEADS * channels
        return dot(query_ref[lanes, start : start + channels], jnp.concatenate(right, axis=0))

    following = scores_of(0)
    for turn, (rows, lanes) in enumerate(heads):
        scores = following
        if turn + 1 < len(heads):
            following = scores_of(turn + 1)
        top = jnp.max(scores, axis=1, keepdims=True)
        powers = jnp.exp2(scores - top)
        weight = 1.0 / jnp.sum(powers, axis=1, keepdims=True)
        high, low = halves(powers)
        right = beside(of_head(value[lanes], rows))
        own = folded(dot(high, right) + dot(low, right), 1) * weight
        all_top, all_weight = [jnp.broadcast_to(part, own.shape) for part in (top, weight)]
        if rows.start:
            own = own + mixed
            all_top, all_weight = of_head(all_top, rows, tops), of_head(all_weight, rows, weights)
        mixed, tops, weights = own, all_top, all_weight
        if rows.stop == channels:
            mixed_ref[lanes], top_ref[lanes], weight_ref[lanes] = mixed, tops, weights
    act_three = act_two + folded(dot(beside(mixed_ref[...]), w_mixer_ref[...]), 1)
    parts = folded(dot(w_velocity_ref[...], stacked(act_three.T)), 0)
    forcing = jnp.zeros((2 * GROUP, cells), F32) + b_velocity_ref[...]
    for column, lon_offset in enumerate((-1, 0, 1)):
        total = None
        for row, lat_offset in enumerate((-1, 0, 1)):
            start = (row * 3 + column) * 2 * GROUP
            part = parts[start : start + 2 * GROUP]
            if lat_offset:
                part = lat_moved(part, lat_offset, lon)
            total = part if total is None else total + part
        forcing = forcing + (lon_moved(total, lon_offset, lon) if lon_offset else total)
    state = state_ref[...]
    flows = state[GROUP:]
    out_ref[:GROUP] = advected(state, step_size, lon)
    out_ref[GROUP:] = flows + step_size * (forcing - flows)
    put_packed(packed_ref, out_ref[...], quantities)


def outlet_back_kernel(
    lon, count, block_size, step_size, quantities, sections, step,
    ids_ref,
    state_ref, d_next_ref, cots_ref, inner_ref, pre_two_ref, sums_two_ref, gain_ref, shift_ref,
    mixed_ref, top_ref, weight_ref,
    w_qkv_ref, w_mixer_ref, w_qkv_back_ref, w_mixer_back_ref, w_velocity_back_ref,
    acc_qkv_ref, acc_mixer_ref, acc_velocity_ref, acc_small_ref,
    d_state_ref, d_two_ref, sums_ref,
    out_qkv_ref, out_mixer_ref, out_velocity_ref, out_small_ref,
    d_mixed_ref, d_qkv_ref, seed_ref, qkv_ref, mixed_rows_ref, top_rows_ref,
):
    channels = inner_ref.shape[1]
    cells = inner_ref.shape[0]
    heads = heads_of(channels, cells, block_size)

    state = state_ref[...]
    packed = cots_ref[lax.rem(ids_ref[0] - step + sections, sections)]
    put_groups(seed_ref, packed[: 3 * quantities])
    seed = seed_ref[...] + d_next_ref[...]
    amount, east, north = state[:GROUP], state[GROUP : 2 * GROUP], state[2 * GROUP :]
    d_amount = seed[:GROUP]
    d_lon = step_size * along_lon(d_amount, lon)
    d_lat = step_size * along_lat(d_amount, lon)
    d_state_ref[:GROUP] = d_amount + d_lon * east + d_lat * north
    d_state_ref[GROUP : 2 * GROUP] = (1.0 - step_size) * seed[GROUP : 2 * GROUP] + d_lon * amount
    d_state_ref[2 * GROUP :] = (1.0 - step_size) * seed[2 * GROUP :] + d_lat * amount
    d_forcing = step_size * seed[GROUP:]
    pieces = []
    for lat_offset in (-1, 0, 1):
        moved_rows = lat_moved(d_forcing, -lat_offset, lon) if lat_offset else d_forcing
        for lon_offset in (-1, 0, 1):
            pieces.append(lon_moved(moved_rows, -lon_offset, lon) if lon_offset else moved_rows)
    d_parts = stacked(jnp.concatenate(pieces, axis=0))
    d_three = folded(dot(w_velocity_back_ref[...], d_parts), 0)
    d_three_halves = stacked(d_three)
    d_mixed_ref[...] = folded(dot(w_mixer_back_ref[...], d_three_halves), 0) * weight_ref[...].T
    mixed_rows_ref[...] = mixed_ref[...].T
    top_rows_ref[...] = top_ref[...].T
    act_two = act_two_of(
        inner_ref[...], pre_two_ref[...], sums_two_ref[...], gain_ref[...], shift_ref[...], count
    ).T
    act_two_halves = stacked(act_two)
    project(w_qkv_ref, act_two_halves, channels // HEADS, qkv_ref)
    d_mixed_cells = d_mixed_ref[...].T
    query_cells = qkv_ref[:channels].T

    def products_of(turn):
        rows, lanes = heads[turn]
        scores = row_products(qkv_ref[below(rows, channels), lanes], qkv_ref[rows, lanes])
        return scores, row_products(qkv_ref[below(rows, 2 * channels), lanes], d_mixed_ref[rows, lanes])

    following = products_of(0)
    for turn, (rows, lanes) in enumerate(heads):
        scores, d_powers = following
        if turn + 1 < len(heads):
            following = products_of(turn + 1)
        inner_sum = jnp.sum(d_mixed_ref[rows, lanes] * mixed_rows_ref[rows, lanes], axis=0, keepdims=True)
        powers = jnp.exp2(scores - top_rows_ref[rows.start : rows.start + 1, lanes])
        power_high, power_low = halves(powers)
        d_high, d_low = halves(powers * (d_powers - inner_sum))
        right = beside(of_head(d_mixed_cells[lanes], rows))
        d_value = dot(power_high, right) + dot(power_low, right) + (d_value if rows.start else 0.0)
        right = beside(of_head(query_cells[lanes], rows))
        d_key = dot(d_high, right) + dot(d_low, right) + (d_key if rows.start else 0.0)
        key_halves = stacked(qkv_ref[below(rows, channels), lanes])
        d_query = folded(dot(key_halves, d_high) + dot(key_halves, d_low), 0)
        d_qkv_ref[rows, lanes] = d_query * (1.0 / math.sqrt(channels // HEADS))
        if rows.stop == channels:
            d_qkv_ref[channels : 2 * channels, lanes] = folded(d_key, 1).T * (1.0 / LOG2_E)
            d_qkv_ref[2 * channels :, lanes] = folded(d_value, 1).T
    d_qkv_halves = stacked(d_qkv_ref[...])
    d_two = (d_three + folded(dot(w_qkv_back_ref[...], d_qkv_halves), 0)).T
    d_two_ref[...] = d_two
    mean, scale, unused_factor = norm_of(sums_two_ref[...], gain_ref[...], count)
    sums = sums_of(d_two, pre_two_ref[...] - mean)
    sums_ref[...] = sums

    def pairs(left, right):
        return folded(folded(dot(left, right, 1, 1), 0), 1)

    mixed_halves = stacked(mixed_rows_ref[...])
    act_three = act_two + folded(dot(w_mixer_ref[...], mixed_halves), 0)
    out_velocity_ref[...] = acc_velocity_ref[...] + pairs(d_parts, stacked(act_three))
    out_mixer_ref[...] = acc_mixer_ref[...] + pairs(mixed_halves, d_three_halves)
    out_qkv_ref[...] = acc_qkv_ref[...] + pairs(act_two_halves, d_qkv_halves)
    bias = jnp.sum(d_forcing, axis=1, keepdims=True)
    row = lax.broadcasted_iota(jnp.int32, (GROUP, channels), 0)
    small = jnp.where(row == 0, sums[1:2] * scale, jnp.where(row == 1, sums[0:1], 0.0))
    out_small_ref[:GROUP] = acc_small_ref[:GROUP] + small
    out_small_ref[GROUP:] = acc_small_ref[GROUP:] + bias


def d_pre_of(d_normed, centred, sums, all_grad_sums, gain, count):
    unused_mean, scale, factor = norm_of(sums, gain, count)
    d_spread = -0.5 * gain * scale * scale * scale * all_grad_sums[1:2]
    return factor * (d_normed - all_grad_sums[0:1] / count) + (2.0 * d_spread / count) * centred


def weight_pairs(acc_ref, out_ref, left_halves, patches_ref, lon):
    cells = patches_ref.shape[0] - 2 * lon
    width = patches_ref.shape[1] // 3
    for tap in range(9):
        row, column = divmod(8 - tap, 3)
        right = patches_ref[lon * row : lon * row + cells, column * width : (column + 1) * width]
        out_ref[tap] = acc_ref[tap] + folded(folded(dot(left_halves, right), 0), 1)


def middle_back_kernel(
    lon, count,
    d_two_ref, pre_two_ref, sums_two_ref, all_two_ref, gain_two_ref,
    pre_one_ref, sums_one_ref, gain_ref, shift_ref, w_second_back_ref,
    acc_weight_ref, acc_small_ref,
    d_normed_ref, sums_ref, out_weight_ref, out_small_ref,
    patches_ref,
):
    sums_two = sums_two_ref[...]
    d_pre = d_pre_of(
        d_two_ref[...], pre_two_ref[...] - sums_two[0:1] / count, sums_two, all_two_ref[...],
        gain_two_ref[...], count,
    )
    fill_patches(patches_ref, d_pre, lon)
    d_act = conv_patches(patches_ref, w_second_back_ref, lon)
    mean, scale, factor = norm_of(sums_one_ref[...], gain_ref[...], count)
    centred = pre_one_ref[...] - mean
    normed = centred * factor + shift_ref[...]
    gate = sigmoid(normed)
    d_normed = d_act * gate * (1.0 + normed * (1.0 - gate))
    d_normed_ref[...] = d_normed
    sums = sums_of(d_normed, centred)
    sums_ref[...] = sums
    weight_pairs(acc_weight_ref, out_weight_ref, stacked((normed * gate).T), patches_ref, lon)
    row = lax.broadcasted_iota(jnp.int32, sums.shape, 0)
    small = jnp.where(row == 0, sums[1:2] * scale, jnp.where(row == 1, sums[0:1], 0.0))
    out_small_ref[...] = acc_small_ref[...] + small


def inlet_back_kernel(
    lon, count, quantities,
    state_ref, d_normed_ref, pre_one_ref, sums_one_ref, all_one_ref, gain_ref,
    inner_ref, d_two_ref, d_state_in_ref, w_first_back_ref, w_input_back_ref,
    acc_first_ref, acc_input_ref, acc_inner_ref,
    d_state_ref, packed_ref, out_first_ref, out_input_ref, out_inner_ref,
    patches_ref,
):
    cells = inner_ref.shape[0]
    sums_one = sums_one_ref[...]
    d_pre = d_pre_of(
        d_normed_ref[...], pre_one_ref[...] - sums_one[0:1] / count, sums_one, all_one_ref[...],
        gain_ref[...], count,
    )
    fill_patches(patches_ref, d_pre, lon)
    d_act = conv_patches(patches_ref, w_first_back_ref, lon) + d_two_ref[...]
    inner = inner_ref[...]
    gate = sigmoid(inner)
    d_inner = d_act * gate * (1.0 + inner * (1.0 - gate))
    weight_pairs(acc_first_ref, out_first_ref, stacked((inner * gate).T), patches_ref, lon)
    out_inner_ref[...] = acc_inner_ref[...] + d_inner
    patches_ref[lon : lon + cells, :256] = beside(d_inner)
    rows = [patches_ref[lon * place : lon * place + cells, :256] for place in range(3)]
    d_moving = folded(dot(jnp.concatenate(rows, axis=1), w_input_back_ref[...]), 1).T
    state = state_ref[...]
    moving_halves = stacked(inlet_channels(state, lon))
    for place in range(3):
        out_input_ref[place] = acc_input_ref[place] + folded(
            folded(dot(moving_halves, rows[2 - place]), 0), 1
        )
    size = 5 * GROUP
    d_groups = (
        lon_moved(d_moving[:size], 1, lon)
        + d_moving[size : 2 * size]
        + lon_moved(d_moving[2 * size : 3 * size], -1, lon)
    )
    d_state = d_state_in_ref[...] + d_groups[: 3 * GROUP]
    d_state_ref[:GROUP] = (
        d_state[:GROUP]
        - along_lon(d_groups[3 * GROUP : 4 * GROUP], lon)
        - along_lat(d_groups[4 * GROUP :], lon)
    )
    d_state_ref[GROUP:] = d_state[GROUP:]
    put_packed(packed_ref, d_state_ref[...], quantities)


def put_groups(out_ref, rows):
    size = rows.shape[0] // 3
    out_ref[...] = jnp.zeros(out_ref.shape, F32)
    for group in range(3):
        out_ref[group * GROUP : group * GROUP + size] = rows[group * size : (group + 1) * size]


def put_packed(out_ref, grouped, size):
    out_ref[...] = jnp.zeros(out_ref.shape, F32)
    for group in range(3):
        out_ref[group * size : (group + 1) * size] = grouped[group * GROUP : group * GROUP + size]


def fetched(far_refs, near_refs, done_ref):
    copies = [
        pltpu.make_async_copy(far_ref, near_ref, done_ref.at[place])
        for place, (far_ref, near_ref) in enumerate(zip(far_refs, near_refs))
    ]
    for copy in copies:
        copy.start()
    return copies


def enter_kernel(plan, ids_ref, order_ref, state_ref, cot_ref, *refs):
    out_refs, (near_ref, near_cot_ref, rows_ref, done_ref) = refs[:-4], refs[-4:]
    copies = fetched([state_ref, cot_ref], [near_ref, near_cot_ref], done_ref)
    size = rows_ref.shape[0]
    copies[0].wait()
    place = order_ref[0, plan.slot(ids_ref[0], ids_ref[1])]
    for row in range(size):
        rows_ref[row : row + 1] = near_ref[row, pl.ds(place, 1)]
    put_groups(out_refs[0].at[: 3 * GROUP], rows_ref[...])
    copies[1].wait()
    for steps, out_ref in enumerate(out_refs):
        start = 0 if steps else 3 * GROUP
        target = lax.rem(ids_ref[0] + steps, plan.sections)
        place = order_ref[0, plan.slot(target, ids_ref[1])]
        out_ref[start:] = jnp.zeros((2 * GROUP, out_ref.shape[1]), F32)
        for row in range(size):
            out_ref[start + row : start + row + 1] = near_cot_ref[row, pl.ds(place, 1)]


def leave_kernel(plan, ids_ref, *refs):
    values_ref = refs[-1]
    size = refs[0].shape[0]
    for step in range(plan.sections):
        values_ref[step, :size] = refs[step][...]
        if step:
            values_ref[step, size:] = refs[plan.sections + step - 1][...]
        else:
            values_ref[step, size:] = jnp.zeros(refs[0].shape, F32)
    for steps, out_ref in enumerate(refs[2 * plan.sections - 1 : -1]):
        out_ref[...] = values_ref[lax.rem(ids_ref[0] + steps, plan.sections)]


def arrive_kernel(plan, start, ids_ref, order_ref, kept_ref, *refs):
    section, dp = ids_ref[0], ids_ref[1]
    out_ref = refs[-1]
    size = kept_ref.shape[0] // 2
    early, late = refs[: plan.sections], refs[plan.sections : -1]
    if late:
        kept_late_ref, *late = late
    for steps, ref in enumerate(early):
        source = lax.rem(section - steps + plan.sections, plan.sections)
        place = order_ref[0, plan.slot(source, dp)]
        value = ref[start : start + size]
        if late:
            value = jnp.where(section == 0, late[steps][...], value)
        if plan.halved and not steps:
            kept = kept_ref[start : start + size]
            if late:
                kept = jnp.where(section == 0, kept_late_ref[...], kept)
            value = jnp.where(plan.stays(section, dp), kept, value)
        for row in range(out_ref.shape[0]):
            out_ref[row, pl.ds(place, 1)] = value[row : row + 1]


def put_conv_weight(out_ref, taps):
    for tap, weight in enumerate(taps):
        wide = beside(weight)
        rows = weight.shape[0]
        out_ref[2 * tap * rows : (2 * tap + 1) * rows] = wide
        out_ref[(2 * tap + 1) * rows : (2 * tap + 2) * rows] = wide


def put_left_weight(out_ref, weight):
    rows = weight.shape[0]
    for place, half in enumerate(halves(weight)):
        out_ref[place * rows : (place + 1) * rows] = jnp.concatenate([half, half], axis=1)


def weights_kernel(
    lon, quantities,
    w_input_ref, maps_ref, b_input_ref, w_first_ref, w_second_ref,
    w_query_ref, w_key_ref, w_value_ref, w_mixer_ref, w_velocity_ref,
    static_part_ref, moving_cat_ref, moving_back_ref, first_cat_ref, second_cat_ref,
    heads_ref, mixer_cells_ref, qkv_ref, qkv_back_ref, mixer_ref, mixer_back_ref, velocity_ref, velocity_back_ref,
    first_back_ref, second_back_ref,
    patches_ref, weight_ref, taps_ref, rows_ref, *near_refs,
):
    near_refs, done_ref = near_refs[:-1], near_refs[-1]
    copies = fetched(
        [w_input_ref, maps_ref, b_input_ref, w_first_ref, w_second_ref,
         w_query_ref, w_key_ref, w_value_ref, w_mixer_ref, w_velocity_ref],
        near_refs, done_ref,
    )
    (
        w_input_ref, maps_ref, b_input_ref, w_first_ref, w_second_ref,
        w_query_ref, w_key_ref, w_value_ref, w_mixer_ref, w_velocity_ref,
    ) = near_refs
    channels = w_input_ref.shape[2]
    moving = 5 * quantities
    statics = maps_ref.shape[0]
    taps_ref[...] = jnp.zeros(taps_ref.shape, F32)
    rows_ref[...] = jnp.zeros(rows_ref.shape, F32)
    copies[0].wait()
    for tap in range(9):
        row, column = divmod(tap, 3)
        for group in range(5):
            start = (column * 5 + group) * GROUP
            taps_ref[9 + row, start : start + quantities] = w_input_ref[
                tap, group * quantities : (group + 1) * quantities
            ]
        taps_ref[tap, :statics] = w_input_ref[tap, moving:]
    put_conv_weight(moving_cat_ref, [taps_ref[9 + row] for row in range(3)])
    put_conv_weight(moving_back_ref, [taps_ref[11 - row].T for row in range(3)])
    put_conv_weight(weight_ref, [taps_ref[tap] for tap in range(9)])
    copies[1].wait()
    copies[2].wait()
    maps = jnp.concatenate(
        [maps_ref[...], jnp.zeros((channels - statics, maps_ref.shape[1]), F32)], axis=0
    )
    fill_patches(patches_ref, maps.T, lon)
    static_part_ref[...] = conv_patches(patches_ref, weight_ref, lon) + b_input_ref[...]
    for copy in copies[3:]:
        copy.wait()
    put_conv_weight(first_cat_ref, [w_first_ref[tap] for tap in range(9)])
    put_conv_weight(second_cat_ref, [w_second_ref[tap] for tap in range(9)])
    put_conv_weight(first_back_ref, [w_first_ref[8 - tap].T for tap in range(9)])
    put_conv_weight(second_back_ref, [w_second_ref[8 - tap].T for tap in range(9)])
    parts = [ref[...] for ref in (w_query_ref, w_key_ref, w_value_ref)]
    turned = [part.T for part in parts]
    width = channels // HEADS
    repeated = [turned[0][head * width : (head + 1) * width] for head in range(HEADS) for unused in range(HEADS)]
    put_conv_weight(heads_ref, [jnp.concatenate([jnp.concatenate(repeated, axis=0).T, parts[1], parts[2]], axis=1)])
    put_conv_weight(mixer_cells_ref, [w_mixer_ref[...]])
    put_left_weight(qkv_ref, jnp.concatenate(turned, axis=0))
    put_left_weight(qkv_back_ref, jnp.concatenate(parts, axis=1))
    put_left_weight(mixer_ref, w_mixer_ref[...].T)
    put_left_weight(mixer_back_ref, w_mixer_ref[...])
    for tap in range(9):
        for group in range(2):
            start = (tap * 2 + group) * GROUP
            rows_ref[start : start + quantities] = w_velocity_ref[
                tap, group * quantities : (group + 1) * quantities
            ]
    size = 18 * GROUP
    put_left_weight(velocity_ref, rows_ref[:size])
    put_left_weight(velocity_back_ref, rows_ref[...].T[:, :size])


def index_of(ids_ref, plan, bits):
    own = ids_ref[0] * plan.dp + ids_ref[1]
    return sum(lax.rem(own // bit, 2) << place for place, bit in enumerate(bits))


def deal(total_ref, own, out_refs):
    rows = out_refs[0].shape[0]
    for turn, out_ref in enumerate(out_refs):
        out_ref[...] = total_ref[pl.ds(pl.multiple_of((own ^ turn) * rows, GROUP), rows)]


def pack_kernel(
    plan, bits, lon, statics, ids_ref, maps_ref, inner_ref, first_ref, second_ref, moving_ref,
    qkv_ref, mixer_ref, velocity_ref, small_one_ref, small_two_ref, *refs,
):
    out_refs, total_ref, patches_ref = refs[:-2], refs[-2], refs[-1]
    cells, channels = inner_ref.shape
    d_inner = inner_ref[...]
    fill_patches(patches_ref, d_inner, lon)
    width = patches_ref.shape[1] // 3
    maps = maps_ref[...]
    blank = jnp.zeros((-statics % GROUP, cells), F32)
    maps = jnp.concatenate([maps, blank], axis=0)
    rows = maps.shape[0]
    left = jnp.concatenate(halves(maps), axis=0)
    start = 0

    def put(value):
        nonlocal start
        total_ref[start : start + value.shape[0]] = value
        start += value.shape[0]

    for tap in range(9):
        put(first_ref[tap])
    for tap in range(9):
        put(second_ref[tap])
    for tap in range(9):
        row, column = divmod(8 - tap, 3)
        right = patches_ref[lon * row : lon * row + cells, column * width : (column + 1) * width]
        put(folded(folded(dot(left, right), 0), 1))
    for place in range(3):
        put(moving_ref[place, : 15 * GROUP])
    for part in range(3):
        put(qkv_ref[:, part * channels : (part + 1) * channels])
    put(mixer_ref[...])
    put(velocity_ref[...])
    put(small_one_ref[...])
    put(small_two_ref[...])
    put(jnp.zeros((GROUP, channels), F32) + jnp.sum(d_inner, axis=0, keepdims=True))
    total_ref[start:] = jnp.zeros((total_ref.shape[0] - start, channels), F32)
    deal(total_ref, index_of(ids_ref, plan, bits), out_refs)


def reduce_kernel(plan, bits, count, ids_ref, *refs):
    total_ref = refs[-1]
    total = refs[0][...]
    for ref in refs[1:count]:
        total = total + ref[...]
    if not bits:
        refs[count][...] = total
        return
    total_ref[...] = total
    deal(total_ref, index_of(ids_ref, plan, bits), refs[count:-1])


def gather_rows(plan, bits, ids_ref, part_refs, out_ref):
    own = index_of(ids_ref, plan, bits)
    rows = part_refs[0].shape[0]
    for turn, ref in enumerate(part_refs):
        out_ref[pl.ds(pl.multiple_of((own ^ turn) * rows, GROUP), rows)] = ref[...]


def gather_kernel(plan, bits, ids_ref, *refs):
    gather_rows(plan, bits, ids_ref, refs[:-1], refs[-1])


def unpack_kernel(
    plan, bits, quantities, statics, ids_ref, *refs,
):
    count = 1 << len(bits)
    (
        input_ref, bias_ref, first_ref, gain_one_ref, shift_one_ref, second_ref, gain_two_ref, shift_two_ref,
        query_ref, key_ref, value_ref, mixer_ref, velocity_ref, velocity_bias_ref, total_ref,
    ) = refs[count:]
    gather_rows(plan, bits, ids_ref, refs[:count], total_ref)
    channels = mixer_ref.shape[0]
    moving = 5 * quantities
    start = 0

    def take(rows):
        nonlocal start
        start += rows
        return total_ref[start - rows : start]

    for tap in range(9):
        first_ref[tap] = take(channels)
    for tap in range(9):
        second_ref[tap] = take(channels)
    for tap in range(9):
        input_ref[tap, moving:] = take(statics + -statics % GROUP)[:statics]
    for row in range(3):
        for column in range(3):
            for group in range(5):
                rows = take(GROUP)
                input_ref[row * 3 + column, group * quantities : (group + 1) * quantities] = rows[:quantities]
    query_ref[...] = take(channels)
    key_ref[...] = take(channels)
    value_ref[...] = take(channels)
    mixer_ref[...] = take(channels)
    for tap in range(9):
        for group in range(2):
            velocity_ref[tap, group * quantities : (group + 1) * quantities] = take(GROUP)[:quantities]
    small = take(GROUP)
    gain_one_ref[...], shift_one_ref[...] = small[0:1], small[1:2]
    small = take(GROUP)
    gain_two_ref[...], shift_two_ref[...] = small[0:1], small[1:2]
    velocity_bias_ref[...] = take(2 * GROUP)
    bias_ref[...] = take(GROUP)[0:1]


def call(kernel, outs, scratch=(), aliases=None, name=None, scalars=0, kinds=None, far_in=(), limit=None):
    kinds = kinds or [F32] * len(outs)

    def run(*operands):
        places = [pltpu.SMEM] * scalars + [pltpu.VMEM] * (len(operands) - scalars)
        for place in far_in:
            places[place] = pltpu.HBM
        return pl.pallas_call(
            kernel,
            out_shape=tuple(jax.ShapeDtypeStruct(shape, kind) for shape, kind in zip(outs, kinds)),
            in_specs=[pl.BlockSpec(memory_space=place) for place in places],
            out_specs=tuple(pl.BlockSpec(memory_space=pltpu.VMEM) for unused in outs),
            scratch_shapes=scratch,
            input_output_aliases=aliases or {},
            compiler_params=pltpu.CompilerParams(vmem_limit_bytes=limit or VMEM_LIMIT),
            name=name,
        )(*operands)

    return run


VMEM_LIMIT = 24 * 1024 * 1024
ALONE_LIMIT = 46 * 1024 * 1024


def in_groups(array, axis, groups):
    shape = array.shape
    split = shape[:axis] + (groups, shape[axis] // groups) + shape[axis + 1 :]
    array = array.reshape(split)
    pads = [(0, 0)] * array.ndim
    pads[axis + 1] = (0, GROUP - split[axis + 1])
    return jnp.pad(array, pads).reshape(shape[:axis] + (groups * GROUP,) + shape[axis + 1 :])


def from_groups(array, axis, groups, size):
    shape = array.shape
    array = array.reshape(shape[:axis] + (groups, GROUP) + shape[axis + 1 :])
    array = lax.slice_in_dim(array, 0, size, axis=axis + 1)
    return array.reshape(shape[:axis] + (groups * size,) + shape[axis + 1 :])


class Plan:
    def __init__(self, sections, dp):
        self.sections, self.dp = sections, dp
        self.halved = sections == 4 and dp >= 4
        self.half = dp // 2
        bits = [1 << place for place in range((sections * dp).bit_length() - 1)]
        dp_bits = [bit for bit in bits if bit < dp]
        section_bits = [bit for bit in bits if bit >= dp]
        if self.halved:
            self.sum_rounds = in_pairs(dp_bits[:-1]) + in_pairs(section_bits)
        else:
            self.sum_rounds = in_pairs(dp_bits) + [section_bits[:1]]
        self.all_rounds = [dp_bits[:1]] + in_pairs(section_bits) + in_pairs(dp_bits[1:])

    def slot(self, section, home):
        if not self.halved:
            return section
        return lax.rem(home // self.half + section // 2 + home, 2) * 2 + lax.rem(section, 2)

    def stays(self, section, dp):
        return lax.rem(section // 2 + dp, 2) == 0

    def other(self, section, dp):
        return dp ^ self.half if self.halved and (section // 2 + dp) % 2 else dp

    def to_workers(self, steps):
        return [
            (section * self.dp + home, self.joint((section + steps) % self.sections, home))
            for section in range(self.sections)
            for home in range(self.dp)
        ]

    def to_homes(self, steps):
        return [
            (section * self.dp + own, (section + steps) % self.sections * self.dp + self.other(section, own))
            for section in range(self.sections)
            for own in range(self.dp)
        ]

    def to_first_home(self, steps):
        return [(source, target) for source, target in self.to_homes(steps) if target < self.dp]

    def joint(self, section, home):
        return section * self.dp + self.other(section, home)


def in_pairs(bits):
    return [bits[start : start + 2] for start in range(0, len(bits), 2)]


def masks_of(bits):
    return [sum(bit for place, bit in enumerate(bits) if turn >> place & 1) for turn in range(1, 1 << len(bits))]


def exchanged(value, mask):
    size = lax.axis_size("section") * lax.axis_size("dp")
    return lax.ppermute(value, ("section", "dp"), [(own, own ^ mask) for own in range(size)])


def moved(value, pairs):
    going = [(source, target) for source, target in pairs if source != target]
    if not going:
        return value
    return lax.ppermute(value, ("section", "dp"), going)


def micro_sum(plan, value, first_core):
    if not plan.halved or plan.half != 4:
        for bits in plan.sum_rounds:
            value = value + sum(exchanged(value, mask) for mask in masks_of(bits))
        return value
    value = value + exchanged(value, 1)
    plane = masks_of([plan.dp, 2 * plan.dp])
    other = [mask ^ 2 for mask in plane + [0]]
    own = range(plan.sections * plan.dp)
    total = value * first_core
    for turn in range(4):
        pairs = [(device, device ^ other[turn]) for device in own if device & 1]
        if turn < 3:
            pairs += [(device, device ^ plane[turn]) for device in own if not device & 1]
        total = total + lax.ppermute(value, ("section", "dp"), pairs)
    return total + exchanged(total, 1)


def on_device(
    state_start,
    static_maps,
    grouping,
    cotangent,
    w_input,
    b_input,
    w_first,
    gain_first,
    shift_first,
    w_second,
    gain_second,
    shift_second,
    w_query,
    w_key,
    w_value,
    w_mixer,
    w_velocity,
    b_velocity,
):
    segments = lax.axis_size("section")
    plan = Plan(segments, lax.axis_size("dp"))
    micro_count = segments // 2
    per_micro = state_start.shape[0] // micro_count
    cells = state_start.shape[2]
    lon = cells // LAT
    count = float(per_micro * cells * plan.dp)
    step_size = 2.0 / segments
    block_size = ATT_ROWS * lon
    channels = w_first.shape[2]
    quantities = state_start.shape[1] // 3
    statics = static_maps.shape[0]
    ids = jnp.stack([lax.axis_index("section"), lax.axis_index("dp")]).astype(jnp.int32)

    plane = (cells, channels)
    small = (GROUP, channels)
    conv = (9 * 2 * channels, 2 * channels)
    patches = pltpu.VMEM((cells + 2 * lon, 6 * channels), BF16)
    wide = pltpu.VMEM((3 * channels, cells), F32)
    narrow = pltpu.VMEM((channels, cells), F32)
    state_shape = (3 * GROUP, cells)

    packed = (2 * GROUP, cells)

    def near(*arrays):
        return [pltpu.VMEM(array.shape, F32) for array in arrays] + [pltpu.SemaphoreType.DMA((len(arrays),))]

    state_rows, cot_rows = jnp.swapaxes(state_start, 0, 1), jnp.swapaxes(cotangent[0], 0, 1)
    entry, *sent_cots = call(
        functools.partial(enter_kernel, plan), [(5 * GROUP, cells)] + [packed] * (segments - 1),
        [pltpu.VMEM(state_rows.shape, F32)] * 2
        + [pltpu.VMEM((3 * quantities, cells), F32), pltpu.SemaphoreType.DMA((2,))],
        name="enter", scalars=2, far_in=[2, 3], limit=ALONE_LIMIT,
    )(ids, grouping, state_rows, cot_rows)
    arrived = moved(entry, plan.to_workers(0))
    first_core = (1.0 - lax.rem(ids[1], 2).astype(F32)) * jnp.ones(small, F32)
    w_velocity_rows = jnp.swapaxes(w_velocity, 1, 2)
    weights = (
        w_input, static_maps, b_input[None], w_first, w_second, w_query, w_key, w_value, w_mixer, w_velocity_rows
    )
    moving_conv, square_conv = (6 * channels, 2 * channels), (2 * channels, 2 * channels)
    (
        static_part, moving_cat, moving_back_cat, first_cat, second_cat,
        heads_cat, mixer_cells, qkv_cat, qkv_back_cat, mixer_cat, mixer_back_cat, out_cat, out_back_cat,
        first_back_cat, second_back_cat,
    ) = call(
        functools.partial(weights_kernel, lon, quantities),
        [plane, moving_conv, moving_conv, conv, conv,
         (2 * channels, 2 * (HEADS + 2) * channels), square_conv, moving_conv, moving_conv[::-1],
         square_conv, square_conv, (36 * GROUP, 2 * channels), (2 * channels, 36 * GROUP), conv, conv],
        [patches, pltpu.VMEM(conv, BF16), pltpu.VMEM((12, channels, channels), F32),
         pltpu.VMEM((2 * channels, channels), F32)] + near(*weights),
        name="weights", kinds=[F32] + [BF16] * 14, far_in=range(10), limit=ALONE_LIMIT,
    )(*weights)
    b_out = in_groups(b_velocity[:, None], 0, 2)
    gain_one, shift_one = gain_first[None], shift_first[None]
    gain_two, shift_two = gain_second[None], shift_second[None]

    inlet = call(
        functools.partial(inlet_kernel, lon), [plane, plane, small], [patches], name="inlet"
    )
    middle = call(
        functools.partial(middle_kernel, lon, count), [plane, small], [patches], name="middle"
    )
    outlet = call(
        functools.partial(outlet_kernel, lon, count, block_size, step_size, quantities),
        [state_shape, packed, plane, plane, plane],
        [pltpu.VMEM((cells, HEADS * channels), BF16)], name="outlet",
    )

    def outlet_back(step):
        return call(
            functools.partial(outlet_back_kernel, lon, count, block_size, step_size, quantities, segments, step),
            [state_shape, plane, small, (channels, 3 * channels), (channels, channels),
             (18 * GROUP, channels), (3 * GROUP, channels)],
            [narrow, wide, pltpu.VMEM(state_shape, F32), wide, narrow, narrow],
            {17: 3, 18: 4, 19: 5, 20: 6}, name="outlet_back", scalars=1,
        )

    middle_back = call(
        functools.partial(middle_back_kernel, lon, count),
        [plane, small, (9, channels, channels), small], [patches],
        {10: 2, 11: 3}, name="middle_back",
    )
    inlet_back = call(
        functools.partial(inlet_back_kernel, lon, count, quantities),
        [state_shape, packed, (9, channels, channels), (3, channels, channels), plane], [patches],
        {11: 2, 12: 3, 13: 4}, name="inlet_back",
    )

    state = entry[: 3 * GROUP]
    path, saved = [], []
    cots = None
    for step in range(segments):
        if not step:
            if not plan.halved:
                arrived = entry
            state, own_cot, inner, pre_one, sums_one = call(
                functools.partial(entered_inlet_kernel, plan, lon), [state_shape, packed, plane, plane, small], [patches],
                name="inlet", scalars=1,
            )(ids, entry, arrived, static_part, moving_cat, first_cat)
        else:
            inner, pre_one, sums_one = inlet(state, static_part, moving_cat, first_cat)
        sums_one = micro_sum(plan, sums_one, first_core)
        pre_two, sums_two = middle(pre_one, sums_one, gain_one, shift_one, second_cat)
        sums_two = micro_sum(plan, sums_two, first_core)
        state_out, state_packed, mixed, top, weight = outlet(
            state, inner, pre_two, sums_two, gain_two, shift_two, heads_cat, mixer_cells, out_cat, b_out
        )
        saved.append((state, inner, pre_one, pre_two, sums_one, sums_two, mixed, top, weight))
        path.append(state_packed)
        state = state_out
        if not step:
            state, sent_cots = lax.optimization_barrier((state, sent_cots))
            cots = jnp.stack(
                [own_cot] + [moved(cot, plan.to_workers(steps + 1)) for steps, cot in enumerate(sent_cots)]
            )

    def put_home(start, parts):
        (out,) = call(
            functools.partial(arrive_kernel, plan, start), [state_rows.shape], name="arrive", scalars=2
        )(ids, grouping, *parts)
        return jnp.swapaxes(out, 0, 1)[None]

    acc = dict(
        qkv=jnp.zeros((channels, 3 * channels), F32),
        mixer=jnp.zeros((channels, channels), F32),
        velocity=jnp.zeros((18 * GROUP, channels), F32),
        small_two=jnp.zeros((3 * GROUP, channels), F32),
        second=jnp.zeros((9, channels, channels), F32),
        small_one=jnp.zeros(small, F32),
        first=jnp.zeros((9, channels, channels), F32),
        moving=jnp.zeros((3, channels, channels), F32),
        inner=jnp.zeros(plane, F32),
    )
    d_state = jnp.zeros(state_shape, F32)
    grads = [None] * segments
    path_out = None
    for step in reversed(range(segments)):
        if not step:
            sent = call(
                functools.partial(leave_kernel, plan), [(4 * GROUP, cells)] * segments,
                [pltpu.VMEM((segments, 4 * GROUP, cells), F32)], name="leave", scalars=1,
            )(ids, *path, *grads[1:])
            early = [sent[0]] + [moved(part, plan.to_homes(steps)) for steps, part in enumerate(sent)]
        state, inner, pre_one, pre_two, sums_one, sums_two, mixed, top, weight = saved[step]
        d_partial, d_two, grad_two, acc["qkv"], acc["mixer"], acc["velocity"], acc["small_two"] = outlet_back(step)(
            ids, state, d_state, cots, inner, pre_two, sums_two, gain_two, shift_two,
            mixed, top, weight,
            qkv_cat, mixer_cat, qkv_back_cat, mixer_back_cat, out_back_cat,
            acc["qkv"], acc["mixer"], acc["velocity"], acc["small_two"],
        )
        if not step:
            d_two, grad_two, early = lax.optimization_barrier((d_two, grad_two, early))
            path_out = put_home(0, early)
        grad_two = micro_sum(plan, grad_two, first_core)
        d_normed, grad_one, acc["second"], acc["small_one"] = middle_back(
            d_two, pre_two, sums_two, grad_two, gain_two,
            pre_one, sums_one, gain_one, shift_one, second_back_cat,
            acc["second"], acc["small_one"],
        )
        grad_one = micro_sum(plan, grad_one, first_core)
        d_state, grads[step], acc["first"], acc["moving"], acc["inner"] = inlet_back(
            state, d_normed, pre_one, sums_one, grad_one, gain_one,
            inner, d_two, d_partial, first_back_cat, moving_back_cat,
            acc["first"], acc["moving"], acc["inner"],
        )
    late = [grads[0]] + [moved(grads[0], plan.to_first_home(steps)) for steps in range(segments)]

    rounds = plan.all_rounds
    rows = 2 * 9 * channels + 9 * (statics + -statics % GROUP) + 45 * GROUP + 4 * channels + 23 * GROUP
    unit = GROUP * segments * plan.dp
    rows = -(-rows // unit) * unit

    def shares(rows, bits):
        return [(rows >> len(bits), channels)] * (1 << len(bits))

    def swap(parts, bits):
        return [parts[0]] + [exchanged(part, mask) for part, mask in zip(parts[1:], masks_of(bits))]

    parts = call(
        functools.partial(pack_kernel, plan, rounds[0], lon, statics), shares(rows, rounds[0]),
        [pltpu.VMEM((rows, channels), F32), patches], name="pack", scalars=1,
    )(
        ids, static_maps, acc["inner"], acc["first"], acc["second"], acc["moving"], acc["qkv"], acc["mixer"],
        acc["velocity"], acc["small_one"], acc["small_two"],
    )
    for place, (bits, later) in enumerate(zip(rounds, rounds[1:] + [[]])):
        parts = swap(parts, bits)
        if place == 1:
            parts, late = lax.optimization_barrier((parts, late))
            grads_out = put_home(2 * GROUP, early + late)
            parts, path_out, grads_out = lax.optimization_barrier((parts, path_out, grads_out))
        rows >>= len(bits)
        parts = call(
            functools.partial(reduce_kernel, plan, later, len(parts)), shares(rows, later),
            [pltpu.VMEM((rows, channels), F32)], name="reduce_part", scalars=1,
        )(ids, *parts)
    for bits in rounds[::-1]:
        parts = swap([parts[0]] * (1 << len(bits)), bits)
        rows <<= len(bits)
        if bits is rounds[0]:
            break
        parts = call(
            functools.partial(gather_kernel, plan, bits), [(rows, channels)], name="gather_part", scalars=1
        )(ids, *parts)
    row = (1, channels)
    square = (channels, channels)
    grads_all = call(
        functools.partial(unpack_kernel, plan, rounds[0], quantities, statics),
        [w_input.shape, row, w_first.shape, row, row, w_second.shape, row, row, square, square, square, square,
         (9, 2 * quantities, channels), (2 * GROUP, channels)],
        [pltpu.VMEM((rows, channels), F32)], name="unpack", scalars=1,
    )(ids, *parts)
    grads_all = [grad[0] if grad.shape == row else grad for grad in grads_all]
    grads_all[-2] = jnp.swapaxes(grads_all[-2], 1, 2)
    grads_all[-1] = from_groups(grads_all[-1][:, :1], 0, 2, quantities)[:, 0]
    return (path_out, grads_out) + tuple(grads_all)


def solution(mesh):
    weights = (P(),) * 14
    return jax.shard_map(
        on_device,
        mesh=mesh,
        in_specs=(P("dp", None, None), P(), P("dp", None), P("section", "dp", None, None)) + weights,
        out_specs=(P("section", "dp", None, None), P("section", "dp", None, None)) + weights,
        check_vma=False,
    )
```

```python
import functools
import math

import jax
import jax.numpy as jnp
from jax import lax
from jax.experimental import pallas as pl
from jax.experimental.pallas import tpu as pltpu
from jax.sharding import PartitionSpec as P

HEADS = 4
LAT = 16
ATT_ROWS = 8
EPSILON = 1e-05
LOG2_E = 1.0 / math.log(2.0)
F32 = jnp.float32
BF16 = jnp.bfloat16
GROUP = 8


def dot(left, right, left_dim=1, right_dim=0):
    return lax.dot_general(
        left, right, (((left_dim,), (right_dim,)), ((), ())), preferred_element_type=F32
    )


def halves(value):
    high = value.astype(BF16)
    return high, (value - high.astype(F32)).astype(BF16)


def stacked(value):
    return jnp.concatenate(halves(value), axis=0)


def beside(value):
    return jnp.concatenate(halves(value), axis=1)


def folded(value, axis):
    size = value.shape[axis] // 2
    if axis == 0:
        return value[:size] + value[size:]
    return value[:, :size] + value[:, size:]


def cells_of(value):
    return lax.broadcasted_iota(jnp.int32, value.shape, value.ndim - 1)


def lon_moved(value, offset, lon):
    cells = value.shape[1]
    column = lax.rem(cells_of(value), lon)
    near = pltpu.roll(value, (-offset) % cells, 1)
    wrapped = pltpu.roll(value, (offset * (lon - 1)) % cells, 1)
    edge = lon - 1 if offset > 0 else 0
    return jnp.where(column == edge, wrapped, near)


def lat_moved(value, offset, lon):
    cells = value.shape[1]
    moved = pltpu.roll(value, (-offset * lon) % cells, 1)
    cell = cells_of(value)
    if offset > 0:
        return jnp.where(cell < cells - lon, moved, 0.0)
    return jnp.where(cell >= lon, moved, 0.0)


def along_lon(value, lon):
    return 0.5 * (lon_moved(value, 1, lon) - lon_moved(value, -1, lon))


def along_lat(value, lon):
    return 0.5 * (lat_moved(value, 1, lon) - lat_moved(value, -1, lon))


def fill_patches(patches_ref, value, lon):
    cells, channels = value.shape
    planes = value.reshape(cells // lon, lon, channels)
    blank = jnp.zeros((lon, patches_ref.shape[1]), BF16)
    patches_ref[:lon] = blank
    patches_ref[lon + cells :] = blank
    for place, offset in enumerate((-1, 0, 1)):
        moved = value
        if offset:
            moved = pltpu.roll(planes, (-offset) % lon, 1).reshape(cells, channels)
        high, low = halves(moved)
        start = place * 2 * channels
        patches_ref[lon : lon + cells, start : start + channels] = high
        patches_ref[lon : lon + cells, start + channels : start + 2 * channels] = low


def doubled(weight_ref, channels):
    taps = weight_ref.shape[0] // channels
    rows = [weight_ref[tap * channels : (tap + 1) * channels] for tap in range(taps) for unused in range(2)]
    return jnp.concatenate(rows, axis=0)


def conv_patches(patches_ref, weight_ref, lon):
    cells = patches_ref.shape[0] - 2 * lon
    rows = [patches_ref[lon * place : lon * place + cells] for place in range(3)]
    channels = patches_ref.shape[1] // 6
    return folded(dot(jnp.concatenate(rows, axis=1), doubled(weight_ref, channels)), 1)


def sigmoid(value):
    return 1.0 / (1.0 + jnp.exp(-value))


def norm_of(sums, gain, count):
    mean = sums[0:1] / count
    spread = sums[1:2] / count - mean * mean
    scale = lax.rsqrt(spread + EPSILON)
    return mean, scale, gain * scale


def sums_of(value, other):
    total = jnp.sum(value, axis=0, keepdims=True)
    product = jnp.sum(value * other, axis=0, keepdims=True)
    row = lax.broadcasted_iota(jnp.int32, (GROUP, value.shape[1]), 0)
    return jnp.where(row == 0, total, jnp.where(row == 1, product, 0.0))


def inlet_channels(state, lon):
    amount = state[:GROUP]
    groups = jnp.concatenate([state, along_lon(amount, lon), along_lat(amount, lon)], axis=0)
    blank = jnp.zeros((GROUP, state.shape[1]), F32)
    return jnp.concatenate(
        [lon_moved(groups, -1, lon), groups, lon_moved(groups, 1, lon), blank], axis=0
    )


def advected(state, step_size, lon):
    amount, east, north = state[:GROUP], state[GROUP : 2 * GROUP], state[2 * GROUP :]
    return amount - step_size * (along_lon(amount * east, lon) + along_lat(amount * north, lon))


def row_products(left_rows, right_rows):
    left_high, left_low = halves(left_rows)
    right_high, right_low = halves(right_rows)
    left = jnp.concatenate([left_high, left_high, left_low, left_low], axis=0)
    right = jnp.concatenate([right_high, right_low, right_high, right_low], axis=0)
    return dot(left, right, 0, 0)


def heads_of(channels, cells, block_size):
    width = channels // HEADS
    return [
        (slice(head * width, (head + 1) * width), slice(start, start + block_size))
        for start in range(0, cells, block_size)
        for head in range(HEADS)
    ]


def of_head(value, rows, other=0.0):
    channel = lax.broadcasted_iota(jnp.int32, value.shape, 1)
    return jnp.where((channel >= rows.start) & (channel < rows.stop), value, other)


def below(rows, offset):
    return slice(rows.start + offset, rows.stop + offset)


def entered_inlet_kernel(plan, lon, ids_ref, own_ref, arrived_ref, *refs):
    state_ref, cot_ref = refs[2], refs[3]
    size = state_ref.shape[0]
    stays = plan.stays(ids_ref[0], ids_ref[1])
    state_ref[...] = jnp.where(stays, own_ref[:size], arrived_ref[:size])
    cot_ref[...] = jnp.where(stays, own_ref[size:], arrived_ref[size:])
    inlet_kernel(lon, state_ref, *refs[:2], *refs[4:])


def inlet_kernel(
    lon, state_ref, static_ref, weights_ref,
    inner_ref, pre_ref, sums_ref, patches_ref,
):
    w_input_ref = part_of(weights_ref, FORWARD_ROWS, "moving")
    w_first_ref = part_of(weights_ref, FORWARD_ROWS, "first")
    cells = state_ref.shape[1]
    moving = inlet_channels(state_ref[...], lon).T
    width = patches_ref.shape[1]
    blank = jnp.zeros((lon, width), BF16)
    patches_ref[:lon] = blank
    patches_ref[lon + cells :] = blank
    patches_ref[lon : lon + cells, :256] = beside(moving)
    rows = [patches_ref[lon * place : lon * place + cells, :256] for place in range(3)]
    inner = folded(dot(jnp.concatenate(rows, axis=1), doubled(w_input_ref, width // 6)), 1) + static_ref[...]
    inner_ref[...] = inner
    fill_patches(patches_ref, inner * sigmoid(inner), lon)
    pre = conv_patches(patches_ref, w_first_ref, lon)
    pre_ref[...] = pre
    sums_ref[...] = sums_of(pre, pre)


def middle_kernel(
    lon, count, pre_one_ref, sums_one_ref, vectors_ref, weights_ref,
    pre_ref, sums_ref, patches_ref,
):
    w_second_ref = part_of(weights_ref, FORWARD_ROWS, "second")
    mean, unused_scale, factor = norm_of(sums_one_ref[...], vectors_ref[0:1], count)
    normed = (pre_one_ref[...] - mean) * factor + vectors_ref[1:2]
    fill_patches(patches_ref, normed * sigmoid(normed), lon)
    pre = conv_patches(patches_ref, w_second_ref, lon)
    pre_ref[...] = pre
    sums_ref[...] = sums_of(pre, pre)


def act_two_of(inner, pre_two, sums, gain, shift, count):
    mean, unused_scale, factor = norm_of(sums, gain, count)
    return inner * sigmoid(inner) + (pre_two - mean) * factor + shift


def project(w_qkv_ref, act_two_halves, head_width, qkv_ref):
    channels = act_two_halves.shape[0] // 2
    rows = folded(dot(w_qkv_ref[...], act_two_halves), 0)
    qkv_ref[:channels] = rows[:channels] * (LOG2_E / math.sqrt(head_width))
    qkv_ref[channels:] = rows[channels:]


def outlet_kernel(
    lon, count, block_size, step_size, quantities,
    state_ref, inner_ref, pre_two_ref, sums_two_ref, vectors_ref,
    weights_ref,
    out_ref, packed_ref, mixed_ref, top_ref, weight_ref,
    query_ref,
):
    cells, channels = inner_ref.shape
    w_mixer_ref = part_of(weights_ref, FORWARD_ROWS, "mixer")
    w_velocity_ref = part_of(weights_ref, FORWARD_ROWS, "out")
    w_heads = side_by_side(part_of(weights_ref, FORWARD_ROWS, "heads"), channels)
    act_two = act_two_of(
        inner_ref[...], pre_two_ref[...], sums_two_ref[...], vectors_ref[2:3], vectors_ref[3:4], count
    )
    projected = folded(dot(beside(act_two), jnp.concatenate([w_heads, w_heads], axis=0)), 1)
    query = projected[:, : HEADS * channels]
    query_high = query.astype(BF16).astype(F32)
    channel = lax.rem(lax.broadcasted_iota(jnp.int32, query.shape, 1), channels)
    query_ref[...] = jnp.where(channel < channels // 2, query_high, query - query_high).astype(BF16)
    key = projected[:, HEADS * channels : (HEADS + 1) * channels]
    key_high, key_low = halves((key * (LOG2_E / math.sqrt(channels // HEADS))).T)
    value = projected[:, (HEADS + 1) * channels :]
    heads = heads_of(channels, cells, block_size)

    def scores_of(turn):
        rows, lanes = heads[turn]
        right = [half[rows, lanes] for half in (key_high, key_low, key_high, key_low)]
        start = turn % HEADS * channels
        return dot(query_ref[lanes, start : start + channels], jnp.concatenate(right, axis=0))

    following = scores_of(0)
    for turn, (rows, lanes) in enumerate(heads):
        scores = following
        if turn + 1 < len(heads):
            following = scores_of(turn + 1)
        top = jnp.max(scores, axis=1, keepdims=True)
        powers = jnp.exp2(scores - top)
        weight = 1.0 / jnp.sum(powers, axis=1, keepdims=True)
        high, low = halves(powers)
        right = beside(of_head(value[lanes], rows))
        own = folded(dot(high, right) + dot(low, right), 1) * weight
        all_top, all_weight = [jnp.broadcast_to(part, own.shape) for part in (top, weight)]
        if rows.start:
            own = own + mixed
            all_top, all_weight = of_head(all_top, rows, tops), of_head(all_weight, rows, weights)
        mixed, tops, weights = own, all_top, all_weight
        if rows.stop == channels:
            mixed_ref[lanes], top_ref[lanes], weight_ref[lanes] = mixed, tops, weights
    act_three = act_two + folded(dot(beside(mixed_ref[...]), doubled(w_mixer_ref, channels)), 1)
    parts = folded(dot(w_velocity_ref[...], stacked(act_three.T)), 0)
    forcing = jnp.concatenate([vectors_ref[GROUP:]] * (cells // channels), axis=1)
    for column, lon_offset in enumerate((-1, 0, 1)):
        total = None
        for row, lat_offset in enumerate((-1, 0, 1)):
            start = (row * 3 + column) * 2 * GROUP
            part = parts[start : start + 2 * GROUP]
            if lat_offset:
                part = lat_moved(part, lat_offset, lon)
            total = part if total is None else total + part
        forcing = forcing + (lon_moved(total, lon_offset, lon) if lon_offset else total)
    state = state_ref[...]
    flows = state[GROUP:]
    out_ref[:GROUP] = advected(state, step_size, lon)
    out_ref[GROUP:] = flows + step_size * (forcing - flows)
    put_packed(packed_ref, out_ref[...], quantities)


def outlet_back_kernel(
    lon, count, block_size, step_size, quantities, sections, step,
    ids_ref,
    state_ref, d_next_ref, cots_ref, inner_ref, pre_two_ref, sums_two_ref, vectors_ref,
    mixed_ref, top_ref, weight_ref,
    weights_ref,
    acc_qkv_ref, acc_mixer_ref, acc_velocity_ref, acc_small_ref,
    d_state_ref, d_two_ref, sums_ref,
    out_qkv_ref, out_mixer_ref, out_velocity_ref, out_small_ref,
    d_mixed_ref, d_qkv_ref, seed_ref, qkv_ref, mixed_rows_ref, top_rows_ref,
):
    channels = inner_ref.shape[1]
    back = functools.partial(part_of, weights_ref, BACK_ROWS)
    w_qkv_ref, w_mixer_ref, w_mixer_back_ref = back("qkv"), back("mixer"), back("mixer_back")
    w_qkv_back = side_by_side(back("qkv_back"), 2 * channels)
    w_velocity_back = side_by_side(back("out_back"), 2 * channels)[:, : 36 * GROUP]
    cells = inner_ref.shape[0]
    heads = heads_of(channels, cells, block_size)

    state = state_ref[...]
    packed = cots_ref[lax.rem(ids_ref[0] - step + sections, sections)]
    put_groups(seed_ref, packed[: 3 * quantities])
    seed = seed_ref[...] + d_next_ref[...]
    amount, east, north = state[:GROUP], state[GROUP : 2 * GROUP], state[2 * GROUP :]
    d_amount = seed[:GROUP]
    d_lon = step_size * along_lon(d_amount, lon)
    d_lat = step_size * along_lat(d_amount, lon)
    d_state_ref[:GROUP] = d_amount + d_lon * east + d_lat * north
    d_state_ref[GROUP : 2 * GROUP] = (1.0 - step_size) * seed[GROUP : 2 * GROUP] + d_lon * amount
    d_state_ref[2 * GROUP :] = (1.0 - step_size) * seed[2 * GROUP :] + d_lat * amount
    d_forcing = step_size * seed[GROUP:]
    pieces = []
    for lat_offset in (-1, 0, 1):
        moved_rows = lat_moved(d_forcing, -lat_offset, lon) if lat_offset else d_forcing
        for lon_offset in (-1, 0, 1):
            pieces.append(lon_moved(moved_rows, -lon_offset, lon) if lon_offset else moved_rows)
    d_parts = stacked(jnp.concatenate(pieces, axis=0))
    d_three = folded(dot(w_velocity_back, d_parts), 0)
    d_three_halves = stacked(d_three)
    d_mixed_ref[...] = folded(dot(w_mixer_back_ref[...], d_three_halves), 0) * weight_ref[...].T
    mixed_rows_ref[...] = mixed_ref[...].T
    top_rows_ref[...] = top_ref[...].T
    act_two = act_two_of(
        inner_ref[...], pre_two_ref[...], sums_two_ref[...], vectors_ref[2:3], vectors_ref[3:4], count
    ).T
    act_two_halves = stacked(act_two)
    project(w_qkv_ref, act_two_halves, channels // HEADS, qkv_ref)
    d_mixed_cells = d_mixed_ref[...].T
    query_cells = qkv_ref[:channels].T

    def products_of(turn):
        rows, lanes = heads[turn]
        scores = row_products(qkv_ref[below(rows, channels), lanes], qkv_ref[rows, lanes])
        return scores, row_products(qkv_ref[below(rows, 2 * channels), lanes], d_mixed_ref[rows, lanes])

    following = products_of(0)
    for turn, (rows, lanes) in enumerate(heads):
        scores, d_powers = following
        if turn + 1 < len(heads):
            following = products_of(turn + 1)
        inner_sum = jnp.sum(d_mixed_ref[rows, lanes] * mixed_rows_ref[rows, lanes], axis=0, keepdims=True)
        powers = jnp.exp2(scores - top_rows_ref[rows.start : rows.start + 1, lanes])
        power_high, power_low = halves(powers)
        d_high, d_low = halves(powers * (d_powers - inner_sum))
        right = beside(of_head(d_mixed_cells[lanes], rows))
        d_value = dot(power_high, right) + dot(power_low, right) + (d_value if rows.start else 0.0)
        right = beside(of_head(query_cells[lanes], rows))
        d_key = dot(d_high, right) + dot(d_low, right) + (d_key if rows.start else 0.0)
        key_halves = stacked(qkv_ref[below(rows, channels), lanes])
        d_query = folded(dot(key_halves, d_high) + dot(key_halves, d_low), 0)
        d_qkv_ref[rows, lanes] = d_query * (1.0 / math.sqrt(channels // HEADS))
        if rows.stop == channels:
            d_qkv_ref[channels : 2 * channels, lanes] = folded(d_key, 1).T * (1.0 / LOG2_E)
            d_qkv_ref[2 * channels :, lanes] = folded(d_value, 1).T
    d_qkv_halves = stacked(d_qkv_ref[...])
    d_two = (d_three + folded(dot(w_qkv_back, d_qkv_halves), 0)).T
    d_two_ref[...] = d_two
    mean, scale, unused_factor = norm_of(sums_two_ref[...], vectors_ref[2:3], count)
    sums = sums_of(d_two, pre_two_ref[...] - mean)
    sums_ref[...] = sums

    def pairs(left, right):
        return folded(folded(dot(left, right, 1, 1), 0), 1)

    mixed_halves = stacked(mixed_rows_ref[...])
    act_three = act_two + folded(dot(w_mixer_ref[...], mixed_halves), 0)
    out_velocity_ref[...] = acc_velocity_ref[...] + pairs(d_parts, stacked(act_three))
    out_mixer_ref[...] = acc_mixer_ref[...] + pairs(mixed_halves, d_three_halves)
    out_qkv_ref[...] = acc_qkv_ref[...] + pairs(act_two_halves, d_qkv_halves)
    bias = jnp.sum(d_forcing, axis=1, keepdims=True)
    row = lax.broadcasted_iota(jnp.int32, (GROUP, channels), 0)
    small = jnp.where(row == 0, sums[1:2] * scale, jnp.where(row == 1, sums[0:1], 0.0))
    out_small_ref[:GROUP] = acc_small_ref[:GROUP] + small
    out_small_ref[GROUP:] = acc_small_ref[GROUP:] + bias


def d_pre_of(d_normed, centred, sums, all_grad_sums, gain, count):
    unused_mean, scale, factor = norm_of(sums, gain, count)
    d_spread = -0.5 * gain * scale * scale * scale * all_grad_sums[1:2]
    return factor * (d_normed - all_grad_sums[0:1] / count) + (2.0 * d_spread / count) * centred


def weight_pairs(acc_ref, out_ref, left_halves, patches_ref, lon):
    cells = patches_ref.shape[0] - 2 * lon
    width = patches_ref.shape[1] // 3
    for tap in range(9):
        row, column = divmod(8 - tap, 3)
        right = patches_ref[lon * row : lon * row + cells, column * width : (column + 1) * width]
        out_ref[tap] = acc_ref[tap] + folded(folded(dot(left_halves, right), 0), 1)


def middle_back_kernel(
    lon, count,
    d_two_ref, pre_two_ref, sums_two_ref, all_two_ref,
    pre_one_ref, sums_one_ref, vectors_ref, weights_ref,
    acc_weight_ref, acc_small_ref,
    d_normed_ref, sums_ref, out_weight_ref, out_small_ref,
    patches_ref,
):
    w_second_back_ref = part_of(weights_ref, BACK_ROWS, "second")
    sums_two = sums_two_ref[...]
    d_pre = d_pre_of(
        d_two_ref[...], pre_two_ref[...] - sums_two[0:1] / count, sums_two, all_two_ref[...],
        vectors_ref[2:3], count,
    )
    fill_patches(patches_ref, d_pre, lon)
    d_act = conv_patches(patches_ref, w_second_back_ref, lon)
    mean, scale, factor = norm_of(sums_one_ref[...], vectors_ref[0:1], count)
    centred = pre_one_ref[...] - mean
    normed = centred * factor + vectors_ref[1:2]
    gate = sigmoid(normed)
    d_normed = d_act * gate * (1.0 + normed * (1.0 - gate))
    d_normed_ref[...] = d_normed
    sums = sums_of(d_normed, centred)
    sums_ref[...] = sums
    weight_pairs(acc_weight_ref, out_weight_ref, stacked((normed * gate).T), patches_ref, lon)
    row = lax.broadcasted_iota(jnp.int32, sums.shape, 0)
    small = jnp.where(row == 0, sums[1:2] * scale, jnp.where(row == 1, sums[0:1], 0.0))
    out_small_ref[...] = acc_small_ref[...] + small


def inlet_back_kernel(
    lon, count, quantities,
    state_ref, d_normed_ref, pre_one_ref, sums_one_ref, all_one_ref, vectors_ref,
    inner_ref, d_two_ref, d_state_in_ref, weights_ref,
    acc_first_ref, acc_input_ref, acc_inner_ref,
    d_state_ref, packed_ref, out_first_ref, out_input_ref, out_inner_ref,
    patches_ref,
):
    cells = inner_ref.shape[0]
    w_first_back_ref = part_of(weights_ref, BACK_ROWS, "first")
    w_input_back_ref = part_of(weights_ref, BACK_ROWS, "moving")
    sums_one = sums_one_ref[...]
    d_pre = d_pre_of(
        d_normed_ref[...], pre_one_ref[...] - sums_one[0:1] / count, sums_one, all_one_ref[...],
        vectors_ref[0:1], count,
    )
    fill_patches(patches_ref, d_pre, lon)
    d_act = conv_patches(patches_ref, w_first_back_ref, lon) + d_two_ref[...]
    inner = inner_ref[...]
    gate = sigmoid(inner)
    d_inner = d_act * gate * (1.0 + inner * (1.0 - gate))
    weight_pairs(acc_first_ref, out_first_ref, stacked((inner * gate).T), patches_ref, lon)
    out_inner_ref[...] = acc_inner_ref[...] + d_inner
    patches_ref[lon : lon + cells, :256] = beside(d_inner)
    rows = [patches_ref[lon * place : lon * place + cells, :256] for place in range(3)]
    d_moving = folded(dot(jnp.concatenate(rows, axis=1), doubled(w_input_back_ref, inner_ref.shape[1])), 1).T
    state = state_ref[...]
    moving_halves = stacked(inlet_channels(state, lon))
    for place in range(3):
        out_input_ref[place] = acc_input_ref[place] + folded(
            folded(dot(moving_halves, rows[2 - place]), 0), 1
        )
    size = 5 * GROUP
    d_groups = (
        lon_moved(d_moving[:size], 1, lon)
        + d_moving[size : 2 * size]
        + lon_moved(d_moving[2 * size : 3 * size], -1, lon)
    )
    d_state = d_state_in_ref[...] + d_groups[: 3 * GROUP]
    d_state_ref[:GROUP] = (
        d_state[:GROUP]
        - along_lon(d_groups[3 * GROUP : 4 * GROUP], lon)
        - along_lat(d_groups[4 * GROUP :], lon)
    )
    d_state_ref[GROUP:] = d_state[GROUP:]
    put_packed(packed_ref, d_state_ref[...], quantities)


def put_groups(out_ref, rows):
    size = rows.shape[0] // 3
    out_ref[...] = jnp.zeros(out_ref.shape, F32)
    for group in range(3):
        out_ref[group * GROUP : group * GROUP + size] = rows[group * size : (group + 1) * size]


def put_packed(out_ref, grouped, size):
    out_ref[...] = jnp.zeros(out_ref.shape, F32)
    for group in range(3):
        out_ref[group * size : (group + 1) * size] = grouped[group * GROUP : group * GROUP + size]


def fetched(far_refs, near_refs, done_ref):
    copies = [
        pltpu.make_async_copy(far_ref, near_ref, done_ref.at[place])
        for place, (far_ref, near_ref) in enumerate(zip(far_refs, near_refs))
    ]
    for copy in copies:
        copy.start()
    return copies


def enter_kernel(plan, ids_ref, order_ref, state_ref, cot_ref, *refs):
    out_refs, (near_ref, near_cot_ref, rows_ref, done_ref) = refs[:-4], refs[-4:]
    copies = fetched([state_ref, cot_ref], [near_ref, near_cot_ref], done_ref)
    size = rows_ref.shape[0]
    copies[0].wait()
    place = order_ref[0, plan.slot(ids_ref[0], ids_ref[1])]
    for row in range(size):
        rows_ref[row : row + 1] = near_ref[row, pl.ds(place, 1)]
    put_groups(out_refs[0].at[: 3 * GROUP], rows_ref[...])
    copies[1].wait()
    for steps, out_ref in enumerate(out_refs):
        start = 0 if steps else 3 * GROUP
        target = lax.rem(ids_ref[0] + steps, plan.sections)
        place = order_ref[0, plan.slot(target, ids_ref[1])]
        out_ref[start:] = jnp.zeros((2 * GROUP, out_ref.shape[1]), F32)
        for row in range(size):
            out_ref[start + row : start + row + 1] = near_cot_ref[row, pl.ds(place, 1)]


def leave_kernel(plan, ids_ref, *refs):
    values_ref = refs[-1]
    size = refs[0].shape[0]
    for step in range(plan.sections):
        values_ref[step, :size] = refs[step][...]
        if step:
            values_ref[step, size:] = refs[plan.sections + step - 1][...]
        else:
            values_ref[step, size:] = jnp.zeros(refs[0].shape, F32)
    for steps, out_ref in enumerate(refs[2 * plan.sections - 1 : -1]):
        out_ref[...] = values_ref[lax.rem(ids_ref[0] + steps, plan.sections)]


def arrive_kernel(plan, start, ids_ref, order_ref, kept_ref, *refs):
    section, dp = ids_ref[0], ids_ref[1]
    out_ref = refs[-1]
    size = kept_ref.shape[0] // 2
    early, late = refs[: plan.sections], refs[plan.sections : -1]
    if late:
        kept_late_ref, *late = late
    for steps, ref in enumerate(early):
        source = lax.rem(section - steps + plan.sections, plan.sections)
        place = order_ref[0, plan.slot(source, dp)]
        value = ref[start : start + size]
        if late:
            value = jnp.where(section == 0, late[steps][...], value)
        if plan.halved and not steps:
            kept = kept_ref[start : start + size]
            if late:
                kept = jnp.where(section == 0, kept_late_ref[...], kept)
            value = jnp.where(plan.stays(section, dp), kept, value)
        for row in range(out_ref.shape[0]):
            out_ref[row, pl.ds(place, 1)] = value[row : row + 1]


def put_conv_weight(out_ref, taps):
    for tap, weight in enumerate(taps):
        rows = weight.shape[0]
        out_ref[tap * rows : (tap + 1) * rows] = beside(weight)


def weights_kernel(
    lon, quantities,
    w_input_ref, maps_ref, b_input_ref, w_first_ref, w_second_ref,
    w_query_ref, w_key_ref, w_value_ref, w_mixer_ref, w_velocity_ref,
    gain_one_ref, shift_one_ref, gain_two_ref, shift_two_ref, b_velocity_ref,
    static_part_ref, forward_ref, back_ref, vectors_ref,
    patches_ref, weight_ref, taps_ref, rows_ref, *near_refs,
):
    forward = functools.partial(part_of, forward_ref, FORWARD_ROWS)
    back = functools.partial(part_of, back_ref, BACK_ROWS)
    near_refs, done_ref = near_refs[:-1], near_refs[-1]
    copies = fetched(
        [w_input_ref, maps_ref, b_input_ref, w_first_ref, w_second_ref,
         w_query_ref, w_key_ref, w_value_ref, w_mixer_ref, w_velocity_ref,
         gain_one_ref, shift_one_ref, gain_two_ref, shift_two_ref, b_velocity_ref],
        near_refs, done_ref,
    )
    (
        w_input_ref, maps_ref, b_input_ref, w_first_ref, w_second_ref,
        w_query_ref, w_key_ref, w_value_ref, w_mixer_ref, w_velocity_ref,
        gain_one_ref, shift_one_ref, gain_two_ref, shift_two_ref, b_velocity_ref,
    ) = near_refs
    channels = w_input_ref.shape[2]
    moving = 5 * quantities
    statics = maps_ref.shape[0]
    taps_ref[...] = jnp.zeros(taps_ref.shape, F32)
    rows_ref[...] = jnp.zeros(rows_ref.shape, F32)
    copies[0].wait()
    for tap in range(9):
        row, column = divmod(tap, 3)
        for group in range(5):
            start = (column * 5 + group) * GROUP
            taps_ref[9 + row, start : start + quantities] = w_input_ref[
                tap, group * quantities : (group + 1) * quantities
            ]
        taps_ref[tap, :statics] = w_input_ref[tap, moving:]
    put_conv_weight(forward("moving"), [taps_ref[9 + row] for row in range(3)])
    put_conv_weight(back("moving"), [taps_ref[11 - row].T for row in range(3)])
    put_conv_weight(weight_ref, [taps_ref[tap] for tap in range(9)])
    copies[1].wait()
    copies[2].wait()
    maps = jnp.concatenate(
        [maps_ref[...], jnp.zeros((channels - statics, maps_ref.shape[1]), F32)], axis=0
    )
    fill_patches(patches_ref, maps.T, lon)
    static_part_ref[...] = conv_patches(patches_ref, weight_ref, lon) + b_input_ref[...]
    for copy in copies[3:]:
        copy.wait()
    put_conv_weight(forward("first"), [w_first_ref[tap] for tap in range(9)])
    put_conv_weight(forward("second"), [w_second_ref[tap] for tap in range(9)])
    put_conv_weight(back("first"), [w_first_ref[8 - tap].T for tap in range(9)])
    put_conv_weight(back("second"), [w_second_ref[8 - tap].T for tap in range(9)])
    parts = [ref[...] for ref in (w_query_ref, w_key_ref, w_value_ref)]
    turned = [part.T for part in parts]
    width = channels // HEADS
    repeated = [turned[0][head * width : (head + 1) * width] for head in range(HEADS) for unused in range(HEADS)]
    heads = jnp.concatenate([jnp.concatenate(repeated, axis=0).T, parts[1], parts[2]], axis=1)
    put_blocks(forward("heads"), beside(heads))
    put_conv_weight(forward("mixer"), [w_mixer_ref[...]])
    back("qkv")[...] = left_form(jnp.concatenate(turned, axis=0))
    put_blocks(back("qkv_back"), left_form(jnp.concatenate(parts, axis=1)))
    back("mixer")[...] = left_form(w_mixer_ref[...].T)
    back("mixer_back")[...] = left_form(w_mixer_ref[...])
    for tap in range(9):
        for group in range(2):
            start = (tap * 2 + group) * GROUP
            rows_ref[start : start + quantities] = w_velocity_ref[
                tap, group * quantities : (group + 1) * quantities
            ]
    size = 18 * GROUP
    vectors_ref[...] = jnp.zeros(vectors_ref.shape, F32)
    for place, ref in enumerate((gain_one_ref, shift_one_ref, gain_two_ref, shift_two_ref)):
        vectors_ref[place : place + 1] = ref[...]
    bias = jnp.concatenate([b_velocity_ref[...], jnp.zeros((1, channels - 2 * quantities), F32)], axis=1)
    bias = jnp.broadcast_to(bias, (channels, channels)).T
    for group in range(2):
        start = (group + 1) * GROUP
        vectors_ref[start : start + quantities] = bias[group * quantities : (group + 1) * quantities]
    forward("out")[...] = left_form(rows_ref[:size])
    put_blocks(back("out_back"), left_form(rows_ref[...].T[:, :size]))


def index_of(ids_ref, plan, bits):
    own = ids_ref[0] * plan.dp + ids_ref[1]
    return sum(lax.rem(own // bit, 2) << place for place, bit in enumerate(bits))


def deal(total_ref, own, out_refs):
    rows = out_refs[0].shape[0]
    for turn, out_ref in enumerate(out_refs):
        out_ref[...] = total_ref[pl.ds(pl.multiple_of((own ^ turn) * rows, GROUP), rows)]


def pack_kernel(
    plan, bits, lon, statics, ids_ref, maps_ref, inner_ref, first_ref, second_ref, moving_ref,
    qkv_ref, mixer_ref, velocity_ref, small_one_ref, small_two_ref, *refs,
):
    out_refs, total_ref, patches_ref = refs[:-2], refs[-2], refs[-1]
    cells, channels = inner_ref.shape
    d_inner = inner_ref[...]
    fill_patches(patches_ref, d_inner, lon)
    width = patches_ref.shape[1] // 3
    maps = maps_ref[...]
    blank = jnp.zeros((-statics % GROUP, cells), F32)
    maps = jnp.concatenate([maps, blank], axis=0)
    rows = maps.shape[0]
    left = jnp.concatenate(halves(maps), axis=0)
    start = 0

    def put(value):
        nonlocal start
        total_ref[start : start + value.shape[0]] = value
        start += value.shape[0]

    for tap in range(9):
        put(first_ref[tap])
    for tap in range(9):
        put(second_ref[tap])
    for tap in range(9):
        row, column = divmod(8 - tap, 3)
        right = patches_ref[lon * row : lon * row + cells, column * width : (column + 1) * width]
        put(folded(folded(dot(left, right), 0), 1))
    for place in range(3):
        put(moving_ref[place, : 15 * GROUP])
    for part in range(3):
        put(qkv_ref[:, part * channels : (part + 1) * channels])
    put(mixer_ref[...])
    put(velocity_ref[...])
    put(small_one_ref[...])
    put(small_two_ref[...])
    put(jnp.zeros((GROUP, channels), F32) + jnp.sum(d_inner, axis=0, keepdims=True))
    total_ref[start:] = jnp.zeros((total_ref.shape[0] - start, channels), F32)
    deal(total_ref, index_of(ids_ref, plan, bits), out_refs)


def reduce_kernel(plan, bits, count, ids_ref, *refs):
    total_ref = refs[-1]
    total = refs[0][...]
    for ref in refs[1:count]:
        total = total + ref[...]
    if not bits:
        refs[count][...] = total
        return
    total_ref[...] = total
    deal(total_ref, index_of(ids_ref, plan, bits), refs[count:-1])


def gather_rows(plan, bits, ids_ref, part_refs, out_ref):
    own = index_of(ids_ref, plan, bits)
    rows = part_refs[0].shape[0]
    for turn, ref in enumerate(part_refs):
        out_ref[pl.ds(pl.multiple_of((own ^ turn) * rows, GROUP), rows)] = ref[...]


def gather_kernel(plan, bits, ids_ref, *refs):
    gather_rows(plan, bits, ids_ref, refs[:-1], refs[-1])


def unpack_kernel(
    plan, bits, quantities, statics, ids_ref, *refs,
):
    count = 1 << len(bits)
    (
        input_ref, bias_ref, first_ref, gain_one_ref, shift_one_ref, second_ref, gain_two_ref, shift_two_ref,
        query_ref, key_ref, value_ref, mixer_ref, velocity_ref, velocity_bias_ref, total_ref,
    ) = refs[count:]
    gather_rows(plan, bits, ids_ref, refs[:count], total_ref)
    channels = mixer_ref.shape[0]
    moving = 5 * quantities
    start = 0

    def take(rows):
        nonlocal start
        start += rows
        return total_ref[start - rows : start]

    for tap in range(9):
        first_ref[tap] = take(channels)
    for tap in range(9):
        second_ref[tap] = take(channels)
    for tap in range(9):
        input_ref[tap, moving:] = take(statics + -statics % GROUP)[:statics]
    for row in range(3):
        for column in range(3):
            for group in range(5):
                rows = take(GROUP)
                input_ref[row * 3 + column, group * quantities : (group + 1) * quantities] = rows[:quantities]
    query_ref[...] = take(channels)
    key_ref[...] = take(channels)
    value_ref[...] = take(channels)
    mixer_ref[...] = take(channels)
    for tap in range(9):
        for group in range(2):
            velocity_ref[tap, group * quantities : (group + 1) * quantities] = take(GROUP)[:quantities]
    small = take(GROUP)
    gain_one_ref[...], shift_one_ref[...] = small[0:1], small[1:2]
    small = take(GROUP)
    gain_two_ref[...], shift_two_ref[...] = small[0:1], small[1:2]
    velocity_bias_ref[...] = take(2 * GROUP)
    bias_ref[...] = take(GROUP)[0:1]


def call(kernel, outs, scratch=(), aliases=None, name=None, scalars=0, kinds=None, far_in=(), limit=None):
    kinds = kinds or [F32] * len(outs)

    def run(*operands):
        places = [pltpu.SMEM] * scalars + [pltpu.VMEM] * (len(operands) - scalars)
        for place in far_in:
            places[place] = pltpu.HBM
        return pl.pallas_call(
            kernel,
            out_shape=tuple(jax.ShapeDtypeStruct(shape, kind) for shape, kind in zip(outs, kinds)),
            in_specs=[pl.BlockSpec(memory_space=place) for place in places],
            out_specs=tuple(pl.BlockSpec(memory_space=pltpu.VMEM) for unused in outs),
            scratch_shapes=scratch,
            input_output_aliases=aliases or {},
            compiler_params=pltpu.CompilerParams(vmem_limit_bytes=limit or VMEM_LIMIT),
            name=name,
        )(*operands)

    return run


VMEM_LIMIT = 24 * 1024 * 1024
ALONE_LIMIT = 56 * 1024 * 1024

FORWARD_ROWS = dict(moving=384, first=1152, second=1152, heads=768, mixer=128, out=288)
BACK_ROWS = dict(moving=384, first=1152, second=1152, qkv=768, mixer=256, mixer_back=256, qkv_back=768, out_back=512)


def part_of(ref, rows, name):
    start = 0
    for other, size in rows.items():
        if other == name:
            return ref.at[start : start + size]
        start += size
    return None


def side_by_side(ref, rows):
    return jnp.concatenate([ref[start : start + rows] for start in range(0, ref.shape[0], rows)], axis=1)


def put_blocks(ref, value):
    rows, width = value.shape[0], ref.shape[1]
    for place in range(ref.shape[0] // rows):
        block = value[:, place * width : (place + 1) * width]
        if block.shape[1] < width:
            block = jnp.concatenate([block, jnp.zeros((rows, width - block.shape[1]), value.dtype)], axis=1)
        ref[place * rows : (place + 1) * rows] = block


def left_form(weight):
    return jnp.concatenate([jnp.concatenate([half, half], axis=1) for half in halves(weight)], axis=0)


def in_groups(array, axis, groups):
    shape = array.shape
    split = shape[:axis] + (groups, shape[axis] // groups) + shape[axis + 1 :]
    array = array.reshape(split)
    pads = [(0, 0)] * array.ndim
    pads[axis + 1] = (0, GROUP - split[axis + 1])
    return jnp.pad(array, pads).reshape(shape[:axis] + (groups * GROUP,) + shape[axis + 1 :])


def from_groups(array, axis, groups, size):
    shape = array.shape
    array = array.reshape(shape[:axis] + (groups, GROUP) + shape[axis + 1 :])
    array = lax.slice_in_dim(array, 0, size, axis=axis + 1)
    return array.reshape(shape[:axis] + (groups * size,) + shape[axis + 1 :])


class Plan:
    def __init__(self, sections, dp):
        self.sections, self.dp = sections, dp
        self.halved = sections == 4 and dp >= 4
        self.half = dp // 2
        bits = [1 << place for place in range((sections * dp).bit_length() - 1)]
        dp_bits = [bit for bit in bits if bit < dp]
        section_bits = [bit for bit in bits if bit >= dp]
        if self.halved:
            self.sum_rounds = in_pairs(dp_bits[:-1]) + in_pairs(section_bits)
        else:
            self.sum_rounds = in_pairs(dp_bits) + [section_bits[:1]]
        self.all_rounds = [dp_bits[:1]] + in_pairs(section_bits) + in_pairs(dp_bits[1:])

    def slot(self, section, home):
        if not self.halved:
            return section
        return lax.rem(home // self.half + section // 2 + home, 2) * 2 + lax.rem(section, 2)

    def stays(self, section, dp):
        return lax.rem(section // 2 + dp, 2) == 0

    def other(self, section, dp):
        return dp ^ self.half if self.halved and (section // 2 + dp) % 2 else dp

    def to_workers(self, steps):
        return [
            (section * self.dp + home, self.joint((section + steps) % self.sections, home))
            for section in range(self.sections)
            for home in range(self.dp)
        ]

    def to_homes(self, steps):
        return [
            (section * self.dp + own, (section + steps) % self.sections * self.dp + self.other(section, own))
            for section in range(self.sections)
            for own in range(self.dp)
        ]

    def to_first_home(self, steps):
        return [(source, target) for source, target in self.to_homes(steps) if target < self.dp]

    def joint(self, section, home):
        return section * self.dp + self.other(section, home)


def in_pairs(bits):
    return [bits[start : start + 2] for start in range(0, len(bits), 2)]


def masks_of(bits):
    return [sum(bit for place, bit in enumerate(bits) if turn >> place & 1) for turn in range(1, 1 << len(bits))]


def exchanged(value, mask):
    size = lax.axis_size("section") * lax.axis_size("dp")
    return lax.ppermute(value, ("section", "dp"), [(own, own ^ mask) for own in range(size)])


def moved(value, pairs):
    going = [(source, target) for source, target in pairs if source != target]
    if not going:
        return value
    return lax.ppermute(value, ("section", "dp"), going)


def micro_sum(plan, value, first_core):
    if not plan.halved or plan.half != 4:
        for bits in plan.sum_rounds:
            value = value + sum(exchanged(value, mask) for mask in masks_of(bits))
        return value
    value = value + exchanged(value, 1)
    plane = masks_of([plan.dp, 2 * plan.dp])
    other = [mask ^ 2 for mask in plane]
    own = range(plan.sections * plan.dp)
    total = value * first_core
    for turn, mask in enumerate(plane + [2]):
        pairs = [(device, device ^ mask) for device in own if not device & 1]
        if turn < 3:
            pairs += [(device, device ^ other[turn]) for device in own if device & 1]
        total = total + lax.ppermute(value, ("section", "dp"), pairs)
    return total + exchanged(total, 1)


def on_device(
    state_start,
    static_maps,
    grouping,
    cotangent,
    w_input,
    b_input,
    w_first,
    gain_first,
    shift_first,
    w_second,
    gain_second,
    shift_second,
    w_query,
    w_key,
    w_value,
    w_mixer,
    w_velocity,
    b_velocity,
):
    segments = lax.axis_size("section")
    plan = Plan(segments, lax.axis_size("dp"))
    micro_count = segments // 2
    per_micro = state_start.shape[0] // micro_count
    cells = state_start.shape[2]
    lon = cells // LAT
    count = float(per_micro * cells * plan.dp)
    step_size = 2.0 / segments
    block_size = ATT_ROWS * lon
    channels = w_first.shape[2]
    quantities = state_start.shape[1] // 3
    statics = static_maps.shape[0]
    ids = jnp.stack([lax.axis_index("section"), lax.axis_index("dp")]).astype(jnp.int32)

    plane = (cells, channels)
    small = (GROUP, channels)
    conv = (9 * channels, 2 * channels)
    patches = pltpu.VMEM((cells + 2 * lon, 6 * channels), BF16)
    wide = pltpu.VMEM((3 * channels, cells), F32)
    narrow = pltpu.VMEM((channels, cells), F32)
    state_shape = (3 * GROUP, cells)

    packed = (2 * GROUP, cells)

    def near(*arrays):
        return [pltpu.VMEM(array.shape, F32) for array in arrays] + [pltpu.SemaphoreType.DMA((len(arrays),))]

    state_rows, cot_rows = jnp.swapaxes(state_start, 0, 1), jnp.swapaxes(cotangent[0], 0, 1)
    entry, *sent_cots = call(
        functools.partial(enter_kernel, plan), [(5 * GROUP, cells)] + [packed] * (segments - 1),
        [pltpu.VMEM(state_rows.shape, F32)] * 2
        + [pltpu.VMEM((3 * quantities, cells), F32), pltpu.SemaphoreType.DMA((2,))],
        name="enter", scalars=2, far_in=[2, 3], limit=ALONE_LIMIT,
    )(ids, grouping, state_rows, cot_rows)
    arrived = moved(entry, plan.to_workers(0))
    first_core = (1.0 - lax.rem(ids[1], 2).astype(F32)) * jnp.ones(small, F32)
    w_velocity_rows = jnp.swapaxes(w_velocity, 1, 2)
    weights = (
        w_input, static_maps, b_input[None], w_first, w_second, w_query, w_key, w_value, w_mixer, w_velocity_rows,
        gain_first[None], shift_first[None], gain_second[None], shift_second[None], b_velocity[None],
    )
    columns = 2 * channels
    static_part, forward_weights, back_weights, vectors = call(
        functools.partial(weights_kernel, lon, quantities),
        [plane, (sum(FORWARD_ROWS.values()), columns), (sum(BACK_ROWS.values()), columns), (3 * GROUP, channels)],
        [patches, pltpu.VMEM(conv, BF16), pltpu.VMEM((12, channels, channels), F32),
         pltpu.VMEM((columns, channels), F32)] + near(*weights),
        name="weights", kinds=[F32, BF16, BF16, F32], far_in=range(15), limit=ALONE_LIMIT,
    )(*weights)

    inlet = call(
        functools.partial(inlet_kernel, lon), [plane, plane, small], [patches], name="inlet"
    )
    middle = call(
        functools.partial(middle_kernel, lon, count), [plane, small], [patches], name="middle"
    )
    outlet = call(
        functools.partial(outlet_kernel, lon, count, block_size, step_size, quantities),
        [state_shape, packed, plane, plane, plane],
        [pltpu.VMEM((cells, HEADS * channels), BF16)], name="outlet",
    )

    def outlet_back(step):
        return call(
            functools.partial(outlet_back_kernel, lon, count, block_size, step_size, quantities, segments, step),
            [state_shape, plane, small, (channels, 3 * channels), (channels, channels),
             (18 * GROUP, channels), (3 * GROUP, channels)],
            [narrow, wide, pltpu.VMEM(state_shape, F32), wide, narrow, narrow],
            {12: 3, 13: 4, 14: 5, 15: 6}, name="outlet_back", scalars=1,
        )

    middle_back = call(
        functools.partial(middle_back_kernel, lon, count),
        [plane, small, (9, channels, channels), small], [patches],
        {8: 2, 9: 3}, name="middle_back",
    )
    inlet_back = call(
        functools.partial(inlet_back_kernel, lon, count, quantities),
        [state_shape, packed, (9, channels, channels), (3, channels, channels), plane], [patches],
        {10: 2, 11: 3, 12: 4}, name="inlet_back",
    )

    state = entry[: 3 * GROUP]
    path, saved = [], []
    cots = None
    for step in range(segments):
        if not step:
            if not plan.halved:
                arrived = entry
            state, own_cot, inner, pre_one, sums_one = call(
                functools.partial(entered_inlet_kernel, plan, lon), [state_shape, packed, plane, plane, small], [patches],
                name="inlet", scalars=1,
            )(ids, entry, arrived, static_part, forward_weights)
        else:
            inner, pre_one, sums_one = inlet(state, static_part, forward_weights)
        sums_one = micro_sum(plan, sums_one, first_core)
        pre_two, sums_two = middle(pre_one, sums_one, vectors, forward_weights)
        sums_two = micro_sum(plan, sums_two, first_core)
        state_out, state_packed, mixed, top, weight = outlet(
            state, inner, pre_two, sums_two, vectors, forward_weights
        )
        saved.append((state, inner, pre_one, pre_two, sums_one, sums_two, mixed, top, weight))
        path.append(state_packed)
        state = state_out
        if not step:
            state, sent_cots = lax.optimization_barrier((state, sent_cots))
            cots = jnp.stack(
                [own_cot] + [moved(cot, plan.to_workers(steps + 1)) for steps, cot in enumerate(sent_cots)]
            )

    def put_home(start, parts):
        (out,) = call(
            functools.partial(arrive_kernel, plan, start), [state_rows.shape], name="arrive", scalars=2
        )(ids, grouping, *parts)
        return jnp.swapaxes(out, 0, 1)[None]

    acc = dict(
        qkv=jnp.zeros((channels, 3 * channels), F32),
        mixer=jnp.zeros((channels, channels), F32),
        velocity=jnp.zeros((18 * GROUP, channels), F32),
        small_two=jnp.zeros((3 * GROUP, channels), F32),
        second=jnp.zeros((9, channels, channels), F32),
        small_one=jnp.zeros(small, F32),
        first=jnp.zeros((9, channels, channels), F32),
        moving=jnp.zeros((3, channels, channels), F32),
        inner=jnp.zeros(plane, F32),
    )
    d_state = jnp.zeros(state_shape, F32)
    grads = [None] * segments
    path_out = None
    for step in reversed(range(segments)):
        if not step:
            sent = call(
                functools.partial(leave_kernel, plan), [(4 * GROUP, cells)] * segments,
                [pltpu.VMEM((segments, 4 * GROUP, cells), F32)], name="leave", scalars=1,
            )(ids, *path, *grads[1:])
            early = [sent[0]] + [moved(part, plan.to_homes(steps)) for steps, part in enumerate(sent)]
        state, inner, pre_one, pre_two, sums_one, sums_two, mixed, top, weight = saved[step]
        d_partial, d_two, grad_two, acc["qkv"], acc["mixer"], acc["velocity"], acc["small_two"] = outlet_back(step)(
            ids, state, d_state, cots, inner, pre_two, sums_two, vectors,
            mixed, top, weight, back_weights,
            acc["qkv"], acc["mixer"], acc["velocity"], acc["small_two"],
        )
        if not step:
            d_two, grad_two, early = lax.optimization_barrier((d_two, grad_two, early))
            path_out = put_home(0, early)
        grad_two = micro_sum(plan, grad_two, first_core)
        d_normed, grad_one, acc["second"], acc["small_one"] = middle_back(
            d_two, pre_two, sums_two, grad_two,
            pre_one, sums_one, vectors, back_weights,
            acc["second"], acc["small_one"],
        )
        grad_one = micro_sum(plan, grad_one, first_core)
        d_state, grads[step], acc["first"], acc["moving"], acc["inner"] = inlet_back(
            state, d_normed, pre_one, sums_one, grad_one, vectors,
            inner, d_two, d_partial, back_weights,
            acc["first"], acc["moving"], acc["inner"],
        )
    late = [grads[0]] + [moved(grads[0], plan.to_first_home(steps)) for steps in range(segments)]

    rounds = plan.all_rounds
    rows = 2 * 9 * channels + 9 * (statics + -statics % GROUP) + 45 * GROUP + 4 * channels + 23 * GROUP
    unit = GROUP * segments * plan.dp
    rows = -(-rows // unit) * unit

    def shares(rows, bits):
        return [(rows >> len(bits), channels)] * (1 << len(bits))

    def swap(parts, bits):
        return [parts[0]] + [exchanged(part, mask) for part, mask in zip(parts[1:], masks_of(bits))]

    parts = call(
        functools.partial(pack_kernel, plan, rounds[0], lon, statics), shares(rows, rounds[0]),
        [pltpu.VMEM((rows, channels), F32), patches], name="pack", scalars=1,
    )(
        ids, static_maps, acc["inner"], acc["first"], acc["second"], acc["moving"], acc["qkv"], acc["mixer"],
        acc["velocity"], acc["small_one"], acc["small_two"],
    )
    for place, (bits, later) in enumerate(zip(rounds, rounds[1:] + [[]])):
        parts = swap(parts, bits)
        if place == 1:
            parts, late = lax.optimization_barrier((parts, late))
            grads_out = put_home(2 * GROUP, early + late)
            parts, path_out, grads_out = lax.optimization_barrier((parts, path_out, grads_out))
        rows >>= len(bits)
        parts = call(
            functools.partial(reduce_kernel, plan, later, len(parts)), shares(rows, later),
            [pltpu.VMEM((rows, channels), F32)], name="reduce_part", scalars=1,
        )(ids, *parts)
    for bits in rounds[::-1]:
        parts = swap([parts[0]] * (1 << len(bits)), bits)
        rows <<= len(bits)
        if bits is rounds[0]:
            break
        parts = call(
            functools.partial(gather_kernel, plan, bits), [(rows, channels)], name="gather_part", scalars=1
        )(ids, *parts)
    row = (1, channels)
    square = (channels, channels)
    grads_all = call(
        functools.partial(unpack_kernel, plan, rounds[0], quantities, statics),
        [w_input.shape, row, w_first.shape, row, row, w_second.shape, row, row, square, square, square, square,
         (9, 2 * quantities, channels), (2 * GROUP, channels)],
        [pltpu.VMEM((rows, channels), F32)], name="unpack", scalars=1,
    )(ids, *parts)
    grads_all = [grad[0] if grad.shape == row else grad for grad in grads_all]
    grads_all[-2] = jnp.swapaxes(grads_all[-2], 1, 2)
    grads_all[-1] = from_groups(grads_all[-1][:, :1], 0, 2, quantities)[:, 0]
    return (path_out, grads_out) + tuple(grads_all)


def solution(mesh):
    weights = (P(),) * 14
    return jax.shard_map(
        on_device,
        mesh=mesh,
        in_specs=(P("dp", None, None), P(), P("dp", None), P("section", "dp", None, None)) + weights,
        out_specs=(P("section", "dp", None, None), P("section", "dp", None, None)) + weights,
        check_vma=False,
    )
```

```python
import functools
import math

import jax
import jax.numpy as jnp
from jax import lax
from jax.experimental import pallas as pl
from jax.experimental.pallas import tpu as pltpu
from jax.sharding import PartitionSpec as P

HEADS = 4
LAT = 16
ATT_ROWS = 8
EPSILON = 1e-05
LOG2_E = 1.0 / math.log(2.0)
F32 = jnp.float32
BF16 = jnp.bfloat16
GROUP = 8


def dot(left, right, left_dim=1, right_dim=0):
    return lax.dot_general(
        left, right, (((left_dim,), (right_dim,)), ((), ())), preferred_element_type=F32
    )


def halves(value):
    high = value.astype(BF16)
    return high, (value - high.astype(F32)).astype(BF16)


def stacked(value):
    return jnp.concatenate(halves(value), axis=0)


def beside(value):
    return jnp.concatenate(halves(value), axis=1)


def folded(value, axis):
    size = value.shape[axis] // 2
    if axis == 0:
        return value[:size] + value[size:]
    return value[:, :size] + value[:, size:]


def cells_of(value):
    return lax.broadcasted_iota(jnp.int32, value.shape, value.ndim - 1)


def lon_moved(value, offset, lon):
    cells = value.shape[1]
    column = lax.rem(cells_of(value), lon)
    near = pltpu.roll(value, (-offset) % cells, 1)
    wrapped = pltpu.roll(value, (offset * (lon - 1)) % cells, 1)
    edge = lon - 1 if offset > 0 else 0
    return jnp.where(column == edge, wrapped, near)


def lat_moved(value, offset, lon):
    cells = value.shape[1]
    moved = pltpu.roll(value, (-offset * lon) % cells, 1)
    cell = cells_of(value)
    if offset > 0:
        return jnp.where(cell < cells - lon, moved, 0.0)
    return jnp.where(cell >= lon, moved, 0.0)


def along_lon(value, lon):
    return 0.5 * (lon_moved(value, 1, lon) - lon_moved(value, -1, lon))


def along_lat(value, lon):
    return 0.5 * (lat_moved(value, 1, lon) - lat_moved(value, -1, lon))


def fill_patches(patches_ref, value, lon):
    cells, channels = value.shape
    planes = value.reshape(cells // lon, lon, channels)
    blank = jnp.zeros((lon, patches_ref.shape[1]), BF16)
    patches_ref[:lon] = blank
    patches_ref[lon + cells :] = blank
    for place, offset in enumerate((-1, 0, 1)):
        moved = value
        if offset:
            moved = pltpu.roll(planes, (-offset) % lon, 1).reshape(cells, channels)
        high, low = halves(moved)
        start = place * 2 * channels
        patches_ref[lon : lon + cells, start : start + channels] = high
        patches_ref[lon : lon + cells, start + channels : start + 2 * channels] = low


def doubled(weight_ref, channels):
    taps = weight_ref.shape[0] // channels
    rows = [weight_ref[tap * channels : (tap + 1) * channels] for tap in range(taps) for unused in range(2)]
    return jnp.concatenate(rows, axis=0)


def conv_patches(patches_ref, weight_ref, lon):
    cells = patches_ref.shape[0] - 2 * lon
    rows = [patches_ref[lon * place : lon * place + cells] for place in range(3)]
    channels = patches_ref.shape[1] // 6
    return folded(dot(jnp.concatenate(rows, axis=1), doubled(weight_ref, channels)), 1)


def sigmoid(value):
    return 1.0 / (1.0 + jnp.exp(-value))


def norm_of(sums, gain, count):
    mean = sums[0:1] / count
    spread = sums[1:2] / count - mean * mean
    scale = lax.rsqrt(spread + EPSILON)
    return mean, scale, gain * scale


def sums_of(value, other):
    total = jnp.sum(value, axis=0, keepdims=True)
    product = jnp.sum(value * other, axis=0, keepdims=True)
    row = lax.broadcasted_iota(jnp.int32, (GROUP, value.shape[1]), 0)
    return jnp.where(row == 0, total, jnp.where(row == 1, product, 0.0))


def inlet_channels(state, lon):
    amount = state[:GROUP]
    groups = jnp.concatenate([state, along_lon(amount, lon), along_lat(amount, lon)], axis=0)
    blank = jnp.zeros((GROUP, state.shape[1]), F32)
    return jnp.concatenate(
        [lon_moved(groups, -1, lon), groups, lon_moved(groups, 1, lon), blank], axis=0
    )


def advected(state, step_size, lon):
    amount, east, north = state[:GROUP], state[GROUP : 2 * GROUP], state[2 * GROUP :]
    return amount - step_size * (along_lon(amount * east, lon) + along_lat(amount * north, lon))


def row_products(left_rows, right_rows):
    left_high, left_low = halves(left_rows)
    right_high, right_low = halves(right_rows)
    left = jnp.concatenate([left_high, left_high, left_low, left_low], axis=0)
    right = jnp.concatenate([right_high, right_low, right_high, right_low], axis=0)
    return dot(left, right, 0, 0)


def heads_of(channels, cells, block_size):
    width = channels // HEADS
    return [
        (slice(head * width, (head + 1) * width), slice(start, start + block_size))
        for start in range(0, cells, block_size)
        for head in range(HEADS)
    ]


def of_head(value, rows, other=0.0):
    channel = lax.broadcasted_iota(jnp.int32, value.shape, 1)
    return jnp.where((channel >= rows.start) & (channel < rows.stop), value, other)


def below(rows, offset):
    return slice(rows.start + offset, rows.stop + offset)


def entered_inlet_kernel(plan, lon, ids_ref, own_ref, arrived_ref, *refs):
    state_ref, cot_ref = refs[2], refs[3]
    size = state_ref.shape[0]
    stays = plan.stays(ids_ref[0], ids_ref[1])
    state_ref[...] = jnp.where(stays, own_ref[:size], arrived_ref[:size])
    cot_ref[...] = jnp.where(stays, own_ref[size:], arrived_ref[size:])
    inlet_kernel(lon, state_ref, *refs[:2], *refs[4:])


def inlet_kernel(
    lon, state_ref, static_ref, weights_ref,
    inner_ref, pre_ref, sums_ref, patches_ref,
):
    w_input_ref = part_of(weights_ref, FORWARD_ROWS, "moving")
    w_first_ref = part_of(weights_ref, FORWARD_ROWS, "first")
    cells = state_ref.shape[1]
    moving = inlet_channels(state_ref[...], lon).T
    width = patches_ref.shape[1]
    blank = jnp.zeros((lon, width), BF16)
    patches_ref[:lon] = blank
    patches_ref[lon + cells :] = blank
    patches_ref[lon : lon + cells, :256] = beside(moving)
    rows = [patches_ref[lon * place : lon * place + cells, :256] for place in range(3)]
    inner = folded(dot(jnp.concatenate(rows, axis=1), doubled(w_input_ref, width // 6)), 1) + static_ref[...]
    inner_ref[...] = inner
    fill_patches(patches_ref, inner * sigmoid(inner), lon)
    pre = conv_patches(patches_ref, w_first_ref, lon)
    pre_ref[...] = pre
    sums_ref[...] = sums_of(pre, pre)


def middle_kernel(
    lon, count, pre_one_ref, sums_one_ref, vectors_ref, weights_ref,
    pre_ref, sums_ref, patches_ref,
):
    w_second_ref = part_of(weights_ref, FORWARD_ROWS, "second")
    mean, unused_scale, factor = norm_of(sums_one_ref[...], vectors_ref[0:1], count)
    normed = (pre_one_ref[...] - mean) * factor + vectors_ref[1:2]
    fill_patches(patches_ref, normed * sigmoid(normed), lon)
    pre = conv_patches(patches_ref, w_second_ref, lon)
    pre_ref[...] = pre
    sums_ref[...] = sums_of(pre, pre)


def act_two_of(inner, pre_two, sums, gain, shift, count):
    mean, unused_scale, factor = norm_of(sums, gain, count)
    return inner * sigmoid(inner) + (pre_two - mean) * factor + shift


def project(w_qkv_ref, act_two_halves, head_width, qkv_ref):
    channels = act_two_halves.shape[0] // 2
    rows = folded(dot(w_qkv_ref[...], act_two_halves), 0)
    qkv_ref[:channels] = rows[:channels] * (LOG2_E / math.sqrt(head_width))
    qkv_ref[channels:] = rows[channels:]


def outlet_kernel(
    lon, count, block_size, step_size, quantities,
    state_ref, inner_ref, pre_two_ref, sums_two_ref, vectors_ref,
    weights_ref,
    out_ref, packed_ref, mixed_ref, top_ref, weight_ref,
    query_ref,
):
    cells, channels = inner_ref.shape
    w_mixer_ref = part_of(weights_ref, FORWARD_ROWS, "mixer")
    w_velocity_ref = part_of(weights_ref, FORWARD_ROWS, "out")
    w_heads = side_by_side(part_of(weights_ref, FORWARD_ROWS, "heads"), channels)
    act_two = act_two_of(
        inner_ref[...], pre_two_ref[...], sums_two_ref[...], vectors_ref[2:3], vectors_ref[3:4], count
    )
    projected = folded(dot(beside(act_two), jnp.concatenate([w_heads, w_heads], axis=0)), 1)
    query = projected[:, : HEADS * channels]
    query_high = query.astype(BF16).astype(F32)
    channel = lax.rem(lax.broadcasted_iota(jnp.int32, query.shape, 1), channels)
    query_ref[...] = jnp.where(channel < channels // 2, query_high, query - query_high).astype(BF16)
    key = projected[:, HEADS * channels : (HEADS + 1) * channels]
    key_high, key_low = halves((key * (LOG2_E / math.sqrt(channels // HEADS))).T)
    value = projected[:, (HEADS + 1) * channels :]
    heads = heads_of(channels, cells, block_size)

    def scores_of(turn):
        rows, lanes = heads[turn]
        right = [half[rows, lanes] for half in (key_high, key_low, key_high, key_low)]
        start = turn % HEADS * channels
        return dot(query_ref[lanes, start : start + channels], jnp.concatenate(right, axis=0))

    following = scores_of(0)
    for turn, (rows, lanes) in enumerate(heads):
        scores = following
        if turn + 1 < len(heads):
            following = scores_of(turn + 1)
        top = jnp.max(scores, axis=1, keepdims=True)
        powers = jnp.exp2(scores - top)
        weight = 1.0 / jnp.sum(powers, axis=1, keepdims=True)
        high, low = halves(powers)
        right = beside(of_head(value[lanes], rows))
        own = folded(dot(high, right) + dot(low, right), 1) * weight
        all_top, all_weight = [jnp.broadcast_to(part, own.shape) for part in (top, weight)]
        if rows.start:
            own = own + mixed
            all_top, all_weight = of_head(all_top, rows, tops), of_head(all_weight, rows, weights)
        mixed, tops, weights = own, all_top, all_weight
        if rows.stop == channels:
            mixed_ref[lanes], top_ref[lanes], weight_ref[lanes] = mixed, tops, weights
    act_three = act_two + folded(dot(beside(mixed_ref[...]), doubled(w_mixer_ref, channels)), 1)
    parts = folded(dot(w_velocity_ref[...], stacked(act_three.T)), 0)
    forcing = jnp.concatenate([vectors_ref[GROUP:]] * (cells // channels), axis=1)
    for column, lon_offset in enumerate((-1, 0, 1)):
        total = None
        for row, lat_offset in enumerate((-1, 0, 1)):
            start = (row * 3 + column) * 2 * GROUP
            part = parts[start : start + 2 * GROUP]
            if lat_offset:
                part = lat_moved(part, lat_offset, lon)
            total = part if total is None else total + part
        forcing = forcing + (lon_moved(total, lon_offset, lon) if lon_offset else total)
    state = state_ref[...]
    flows = state[GROUP:]
    out_ref[:GROUP] = advected(state, step_size, lon)
    out_ref[GROUP:] = flows + step_size * (forcing - flows)
    put_packed(packed_ref, out_ref[...], quantities)


def outlet_back_kernel(
    lon, count, block_size, step_size, quantities, sections, step,
    ids_ref,
    state_ref, d_next_ref, cots_ref, inner_ref, pre_two_ref, sums_two_ref, vectors_ref,
    mixed_ref, top_ref, weight_ref,
    weights_ref,
    acc_qkv_ref, acc_mixer_ref, acc_velocity_ref, acc_small_ref,
    d_state_ref, d_two_ref, sums_ref,
    out_qkv_ref, out_mixer_ref, out_velocity_ref, out_small_ref,
    d_mixed_ref, d_qkv_ref, seed_ref, qkv_ref, mixed_rows_ref, top_rows_ref,
):
    channels = inner_ref.shape[1]
    back = functools.partial(part_of, weights_ref, BACK_ROWS)
    w_qkv_ref, w_mixer_ref, w_mixer_back_ref = back("qkv"), back("mixer"), back("mixer_back")
    w_qkv_back = side_by_side(back("qkv_back"), 2 * channels)
    w_velocity_back = side_by_side(back("out_back"), 2 * channels)[:, : 36 * GROUP]
    cells = inner_ref.shape[0]
    heads = heads_of(channels, cells, block_size)

    state = state_ref[...]
    packed = cots_ref[lax.rem(ids_ref[0] - step + sections, sections)]
    put_groups(seed_ref, packed[: 3 * quantities])
    seed = seed_ref[...] + d_next_ref[...]
    amount, east, north = state[:GROUP], state[GROUP : 2 * GROUP], state[2 * GROUP :]
    d_amount = seed[:GROUP]
    d_lon = step_size * along_lon(d_amount, lon)
    d_lat = step_size * along_lat(d_amount, lon)
    d_state_ref[:GROUP] = d_amount + d_lon * east + d_lat * north
    d_state_ref[GROUP : 2 * GROUP] = (1.0 - step_size) * seed[GROUP : 2 * GROUP] + d_lon * amount
    d_state_ref[2 * GROUP :] = (1.0 - step_size) * seed[2 * GROUP :] + d_lat * amount
    d_forcing = step_size * seed[GROUP:]
    pieces = []
    for lat_offset in (-1, 0, 1):
        moved_rows = lat_moved(d_forcing, -lat_offset, lon) if lat_offset else d_forcing
        for lon_offset in (-1, 0, 1):
            pieces.append(lon_moved(moved_rows, -lon_offset, lon) if lon_offset else moved_rows)
    d_parts = stacked(jnp.concatenate(pieces, axis=0))
    d_three = folded(dot(w_velocity_back, d_parts), 0)
    d_three_halves = stacked(d_three)
    d_mixed_ref[...] = folded(dot(w_mixer_back_ref[...], d_three_halves), 0) * weight_ref[...].T
    mixed_rows_ref[...] = mixed_ref[...].T
    top_rows_ref[...] = top_ref[...].T
    act_two = act_two_of(
        inner_ref[...], pre_two_ref[...], sums_two_ref[...], vectors_ref[2:3], vectors_ref[3:4], count
    ).T
    act_two_halves = stacked(act_two)
    project(w_qkv_ref, act_two_halves, channels // HEADS, qkv_ref)
    d_mixed_cells = d_mixed_ref[...].T
    query_cells = qkv_ref[:channels].T

    def products_of(turn):
        rows, lanes = heads[turn]
        scores = row_products(qkv_ref[below(rows, channels), lanes], qkv_ref[rows, lanes])
        return scores, row_products(qkv_ref[below(rows, 2 * channels), lanes], d_mixed_ref[rows, lanes])

    following = products_of(0)
    for turn, (rows, lanes) in enumerate(heads):
        scores, d_powers = following
        if turn + 1 < len(heads):
            following = products_of(turn + 1)
        inner_sum = jnp.sum(d_mixed_ref[rows, lanes] * mixed_rows_ref[rows, lanes], axis=0, keepdims=True)
        powers = jnp.exp2(scores - top_rows_ref[rows.start : rows.start + 1, lanes])
        power_high, power_low = halves(powers)
        d_high, d_low = halves(powers * (d_powers - inner_sum))
        right = beside(of_head(d_mixed_cells[lanes], rows))
        d_value = dot(power_high, right) + dot(power_low, right) + (d_value if rows.start else 0.0)
        right = beside(of_head(query_cells[lanes], rows))
        d_key = dot(d_high, right) + dot(d_low, right) + (d_key if rows.start else 0.0)
        key_halves = stacked(qkv_ref[below(rows, channels), lanes])
        d_query = folded(dot(key_halves, d_high) + dot(key_halves, d_low), 0)
        d_qkv_ref[rows, lanes] = d_query * (1.0 / math.sqrt(channels // HEADS))
        if rows.stop == channels:
            d_qkv_ref[channels : 2 * channels, lanes] = folded(d_key, 1).T * (1.0 / LOG2_E)
            d_qkv_ref[2 * channels :, lanes] = folded(d_value, 1).T
    d_qkv_halves = stacked(d_qkv_ref[...])
    d_two = (d_three + folded(dot(w_qkv_back, d_qkv_halves), 0)).T
    d_two_ref[...] = d_two
    mean, scale, unused_factor = norm_of(sums_two_ref[...], vectors_ref[2:3], count)
    sums = sums_of(d_two, pre_two_ref[...] - mean)
    sums_ref[...] = sums

    def pairs(left, right):
        return folded(folded(dot(left, right, 1, 1), 0), 1)

    mixed_halves = stacked(mixed_rows_ref[...])
    act_three = act_two + folded(dot(w_mixer_ref[...], mixed_halves), 0)
    out_velocity_ref[...] = acc_velocity_ref[...] + pairs(d_parts, stacked(act_three))
    out_mixer_ref[...] = acc_mixer_ref[...] + pairs(mixed_halves, d_three_halves)
    out_qkv_ref[...] = acc_qkv_ref[...] + pairs(act_two_halves, d_qkv_halves)
    bias = jnp.sum(d_forcing, axis=1, keepdims=True)
    row = lax.broadcasted_iota(jnp.int32, (GROUP, channels), 0)
    small = jnp.where(row == 0, sums[1:2] * scale, jnp.where(row == 1, sums[0:1], 0.0))
    out_small_ref[:GROUP] = acc_small_ref[:GROUP] + small
    out_small_ref[GROUP:] = acc_small_ref[GROUP:] + bias


def d_pre_of(d_normed, centred, sums, all_grad_sums, gain, count):
    unused_mean, scale, factor = norm_of(sums, gain, count)
    d_spread = -0.5 * gain * scale * scale * scale * all_grad_sums[1:2]
    return factor * (d_normed - all_grad_sums[0:1] / count) + (2.0 * d_spread / count) * centred


def weight_pairs(acc_ref, out_ref, left_halves, patches_ref, lon):
    cells = patches_ref.shape[0] - 2 * lon
    width = patches_ref.shape[1] // 3
    for tap in range(9):
        row, column = divmod(8 - tap, 3)
        right = patches_ref[lon * row : lon * row + cells, column * width : (column + 1) * width]
        out_ref[tap] = acc_ref[tap] + folded(folded(dot(left_halves, right), 0), 1)


def middle_back_kernel(
    lon, count,
    d_two_ref, pre_two_ref, sums_two_ref, all_two_ref,
    pre_one_ref, sums_one_ref, vectors_ref, weights_ref,
    acc_small_ref,
    d_normed_ref, sums_ref, act_ref, patches_ref, out_small_ref,
):
    w_second_back_ref = part_of(weights_ref, BACK_ROWS, "second")
    sums_two = sums_two_ref[...]
    d_pre = d_pre_of(
        d_two_ref[...], pre_two_ref[...] - sums_two[0:1] / count, sums_two, all_two_ref[...],
        vectors_ref[2:3], count,
    )
    fill_patches(patches_ref, d_pre, lon)
    d_act = conv_patches(patches_ref, w_second_back_ref, lon)
    mean, scale, factor = norm_of(sums_one_ref[...], vectors_ref[0:1], count)
    centred = pre_one_ref[...] - mean
    normed = centred * factor + vectors_ref[1:2]
    gate = sigmoid(normed)
    d_normed = d_act * gate * (1.0 + normed * (1.0 - gate))
    d_normed_ref[...] = d_normed
    sums = sums_of(d_normed, centred)
    sums_ref[...] = sums
    act_ref[...] = normed * gate
    row = lax.broadcasted_iota(jnp.int32, sums.shape, 0)
    small = jnp.where(row == 0, sums[1:2] * scale, jnp.where(row == 1, sums[0:1], 0.0))
    out_small_ref[...] = acc_small_ref[...] + small


def middle_grads_kernel(lon, act_ref, patches_ref, acc_ref, out_ref):
    weight_pairs(acc_ref, out_ref, stacked(act_ref[...].T), patches_ref, lon)


def inlet_grads_kernel(
    lon, act_ref, patches_ref, d_inner_ref, state_ref, acc_first_ref, acc_input_ref, acc_inner_ref,
    out_first_ref, out_input_ref, out_inner_ref, rows_ref,
):
    weight_pairs(acc_first_ref, out_first_ref, stacked(act_ref[...].T), patches_ref, lon)
    d_inner = d_inner_ref[...]
    out_inner_ref[...] = acc_inner_ref[...] + d_inner
    cells = d_inner.shape[0]
    blank = jnp.zeros((lon, rows_ref.shape[1]), BF16)
    rows_ref[:lon] = blank
    rows_ref[lon + cells :] = blank
    rows_ref[lon : lon + cells] = beside(d_inner)
    moving_halves = stacked(inlet_channels(state_ref[...], lon))
    for place in range(3):
        start = lon * (2 - place)
        out_input_ref[place] = acc_input_ref[place] + folded(
            folded(dot(moving_halves, rows_ref[start : start + cells]), 0), 1
        )


def inlet_back_kernel(
    lon, count, quantities,
    d_normed_ref, pre_one_ref, sums_one_ref, all_one_ref, vectors_ref,
    inner_ref, d_two_ref, d_state_in_ref, weights_ref,
    d_state_ref, packed_ref, act_ref, patches_ref, d_inner_ref,
    rows_ref,
):
    cells = inner_ref.shape[0]
    w_first_back_ref = part_of(weights_ref, BACK_ROWS, "first")
    w_input_back_ref = part_of(weights_ref, BACK_ROWS, "moving")
    sums_one = sums_one_ref[...]
    d_pre = d_pre_of(
        d_normed_ref[...], pre_one_ref[...] - sums_one[0:1] / count, sums_one, all_one_ref[...],
        vectors_ref[0:1], count,
    )
    fill_patches(patches_ref, d_pre, lon)
    d_act = conv_patches(patches_ref, w_first_back_ref, lon) + d_two_ref[...]
    inner = inner_ref[...]
    gate = sigmoid(inner)
    d_inner = d_act * gate * (1.0 + inner * (1.0 - gate))
    act_ref[...] = inner * gate
    d_inner_ref[...] = d_inner
    blank = jnp.zeros((lon, rows_ref.shape[1]), BF16)
    rows_ref[:lon] = blank
    rows_ref[lon + cells :] = blank
    rows_ref[lon : lon + cells] = beside(d_inner)
    rows = [rows_ref[lon * place : lon * place + cells] for place in range(3)]
    d_moving = folded(dot(jnp.concatenate(rows, axis=1), doubled(w_input_back_ref, inner_ref.shape[1])), 1).T
    size = 5 * GROUP
    d_groups = (
        lon_moved(d_moving[:size], 1, lon)
        + d_moving[size : 2 * size]
        + lon_moved(d_moving[2 * size : 3 * size], -1, lon)
    )
    d_state = d_state_in_ref[...] + d_groups[: 3 * GROUP]
    d_state_ref[:GROUP] = (
        d_state[:GROUP]
        - along_lon(d_groups[3 * GROUP : 4 * GROUP], lon)
        - along_lat(d_groups[4 * GROUP :], lon)
    )
    d_state_ref[GROUP:] = d_state[GROUP:]
    put_packed(packed_ref, d_state_ref[...], quantities)


def put_groups(out_ref, rows):
    size = rows.shape[0] // 3
    out_ref[...] = jnp.zeros(out_ref.shape, F32)
    for group in range(3):
        out_ref[group * GROUP : group * GROUP + size] = rows[group * size : (group + 1) * size]


def put_packed(out_ref, grouped, size):
    out_ref[...] = jnp.zeros(out_ref.shape, F32)
    for group in range(3):
        out_ref[group * size : (group + 1) * size] = grouped[group * GROUP : group * GROUP + size]


def fetched(far_refs, near_refs, done_ref):
    copies = [
        pltpu.make_async_copy(far_ref, near_ref, done_ref.at[place])
        for place, (far_ref, near_ref) in enumerate(zip(far_refs, near_refs))
    ]
    for copy in copies:
        copy.start()
    return copies


def enter_kernel(plan, ids_ref, order_ref, state_ref, cot_ref, *refs):
    out_refs, (near_ref, near_cot_ref, rows_ref, done_ref) = refs[:-4], refs[-4:]
    copies = fetched([state_ref, cot_ref], [near_ref, near_cot_ref], done_ref)
    size = rows_ref.shape[0]
    copies[0].wait()
    place = order_ref[0, plan.slot(ids_ref[0], ids_ref[1])]
    for row in range(size):
        rows_ref[row : row + 1] = near_ref[row, pl.ds(place, 1)]
    put_groups(out_refs[0].at[: 3 * GROUP], rows_ref[...])
    copies[1].wait()
    for steps, out_ref in enumerate(out_refs):
        start = 0 if steps else 3 * GROUP
        target = lax.rem(ids_ref[0] + steps, plan.sections)
        place = order_ref[0, plan.slot(target, ids_ref[1])]
        out_ref[start:] = jnp.zeros((2 * GROUP, out_ref.shape[1]), F32)
        for row in range(size):
            out_ref[start + row : start + row + 1] = near_cot_ref[row, pl.ds(place, 1)]


def leave_kernel(plan, ids_ref, *refs):
    values_ref = refs[-1]
    size = refs[0].shape[0]
    for step in range(plan.sections):
        values_ref[step, :size] = refs[step][...]
        if step:
            values_ref[step, size:] = refs[plan.sections + step - 1][...]
        else:
            values_ref[step, size:] = jnp.zeros(refs[0].shape, F32)
    for steps, out_ref in enumerate(refs[2 * plan.sections - 1 : -1]):
        out_ref[...] = values_ref[lax.rem(ids_ref[0] + steps, plan.sections)]


def arrive_kernel(plan, start, ids_ref, order_ref, kept_ref, *refs):
    section, dp = ids_ref[0], ids_ref[1]
    out_ref = refs[-1]
    size = kept_ref.shape[0] // 2
    early, late = refs[: plan.sections], refs[plan.sections : -1]
    if late:
        kept_late_ref, *late = late
    for steps, ref in enumerate(early):
        source = lax.rem(section - steps + plan.sections, plan.sections)
        place = order_ref[0, plan.slot(source, dp)]
        value = ref[start : start + size]
        if late:
            value = jnp.where(section == 0, late[steps][...], value)
        if plan.halved and not steps:
            kept = kept_ref[start : start + size]
            if late:
                kept = jnp.where(section == 0, kept_late_ref[...], kept)
            value = jnp.where(plan.stays(section, dp), kept, value)
        for row in range(out_ref.shape[0]):
            out_ref[row, pl.ds(place, 1)] = value[row : row + 1]


def put_conv_weight(out_ref, taps):
    for tap, weight in enumerate(taps):
        rows = weight.shape[0]
        out_ref[tap * rows : (tap + 1) * rows] = beside(weight)


def weights_kernel(
    lon, quantities,
    w_input_ref, maps_ref, b_input_ref, w_first_ref, w_second_ref,
    w_query_ref, w_key_ref, w_value_ref, w_mixer_ref, w_velocity_ref,
    gain_one_ref, shift_one_ref, gain_two_ref, shift_two_ref, b_velocity_ref,
    static_part_ref, forward_ref, back_ref, vectors_ref,
    patches_ref, weight_ref, taps_ref, rows_ref, *near_refs,
):
    forward = functools.partial(part_of, forward_ref, FORWARD_ROWS)
    back = functools.partial(part_of, back_ref, BACK_ROWS)
    near_refs, done_ref = near_refs[:-1], near_refs[-1]
    copies = fetched(
        [w_input_ref, maps_ref, b_input_ref, w_first_ref, w_second_ref,
         w_query_ref, w_key_ref, w_value_ref, w_mixer_ref, w_velocity_ref,
         gain_one_ref, shift_one_ref, gain_two_ref, shift_two_ref, b_velocity_ref],
        near_refs, done_ref,
    )
    (
        w_input_ref, maps_ref, b_input_ref, w_first_ref, w_second_ref,
        w_query_ref, w_key_ref, w_value_ref, w_mixer_ref, w_velocity_ref,
        gain_one_ref, shift_one_ref, gain_two_ref, shift_two_ref, b_velocity_ref,
    ) = near_refs
    channels = w_input_ref.shape[2]
    moving = 5 * quantities
    statics = maps_ref.shape[0]
    taps_ref[...] = jnp.zeros(taps_ref.shape, F32)
    rows_ref[...] = jnp.zeros(rows_ref.shape, F32)
    copies[0].wait()
    for tap in range(9):
        row, column = divmod(tap, 3)
        for group in range(5):
            start = (column * 5 + group) * GROUP
            taps_ref[9 + row, start : start + quantities] = w_input_ref[
                tap, group * quantities : (group + 1) * quantities
            ]
        taps_ref[tap, :statics] = w_input_ref[tap, moving:]
    put_conv_weight(forward("moving"), [taps_ref[9 + row] for row in range(3)])
    put_conv_weight(back("moving"), [taps_ref[11 - row].T for row in range(3)])
    put_conv_weight(weight_ref, [taps_ref[tap] for tap in range(9)])
    copies[1].wait()
    copies[2].wait()
    maps = jnp.concatenate(
        [maps_ref[...], jnp.zeros((channels - statics, maps_ref.shape[1]), F32)], axis=0
    )
    fill_patches(patches_ref, maps.T, lon)
    static_part_ref[...] = conv_patches(patches_ref, weight_ref, lon) + b_input_ref[...]
    for copy in copies[3:]:
        copy.wait()
    put_conv_weight(forward("first"), [w_first_ref[tap] for tap in range(9)])
    put_conv_weight(forward("second"), [w_second_ref[tap] for tap in range(9)])
    put_conv_weight(back("first"), [w_first_ref[8 - tap].T for tap in range(9)])
    put_conv_weight(back("second"), [w_second_ref[8 - tap].T for tap in range(9)])
    parts = [ref[...] for ref in (w_query_ref, w_key_ref, w_value_ref)]
    turned = [part.T for part in parts]
    width = channels // HEADS
    repeated = [turned[0][head * width : (head + 1) * width] for head in range(HEADS) for unused in range(HEADS)]
    heads = jnp.concatenate([jnp.concatenate(repeated, axis=0).T, parts[1], parts[2]], axis=1)
    put_blocks(forward("heads"), beside(heads))
    put_conv_weight(forward("mixer"), [w_mixer_ref[...]])
    back("qkv")[...] = left_form(jnp.concatenate(turned, axis=0))
    put_blocks(back("qkv_back"), left_form(jnp.concatenate(parts, axis=1)))
    back("mixer")[...] = left_form(w_mixer_ref[...].T)
    back("mixer_back")[...] = left_form(w_mixer_ref[...])
    for tap in range(9):
        for group in range(2):
            start = (tap * 2 + group) * GROUP
            rows_ref[start : start + quantities] = w_velocity_ref[
                tap, group * quantities : (group + 1) * quantities
            ]
    size = 18 * GROUP
    vectors_ref[...] = jnp.zeros(vectors_ref.shape, F32)
    for place, ref in enumerate((gain_one_ref, shift_one_ref, gain_two_ref, shift_two_ref)):
        vectors_ref[place : place + 1] = ref[...]
    bias = jnp.concatenate([b_velocity_ref[...], jnp.zeros((1, channels - 2 * quantities), F32)], axis=1)
    bias = jnp.broadcast_to(bias, (channels, channels)).T
    for group in range(2):
        start = (group + 1) * GROUP
        vectors_ref[start : start + quantities] = bias[group * quantities : (group + 1) * quantities]
    forward("out")[...] = left_form(rows_ref[:size])
    put_blocks(back("out_back"), left_form(rows_ref[...].T[:, :size]))


def index_of(ids_ref, plan, bits):
    own = ids_ref[0] * plan.dp + ids_ref[1]
    return sum(lax.rem(own // bit, 2) << place for place, bit in enumerate(bits))


def deal(total_ref, own, out_refs):
    rows = out_refs[0].shape[0]
    for turn, out_ref in enumerate(out_refs):
        out_ref[...] = total_ref[pl.ds(pl.multiple_of((own ^ turn) * rows, GROUP), rows)]


def pack_kernel(
    plan, bits, lon, statics, ids_ref, maps_ref, inner_ref, first_ref, second_ref, moving_ref,
    qkv_ref, mixer_ref, velocity_ref, small_one_ref, small_two_ref, *refs,
):
    out_refs, total_ref, patches_ref = refs[:-2], refs[-2], refs[-1]
    cells, channels = inner_ref.shape
    d_inner = inner_ref[...]
    fill_patches(patches_ref, d_inner, lon)
    width = patches_ref.shape[1] // 3
    maps = maps_ref[...]
    blank = jnp.zeros((-statics % GROUP, cells), F32)
    maps = jnp.concatenate([maps, blank], axis=0)
    rows = maps.shape[0]
    left = jnp.concatenate(halves(maps), axis=0)
    start = 0

    def put(value):
        nonlocal start
        total_ref[start : start + value.shape[0]] = value
        start += value.shape[0]

    for tap in range(9):
        put(first_ref[tap])
    for tap in range(9):
        put(second_ref[tap])
    for tap in range(9):
        row, column = divmod(8 - tap, 3)
        right = patches_ref[lon * row : lon * row + cells, column * width : (column + 1) * width]
        put(folded(folded(dot(left, right), 0), 1))
    for place in range(3):
        put(moving_ref[place, : 15 * GROUP])
    for part in range(3):
        put(qkv_ref[:, part * channels : (part + 1) * channels])
    put(mixer_ref[...])
    put(velocity_ref[...])
    put(small_one_ref[...])
    put(small_two_ref[...])
    put(jnp.zeros((GROUP, channels), F32) + jnp.sum(d_inner, axis=0, keepdims=True))
    total_ref[start:] = jnp.zeros((total_ref.shape[0] - start, channels), F32)
    deal(total_ref, index_of(ids_ref, plan, bits), out_refs)


def reduce_kernel(plan, bits, count, ids_ref, *refs):
    total_ref = refs[-1]
    total = refs[0][...]
    for ref in refs[1:count]:
        total = total + ref[...]
    if not bits:
        refs[count][...] = total
        return
    total_ref[...] = total
    deal(total_ref, index_of(ids_ref, plan, bits), refs[count:-1])


def gather_rows(plan, bits, ids_ref, part_refs, out_ref):
    own = index_of(ids_ref, plan, bits)
    rows = part_refs[0].shape[0]
    for turn, ref in enumerate(part_refs):
        out_ref[pl.ds(pl.multiple_of((own ^ turn) * rows, GROUP), rows)] = ref[...]


def gather_kernel(plan, bits, ids_ref, *refs):
    gather_rows(plan, bits, ids_ref, refs[:-1], refs[-1])


def unpack_kernel(
    plan, bits, quantities, statics, ids_ref, *refs,
):
    count = 1 << len(bits)
    (
        input_ref, bias_ref, first_ref, gain_one_ref, shift_one_ref, second_ref, gain_two_ref, shift_two_ref,
        query_ref, key_ref, value_ref, mixer_ref, velocity_ref, velocity_bias_ref, total_ref,
    ) = refs[count:]
    gather_rows(plan, bits, ids_ref, refs[:count], total_ref)
    channels = mixer_ref.shape[0]
    moving = 5 * quantities
    start = 0

    def take(rows):
        nonlocal start
        start += rows
        return total_ref[start - rows : start]

    for tap in range(9):
        first_ref[tap] = take(channels)
    for tap in range(9):
        second_ref[tap] = take(channels)
    for tap in range(9):
        input_ref[tap, moving:] = take(statics + -statics % GROUP)[:statics]
    for row in range(3):
        for column in range(3):
            for group in range(5):
                rows = take(GROUP)
                input_ref[row * 3 + column, group * quantities : (group + 1) * quantities] = rows[:quantities]
    query_ref[...] = take(channels)
    key_ref[...] = take(channels)
    value_ref[...] = take(channels)
    mixer_ref[...] = take(channels)
    for tap in range(9):
        for group in range(2):
            velocity_ref[tap, group * quantities : (group + 1) * quantities] = take(GROUP)[:quantities]
    small = take(GROUP)
    gain_one_ref[...], shift_one_ref[...] = small[0:1], small[1:2]
    small = take(GROUP)
    gain_two_ref[...], shift_two_ref[...] = small[0:1], small[1:2]
    velocity_bias_ref[...] = take(2 * GROUP)
    bias_ref[...] = take(GROUP)[0:1]


def call(kernel, outs, scratch=(), aliases=None, name=None, scalars=0, kinds=None, far_in=(), limit=None):
    kinds = kinds or [F32] * len(outs)

    def run(*operands):
        places = [pltpu.SMEM] * scalars + [pltpu.VMEM] * (len(operands) - scalars)
        for place in far_in:
            places[place] = pltpu.HBM
        return pl.pallas_call(
            kernel,
            out_shape=tuple(jax.ShapeDtypeStruct(shape, kind) for shape, kind in zip(outs, kinds)),
            in_specs=[pl.BlockSpec(memory_space=place) for place in places],
            out_specs=tuple(pl.BlockSpec(memory_space=pltpu.VMEM) for unused in outs),
            scratch_shapes=scratch,
            input_output_aliases=aliases or {},
            compiler_params=pltpu.CompilerParams(vmem_limit_bytes=limit or VMEM_LIMIT),
            name=name,
        )(*operands)

    return run


VMEM_LIMIT = 24 * 1024 * 1024
ALONE_LIMIT = 56 * 1024 * 1024

FORWARD_ROWS = dict(moving=384, first=1152, second=1152, heads=768, mixer=128, out=288)
BACK_ROWS = dict(moving=384, first=1152, second=1152, qkv=768, mixer=256, mixer_back=256, qkv_back=768, out_back=512)


def part_of(ref, rows, name):
    start = 0
    for other, size in rows.items():
        if other == name:
            return ref.at[start : start + size]
        start += size
    return None


def side_by_side(ref, rows):
    return jnp.concatenate([ref[start : start + rows] for start in range(0, ref.shape[0], rows)], axis=1)


def put_blocks(ref, value):
    rows, width = value.shape[0], ref.shape[1]
    for place in range(ref.shape[0] // rows):
        block = value[:, place * width : (place + 1) * width]
        if block.shape[1] < width:
            block = jnp.concatenate([block, jnp.zeros((rows, width - block.shape[1]), value.dtype)], axis=1)
        ref[place * rows : (place + 1) * rows] = block


def left_form(weight):
    return jnp.concatenate([jnp.concatenate([half, half], axis=1) for half in halves(weight)], axis=0)


def in_groups(array, axis, groups):
    shape = array.shape
    split = shape[:axis] + (groups, shape[axis] // groups) + shape[axis + 1 :]
    array = array.reshape(split)
    pads = [(0, 0)] * array.ndim
    pads[axis + 1] = (0, GROUP - split[axis + 1])
    return jnp.pad(array, pads).reshape(shape[:axis] + (groups * GROUP,) + shape[axis + 1 :])


def from_groups(array, axis, groups, size):
    shape = array.shape
    array = array.reshape(shape[:axis] + (groups, GROUP) + shape[axis + 1 :])
    array = lax.slice_in_dim(array, 0, size, axis=axis + 1)
    return array.reshape(shape[:axis] + (groups * size,) + shape[axis + 1 :])


class Plan:
    def __init__(self, sections, dp):
        self.sections, self.dp = sections, dp
        self.halved = sections == 4 and dp >= 4
        self.half = dp // 2
        bits = [1 << place for place in range((sections * dp).bit_length() - 1)]
        dp_bits = [bit for bit in bits if bit < dp]
        section_bits = [bit for bit in bits if bit >= dp]
        if self.halved:
            self.sum_rounds = in_pairs(dp_bits[:-1]) + in_pairs(section_bits)
        else:
            self.sum_rounds = in_pairs(dp_bits) + [section_bits[:1]]
        self.all_rounds = [dp_bits[:1]] + in_pairs(section_bits) + in_pairs(dp_bits[1:])

    def slot(self, section, home):
        if not self.halved:
            return section
        return lax.rem(home // self.half + section // 2 + home, 2) * 2 + lax.rem(section, 2)

    def stays(self, section, dp):
        return lax.rem(section // 2 + dp, 2) == 0

    def other(self, section, dp):
        return dp ^ self.half if self.halved and (section // 2 + dp) % 2 else dp

    def to_workers(self, steps):
        return [
            (section * self.dp + home, self.joint((section + steps) % self.sections, home))
            for section in range(self.sections)
            for home in range(self.dp)
        ]

    def to_homes(self, steps):
        return [
            (section * self.dp + own, (section + steps) % self.sections * self.dp + self.other(section, own))
            for section in range(self.sections)
            for own in range(self.dp)
        ]

    def to_first_home(self, steps):
        return [(source, target) for source, target in self.to_homes(steps) if target < self.dp]

    def joint(self, section, home):
        return section * self.dp + self.other(section, home)


def in_pairs(bits):
    return [bits[start : start + 2] for start in range(0, len(bits), 2)]


def masks_of(bits):
    return [sum(bit for place, bit in enumerate(bits) if turn >> place & 1) for turn in range(1, 1 << len(bits))]


def exchanged(value, mask):
    size = lax.axis_size("section") * lax.axis_size("dp")
    return lax.ppermute(value, ("section", "dp"), [(own, own ^ mask) for own in range(size)])


def moved(value, pairs):
    going = [(source, target) for source, target in pairs if source != target]
    if not going:
        return value
    return lax.ppermute(value, ("section", "dp"), going)


def micro_sum(plan, value, first_core, work=None):
    if not plan.halved or plan.half != 4:
        for bits in plan.sum_rounds:
            value = value + sum(exchanged(value, mask) for mask in masks_of(bits))
        return value, work and work[0](*work[1])
    value = value + exchanged(value, 1)
    if work:
        value, operands = lax.optimization_barrier((value, work[1]))
    plane = masks_of([plan.dp, 2 * plan.dp])
    other = [mask ^ 2 for mask in plane + [0]]
    own = range(plan.sections * plan.dp)
    total = value * first_core
    for turn in range(4):
        pairs = [(device, device ^ other[turn]) for device in own if device & 1]
        if turn < 3:
            pairs += [(device, device ^ plane[turn]) for device in own if not device & 1]
        total = total + lax.ppermute(value, ("section", "dp"), pairs)
    done = None
    if work:
        total, done = lax.optimization_barrier((total, work[0](*operands)))
    return total + exchanged(total, 1), done


def on_device(
    state_start,
    static_maps,
    grouping,
    cotangent,
    w_input,
    b_input,
    w_first,
    gain_first,
    shift_first,
    w_second,
    gain_second,
    shift_second,
    w_query,
    w_key,
    w_value,
    w_mixer,
    w_velocity,
    b_velocity,
):
    segments = lax.axis_size("section")
    plan = Plan(segments, lax.axis_size("dp"))
    micro_count = segments // 2
    per_micro = state_start.shape[0] // micro_count
    cells = state_start.shape[2]
    lon = cells // LAT
    count = float(per_micro * cells * plan.dp)
    step_size = 2.0 / segments
    block_size = ATT_ROWS * lon
    channels = w_first.shape[2]
    quantities = state_start.shape[1] // 3
    statics = static_maps.shape[0]
    ids = jnp.stack([lax.axis_index("section"), lax.axis_index("dp")]).astype(jnp.int32)

    plane = (cells, channels)
    small = (GROUP, channels)
    conv = (9 * channels, 2 * channels)
    patches = pltpu.VMEM((cells + 2 * lon, 6 * channels), BF16)
    wide = pltpu.VMEM((3 * channels, cells), F32)
    narrow = pltpu.VMEM((channels, cells), F32)
    state_shape = (3 * GROUP, cells)

    packed = (2 * GROUP, cells)

    def near(*arrays):
        return [pltpu.VMEM(array.shape, F32) for array in arrays] + [pltpu.SemaphoreType.DMA((len(arrays),))]

    state_rows, cot_rows = jnp.swapaxes(state_start, 0, 1), jnp.swapaxes(cotangent[0], 0, 1)
    entry, *sent_cots = call(
        functools.partial(enter_kernel, plan), [(5 * GROUP, cells)] + [packed] * (segments - 1),
        [pltpu.VMEM(state_rows.shape, F32)] * 2
        + [pltpu.VMEM((3 * quantities, cells), F32), pltpu.SemaphoreType.DMA((2,))],
        name="enter", scalars=2, far_in=[2, 3], limit=ALONE_LIMIT,
    )(ids, grouping, state_rows, cot_rows)
    arrived = moved(entry, plan.to_workers(0))
    first_core = (1.0 - lax.rem(ids[1], 2).astype(F32)) * jnp.ones(small, F32)
    w_velocity_rows = jnp.swapaxes(w_velocity, 1, 2)
    weights = (
        w_input, static_maps, b_input[None], w_first, w_second, w_query, w_key, w_value, w_mixer, w_velocity_rows,
        gain_first[None], shift_first[None], gain_second[None], shift_second[None], b_velocity[None],
    )
    columns = 2 * channels
    static_part, forward_weights, back_weights, vectors = call(
        functools.partial(weights_kernel, lon, quantities),
        [plane, (sum(FORWARD_ROWS.values()), columns), (sum(BACK_ROWS.values()), columns), (3 * GROUP, channels)],
        [patches, pltpu.VMEM(conv, BF16), pltpu.VMEM((12, channels, channels), F32),
         pltpu.VMEM((columns, channels), F32)] + near(*weights),
        name="weights", kinds=[F32, BF16, BF16, F32], far_in=range(15), limit=ALONE_LIMIT,
    )(*weights)

    inlet = call(
        functools.partial(inlet_kernel, lon), [plane, plane, small], [patches], name="inlet"
    )
    middle = call(
        functools.partial(middle_kernel, lon, count), [plane, small], [patches], name="middle"
    )
    outlet = call(
        functools.partial(outlet_kernel, lon, count, block_size, step_size, quantities),
        [state_shape, packed, plane, plane, plane],
        [pltpu.VMEM((cells, HEADS * channels), BF16)], name="outlet",
    )

    def outlet_back(step):
        return call(
            functools.partial(outlet_back_kernel, lon, count, block_size, step_size, quantities, segments, step),
            [state_shape, plane, small, (channels, 3 * channels), (channels, channels),
             (18 * GROUP, channels), (3 * GROUP, channels)],
            [narrow, wide, pltpu.VMEM(state_shape, F32), wide, narrow, narrow],
            {12: 3, 13: 4, 14: 5, 15: 6}, name="outlet_back", scalars=1,
        )

    patch_shape = (cells + 2 * lon, 6 * channels)
    middle_back = call(
        functools.partial(middle_back_kernel, lon, count),
        [plane, small, plane, patch_shape, small],
        aliases={8: 4}, name="middle_back", kinds=[F32, F32, F32, BF16, F32],
    )
    middle_grads = call(
        functools.partial(middle_grads_kernel, lon), [(9, channels, channels)], aliases={2: 0}, name="middle_grads",
    )
    inlet_back = call(
        functools.partial(inlet_back_kernel, lon, count, quantities),
        [state_shape, packed, plane, patch_shape, plane],
        [pltpu.VMEM((cells + 2 * lon, 2 * channels), BF16)], name="inlet_back", kinds=[F32, F32, F32, BF16, F32],
    )
    inlet_grads = call(
        functools.partial(inlet_grads_kernel, lon),
        [(9, channels, channels), (3, channels, channels), plane],
        [pltpu.VMEM((cells + 2 * lon, 2 * channels), BF16)],
        {4: 0, 5: 1, 6: 2}, name="inlet_grads",
    )

    state = entry[: 3 * GROUP]
    path, saved = [], []
    cots = None
    for step in range(segments):
        if not step:
            if not plan.halved:
                arrived = entry
            state, own_cot, inner, pre_one, sums_one = call(
                functools.partial(entered_inlet_kernel, plan, lon), [state_shape, packed, plane, plane, small], [patches],
                name="inlet", scalars=1,
            )(ids, entry, arrived, static_part, forward_weights)
        else:
            inner, pre_one, sums_one = inlet(state, static_part, forward_weights)
        sums_one, unused = micro_sum(plan, sums_one, first_core)
        pre_two, sums_two = middle(pre_one, sums_one, vectors, forward_weights)
        sums_two, unused = micro_sum(plan, sums_two, first_core)
        state_out, state_packed, mixed, top, weight = outlet(
            state, inner, pre_two, sums_two, vectors, forward_weights
        )
        saved.append((state, inner, pre_one, pre_two, sums_one, sums_two, mixed, top, weight))
        path.append(state_packed)
        state = state_out
        if not step:
            state, sent_cots = lax.optimization_barrier((state, sent_cots))
            cots = jnp.stack(
                [own_cot] + [moved(cot, plan.to_workers(steps + 1)) for steps, cot in enumerate(sent_cots)]
            )

    def put_home(start, parts):
        (out,) = call(
            functools.partial(arrive_kernel, plan, start), [state_rows.shape], name="arrive", scalars=2
        )(ids, grouping, *parts)
        return jnp.swapaxes(out, 0, 1)[None]

    acc = dict(
        qkv=jnp.zeros((channels, 3 * channels), F32),
        mixer=jnp.zeros((channels, channels), F32),
        velocity=jnp.zeros((18 * GROUP, channels), F32),
        small_two=jnp.zeros((3 * GROUP, channels), F32),
        second=jnp.zeros((9, channels, channels), F32),
        small_one=jnp.zeros(small, F32),
        first=jnp.zeros((9, channels, channels), F32),
        moving=jnp.zeros((3, channels, channels), F32),
        inner=jnp.zeros(plane, F32),
    )
    d_state = jnp.zeros(state_shape, F32)
    grads = [None] * segments
    inlet_work = None
    path_out = None
    for step in reversed(range(segments)):
        if not step:
            sent = call(
                functools.partial(leave_kernel, plan), [(4 * GROUP, cells)] * segments,
                [pltpu.VMEM((segments, 4 * GROUP, cells), F32)], name="leave", scalars=1,
            )(ids, *path, *grads[1:])
            early = [sent[0]] + [moved(part, plan.to_homes(steps)) for steps, part in enumerate(sent)]
        state, inner, pre_one, pre_two, sums_one, sums_two, mixed, top, weight = saved[step]
        d_partial, d_two, grad_two, acc["qkv"], acc["mixer"], acc["velocity"], acc["small_two"] = outlet_back(step)(
            ids, state, d_state, cots, inner, pre_two, sums_two, vectors,
            mixed, top, weight, back_weights,
            acc["qkv"], acc["mixer"], acc["velocity"], acc["small_two"],
        )
        if not step:
            d_two, grad_two, early = lax.optimization_barrier((d_two, grad_two, early))
            path_out = put_home(0, early)
        work = inlet_work and (inlet_grads, inlet_work + (acc["first"], acc["moving"], acc["inner"]))
        grad_two, done = micro_sum(plan, grad_two, first_core, work)
        if done:
            acc["first"], acc["moving"], acc["inner"] = done
        d_normed, grad_one, act, act_patches, acc["small_one"] = middle_back(
            d_two, pre_two, sums_two, grad_two,
            pre_one, sums_one, vectors, back_weights,
            acc["small_one"],
        )
        grad_one, (acc["second"],) = micro_sum(
            plan, grad_one, first_core, (middle_grads, (act, act_patches, acc["second"]))
        )
        d_state, grads[step], act, act_patches, d_inner = inlet_back(
            d_normed, pre_one, sums_one, grad_one, vectors,
            inner, d_two, d_partial, back_weights,
        )
        inlet_work = (act, act_patches, d_inner, state)
    acc["first"], acc["moving"], acc["inner"] = inlet_grads(*inlet_work, acc["first"], acc["moving"], acc["inner"])
    late = [grads[0]] + [moved(grads[0], plan.to_first_home(steps)) for steps in range(segments)]

    rounds = plan.all_rounds
    rows = 2 * 9 * channels + 9 * (statics + -statics % GROUP) + 45 * GROUP + 4 * channels + 23 * GROUP
    unit = GROUP * segments * plan.dp
    rows = -(-rows // unit) * unit

    def shares(rows, bits):
        return [(rows >> len(bits), channels)] * (1 << len(bits))

    def swap(parts, bits):
        return [parts[0]] + [exchanged(part, mask) for part, mask in zip(parts[1:], masks_of(bits))]

    parts = call(
        functools.partial(pack_kernel, plan, rounds[0], lon, statics), shares(rows, rounds[0]),
        [pltpu.VMEM((rows, channels), F32), patches], name="pack", scalars=1,
    )(
        ids, static_maps, acc["inner"], acc["first"], acc["second"], acc["moving"], acc["qkv"], acc["mixer"],
        acc["velocity"], acc["small_one"], acc["small_two"],
    )
    for place, (bits, later) in enumerate(zip(rounds, rounds[1:] + [[]])):
        parts = swap(parts, bits)
        if not place:
            parts, late = lax.optimization_barrier((parts, late))
        elif place == 1:
            grads_out = put_home(2 * GROUP, early + late)
            parts, path_out, grads_out = lax.optimization_barrier((parts, path_out, grads_out))
        rows >>= len(bits)
        parts = call(
            functools.partial(reduce_kernel, plan, later, len(parts)), shares(rows, later),
            [pltpu.VMEM((rows, channels), F32)], name="reduce_part", scalars=1,
        )(ids, *parts)
    for bits in rounds[::-1]:
        parts = swap([parts[0]] * (1 << len(bits)), bits)
        rows <<= len(bits)
        if bits is rounds[0]:
            break
        parts = call(
            functools.partial(gather_kernel, plan, bits), [(rows, channels)], name="gather_part", scalars=1
        )(ids, *parts)
    row = (1, channels)
    square = (channels, channels)
    grads_all = call(
        functools.partial(unpack_kernel, plan, rounds[0], quantities, statics),
        [w_input.shape, row, w_first.shape, row, row, w_second.shape, row, row, square, square, square, square,
         (9, 2 * quantities, channels), (2 * GROUP, channels)],
        [pltpu.VMEM((rows, channels), F32)], name="unpack", scalars=1,
    )(ids, *parts)
    grads_all = [grad[0] if grad.shape == row else grad for grad in grads_all]
    grads_all[-2] = jnp.swapaxes(grads_all[-2], 1, 2)
    grads_all[-1] = from_groups(grads_all[-1][:, :1], 0, 2, quantities)[:, 0]
    return (path_out, grads_out) + tuple(grads_all)


def solution(mesh):
    weights = (P(),) * 14
    return jax.shard_map(
        on_device,
        mesh=mesh,
        in_specs=(P("dp", None, None), P(), P("dp", None), P("section", "dp", None, None)) + weights,
        out_specs=(P("section", "dp", None, None), P("section", "dp", None, None)) + weights,
        check_vma=False,
    )
```

```python
import functools
import math

import jax
import jax.numpy as jnp
from jax import lax
from jax.experimental import pallas as pl
from jax.experimental.pallas import tpu as pltpu
from jax.sharding import PartitionSpec as P

HEADS = 4
LAT = 16
ATT_ROWS = 8
EPSILON = 1e-05
LOG2_E = 1.0 / math.log(2.0)
F32 = jnp.float32
BF16 = jnp.bfloat16
GROUP = 8


def dot(left, right, left_dim=1, right_dim=0):
    return lax.dot_general(
        left, right, (((left_dim,), (right_dim,)), ((), ())), preferred_element_type=F32
    )


def halves(value):
    high = value.astype(BF16)
    return high, (value - high.astype(F32)).astype(BF16)


def stacked(value):
    return jnp.concatenate(halves(value), axis=0)


def beside(value):
    return jnp.concatenate(halves(value), axis=1)


def folded(value, axis):
    size = value.shape[axis] // 2
    if axis == 0:
        return value[:size] + value[size:]
    return value[:, :size] + value[:, size:]


def cells_of(value):
    return lax.broadcasted_iota(jnp.int32, value.shape, value.ndim - 1)


def lon_moved(value, offset, lon):
    cells = value.shape[1]
    column = lax.rem(cells_of(value), lon)
    near = pltpu.roll(value, (-offset) % cells, 1)
    wrapped = pltpu.roll(value, (offset * (lon - 1)) % cells, 1)
    edge = lon - 1 if offset > 0 else 0
    return jnp.where(column == edge, wrapped, near)


def lat_moved(value, offset, lon):
    cells = value.shape[1]
    moved = pltpu.roll(value, (-offset * lon) % cells, 1)
    cell = cells_of(value)
    if offset > 0:
        return jnp.where(cell < cells - lon, moved, 0.0)
    return jnp.where(cell >= lon, moved, 0.0)


def along_lon(value, lon):
    return 0.5 * (lon_moved(value, 1, lon) - lon_moved(value, -1, lon))


def along_lat(value, lon):
    return 0.5 * (lat_moved(value, 1, lon) - lat_moved(value, -1, lon))


def fill_patches(patches_ref, value, lon):
    cells, channels = value.shape
    planes = value.reshape(cells // lon, lon, channels)
    blank = jnp.zeros((lon, patches_ref.shape[1]), BF16)
    patches_ref[:lon] = blank
    patches_ref[lon + cells :] = blank
    for place, offset in enumerate((-1, 0, 1)):
        moved = value
        if offset:
            moved = pltpu.roll(planes, (-offset) % lon, 1).reshape(cells, channels)
        high, low = halves(moved)
        start = place * 2 * channels
        patches_ref[lon : lon + cells, start : start + channels] = high
        patches_ref[lon : lon + cells, start + channels : start + 2 * channels] = low


def doubled(weight_ref, channels):
    taps = weight_ref.shape[0] // channels
    rows = [weight_ref[tap * channels : (tap + 1) * channels] for tap in range(taps) for unused in range(2)]
    return jnp.concatenate(rows, axis=0)


def conv_patches(patches_ref, weight_ref, lon):
    cells = patches_ref.shape[0] - 2 * lon
    rows = [patches_ref[lon * place : lon * place + cells] for place in range(3)]
    channels = patches_ref.shape[1] // 6
    return folded(dot(jnp.concatenate(rows, axis=1), doubled(weight_ref, channels)), 1)


def sigmoid(value):
    return 1.0 / (1.0 + jnp.exp(-value))


def norm_of(sums, gain, count):
    mean = sums[0:1] / count
    spread = sums[1:2] / count - mean * mean
    scale = lax.rsqrt(spread + EPSILON)
    return mean, scale, gain * scale


def sums_of(value, other):
    total = jnp.sum(value, axis=0, keepdims=True)
    product = jnp.sum(value * other, axis=0, keepdims=True)
    row = lax.broadcasted_iota(jnp.int32, (GROUP, value.shape[1]), 0)
    return jnp.where(row == 0, total, jnp.where(row == 1, product, 0.0))


def inlet_channels(state, lon):
    amount = state[:GROUP]
    groups = jnp.concatenate([state, along_lon(amount, lon), along_lat(amount, lon)], axis=0)
    blank = jnp.zeros((GROUP, state.shape[1]), F32)
    return jnp.concatenate(
        [lon_moved(groups, -1, lon), groups, lon_moved(groups, 1, lon), blank], axis=0
    )


def advected(state, step_size, lon):
    amount, east, north = state[:GROUP], state[GROUP : 2 * GROUP], state[2 * GROUP :]
    return amount - step_size * (along_lon(amount * east, lon) + along_lat(amount * north, lon))


def row_products(left_rows, right_rows):
    left_high, left_low = halves(left_rows)
    right_high, right_low = halves(right_rows)
    left = jnp.concatenate([left_high, left_high, left_low, left_low], axis=0)
    right = jnp.concatenate([right_high, right_low, right_high, right_low], axis=0)
    return dot(left, right, 0, 0)


def heads_of(channels, cells, block_size):
    width = channels // HEADS
    return [
        (slice(head * width, (head + 1) * width), slice(start, start + block_size))
        for start in range(0, cells, block_size)
        for head in range(HEADS)
    ]


def of_head(value, rows, other=0.0):
    channel = lax.broadcasted_iota(jnp.int32, value.shape, 1)
    return jnp.where((channel >= rows.start) & (channel < rows.stop), value, other)


def below(rows, offset):
    return slice(rows.start + offset, rows.stop + offset)


def entered_inlet_kernel(plan, lon, ids_ref, own_ref, arrived_ref, *refs):
    state_ref, cot_ref = refs[2], refs[3]
    size = state_ref.shape[0]
    stays = plan.stays(ids_ref[0], ids_ref[1])
    state_ref[...] = jnp.where(stays, own_ref[:size], arrived_ref[:size])
    cot_ref[...] = jnp.where(stays, own_ref[size:], arrived_ref[size:])
    inlet_kernel(lon, state_ref, *refs[:2], *refs[4:])


def inlet_kernel(
    lon, state_ref, static_ref, weights_ref,
    inner_ref, pre_ref, sums_ref, patches_ref,
):
    w_input_ref = part_of(weights_ref, FORWARD_ROWS, "moving")
    w_first_ref = part_of(weights_ref, FORWARD_ROWS, "first")
    cells = state_ref.shape[1]
    moving = inlet_channels(state_ref[...], lon).T
    width = patches_ref.shape[1]
    blank = jnp.zeros((lon, width), BF16)
    patches_ref[:lon] = blank
    patches_ref[lon + cells :] = blank
    patches_ref[lon : lon + cells, :256] = beside(moving)
    rows = [patches_ref[lon * place : lon * place + cells, :256] for place in range(3)]
    inner = folded(dot(jnp.concatenate(rows, axis=1), doubled(w_input_ref, width // 6)), 1) + static_ref[...]
    inner_ref[...] = inner
    fill_patches(patches_ref, inner * sigmoid(inner), lon)
    pre = conv_patches(patches_ref, w_first_ref, lon)
    pre_ref[...] = pre
    sums_ref[...] = sums_of(pre, pre)


def middle_kernel(
    lon, count, pre_one_ref, sums_one_ref, vectors_ref, weights_ref,
    pre_ref, sums_ref, patches_ref,
):
    w_second_ref = part_of(weights_ref, FORWARD_ROWS, "second")
    mean, unused_scale, factor = norm_of(sums_one_ref[...], vectors_ref[0:1], count)
    normed = (pre_one_ref[...] - mean) * factor + vectors_ref[1:2]
    fill_patches(patches_ref, normed * sigmoid(normed), lon)
    pre = conv_patches(patches_ref, w_second_ref, lon)
    pre_ref[...] = pre
    sums_ref[...] = sums_of(pre, pre)


def act_two_of(inner, pre_two, sums, gain, shift, count):
    mean, unused_scale, factor = norm_of(sums, gain, count)
    return inner * sigmoid(inner) + (pre_two - mean) * factor + shift


def project(w_qkv_ref, act_two_halves, head_width, qkv_ref):
    channels = act_two_halves.shape[0] // 2
    rows = folded(dot(w_qkv_ref[...], act_two_halves), 0)
    qkv_ref[:channels] = rows[:channels] * (LOG2_E / math.sqrt(head_width))
    qkv_ref[channels:] = rows[channels:]


def outlet_kernel(
    lon, count, block_size, step_size, quantities,
    state_ref, inner_ref, pre_two_ref, sums_two_ref, vectors_ref,
    weights_ref,
    out_ref, packed_ref, mixed_ref, top_ref, weight_ref,
    query_ref,
):
    cells, channels = inner_ref.shape
    w_mixer_ref = part_of(weights_ref, FORWARD_ROWS, "mixer")
    w_velocity_ref = part_of(weights_ref, FORWARD_ROWS, "out")
    w_heads = side_by_side(part_of(weights_ref, FORWARD_ROWS, "heads"), channels)
    act_two = act_two_of(
        inner_ref[...], pre_two_ref[...], sums_two_ref[...], vectors_ref[2:3], vectors_ref[3:4], count
    )
    projected = folded(dot(beside(act_two), jnp.concatenate([w_heads, w_heads], axis=0)), 1)
    query = projected[:, : HEADS * channels]
    query_high = query.astype(BF16).astype(F32)
    channel = lax.rem(lax.broadcasted_iota(jnp.int32, query.shape, 1), channels)
    query_ref[...] = jnp.where(channel < channels // 2, query_high, query - query_high).astype(BF16)
    key = projected[:, HEADS * channels : (HEADS + 1) * channels]
    key_high, key_low = halves((key * (LOG2_E / math.sqrt(channels // HEADS))).T)
    value = projected[:, (HEADS + 1) * channels :]
    heads = heads_of(channels, cells, block_size)

    def scores_of(turn):
        rows, lanes = heads[turn]
        right = [half[rows, lanes] for half in (key_high, key_low, key_high, key_low)]
        start = turn % HEADS * channels
        return dot(query_ref[lanes, start : start + channels], jnp.concatenate(right, axis=0))

    following = scores_of(0)
    for turn, (rows, lanes) in enumerate(heads):
        scores = following
        if turn + 1 < len(heads):
            following = scores_of(turn + 1)
        top = jnp.max(scores, axis=1, keepdims=True)
        powers = jnp.exp2(scores - top)
        weight = 1.0 / jnp.sum(powers, axis=1, keepdims=True)
        high, low = halves(powers)
        right = beside(of_head(value[lanes], rows))
        own = folded(dot(high, right) + dot(low, right), 1) * weight
        all_top, all_weight = [jnp.broadcast_to(part, own.shape) for part in (top, weight)]
        if rows.start:
            own = own + mixed
            all_top, all_weight = of_head(all_top, rows, tops), of_head(all_weight, rows, weights)
        mixed, tops, weights = own, all_top, all_weight
        if rows.stop == channels:
            mixed_ref[lanes], top_ref[lanes], weight_ref[lanes] = mixed, tops, weights
    act_three = act_two + folded(dot(beside(mixed_ref[...]), doubled(w_mixer_ref, channels)), 1)
    parts = folded(dot(w_velocity_ref[...], stacked(act_three.T)), 0)
    forcing = jnp.concatenate([vectors_ref[GROUP:]] * (cells // channels), axis=1)
    for column, lon_offset in enumerate((-1, 0, 1)):
        total = None
        for row, lat_offset in enumerate((-1, 0, 1)):
            start = (row * 3 + column) * 2 * GROUP
            part = parts[start : start + 2 * GROUP]
            if lat_offset:
                part = lat_moved(part, lat_offset, lon)
            total = part if total is None else total + part
        forcing = forcing + (lon_moved(total, lon_offset, lon) if lon_offset else total)
    state = state_ref[...]
    flows = state[GROUP:]
    out_ref[:GROUP] = advected(state, step_size, lon)
    out_ref[GROUP:] = flows + step_size * (forcing - flows)
    put_packed(packed_ref, out_ref[...], quantities)


def outlet_back_kernel(
    lon, count, block_size, step_size, quantities, sections, step,
    ids_ref,
    state_ref, d_next_ref, cots_ref, inner_ref, pre_two_ref, sums_two_ref, vectors_ref,
    mixed_ref, top_ref, weight_ref,
    weights_ref,
    acc_qkv_ref, acc_mixer_ref, acc_velocity_ref, acc_small_ref,
    d_state_ref, d_two_ref, sums_ref,
    out_qkv_ref, out_mixer_ref, out_velocity_ref, out_small_ref,
    d_mixed_ref, d_qkv_ref, seed_ref, qkv_ref, mixed_rows_ref, top_rows_ref,
):
    channels = inner_ref.shape[1]
    back = functools.partial(part_of, weights_ref, BACK_ROWS)
    w_qkv_ref, w_mixer_ref, w_mixer_back_ref = back("qkv"), back("mixer"), back("mixer_back")
    w_qkv_back = side_by_side(back("qkv_back"), 2 * channels)
    w_velocity_back = side_by_side(back("out_back"), 2 * channels)[:, : 36 * GROUP]
    cells = inner_ref.shape[0]
    heads = heads_of(channels, cells, block_size)

    state = state_ref[...]
    packed = cots_ref[lax.rem(ids_ref[0] - step + sections, sections)]
    put_groups(seed_ref, packed[: 3 * quantities])
    seed = seed_ref[...] + d_next_ref[...]
    amount, east, north = state[:GROUP], state[GROUP : 2 * GROUP], state[2 * GROUP :]
    d_amount = seed[:GROUP]
    d_lon = step_size * along_lon(d_amount, lon)
    d_lat = step_size * along_lat(d_amount, lon)
    d_state_ref[:GROUP] = d_amount + d_lon * east + d_lat * north
    d_state_ref[GROUP : 2 * GROUP] = (1.0 - step_size) * seed[GROUP : 2 * GROUP] + d_lon * amount
    d_state_ref[2 * GROUP :] = (1.0 - step_size) * seed[2 * GROUP :] + d_lat * amount
    d_forcing = step_size * seed[GROUP:]
    pieces = []
    for lat_offset in (-1, 0, 1):
        moved_rows = lat_moved(d_forcing, -lat_offset, lon) if lat_offset else d_forcing
        for lon_offset in (-1, 0, 1):
            pieces.append(lon_moved(moved_rows, -lon_offset, lon) if lon_offset else moved_rows)
    d_parts = stacked(jnp.concatenate(pieces, axis=0))
    d_three = folded(dot(w_velocity_back, d_parts), 0)
    d_three_halves = stacked(d_three)
    d_mixed_ref[...] = folded(dot(w_mixer_back_ref[...], d_three_halves), 0) * weight_ref[...].T
    mixed_rows_ref[...] = mixed_ref[...].T
    top_rows_ref[...] = top_ref[...].T
    act_two = act_two_of(
        inner_ref[...], pre_two_ref[...], sums_two_ref[...], vectors_ref[2:3], vectors_ref[3:4], count
    ).T
    act_two_halves = stacked(act_two)
    project(w_qkv_ref, act_two_halves, channels // HEADS, qkv_ref)
    d_mixed_cells = d_mixed_ref[...].T
    query_cells = qkv_ref[:channels].T

    def products_of(turn):
        rows, lanes = heads[turn]
        scores = row_products(qkv_ref[below(rows, channels), lanes], qkv_ref[rows, lanes])
        return scores, row_products(qkv_ref[below(rows, 2 * channels), lanes], d_mixed_ref[rows, lanes])

    following = products_of(0)
    for turn, (rows, lanes) in enumerate(heads):
        scores, d_powers = following
        if turn + 1 < len(heads):
            following = products_of(turn + 1)
        inner_sum = jnp.sum(d_mixed_ref[rows, lanes] * mixed_rows_ref[rows, lanes], axis=0, keepdims=True)
        powers = jnp.exp2(scores - top_rows_ref[rows.start : rows.start + 1, lanes])
        power_high, power_low = halves(powers)
        d_high, d_low = halves(powers * (d_powers - inner_sum))
        right = beside(of_head(d_mixed_cells[lanes], rows))
        d_value = dot(power_high, right) + dot(power_low, right) + (d_value if rows.start else 0.0)
        right = beside(of_head(query_cells[lanes], rows))
        d_key = dot(d_high, right) + dot(d_low, right) + (d_key if rows.start else 0.0)
        key_halves = stacked(qkv_ref[below(rows, channels), lanes])
        d_query = folded(dot(key_halves, d_high) + dot(key_halves, d_low), 0)
        d_qkv_ref[rows, lanes] = d_query * (1.0 / math.sqrt(channels // HEADS))
        if rows.stop == channels:
            d_qkv_ref[channels : 2 * channels, lanes] = folded(d_key, 1).T * (1.0 / LOG2_E)
            d_qkv_ref[2 * channels :, lanes] = folded(d_value, 1).T
    d_qkv_halves = stacked(d_qkv_ref[...])
    d_two = (d_three + folded(dot(w_qkv_back, d_qkv_halves), 0)).T
    d_two_ref[...] = d_two
    mean, scale, unused_factor = norm_of(sums_two_ref[...], vectors_ref[2:3], count)
    sums = sums_of(d_two, pre_two_ref[...] - mean)
    sums_ref[...] = sums

    def pairs(left, right):
        return folded(folded(dot(left, right, 1, 1), 0), 1)

    mixed_halves = stacked(mixed_rows_ref[...])
    act_three = act_two + folded(dot(w_mixer_ref[...], mixed_halves), 0)
    out_velocity_ref[...] = acc_velocity_ref[...] + pairs(d_parts, stacked(act_three))
    out_mixer_ref[...] = acc_mixer_ref[...] + pairs(mixed_halves, d_three_halves)
    out_qkv_ref[...] = acc_qkv_ref[...] + pairs(act_two_halves, d_qkv_halves)
    bias = jnp.sum(d_forcing, axis=1, keepdims=True)
    row = lax.broadcasted_iota(jnp.int32, (GROUP, channels), 0)
    small = jnp.where(row == 0, sums[1:2] * scale, jnp.where(row == 1, sums[0:1], 0.0))
    out_small_ref[:GROUP] = acc_small_ref[:GROUP] + small
    out_small_ref[GROUP:] = acc_small_ref[GROUP:] + bias


def d_pre_of(d_normed, centred, sums, all_grad_sums, gain, count):
    unused_mean, scale, factor = norm_of(sums, gain, count)
    d_spread = -0.5 * gain * scale * scale * scale * all_grad_sums[1:2]
    return factor * (d_normed - all_grad_sums[0:1] / count) + (2.0 * d_spread / count) * centred


def weight_pairs(acc_ref, out_ref, left_halves, patches_ref, lon):
    cells = patches_ref.shape[0] - 2 * lon
    width = patches_ref.shape[1] // 3
    for tap in range(9):
        row, column = divmod(8 - tap, 3)
        right = patches_ref[lon * row : lon * row + cells, column * width : (column + 1) * width]
        out_ref[tap] = acc_ref[tap] + folded(folded(dot(left_halves, right), 0), 1)


def middle_back_kernel(
    lon, count,
    d_two_ref, pre_two_ref, sums_two_ref, all_two_ref,
    pre_one_ref, sums_one_ref, vectors_ref, weights_ref,
    acc_small_ref,
    d_normed_ref, sums_ref, act_ref, patches_ref, out_small_ref,
):
    w_second_back_ref = part_of(weights_ref, BACK_ROWS, "second")
    sums_two = sums_two_ref[...]
    d_pre = d_pre_of(
        d_two_ref[...], pre_two_ref[...] - sums_two[0:1] / count, sums_two, all_two_ref[...],
        vectors_ref[2:3], count,
    )
    fill_patches(patches_ref, d_pre, lon)
    d_act = conv_patches(patches_ref, w_second_back_ref, lon)
    mean, scale, factor = norm_of(sums_one_ref[...], vectors_ref[0:1], count)
    centred = pre_one_ref[...] - mean
    normed = centred * factor + vectors_ref[1:2]
    gate = sigmoid(normed)
    d_normed = d_act * gate * (1.0 + normed * (1.0 - gate))
    d_normed_ref[...] = d_normed
    sums = sums_of(d_normed, centred)
    sums_ref[...] = sums
    act_ref[...] = normed * gate
    row = lax.broadcasted_iota(jnp.int32, sums.shape, 0)
    small = jnp.where(row == 0, sums[1:2] * scale, jnp.where(row == 1, sums[0:1], 0.0))
    out_small_ref[...] = acc_small_ref[...] + small


def middle_grads_kernel(lon, act_ref, patches_ref, acc_ref, out_ref):
    weight_pairs(acc_ref, out_ref, stacked(act_ref[...].T), patches_ref, lon)


def inlet_grads_kernel(
    lon, act_ref, patches_ref, d_inner_ref, state_ref, acc_first_ref, acc_input_ref, acc_inner_ref,
    out_first_ref, out_input_ref, out_inner_ref, rows_ref,
):
    weight_pairs(acc_first_ref, out_first_ref, stacked(act_ref[...].T), patches_ref, lon)
    d_inner = d_inner_ref[...]
    out_inner_ref[...] = acc_inner_ref[...] + d_inner
    cells = d_inner.shape[0]
    blank = jnp.zeros((lon, rows_ref.shape[1]), BF16)
    rows_ref[:lon] = blank
    rows_ref[lon + cells :] = blank
    rows_ref[lon : lon + cells] = beside(d_inner)
    moving_halves = stacked(inlet_channels(state_ref[...], lon))
    for place in range(3):
        start = lon * (2 - place)
        out_input_ref[place] = acc_input_ref[place] + folded(
            folded(dot(moving_halves, rows_ref[start : start + cells]), 0), 1
        )


def inlet_back_kernel(
    lon, count, quantities,
    d_normed_ref, pre_one_ref, sums_one_ref, all_one_ref, vectors_ref,
    inner_ref, d_two_ref, d_state_in_ref, weights_ref,
    d_state_ref, packed_ref, act_ref, patches_ref, d_inner_ref,
    rows_ref,
):
    cells = inner_ref.shape[0]
    w_first_back_ref = part_of(weights_ref, BACK_ROWS, "first")
    w_input_back_ref = part_of(weights_ref, BACK_ROWS, "moving")
    sums_one = sums_one_ref[...]
    d_pre = d_pre_of(
        d_normed_ref[...], pre_one_ref[...] - sums_one[0:1] / count, sums_one, all_one_ref[...],
        vectors_ref[0:1], count,
    )
    fill_patches(patches_ref, d_pre, lon)
    d_act = conv_patches(patches_ref, w_first_back_ref, lon) + d_two_ref[...]
    inner = inner_ref[...]
    gate = sigmoid(inner)
    d_inner = d_act * gate * (1.0 + inner * (1.0 - gate))
    act_ref[...] = inner * gate
    d_inner_ref[...] = d_inner
    blank = jnp.zeros((lon, rows_ref.shape[1]), BF16)
    rows_ref[:lon] = blank
    rows_ref[lon + cells :] = blank
    rows_ref[lon : lon + cells] = beside(d_inner)
    rows = [rows_ref[lon * place : lon * place + cells] for place in range(3)]
    d_moving = folded(dot(jnp.concatenate(rows, axis=1), doubled(w_input_back_ref, inner_ref.shape[1])), 1).T
    size = 5 * GROUP
    d_groups = (
        lon_moved(d_moving[:size], 1, lon)
        + d_moving[size : 2 * size]
        + lon_moved(d_moving[2 * size : 3 * size], -1, lon)
    )
    d_state = d_state_in_ref[...] + d_groups[: 3 * GROUP]
    d_state_ref[:GROUP] = (
        d_state[:GROUP]
        - along_lon(d_groups[3 * GROUP : 4 * GROUP], lon)
        - along_lat(d_groups[4 * GROUP :], lon)
    )
    d_state_ref[GROUP:] = d_state[GROUP:]
    put_packed(packed_ref, d_state_ref[...], quantities)


def put_groups(out_ref, rows):
    size = rows.shape[0] // 3
    out_ref[...] = jnp.zeros(out_ref.shape, F32)
    for group in range(3):
        out_ref[group * GROUP : group * GROUP + size] = rows[group * size : (group + 1) * size]


def put_packed(out_ref, grouped, size):
    out_ref[...] = jnp.zeros(out_ref.shape, F32)
    for group in range(3):
        out_ref[group * size : (group + 1) * size] = grouped[group * GROUP : group * GROUP + size]


def fetched(far_refs, near_refs, done_ref):
    copies = [
        pltpu.make_async_copy(far_ref, near_ref, done_ref.at[place])
        for place, (far_ref, near_ref) in enumerate(zip(far_refs, near_refs))
    ]
    for copy in copies:
        copy.start()
    return copies


def enter_kernel(plan, ids_ref, order_ref, state_ref, cot_ref, *refs):
    out_refs, (near_ref, near_cot_ref, rows_ref, done_ref) = refs[:-4], refs[-4:]
    copies = fetched([state_ref, cot_ref], [near_ref, near_cot_ref], done_ref)
    size = rows_ref.shape[0]
    copies[0].wait()
    place = order_ref[0, plan.slot(ids_ref[0], ids_ref[1])]
    for row in range(size):
        rows_ref[row : row + 1] = near_ref[row, pl.ds(place, 1)]
    put_groups(out_refs[0].at[: 3 * GROUP], rows_ref[...])
    copies[1].wait()
    for steps, out_ref in enumerate(out_refs):
        start = 0 if steps else 3 * GROUP
        target = lax.rem(ids_ref[0] + steps, plan.sections)
        place = order_ref[0, plan.slot(target, ids_ref[1])]
        out_ref[start:] = jnp.zeros((2 * GROUP, out_ref.shape[1]), F32)
        for row in range(size):
            out_ref[start + row : start + row + 1] = near_cot_ref[row, pl.ds(place, 1)]


def leave_kernel(plan, ids_ref, *refs):
    values_ref = refs[-1]
    size = refs[0].shape[0]
    for step in range(plan.sections):
        values_ref[step, :size] = refs[step][...]
        if step:
            values_ref[step, size:] = refs[plan.sections + step - 1][...]
        else:
            values_ref[step, size:] = jnp.zeros(refs[0].shape, F32)
    for steps, out_ref in enumerate(refs[2 * plan.sections - 1 : -1]):
        out_ref[...] = values_ref[lax.rem(ids_ref[0] + steps, plan.sections)]


def arrive_kernel(plan, start, ids_ref, order_ref, kept_ref, *refs):
    section, dp = ids_ref[0], ids_ref[1]
    out_ref = refs[-1]
    size = kept_ref.shape[0] // 2
    early, late = refs[: plan.sections], refs[plan.sections : -1]
    if late:
        kept_late_ref, *late = late
    for steps, ref in enumerate(early):
        source = lax.rem(section - steps + plan.sections, plan.sections)
        place = order_ref[0, plan.slot(source, dp)]
        value = ref[start : start + size]
        if late:
            value = jnp.where(section == 0, late[steps][...], value)
        if plan.halved and not steps:
            kept = kept_ref[start : start + size]
            if late:
                kept = jnp.where(section == 0, kept_late_ref[...], kept)
            value = jnp.where(plan.stays(section, dp), kept, value)
        for row in range(out_ref.shape[0]):
            out_ref[row, pl.ds(place, 1)] = value[row : row + 1]


def put_conv_weight(out_ref, taps):
    for tap, weight in enumerate(taps):
        rows = weight.shape[0]
        out_ref[tap * rows : (tap + 1) * rows] = beside(weight)


def weights_kernel(
    lon, quantities,
    w_input_ref, maps_ref, b_input_ref, w_first_ref, w_second_ref,
    w_query_ref, w_key_ref, w_value_ref, w_mixer_ref, w_velocity_ref,
    gain_one_ref, shift_one_ref, gain_two_ref, shift_two_ref, b_velocity_ref,
    static_part_ref, forward_ref, back_ref, vectors_ref,
    patches_ref, weight_ref, taps_ref, rows_ref, *near_refs,
):
    forward = functools.partial(part_of, forward_ref, FORWARD_ROWS)
    back = functools.partial(part_of, back_ref, BACK_ROWS)
    near_refs, done_ref = near_refs[:-1], near_refs[-1]
    copies = fetched(
        [w_input_ref, maps_ref, b_input_ref, w_first_ref, w_second_ref,
         w_query_ref, w_key_ref, w_value_ref, w_mixer_ref, w_velocity_ref,
         gain_one_ref, shift_one_ref, gain_two_ref, shift_two_ref, b_velocity_ref],
        near_refs, done_ref,
    )
    (
        w_input_ref, maps_ref, b_input_ref, w_first_ref, w_second_ref,
        w_query_ref, w_key_ref, w_value_ref, w_mixer_ref, w_velocity_ref,
        gain_one_ref, shift_one_ref, gain_two_ref, shift_two_ref, b_velocity_ref,
    ) = near_refs
    channels = w_input_ref.shape[2]
    moving = 5 * quantities
    statics = maps_ref.shape[0]
    taps_ref[...] = jnp.zeros(taps_ref.shape, F32)
    rows_ref[...] = jnp.zeros(rows_ref.shape, F32)
    copies[0].wait()
    for tap in range(9):
        row, column = divmod(tap, 3)
        for group in range(5):
            start = (column * 5 + group) * GROUP
            taps_ref[9 + row, start : start + quantities] = w_input_ref[
                tap, group * quantities : (group + 1) * quantities
            ]
        taps_ref[tap, :statics] = w_input_ref[tap, moving:]
    put_conv_weight(forward("moving"), [taps_ref[9 + row] for row in range(3)])
    put_conv_weight(back("moving"), [taps_ref[11 - row].T for row in range(3)])
    put_conv_weight(weight_ref, [taps_ref[tap] for tap in range(9)])
    copies[1].wait()
    copies[2].wait()
    maps = jnp.concatenate(
        [maps_ref[...], jnp.zeros((channels - statics, maps_ref.shape[1]), F32)], axis=0
    )
    fill_patches(patches_ref, maps.T, lon)
    static_part_ref[...] = conv_patches(patches_ref, weight_ref, lon) + b_input_ref[...]
    for copy in copies[3:]:
        copy.wait()
    put_conv_weight(forward("first"), [w_first_ref[tap] for tap in range(9)])
    put_conv_weight(forward("second"), [w_second_ref[tap] for tap in range(9)])
    put_conv_weight(back("first"), [w_first_ref[8 - tap].T for tap in range(9)])
    put_conv_weight(back("second"), [w_second_ref[8 - tap].T for tap in range(9)])
    parts = [ref[...] for ref in (w_query_ref, w_key_ref, w_value_ref)]
    turned = [part.T for part in parts]
    width = channels // HEADS
    repeated = [turned[0][head * width : (head + 1) * width] for head in range(HEADS) for unused in range(HEADS)]
    heads = jnp.concatenate([jnp.concatenate(repeated, axis=0).T, parts[1], parts[2]], axis=1)
    put_blocks(forward("heads"), beside(heads))
    put_conv_weight(forward("mixer"), [w_mixer_ref[...]])
    back("qkv")[...] = left_form(jnp.concatenate(turned, axis=0))
    put_blocks(back("qkv_back"), left_form(jnp.concatenate(parts, axis=1)))
    back("mixer")[...] = left_form(w_mixer_ref[...].T)
    back("mixer_back")[...] = left_form(w_mixer_ref[...])
    for tap in range(9):
        for group in range(2):
            start = (tap * 2 + group) * GROUP
            rows_ref[start : start + quantities] = w_velocity_ref[
                tap, group * quantities : (group + 1) * quantities
            ]
    size = 18 * GROUP
    vectors_ref[...] = jnp.zeros(vectors_ref.shape, F32)
    for place, ref in enumerate((gain_one_ref, shift_one_ref, gain_two_ref, shift_two_ref)):
        vectors_ref[place : place + 1] = ref[...]
    bias = jnp.concatenate([b_velocity_ref[...], jnp.zeros((1, channels - 2 * quantities), F32)], axis=1)
    bias = jnp.broadcast_to(bias, (channels, channels)).T
    for group in range(2):
        start = (group + 1) * GROUP
        vectors_ref[start : start + quantities] = bias[group * quantities : (group + 1) * quantities]
    forward("out")[...] = left_form(rows_ref[:size])
    put_blocks(back("out_back"), left_form(rows_ref[...].T[:, :size]))


def index_of(ids_ref, plan, bits):
    own = ids_ref[0] * plan.dp + ids_ref[1]
    return sum(lax.rem(own // bit, 2) << place for place, bit in enumerate(bits))


def deal(total_ref, own, out_refs):
    rows = out_refs[0].shape[0]
    for turn, out_ref in enumerate(out_refs):
        out_ref[...] = total_ref[pl.ds(pl.multiple_of((own ^ turn) * rows, GROUP), rows)]


def pack_kernel(
    plan, bits, lon, statics, ids_ref, maps_ref, inner_ref, first_ref, second_ref, moving_ref,
    qkv_ref, mixer_ref, velocity_ref, small_one_ref, small_two_ref, *refs,
):
    out_refs, total_ref, patches_ref = refs[:-2], refs[-2], refs[-1]
    cells, channels = inner_ref.shape
    d_inner = inner_ref[...]
    fill_patches(patches_ref, d_inner, lon)
    width = patches_ref.shape[1] // 3
    maps = maps_ref[...]
    blank = jnp.zeros((-statics % GROUP, cells), F32)
    maps = jnp.concatenate([maps, blank], axis=0)
    rows = maps.shape[0]
    left = jnp.concatenate(halves(maps), axis=0)
    start = 0

    def put(value):
        nonlocal start
        total_ref[start : start + value.shape[0]] = value
        start += value.shape[0]

    for tap in range(9):
        put(first_ref[tap])
    for tap in range(9):
        put(second_ref[tap])
    for tap in range(9):
        row, column = divmod(8 - tap, 3)
        right = patches_ref[lon * row : lon * row + cells, column * width : (column + 1) * width]
        put(folded(folded(dot(left, right), 0), 1))
    for place in range(3):
        put(moving_ref[place, : 15 * GROUP])
    for part in range(3):
        put(qkv_ref[:, part * channels : (part + 1) * channels])
    put(mixer_ref[...])
    put(velocity_ref[...])
    put(small_one_ref[...])
    put(small_two_ref[...])
    put(jnp.zeros((GROUP, channels), F32) + jnp.sum(d_inner, axis=0, keepdims=True))
    total_ref[start:] = jnp.zeros((total_ref.shape[0] - start, channels), F32)
    deal(total_ref, index_of(ids_ref, plan, bits), out_refs)


def reduce_kernel(plan, bits, count, ids_ref, *refs):
    total_ref = refs[-1]
    total = refs[0][...]
    for ref in refs[1:count]:
        total = total + ref[...]
    if not bits:
        refs[count][...] = total
        return
    total_ref[...] = total
    deal(total_ref, index_of(ids_ref, plan, bits), refs[count:-1])


def gather_rows(plan, bits, ids_ref, part_refs, out_ref):
    own = index_of(ids_ref, plan, bits)
    rows = part_refs[0].shape[0]
    for turn, ref in enumerate(part_refs):
        out_ref[pl.ds(pl.multiple_of((own ^ turn) * rows, GROUP), rows)] = ref[...]


def gather_kernel(plan, bits, ids_ref, *refs):
    gather_rows(plan, bits, ids_ref, refs[:-1], refs[-1])


def unpack_kernel(
    plan, bits, quantities, statics, ids_ref, *refs,
):
    count = 1 << len(bits)
    (
        input_ref, bias_ref, first_ref, gain_one_ref, shift_one_ref, second_ref, gain_two_ref, shift_two_ref,
        query_ref, key_ref, value_ref, mixer_ref, velocity_ref, velocity_bias_ref, total_ref,
    ) = refs[count:]
    gather_rows(plan, bits, ids_ref, refs[:count], total_ref)
    channels = mixer_ref.shape[0]
    moving = 5 * quantities
    start = 0

    def take(rows):
        nonlocal start
        start += rows
        return total_ref[start - rows : start]

    for tap in range(9):
        first_ref[tap] = take(channels)
    for tap in range(9):
        second_ref[tap] = take(channels)
    for tap in range(9):
        input_ref[tap, moving:] = take(statics + -statics % GROUP)[:statics]
    for row in range(3):
        for column in range(3):
            for group in range(5):
                rows = take(GROUP)
                input_ref[row * 3 + column, group * quantities : (group + 1) * quantities] = rows[:quantities]
    query_ref[...] = take(channels)
    key_ref[...] = take(channels)
    value_ref[...] = take(channels)
    mixer_ref[...] = take(channels)
    for tap in range(9):
        for group in range(2):
            velocity_ref[tap, group * quantities : (group + 1) * quantities] = take(GROUP)[:quantities]
    small = take(GROUP)
    gain_one_ref[...], shift_one_ref[...] = small[0:1], small[1:2]
    small = take(GROUP)
    gain_two_ref[...], shift_two_ref[...] = small[0:1], small[1:2]
    velocity_bias_ref[...] = take(2 * GROUP)
    bias_ref[...] = take(GROUP)[0:1]


def call(kernel, outs, scratch=(), aliases=None, name=None, scalars=0, kinds=None, far_in=(), limit=None):
    kinds = kinds or [F32] * len(outs)

    def run(*operands):
        places = [pltpu.SMEM] * scalars + [pltpu.VMEM] * (len(operands) - scalars)
        for place in far_in:
            places[place] = pltpu.HBM
        return pl.pallas_call(
            kernel,
            out_shape=tuple(jax.ShapeDtypeStruct(shape, kind) for shape, kind in zip(outs, kinds)),
            in_specs=[pl.BlockSpec(memory_space=place) for place in places],
            out_specs=tuple(pl.BlockSpec(memory_space=pltpu.VMEM) for unused in outs),
            scratch_shapes=scratch,
            input_output_aliases=aliases or {},
            compiler_params=pltpu.CompilerParams(vmem_limit_bytes=limit or VMEM_LIMIT),
            name=name,
        )(*operands)

    return run


VMEM_LIMIT = 24 * 1024 * 1024
ALONE_LIMIT = 56 * 1024 * 1024

FORWARD_ROWS = dict(moving=384, first=1152, second=1152, heads=768, mixer=128, out=288)
BACK_ROWS = dict(moving=384, first=1152, second=1152, qkv=768, mixer=256, mixer_back=256, qkv_back=768, out_back=512)


def part_of(ref, rows, name):
    start = 0
    for other, size in rows.items():
        if other == name:
            return ref.at[start : start + size]
        start += size
    return None


def side_by_side(ref, rows):
    return jnp.concatenate([ref[start : start + rows] for start in range(0, ref.shape[0], rows)], axis=1)


def put_blocks(ref, value):
    rows, width = value.shape[0], ref.shape[1]
    for place in range(ref.shape[0] // rows):
        block = value[:, place * width : (place + 1) * width]
        if block.shape[1] < width:
            block = jnp.concatenate([block, jnp.zeros((rows, width - block.shape[1]), value.dtype)], axis=1)
        ref[place * rows : (place + 1) * rows] = block


def left_form(weight):
    return jnp.concatenate([jnp.concatenate([half, half], axis=1) for half in halves(weight)], axis=0)


def in_groups(array, axis, groups):
    shape = array.shape
    split = shape[:axis] + (groups, shape[axis] // groups) + shape[axis + 1 :]
    array = array.reshape(split)
    pads = [(0, 0)] * array.ndim
    pads[axis + 1] = (0, GROUP - split[axis + 1])
    return jnp.pad(array, pads).reshape(shape[:axis] + (groups * GROUP,) + shape[axis + 1 :])


def from_groups(array, axis, groups, size):
    shape = array.shape
    array = array.reshape(shape[:axis] + (groups, GROUP) + shape[axis + 1 :])
    array = lax.slice_in_dim(array, 0, size, axis=axis + 1)
    return array.reshape(shape[:axis] + (groups * size,) + shape[axis + 1 :])


class Plan:
    def __init__(self, sections, dp):
        self.sections, self.dp = sections, dp
        self.halved = sections == 4 and dp >= 4
        self.half = dp // 2
        bits = [1 << place for place in range((sections * dp).bit_length() - 1)]
        dp_bits = [bit for bit in bits if bit < dp]
        section_bits = [bit for bit in bits if bit >= dp]
        if self.halved:
            self.sum_rounds = in_pairs(dp_bits[:-1]) + in_pairs(section_bits)
        else:
            self.sum_rounds = in_pairs(dp_bits) + [section_bits[:1]]
        self.all_rounds = [dp_bits[:1]] + in_pairs(section_bits) + [[bit] for bit in dp_bits[1:]]

    def slot(self, section, home):
        if not self.halved:
            return section
        return lax.rem(home // self.half + section // 2 + home, 2) * 2 + lax.rem(section, 2)

    def stays(self, section, dp):
        return lax.rem(section // 2 + dp, 2) == 0

    def other(self, section, dp):
        return dp ^ self.half if self.halved and (section // 2 + dp) % 2 else dp

    def to_workers(self, steps):
        return [
            (section * self.dp + home, self.joint((section + steps) % self.sections, home))
            for section in range(self.sections)
            for home in range(self.dp)
        ]

    def to_homes(self, steps):
        return [
            (section * self.dp + own, (section + steps) % self.sections * self.dp + self.other(section, own))
            for section in range(self.sections)
            for own in range(self.dp)
        ]

    def to_first_home(self, steps):
        return [(source, target) for source, target in self.to_homes(steps) if target < self.dp]

    def joint(self, section, home):
        return section * self.dp + self.other(section, home)


def in_pairs(bits):
    return [bits[start : start + 2] for start in range(0, len(bits), 2)]


def masks_of(bits):
    return [sum(bit for place, bit in enumerate(bits) if turn >> place & 1) for turn in range(1, 1 << len(bits))]


def exchanged(value, mask):
    size = lax.axis_size("section") * lax.axis_size("dp")
    return lax.ppermute(value, ("section", "dp"), [(own, own ^ mask) for own in range(size)])


def moved(value, pairs):
    going = [(source, target) for source, target in pairs if source != target]
    if not going:
        return value
    return lax.ppermute(value, ("section", "dp"), going)


def micro_sum(plan, value, first_core, work=None):
    if not plan.halved or plan.half != 4:
        for bits in plan.sum_rounds:
            value = value + sum(exchanged(value, mask) for mask in masks_of(bits))
        return value, work and work[0](*work[1])
    value = value + exchanged(value, 1)
    if work:
        value, operands = lax.optimization_barrier((value, work[1]))
    plane = masks_of([plan.dp, 2 * plan.dp])
    other = [mask ^ 2 for mask in plane + [0]]
    own = range(plan.sections * plan.dp)
    total = value * first_core
    for turn in range(4):
        pairs = [(device, device ^ other[turn]) for device in own if device & 1]
        if turn < 3:
            pairs += [(device, device ^ plane[turn]) for device in own if not device & 1]
        total = total + lax.ppermute(value, ("section", "dp"), pairs)
    done = None
    if work:
        total, done = lax.optimization_barrier((total, work[0](*operands)))
    return total + exchanged(total, 1), done


def on_device(
    state_start,
    static_maps,
    grouping,
    cotangent,
    w_input,
    b_input,
    w_first,
    gain_first,
    shift_first,
    w_second,
    gain_second,
    shift_second,
    w_query,
    w_key,
    w_value,
    w_mixer,
    w_velocity,
    b_velocity,
):
    segments = lax.axis_size("section")
    plan = Plan(segments, lax.axis_size("dp"))
    micro_count = segments // 2
    per_micro = state_start.shape[0] // micro_count
    cells = state_start.shape[2]
    lon = cells // LAT
    count = float(per_micro * cells * plan.dp)
    step_size = 2.0 / segments
    block_size = ATT_ROWS * lon
    channels = w_first.shape[2]
    quantities = state_start.shape[1] // 3
    statics = static_maps.shape[0]
    ids = jnp.stack([lax.axis_index("section"), lax.axis_index("dp")]).astype(jnp.int32)

    plane = (cells, channels)
    small = (GROUP, channels)
    conv = (9 * channels, 2 * channels)
    patches = pltpu.VMEM((cells + 2 * lon, 6 * channels), BF16)
    wide = pltpu.VMEM((3 * channels, cells), F32)
    narrow = pltpu.VMEM((channels, cells), F32)
    state_shape = (3 * GROUP, cells)

    packed = (2 * GROUP, cells)

    def near(*arrays):
        return [pltpu.VMEM(array.shape, F32) for array in arrays] + [pltpu.SemaphoreType.DMA((len(arrays),))]

    state_rows, cot_rows = jnp.swapaxes(state_start, 0, 1), jnp.swapaxes(cotangent[0], 0, 1)
    entry, *sent_cots = call(
        functools.partial(enter_kernel, plan), [(5 * GROUP, cells)] + [packed] * (segments - 1),
        [pltpu.VMEM(state_rows.shape, F32)] * 2
        + [pltpu.VMEM((3 * quantities, cells), F32), pltpu.SemaphoreType.DMA((2,))],
        name="enter", scalars=2, far_in=[2, 3], limit=ALONE_LIMIT,
    )(ids, grouping, state_rows, cot_rows)
    arrived = moved(entry, plan.to_workers(0))
    first_core = (1.0 - lax.rem(ids[1], 2).astype(F32)) * jnp.ones(small, F32)
    w_velocity_rows = jnp.swapaxes(w_velocity, 1, 2)
    weights = (
        w_input, static_maps, b_input[None], w_first, w_second, w_query, w_key, w_value, w_mixer, w_velocity_rows,
        gain_first[None], shift_first[None], gain_second[None], shift_second[None], b_velocity[None],
    )
    columns = 2 * channels
    static_part, forward_weights, back_weights, vectors = call(
        functools.partial(weights_kernel, lon, quantities),
        [plane, (sum(FORWARD_ROWS.values()), columns), (sum(BACK_ROWS.values()), columns), (3 * GROUP, channels)],
        [patches, pltpu.VMEM(conv, BF16), pltpu.VMEM((12, channels, channels), F32),
         pltpu.VMEM((columns, channels), F32)] + near(*weights),
        name="weights", kinds=[F32, BF16, BF16, F32], far_in=range(15), limit=ALONE_LIMIT,
    )(*weights)

    inlet = call(
        functools.partial(inlet_kernel, lon), [plane, plane, small], [patches], name="inlet"
    )
    middle = call(
        functools.partial(middle_kernel, lon, count), [plane, small], [patches], name="middle"
    )
    outlet = call(
        functools.partial(outlet_kernel, lon, count, block_size, step_size, quantities),
        [state_shape, packed, plane, plane, plane],
        [pltpu.VMEM((cells, HEADS * channels), BF16)], name="outlet",
    )

    def outlet_back(step):
        return call(
            functools.partial(outlet_back_kernel, lon, count, block_size, step_size, quantities, segments, step),
            [state_shape, plane, small, (channels, 3 * channels), (channels, channels),
             (18 * GROUP, channels), (3 * GROUP, channels)],
            [narrow, wide, pltpu.VMEM(state_shape, F32), wide, narrow, narrow],
            {12: 3, 13: 4, 14: 5, 15: 6}, name="outlet_back", scalars=1,
        )

    patch_shape = (cells + 2 * lon, 6 * channels)
    middle_back = call(
        functools.partial(middle_back_kernel, lon, count),
        [plane, small, plane, patch_shape, small],
        aliases={8: 4}, name="middle_back", kinds=[F32, F32, F32, BF16, F32],
    )
    middle_grads = call(
        functools.partial(middle_grads_kernel, lon), [(9, channels, channels)], aliases={2: 0}, name="middle_grads",
    )
    inlet_back = call(
        functools.partial(inlet_back_kernel, lon, count, quantities),
        [state_shape, packed, plane, patch_shape, plane],
        [pltpu.VMEM((cells + 2 * lon, 2 * channels), BF16)], name="inlet_back", kinds=[F32, F32, F32, BF16, F32],
    )
    inlet_grads = call(
        functools.partial(inlet_grads_kernel, lon),
        [(9, channels, channels), (3, channels, channels), plane],
        [pltpu.VMEM((cells + 2 * lon, 2 * channels), BF16)],
        {4: 0, 5: 1, 6: 2}, name="inlet_grads",
    )

    state = entry[: 3 * GROUP]
    path, saved = [], []
    cots = None
    for step in range(segments):
        if not step:
            if not plan.halved:
                arrived = entry
            state, own_cot, inner, pre_one, sums_one = call(
                functools.partial(entered_inlet_kernel, plan, lon), [state_shape, packed, plane, plane, small], [patches],
                name="inlet", scalars=1,
            )(ids, entry, arrived, static_part, forward_weights)
        else:
            inner, pre_one, sums_one = inlet(state, static_part, forward_weights)
        sums_one, unused = micro_sum(plan, sums_one, first_core)
        pre_two, sums_two = middle(pre_one, sums_one, vectors, forward_weights)
        sums_two, unused = micro_sum(plan, sums_two, first_core)
        state_out, state_packed, mixed, top, weight = outlet(
            state, inner, pre_two, sums_two, vectors, forward_weights
        )
        saved.append((state, inner, pre_one, pre_two, sums_one, sums_two, mixed, top, weight))
        path.append(state_packed)
        state = state_out
        if not step:
            state, sent_cots = lax.optimization_barrier((state, sent_cots))
            cots = jnp.stack(
                [own_cot] + [moved(cot, plan.to_workers(steps + 1)) for steps, cot in enumerate(sent_cots)]
            )

    def put_home(start, parts):
        (out,) = call(
            functools.partial(arrive_kernel, plan, start), [state_rows.shape], name="arrive", scalars=2
        )(ids, grouping, *parts)
        return jnp.swapaxes(out, 0, 1)[None]

    acc = dict(
        qkv=jnp.zeros((channels, 3 * channels), F32),
        mixer=jnp.zeros((channels, channels), F32),
        velocity=jnp.zeros((18 * GROUP, channels), F32),
        small_two=jnp.zeros((3 * GROUP, channels), F32),
        second=jnp.zeros((9, channels, channels), F32),
        small_one=jnp.zeros(small, F32),
        first=jnp.zeros((9, channels, channels), F32),
        moving=jnp.zeros((3, channels, channels), F32),
        inner=jnp.zeros(plane, F32),
    )
    d_state = jnp.zeros(state_shape, F32)
    grads = [None] * segments
    inlet_work = None
    path_out = None
    for step in reversed(range(segments)):
        if not step:
            sent = call(
                functools.partial(leave_kernel, plan), [(4 * GROUP, cells)] * segments,
                [pltpu.VMEM((segments, 4 * GROUP, cells), F32)], name="leave", scalars=1,
            )(ids, *path, *grads[1:])
            early = [sent[0]] + [moved(part, plan.to_homes(steps)) for steps, part in enumerate(sent)]
        state, inner, pre_one, pre_two, sums_one, sums_two, mixed, top, weight = saved[step]
        d_partial, d_two, grad_two, acc["qkv"], acc["mixer"], acc["velocity"], acc["small_two"] = outlet_back(step)(
            ids, state, d_state, cots, inner, pre_two, sums_two, vectors,
            mixed, top, weight, back_weights,
            acc["qkv"], acc["mixer"], acc["velocity"], acc["small_two"],
        )
        if not step:
            d_two, grad_two, early = lax.optimization_barrier((d_two, grad_two, early))
            path_out = put_home(0, early)
        work = inlet_work and (inlet_grads, inlet_work + (acc["first"], acc["moving"], acc["inner"]))
        grad_two, done = micro_sum(plan, grad_two, first_core, work)
        if done:
            acc["first"], acc["moving"], acc["inner"] = done
        d_normed, grad_one, act, act_patches, acc["small_one"] = middle_back(
            d_two, pre_two, sums_two, grad_two,
            pre_one, sums_one, vectors, back_weights,
            acc["small_one"],
        )
        grad_one, (acc["second"],) = micro_sum(
            plan, grad_one, first_core, (middle_grads, (act, act_patches, acc["second"]))
        )
        d_state, grads[step], act, act_patches, d_inner = inlet_back(
            d_normed, pre_one, sums_one, grad_one, vectors,
            inner, d_two, d_partial, back_weights,
        )
        inlet_work = (act, act_patches, d_inner, state)
    acc["first"], acc["moving"], acc["inner"] = inlet_grads(*inlet_work, acc["first"], acc["moving"], acc["inner"])
    late = [grads[0]] + [moved(grads[0], plan.to_first_home(steps)) for steps in range(segments)]

    rounds = plan.all_rounds
    rows = 2 * 9 * channels + 9 * (statics + -statics % GROUP) + 45 * GROUP + 4 * channels + 23 * GROUP
    unit = GROUP * segments * plan.dp
    rows = -(-rows // unit) * unit

    def shares(rows, bits):
        return [(rows >> len(bits), channels)] * (1 << len(bits))

    def swap(parts, bits):
        return [parts[0]] + [exchanged(part, mask) for part, mask in zip(parts[1:], masks_of(bits))]

    parts = call(
        functools.partial(pack_kernel, plan, rounds[0], lon, statics), shares(rows, rounds[0]),
        [pltpu.VMEM((rows, channels), F32), patches], name="pack", scalars=1,
    )(
        ids, static_maps, acc["inner"], acc["first"], acc["second"], acc["moving"], acc["qkv"], acc["mixer"],
        acc["velocity"], acc["small_one"], acc["small_two"],
    )
    for place, (bits, later) in enumerate(zip(rounds, rounds[1:] + [[]])):
        parts = swap(parts, bits)
        if not place:
            parts, late = lax.optimization_barrier((parts, late))
        elif place == 1:
            grads_out = put_home(2 * GROUP, early + late)
            parts, path_out, grads_out = lax.optimization_barrier((parts, path_out, grads_out))
        rows >>= len(bits)
        parts = call(
            functools.partial(reduce_kernel, plan, later, len(parts)), shares(rows, later),
            [pltpu.VMEM((rows, channels), F32)], name="reduce_part", scalars=1,
        )(ids, *parts)
    for bits in rounds[::-1]:
        parts = swap([parts[0]] * (1 << len(bits)), bits)
        rows <<= len(bits)
        if bits is rounds[0]:
            break
        parts = call(
            functools.partial(gather_kernel, plan, bits), [(rows, channels)], name="gather_part", scalars=1
        )(ids, *parts)
    row = (1, channels)
    square = (channels, channels)
    grads_all = call(
        functools.partial(unpack_kernel, plan, rounds[0], quantities, statics),
        [w_input.shape, row, w_first.shape, row, row, w_second.shape, row, row, square, square, square, square,
         (9, 2 * quantities, channels), (2 * GROUP, channels)],
        [pltpu.VMEM((rows, channels), F32)], name="unpack", scalars=1,
    )(ids, *parts)
    grads_all = [grad[0] if grad.shape == row else grad for grad in grads_all]
    grads_all[-2] = jnp.swapaxes(grads_all[-2], 1, 2)
    grads_all[-1] = from_groups(grads_all[-1][:, :1], 0, 2, quantities)[:, 0]
    return (path_out, grads_out) + tuple(grads_all)


def solution(mesh):
    weights = (P(),) * 14
    return jax.shard_map(
        on_device,
        mesh=mesh,
        in_specs=(P("dp", None, None), P(), P("dp", None), P("section", "dp", None, None)) + weights,
        out_specs=(P("section", "dp", None, None), P("section", "dp", None, None)) + weights,
        check_vma=False,
    )
```
